32 devices in a mesh: groups: 2 (over x), samples: 8 (over z, y), cols: 2 (over core).
Axes of the slice: x: 2, y: 2, z: 4, core: 2. Of those that a mesh axis runs over, the one named last changes fastest.
Arguments:
- kinship: float32 [64, 4, 128, 128], P(('groups', 'samples')), parts along dimension 0, may hold values from 0 to 0.5, as said below
- relatives: int32 [64, 3], P('groups'), parts along dimension 0, may hold values from -1 to 31, as said below
- variance: float32 [8192], P(('groups', 'samples')), parts along dimension 0, may hold values from 0.5 to 2
- phenotypes: float32 [8192, 512], P(('groups', 'samples'), 'cols'), parts along dimension 0, may hold values from -120 to 120
- dosage: float32 [8192, 1024], P(('groups', 'samples'), 'cols'), parts along dimension 0, may hold values from -5 to 5
Outputs:
- solved: float32 [8192, 512], P(('groups', 'samples'), 'cols'), parts along dimension 0
- scores: float32 [2048, 512], P(('groups', 'cols', 'samples')), parts along dimension 0
The draws below stay inside these ranges and needn't reach their ends.
There are 2 independent parts, one for each index of `groups`. The reference program is written for one: setup_inputs(seed, part) draws one part's arguments, and reference() takes and returns one part's arrays. A program takes and returns all parts, laid end to end along the dimension named above; each array names one. Nothing has to cross between parts.
Inputs may be any that keep to these rules, and one draw needn't show every extreme that they name: `relatives`: each entry names a column block held by another device along samples, or is -1. The row blocks of one device name at most 2 blocks held by any single other device, counted with repetition, and some pair of devices reaches 2. The list is mirrored: row block r names column block c exactly as often as c names r. kinship[r, 1 + k] is zero where relatives[r, k] is -1. Where row block r names column block c with tile W, c names r with tile W transposed, pairing every such entry once. Each kinship[r, 0] is symmetric.
All inputs are finite; a program needn't handle non-finite values.
Results may differ from the reference program's by a relative error of at most 0.0001.
Values sent between devices are 32-bit elements; how exact they have to be, the bound alone decides.
No kernel may reach another device: no remote copies, remote signals or barrier semaphores. Data moves between devices by JAX's collectives and lax.ppermute only.
A program may use at most 128 MiB of HBM per device.

```python
import math
import jax
import jax.numpy as jnp
from jax import lax

TILE = 128
PH = 512
BLK_DEV = 4
ITERS = 2
NB = 32
PEOPLE = 4096
NREL = 3
RELS = 12
VARIANTS = 1024
N_SAMPLES = 8


def layout(key):
    devices = N_SAMPLES
    rounds = devices - 1
    entry_count = RELS
    key_label, key_round, key_turn, key_load, key_anchor = jax.random.split(key, 5)
    labels = jax.random.permutation(key_label, devices)
    inverse = jnp.argsort(labels)
    plan = jax.random.permutation(key_round, rounds)
    offsets = jax.random.randint(key_turn, (devices,), 0, BLK_DEV)
    entry_ids = jnp.arange(entry_count)
    played = plan[entry_ids % rounds][None, :]
    own_label = labels[:, None]
    mate_label = jnp.where(own_label == rounds, played, jnp.where(own_label == played, rounds, (2 * played - own_label) % rounds))
    partner = inverse[mate_label]
    link_loads = jax.random.randint(key_load, (devices,), entry_count // 2, entry_count + 1)
    anchor = jax.random.randint(key_anchor, (), 0, devices)
    second = partner[anchor, 0]
    device = jnp.arange(devices)
    is_full = (device == anchor) | (device == second)
    link_loads = jnp.where(is_full, entry_count, link_loads)
    is_kept = entry_ids[None, :] < jnp.maximum(link_loads[:, None], link_loads[partner])
    return (partner, offsets, is_kept)


def entries(key):
    partner, offsets, is_kept = layout(key)
    devices = N_SAMPLES
    device = jnp.arange(devices)[:, None, None]
    block_ids = jnp.arange(BLK_DEV)[None, :, None]
    position = jnp.arange(NREL)[None, None, :]
    round_ids = position * BLK_DEV + (block_ids - offsets[:, None, None]) % BLK_DEV
    flat_round = round_ids.reshape(devices, -1)
    partner_dev = jnp.take_along_axis(partner, flat_round, axis=1).reshape(round_ids.shape)
    is_live = jnp.take_along_axis(is_kept, flat_round, axis=1).reshape(round_ids.shape)
    mate_block = (round_ids + offsets[partner_dev]) % BLK_DEV
    column = jnp.where(is_live, partner_dev * BLK_DEV + mate_block, -1)
    pair_ids = jnp.minimum(device, partner_dev) * RELS + round_ids
    is_flipped = device > partner_dev
    return (column.reshape(NB, NREL), pair_ids.reshape(NB, NREL), is_flipped.reshape(NB, NREL), is_live.reshape(NB, NREL))


def draw_relatives(key, part):
    column, pair_ids, is_flipped, is_live = entries(key)
    return column.astype(jnp.int32)


def draw_kinship(key, part):
    column, pair_ids, is_flipped, is_live = entries(key)
    key = jax.random.fold_in(key, 7)
    key_own, key_far = jax.random.split(key, 2)
    low_value = 0.05

    def far_tile(pair_id):
        tile_key = jax.random.fold_in(key_far, pair_id)
        key_value, key_keep = jax.random.split(tile_key, 2)
        strength = jax.random.uniform(key_value, (TILE, TILE), minval=low_value, maxval=0.5)
        present = jax.random.uniform(key_keep, (TILE, TILE)) < 1.0 / TILE
        return jnp.where(present, strength, 0.0)
    far_block = jax.vmap(far_tile)(pair_ids.reshape(-1)).reshape(NB, NREL, TILE, TILE)
    far_block = jnp.where(is_flipped[:, :, None, None], jnp.swapaxes(far_block, 2, 3), far_block)
    far_block = jnp.where(is_live[:, :, None, None], far_block, 0.0)
    key_value, key_keep = jax.random.split(key_own, 2)
    raw_own = jax.random.uniform(key_value, (NB, TILE, TILE), minval=low_value, maxval=0.5)
    present = jax.random.uniform(key_keep, (NB, TILE, TILE)) < 1.0 / TILE
    raw_own = jnp.where(present, raw_own, 0.0)
    upper = jnp.arange(TILE)[:, None] < jnp.arange(TILE)[None, :]
    lower = jnp.arange(TILE)[:, None] > jnp.arange(TILE)[None, :]
    own_block = jnp.where(upper[None], raw_own, jnp.where(lower[None], jnp.swapaxes(raw_own, 1, 2), 0.0))
    return jnp.concatenate([own_block[:, None], far_block], axis=1).astype(jnp.float32)


def draw_phenotypes(key, part):
    key = jax.random.fold_in(key, 11)
    key_noise, key_row, key_col = jax.random.split(key, 3)
    people = jnp.arange(PEOPLE, dtype=jnp.float32) / PEOPLE
    row_scale = jnp.exp(jax.random.uniform(key_row, (PEOPLE,), minval=jnp.log(0.3), maxval=jnp.log(3.0)))
    col_scale = jnp.exp(jax.random.uniform(key_col, (PH,), minval=jnp.log(0.3), maxval=jnp.log(3.0)))
    noise = jnp.clip(jax.random.normal(key_noise, (PEOPLE, PH)), -5.0, 5.0)
    growth = jnp.sqrt(1.0 + 2.0 * people)
    return (noise * (row_scale * growth)[:, None] * col_scale[None, :]).astype(jnp.float32)


def spiked(values, rng, source, target, blocks, factor):
    def block_of(dim):
        return (jnp.arange(values.shape[dim]) // (values.shape[dim] // blocks)).reshape((-1,) + (1,) * (values.ndim - 1 - dim))

    near = jax.random.permutation(rng, blocks)[block_of(target)]
    far = (block_of(target) + blocks // 2) % blocks
    return jnp.where((block_of(source) == near) | (block_of(source) == far), factor * values, values)


def steps_of(key, shape, shards, low, high):
    loudness = 1.0
    for dim, parts in shards:
        draws = jax.random.uniform(jax.random.fold_in(jax.random.fold_in(key, 6), dim), (parts,), jnp.float32, low / len(shards), high / len(shards))
        loudness = loudness * jnp.repeat(jnp.exp(draws), shape[dim] // parts).reshape((-1,) + (1,) * (len(shape) - 1 - dim))
    return loudness


def heavy_noise(own_key, shape, width, limit, cuts, heavy, held_as=jnp.bfloat16):
    array = width * jax.random.normal(own_key, shape, jnp.float32)
    if cuts:
        array = array * steps_of(own_key, shape, cuts, -0.22, 0.18)
    return jnp.clip(spiked(array, jax.random.fold_in(own_key, 3), *heavy), -limit, limit).astype(held_as)


def setup_inputs(seed: int = 0, part: int = 0) -> dict:
    seeds = jax.random.split(jax.random.key(seed), 6)
    part_keys = jax.random.split(jax.random.fold_in(seeds[5], part), 6)
    return {
        "kinship": draw_kinship(jax.random.fold_in(jax.random.fold_in(seeds[5], part), 71), part),
        "relatives": draw_relatives(jax.random.fold_in(jax.random.fold_in(seeds[5], part), 71), part),
        "variance": jnp.clip(jnp.exp(math.log(2.0) - 1.3862944 * jax.random.uniform(part_keys[2], (PEOPLE,), jnp.float32) ** steps_of(part_keys[2], (PEOPLE,), ((0, 8),), -0.2, 0.2)), 0.5, 2.0),
        "phenotypes": draw_phenotypes(jax.random.fold_in(jax.random.fold_in(seeds[5], part), 71), part),
        "dosage": heavy_noise(part_keys[4], (PEOPLE, VARIANTS), 1.0, 5.0, ((0, 8), (1, 2)), (0, 1, 8, 2.0), jnp.float32),
    }


HIGHEST = lax.Precision.HIGHEST

def operator_parts(kinship, relatives):
    tile_rows = kinship.shape[2]
    diagonal_mask = jnp.arange(tile_rows)[:, None] == jnp.arange(tile_rows)[None, :]
    own_tiles = jnp.where(diagonal_mask[None], 0.0, kinship[:, 0])
    far_tiles = jnp.where((relatives >= 0)[:, :, None, None], kinship[:, 1:], 0.0)
    row_totals = lax.optimization_barrier(jnp.sum(own_tiles, axis=2)) + lax.optimization_barrier(jnp.sum(far_tiles, axis=(1, 3)))
    return (own_tiles, far_tiles, row_totals.reshape(-1))

def apply_operator(values, own_tiles, far_tiles, relatives, diagonal):
    block_count = own_tiles.shape[0]
    tile_rows = own_tiles.shape[1]
    pieces = values.reshape(block_count, tile_rows, values.shape[1])
    column_ids = jnp.clip(relatives, 0, block_count - 1).astype(jnp.int32)

    def one_block(packed):
        own_tile, far_tile, listed, own_piece = packed
        gathered = jnp.take(pieces, listed, axis=0)
        near_term = jnp.dot(own_tile, own_piece, precision=HIGHEST)
        far_term = jnp.einsum('kij,kjp->ip', far_tile, gathered, precision=HIGHEST)
        return near_term + far_term
    block_out = lax.map(one_block, (own_tiles, far_tiles, column_ids, pieces))
    return diagonal[:, None] * values + block_out.reshape(values.shape)

def reference(kinship, relatives, variance, phenotypes, dosage):
    own_tiles, far_tiles, row_totals = operator_parts(kinship, relatives)
    diagonal = variance + row_totals
    solved = jnp.zeros_like(phenotypes)
    residual = phenotypes
    scaled = residual / diagonal[:, None]
    direction = scaled
    norm_now = lax.optimization_barrier(jnp.sum(residual * scaled, axis=0))
    for iteration in range(ITERS):
        mapped = apply_operator(direction, own_tiles, far_tiles, relatives, diagonal)
        step_size = norm_now / lax.optimization_barrier(jnp.sum(direction * mapped, axis=0))
        solved = solved + step_size * direction
        if iteration + 1 < ITERS:
            residual = residual - step_size * mapped
            scaled = residual / diagonal[:, None]
            norm_next = lax.optimization_barrier(jnp.sum(residual * scaled, axis=0))
            direction = scaled + norm_next / norm_now * direction
            norm_now = norm_next
    norm_scale = 1.0 / math.sqrt(PEOPLE)
    scores = jnp.dot(dosage.T, solved, precision=HIGHEST, preferred_element_type=jnp.float32) * norm_scale
    return (solved, scores)
```

```python
import functools
import math

import jax
import jax.numpy as jnp
from jax import lax
from jax.experimental import pallas as pl
from jax.experimental.pallas import tpu as pltpu
from jax.sharding import PartitionSpec as P

VMEM_LIMIT = 40 * 1024 * 1024


def split(values):
    high = values.astype(jnp.bfloat16)
    low = (values - high.astype(jnp.float32)).astype(jnp.bfloat16)
    return high, low


def product(left, right):
    left_high, left_low = split(left)
    right_high, right_low = split(right)
    dot = functools.partial(jnp.dot, preferred_element_type=jnp.float32)
    return dot(left_high, right_high) + (dot(left_high, right_low) + dot(left_low, right_high))


def on_diagonal(size):
    rows = lax.broadcasted_iota(jnp.int32, (size, size), 0)
    return rows == lax.broadcasted_iota(jnp.int32, (size, size), 1)


def prepare_kernel(devices, capacity, me_ref, list_ref, kinship_ref, variance_ref, phenotypes_ref,
                   direction_ref, diagonal_ref, outgoing_ref, table_ref, first_ref, last_ref):
    block_count, positions, tile = kinship_ref.shape[:3]
    me = me_ref[0]
    for j in range(devices):
        first_ref[j] = jnp.int32(block_count * block_count)
        last_ref[j] = jnp.int32(-1)

    def entry_key(row, position):
        listed = list_ref[me * block_count + row, position]
        safe = jnp.maximum(listed, 0)
        other = safe // block_count
        far_block = safe - other * block_count
        key = jnp.where(me < other, row * block_count + far_block, far_block * block_count + row)
        return listed >= 0, other, key

    def collect(entry, carry):
        row = entry // (positions - 1)
        live, other, key = entry_key(row, entry - row * (positions - 1))

        @pl.when(live)
        def _():
            first_ref[other] = jnp.minimum(first_ref[other], key)
            last_ref[other] = jnp.maximum(last_ref[other], key)

        return carry

    lax.fori_loop(0, block_count * (positions - 1), collect, 0)

    def tabulate(entry, carry):
        row = entry // (positions - 1)
        live, other, key = entry_key(row, entry - row * (positions - 1))
        spare = jnp.where(me == 0, 1, 0)
        is_first = key == first_ref[other]
        handled = jnp.where(me < other, first_ref[other], last_ref[other])
        weight = jnp.where(first_ref[other] == last_ref[other], 1, 2)
        table_ref[0, entry] = jnp.where(live, other, spare)
        table_ref[1, entry] = jnp.where(live & jnp.logical_not(is_first), capacity - 1, 0)
        table_ref[2, entry] = jnp.where(live & (key == handled), weight, 0)
        return carry

    lax.fori_loop(0, block_count * (positions - 1), tabulate, 0)

    def mine(key, other):
        block = jnp.where(me < other, key // block_count, key % block_count)
        return jnp.where((key >= 0) & (key < block_count * block_count), block, 0)

    def send(other, carry):
        first = mine(first_ref[other], other)
        last = mine(last_ref[other], other)
        table_ref[3, other] = jnp.where(me < other, last, first)
        outgoing_ref[other, 0] = direction_ref[pl.ds(pl.multiple_of(first * tile, tile), tile), :]
        if capacity > 1:
            outgoing_ref[other, capacity - 1] = direction_ref[pl.ds(pl.multiple_of(last * tile, tile), tile), :]
        return carry

    diagonal_mask = on_diagonal(tile)
    for row in range(block_count):
        block = slice(row * tile, (row + 1) * tile)
        total = jnp.where(diagonal_mask, variance_ref[row:row + 1, :], kinship_ref[row, 0])
        for position in range(1, positions):
            total = total + kinship_ref[row, position]
        diagonal = jnp.sum(total, axis=1, keepdims=True)
        diagonal_ref[block, :] = diagonal
        direction_ref[block, :] = phenotypes_ref[block, :] / diagonal
    lax.fori_loop(0, devices, send, 0)


def apply_kernel(devices, table_ref, kinship_ref, direction_ref, diagonal_ref, received_ref, phenotypes_ref,
                 scaled_ref, outgoing_ref, sums_ref):
    block_count, positions, tile = kinship_ref.shape[:3]
    diagonal_mask = on_diagonal(tile)
    norm = jnp.zeros((8, direction_ref.shape[1]), jnp.float32)
    cross = jnp.zeros((8, direction_ref.shape[1]), jnp.float32)
    for row in range(block_count):
        block = slice(row * tile, (row + 1) * tile)
        here = direction_ref[block, :]
        mapped = product(jnp.where(diagonal_mask, 0.0, kinship_ref[row, 0]), here)
        for position in range(1, positions):
            entry = row * (positions - 1) + position - 1
            there = received_ref[table_ref[0, entry], table_ref[1, entry]]
            mapped = mapped + product(kinship_ref[row, position], there)
        scaled_ref[block, :] = mapped / diagonal_ref[block, :]
        norm = norm + jnp.sum((here * phenotypes_ref[block, :]).reshape(tile // 8, 8, -1), axis=0)
        cross = cross + jnp.sum((here * mapped).reshape(tile // 8, 8, -1), axis=0)
    sums_ref[0:1, :] = jnp.sum(norm, axis=0, keepdims=True)
    sums_ref[1:2, :] = jnp.sum(cross, axis=0, keepdims=True)

    def send(other, carry):
        block = table_ref[3, other]
        outgoing_ref[other] = scaled_ref[pl.ds(pl.multiple_of(block * tile, tile), tile), :]
        return carry

    lax.fori_loop(0, devices, send, 0)


def curvature_kernel(devices, table_ref, kinship_ref, direction_ref, diagonal_ref, scaled_ref, received_ref,
                     later_ref, all_sums_ref, sums_ref):
    block_count, positions, tile = kinship_ref.shape[:3]
    diagonal_mask = on_diagonal(tile)
    first_sums = jnp.sum(all_sums_ref[...], axis=0)
    rho = first_sums[1:2, :] / first_sums[0:1, :]
    norm = jnp.zeros((8, direction_ref.shape[1]), jnp.float32)
    bend = jnp.zeros((8, direction_ref.shape[1]), jnp.float32)
    for row in range(block_count):
        block = slice(row * tile, (row + 1) * tile)
        here = scaled_ref[block, :] - rho * direction_ref[block, :]
        mapped = product(jnp.where(diagonal_mask, 0.0, kinship_ref[row, 0]), here)
        for position in range(1, positions):
            entry = row * (positions - 1) + position - 1
            other = table_ref[0, entry]
            weight = table_ref[2, entry].astype(jnp.float32)
            there = weight * (later_ref[other] - rho * received_ref[other, table_ref[1, entry]])
            mapped = mapped + product(kinship_ref[row, position], there)
        norm = norm + jnp.sum((here * here * diagonal_ref[block, :]).reshape(tile // 8, 8, -1), axis=0)
        bend = bend + jnp.sum((here * mapped).reshape(tile // 8, 8, -1), axis=0)
    sums_ref[0:1, :] = jnp.sum(norm, axis=0, keepdims=True)
    sums_ref[1:2, :] = jnp.sum(bend, axis=0, keepdims=True)


def call(kernel, out_shape, in_specs, out_specs, scratch_shapes=()):
    return pl.pallas_call(
        kernel,
        out_shape=out_shape,
        in_specs=in_specs,
        out_specs=out_specs,
        scratch_shapes=list(scratch_shapes),
        compiler_params=pltpu.CompilerParams(vmem_limit_bytes=VMEM_LIMIT),
    )


def share(values, axis, devices):
    me = lax.axis_index(axis)
    rows = values.shape[0] // devices
    values = values.reshape(devices, rows, -1)
    step = 1
    while step < devices:
        pairs = [(i, i ^ step) for i in range(devices)]
        bit = (me // step) % 2
        halves = values.reshape(-1, 2, rows, values.shape[-1])
        kept = lax.dynamic_index_in_dim(halves, bit, 1, keepdims=False)
        given = lax.dynamic_index_in_dim(halves, 1 - bit, 1, keepdims=False)
        values = kept + lax.ppermute(given, axis, pairs)
        step *= 2
    return values.reshape(rows, -1)


def per_device(kinship, relatives, variance, phenotypes, dosage):
    devices = lax.axis_size("samples")
    me = lax.axis_index("samples").astype(jnp.int32).reshape(1)
    block_count, positions, tile = kinship.shape[:3]
    people, columns = phenotypes.shape
    entries = block_count * (positions - 1)
    capacity = -(-entries // (devices - 1))
    assert capacity <= 2
    vmem = pl.BlockSpec(memory_space=pltpu.VMEM)
    smem = pl.BlockSpec(memory_space=pltpu.SMEM)
    full = jax.ShapeDtypeStruct((people, columns), jnp.float32)
    sums = jax.ShapeDtypeStruct((2, columns), jnp.float32)
    direction, diagonal, outgoing, table = call(
        functools.partial(prepare_kernel, devices, capacity),
        (
            full,
            jax.ShapeDtypeStruct((people, 1), jnp.float32),
            jax.ShapeDtypeStruct((devices, capacity, tile, columns), jnp.float32),
            jax.ShapeDtypeStruct((4, max(entries, devices)), jnp.int32),
        ),
        [smem, smem, vmem, vmem, vmem],
        (vmem, vmem, vmem, smem),
        [pltpu.SMEM((devices,), jnp.int32), pltpu.SMEM((devices,), jnp.int32)],
    )(me, relatives, kinship, variance.reshape(block_count, tile), phenotypes)

    def variant_sums(values):
        both = lax.all_gather(values, "cols", axis=1, tiled=True)
        partial = lax.dot_general(
            dosage, both, (((0,), (0,)), ((), ())), precision=lax.Precision.HIGH,
            preferred_element_type=jnp.float32,
        )
        return share(partial, "samples", devices)

    received = lax.all_to_all(outgoing, "samples", split_axis=0, concat_axis=0, tiled=True)
    direction_scores = variant_sums(direction)
    scaled, outgoing, first_sums = call(
        functools.partial(apply_kernel, devices),
        (full, jax.ShapeDtypeStruct((devices, tile, columns), jnp.float32), sums),
        [smem, vmem, vmem, vmem, vmem, vmem],
        (vmem, vmem, vmem),
    )(table, kinship, direction, diagonal, received, phenotypes)
    all_first = lax.all_gather(first_sums, ("cols", "samples"), axis=0)
    later = lax.all_to_all(outgoing, "samples", split_axis=0, concat_axis=0, tiled=True)
    scaled_scores = variant_sums(scaled)
    own_col = lax.axis_index("cols")
    own_first = lax.dynamic_slice_in_dim(all_first, own_col * devices, devices, 0)
    second_sums = call(
        functools.partial(curvature_kernel, devices),
        sums,
        [smem] + [vmem] * 7,
        vmem,
    )(table, kinship, direction, diagonal, scaled, received, later, own_first)
    all_second = lax.all_gather(second_sums, ("cols", "samples"), axis=0)

    def coefficients(first, second):
        norm, cross = first[..., 0, :], first[..., 1, :]
        later_norm, bend = second[..., 0, :], second[..., 1, :]
        curve = norm + cross
        ratio = later_norm / curve
        step = jnp.where(later_norm > 0, later_norm / (later_norm + bend - later_norm * ratio), 0.0)
        start = norm / curve
        return start * (1.0 + step * (ratio + cross / norm)), -start * step

    first_both = jnp.sum(all_first.reshape(-1, devices, 2, columns), axis=1)
    second_both = jnp.sum(all_second.reshape(-1, devices, 2, columns), axis=1)
    along, across = coefficients(first_both, second_both)
    own_along = lax.dynamic_index_in_dim(along, own_col, 0, keepdims=True)
    own_across = lax.dynamic_index_in_dim(across, own_col, 0, keepdims=True)
    solved = own_along * direction + own_across * scaled
    norm_scale = 1.0 / math.sqrt(people * devices)
    scores = (along.reshape(1, -1) * direction_scores + across.reshape(1, -1) * scaled_scores) * norm_scale
    return (solved, scores)


def solution(mesh):
    return jax.shard_map(
        per_device,
        mesh=mesh,
        in_specs=(
            P(("groups", "samples"), None, None, None),
            P("groups", None),
            P(("groups", "samples")),
            P(("groups", "samples"), "cols"),
            P(("groups", "samples"), "cols"),
        ),
        out_specs=(P(("groups", "samples"), "cols"), P(("groups", "cols", "samples"), None)),
        check_vma=False,
    )
```

```python
import functools
import math

import jax
import jax.numpy as jnp
from jax import lax
from jax.experimental import pallas as pl
from jax.experimental.pallas import tpu as pltpu
from jax.sharding import PartitionSpec as P

VMEM_LIMIT = 40 * 1024 * 1024
SUBLANES = 8


def split(values):
    high = values.astype(jnp.bfloat16)
    low = (values - high.astype(jnp.float32)).astype(jnp.bfloat16)
    return high, low


def product(left, right):
    left_high, left_low = split(left)
    right_high, right_low = split(right)
    dot = functools.partial(jnp.dot, preferred_element_type=jnp.float32)
    return dot(left_high, right_high) + (dot(left_high, right_low) + dot(left_low, right_high))


def on_diagonal(size):
    rows = lax.broadcasted_iota(jnp.int32, (size, size), 0)
    return rows == lax.broadcasted_iota(jnp.int32, (size, size), 1)


def column_sums(values):
    rows, columns = values.shape
    return jnp.sum(values.reshape(rows // SUBLANES, SUBLANES, columns), axis=0)


class Copies:
    def __init__(self, semaphores):
        self.semaphores = semaphores
        self.count = 0

    def start(self, source, target):
        copy = pltpu.make_async_copy(source, target, self.semaphores.at[self.count])
        self.count += 1
        copy.start()
        return copy


def wait_all(copies):
    for copy in copies:
        copy.wait()


def prepare_kernel(devices, capacity, place_ref, list_ref, kinship_hbm, variance_ref, phenotypes_hbm, *refs):
    direction_hbm, diagonal_ref, table_ref = refs[:3]
    outgoing_hbm = refs[3:3 + devices - 1]
    kinship_ref, phenotypes_ref, direction_ref, first_ref, last_ref, semaphores = refs[3 + devices - 1:]
    block_count, positions, tile = kinship_ref.shape[:3]
    copies = Copies(semaphores)
    loads = []
    for row in range(block_count):
        block = pl.ds(row * tile, tile)
        loads.append((
            copies.start(kinship_hbm.at[row], kinship_ref.at[row]),
            copies.start(phenotypes_hbm.at[block], phenotypes_ref.at[block]),
        ))
    me = place_ref[0]
    for j in range(devices):
        first_ref[j] = jnp.int32(block_count * block_count)
        last_ref[j] = jnp.int32(-1)

    def entry_key(row, position):
        listed = list_ref[me * block_count + row, position]
        safe = jnp.maximum(listed, 0)
        other = safe // block_count
        far_block = safe - other * block_count
        key = jnp.where(me < other, row * block_count + far_block, far_block * block_count + row)
        return listed >= 0, other, key

    def collect(entry, carry):
        row = entry // (positions - 1)
        live, other, key = entry_key(row, entry - row * (positions - 1))

        @pl.when(live)
        def _():
            first_ref[other] = jnp.minimum(first_ref[other], key)
            last_ref[other] = jnp.maximum(last_ref[other], key)

        return carry

    lax.fori_loop(0, block_count * (positions - 1), collect, 0)

    def tabulate(entry, carry):
        row = entry // (positions - 1)
        live, other, key = entry_key(row, entry - row * (positions - 1))
        spare = jnp.where(me == 0, 1, 0)
        is_first = key == first_ref[other]
        handled = jnp.where(me < other, first_ref[other], last_ref[other])
        weight = jnp.where(first_ref[other] == last_ref[other], 1, 2)
        table_ref[0, entry] = jnp.where(live, other, spare)
        table_ref[1, entry] = jnp.where(live & jnp.logical_not(is_first), capacity - 1, 0)
        table_ref[2, entry] = jnp.where(live & (key == handled), weight, 0)
        return carry

    lax.fori_loop(0, block_count * (positions - 1), tabulate, 0)

    def mine(key, other):
        block = jnp.where(me < other, key // block_count, key % block_count)
        return jnp.where((key >= 0) & (key < block_count * block_count), block, 0)

    stores = []
    diagonal_mask = on_diagonal(tile)
    for row in range(block_count):
        wait_all(loads[row])
        block = pl.ds(row * tile, tile)
        total = jnp.where(diagonal_mask, variance_ref[row:row + 1, :], kinship_ref[row, 0])
        for position in range(1, positions):
            total = total + kinship_ref[row, position]
        diagonal = jnp.sum(total, axis=1, keepdims=True)
        diagonal_ref[block, :] = diagonal
        direction_ref[block, :] = phenotypes_ref[block, :] / diagonal
    for k in range(1, devices):
        other = me ^ k
        keys = (first_ref[other], last_ref[other])
        blocks = [mine(key, other) for key in keys]
        table_ref[3, k] = jnp.where(me < other, blocks[1], blocks[0])
        for slot in range(capacity):
            start = pl.multiple_of(blocks[slot] * tile, tile)
            stores.append(copies.start(direction_ref.at[pl.ds(start, tile)], outgoing_hbm[k - 1].at[slot]))
    stores.append(copies.start(direction_ref, direction_hbm))
    wait_all(stores)


def apply_kernel(devices, capacity, place_ref, table_ref, kinship_hbm, direction_hbm, diagonal_ref, phenotypes_hbm,
                 *refs):
    received_hbm, refs = refs[:devices - 1], refs[devices - 1:]
    scaled_hbm, sums_ref = refs[:2]
    outgoing_hbm, refs = refs[2:2 + devices - 1], refs[2 + devices - 1:]
    kinship_ref, direction_ref, phenotypes_ref, received_ref, scaled_ref, mapped_ref, semaphores = refs
    block_count, positions, tile = kinship_ref.shape[:3]
    columns = direction_ref.shape[1]
    me = place_ref[0]
    copies = Copies(semaphores)
    loads = [
        copies.start(kinship_hbm, kinship_ref),
        copies.start(direction_hbm, direction_ref),
        copies.start(phenotypes_hbm, phenotypes_ref),
    ]
    arrivals = [copies.start(received_hbm[k - 1], received_ref.at[me ^ k]) for k in range(1, devices)]
    wait_all(loads)
    diagonal_mask = on_diagonal(tile)
    norm = jnp.zeros((SUBLANES, columns), jnp.float32)
    cross = jnp.zeros((SUBLANES, columns), jnp.float32)
    for row in range(block_count):
        block = pl.ds(row * tile, tile)
        here = direction_ref[block, :]
        norm = norm + column_sums(here * phenotypes_ref[block, :])
        mapped_ref[block, :] = product(jnp.where(diagonal_mask, 0.0, kinship_ref[row, 0]), here)
    wait_all(arrivals)
    for row in range(block_count):
        block = pl.ds(row * tile, tile)
        mapped = mapped_ref[block, :]
        for position in range(1, positions):
            entry = row * (positions - 1) + position - 1
            there = received_ref[table_ref[0, entry], table_ref[1, entry]]
            mapped = mapped + product(kinship_ref[row, position], there)
        scaled_ref[block, :] = mapped / diagonal_ref[block, :]
        cross = cross + column_sums(direction_ref[block, :] * mapped)
    sums_ref[...] = jnp.zeros_like(sums_ref)
    sums_ref[0:1, :] = jnp.sum(norm, axis=0, keepdims=True)
    sums_ref[1:2, :] = jnp.sum(cross, axis=0, keepdims=True)
    stores = []
    for k in range(1, devices):
        start = pl.multiple_of(table_ref[3, k] * tile, tile)
        stores.append(copies.start(scaled_ref.at[pl.ds(start, tile)], outgoing_hbm[k - 1].at[pl.ds(0, tile)]))
        stores.append(copies.start(sums_ref, outgoing_hbm[k - 1].at[pl.ds(tile, SUBLANES)]))
    stores.append(copies.start(scaled_ref, scaled_hbm))
    wait_all(stores)


def curvature_kernel(devices, capacity, place_ref, table_ref, kinship_hbm, direction_hbm, diagonal_ref, scaled_hbm,
                     first_sums_ref, *refs):
    received_hbm, refs = refs[:devices - 1], refs[devices - 1:]
    later_hbm, refs = refs[:devices - 1], refs[devices - 1:]
    sums_ref, kinship_ref, direction_ref, scaled_ref, received_ref, later_ref, semaphores = refs
    block_count, positions, tile = kinship_ref.shape[:3]
    columns = direction_ref.shape[1]
    me = place_ref[0]
    copies = Copies(semaphores)
    loads = [copies.start(later_hbm[k - 1], later_ref.at[me ^ k]) for k in range(1, devices)]
    loads += [
        copies.start(kinship_hbm, kinship_ref),
        copies.start(direction_hbm, direction_ref),
        copies.start(scaled_hbm, scaled_ref),
    ]
    arrivals = [copies.start(received_hbm[k - 1], received_ref.at[me ^ k]) for k in range(1, devices)]
    wait_all(loads)
    first_sums = first_sums_ref[...]
    for k in range(1, devices):
        first_sums = first_sums + later_ref[me ^ k, pl.ds(tile, SUBLANES), :]
    rho = first_sums[1:2, :] / first_sums[0:1, :]
    diagonal_mask = on_diagonal(tile)
    norm = jnp.zeros((SUBLANES, columns), jnp.float32)
    bend = jnp.zeros((SUBLANES, columns), jnp.float32)
    for row in range(block_count):
        block = pl.ds(row * tile, tile)
        here = scaled_ref[block, :] - rho * direction_ref[block, :]
        scaled_ref[block, :] = here
        norm = norm + column_sums(here * here * diagonal_ref[block, :])
        bend = bend + column_sums(here * product(jnp.where(diagonal_mask, 0.0, kinship_ref[row, 0]), here))
    wait_all(arrivals)
    for row in range(block_count):
        mapped = jnp.zeros((tile, columns), jnp.float32)
        for position in range(1, positions):
            entry = row * (positions - 1) + position - 1
            other = table_ref[0, entry]
            weight = table_ref[2, entry].astype(jnp.float32)
            there = weight * (
                later_ref[other, pl.ds(0, tile), :] - rho * received_ref[other, table_ref[1, entry]]
            )
            mapped = mapped + product(kinship_ref[row, position], there)
        bend = bend + column_sums(scaled_ref[pl.ds(row * tile, tile), :] * mapped)
    sums_ref[...] = first_sums
    sums_ref[2:3, :] = jnp.sum(norm, axis=0, keepdims=True)
    sums_ref[3:4, :] = jnp.sum(bend, axis=0, keepdims=True)


def coefficients(own, shares):
    norm, cross = own[0:1, :], own[1:2, :]
    total = shares[0]
    for other in shares[1:]:
        total = total + other
    later_norm, bend = total[2:3, :], total[3:4, :]
    curve = norm + cross
    ratio = later_norm / curve
    step = jnp.where(later_norm > 0, later_norm / (later_norm + bend - later_norm * ratio), 0.0)
    start = norm / curve
    return start * (1.0 + step * (ratio + cross / norm)), -start * step


def finish_kernel(devices, norm_scale, place_ref, direction_hbm, scaled_hbm, direction_scores_hbm, scaled_scores_hbm,
                  sums_hbm, *refs):
    others = 2 * devices - 1
    others_hbm, refs = refs[:others], refs[others:]
    (solved_hbm, scores_ref, direction_ref, scaled_ref, direction_scores_ref, scaled_scores_ref, sums_ref,
     semaphores) = refs
    people, columns = direction_ref.shape
    copies = Copies(semaphores)
    arrivals = [copies.start(sums_hbm, sums_ref.at[0])]
    arrivals += [copies.start(others_hbm[i], sums_ref.at[i + 1]) for i in range(others)]
    loads = [
        copies.start(direction_hbm, direction_ref),
        copies.start(scaled_hbm, scaled_ref),
        copies.start(direction_scores_hbm, direction_scores_ref),
        copies.start(scaled_scores_hbm, scaled_scores_ref),
    ]
    wait_all(arrivals)
    own = [sums_ref[i] for i in range(devices)]
    other = [sums_ref[devices + i] for i in range(devices)]
    along, across = coefficients(own[0], own)
    other_along, other_across = coefficients(other[0], other)
    wait_all(loads)
    stores = []
    rows = people // 4
    for part in range(4):
        block = pl.ds(part * rows, rows)
        direction_ref[block, :] = along * direction_ref[block, :] + across * scaled_ref[block, :]
        stores.append(copies.start(direction_ref.at[block], solved_hbm.at[block]))
    column = place_ref[1]
    for start, first, second, offset in (
        (0, along, across, column * columns),
        (columns, other_along, other_across, (1 - column) * columns),
    ):
        here = pl.ds(start, columns)
        scores_ref[:, pl.ds(pl.multiple_of(offset, columns), columns)] = norm_scale * (
            first * direction_scores_ref[:, here] + second * scaled_scores_ref[:, here]
        )
    wait_all(stores)


def call(kernel, out_shape, in_specs, out_specs, scratch_shapes):
    return pl.pallas_call(
        kernel,
        out_shape=out_shape,
        in_specs=in_specs,
        out_specs=out_specs,
        scratch_shapes=list(scratch_shapes),
        compiler_params=pltpu.CompilerParams(vmem_limit_bytes=VMEM_LIMIT),
    )


def swap(values, axis, devices, step):
    return lax.ppermute(values, axis, [(i, i ^ step) for i in range(devices)])


def share(values, devices):
    me = lax.axis_index("samples")
    rows = values.shape[0] // devices
    values = values.reshape(devices, rows, -1)
    step = 1
    while step < devices:
        bit = (me // step) % 2
        halves = values.reshape(-1, 2, rows, values.shape[-1])
        kept = lax.dynamic_index_in_dim(halves, bit, 1, keepdims=False)
        given = lax.dynamic_index_in_dim(halves, 1 - bit, 1, keepdims=False)
        values = kept + swap(given, "samples", devices, step)
        step *= 2
    return values.reshape(rows, -1)


def per_device(kinship, relatives, variance, phenotypes, dosage):
    devices = lax.axis_size("samples")
    place = jnp.stack([lax.axis_index("samples"), lax.axis_index("cols")]).astype(jnp.int32)
    block_count, positions, tile = kinship.shape[:3]
    people, columns = phenotypes.shape
    variants = dosage.shape[1]
    entries = block_count * (positions - 1)
    capacity = -(-entries // (devices - 1))
    assert capacity <= 2
    anywhere = pl.BlockSpec(memory_space=pl.ANY)
    vmem = pl.BlockSpec(memory_space=pltpu.VMEM)
    smem = pl.BlockSpec(memory_space=pltpu.SMEM)
    float_of = lambda *shape: jax.ShapeDtypeStruct(shape, jnp.float32)
    room = lambda *shape: pltpu.VMEM(shape, jnp.float32)
    full = float_of(people, columns)
    full_room = room(people, columns)
    peers = devices - 1
    direction, diagonal, table, *outgoing = call(
        functools.partial(prepare_kernel, devices, capacity),
        [
            full,
            float_of(people, 1),
            jax.ShapeDtypeStruct((4, max(entries, devices)), jnp.int32),
        ] + [float_of(capacity, tile, columns)] * peers,
        [smem, smem, anywhere, vmem, anywhere],
        [anywhere, vmem, smem] + [anywhere] * peers,
        [
            room(*kinship.shape), full_room, full_room,
            pltpu.SMEM((devices,), jnp.int32), pltpu.SMEM((devices,), jnp.int32),
            pltpu.SemaphoreType.DMA((2 * block_count + capacity * peers + 1,)),
        ],
    )(place, relatives, kinship, variance.reshape(block_count, tile), phenotypes)

    def exchange(blocks):
        return [swap(blocks[k - 1], "samples", devices, k) for k in range(1, devices)]

    def variant_sums(values):
        both = jnp.concatenate([values, swap(values, "cols", 2, 1)], axis=1)
        partial = lax.dot_general(
            dosage, both, (((0,), (0,)), ((), ())), precision=lax.Precision.HIGH,
            preferred_element_type=jnp.float32,
        )
        return share(partial, devices)

    received = exchange(outgoing)
    direction_scores = variant_sums(direction)
    scaled, first_sums, *outgoing = call(
        functools.partial(apply_kernel, devices, capacity),
        [full, float_of(SUBLANES, columns)] + [float_of(tile + SUBLANES, columns)] * peers,
        [smem, smem, anywhere, anywhere, vmem, anywhere] + [anywhere] * peers,
        [anywhere, vmem] + [anywhere] * peers,
        [
            room(*kinship.shape), full_room, full_room, room(devices, capacity, tile, columns), full_room, full_room,
            pltpu.SemaphoreType.DMA((3 * peers + 4,)),
        ],
    )(place, table, kinship, direction, diagonal, phenotypes, *received)
    later = exchange(outgoing)
    scaled_scores = variant_sums(scaled)
    sums = call(
        functools.partial(curvature_kernel, devices, capacity),
        float_of(SUBLANES, columns),
        [smem, smem, anywhere, anywhere, vmem, anywhere, vmem] + [anywhere] * (2 * peers),
        vmem,
        [
            room(*kinship.shape), full_room, full_room, room(devices, capacity, tile, columns),
            room(devices, tile + SUBLANES, columns),
            pltpu.SemaphoreType.DMA((2 * peers + 3,)),
        ],
    )(place, table, kinship, direction, diagonal, scaled, first_sums, *received, *later)
    others = [swap(sums, ("samples", "cols"), 2 * devices, 2 * k) for k in range(1, devices)]
    others += [swap(sums, ("samples", "cols"), 2 * devices, 2 * k + 1) for k in range(devices)]
    solved, scores = call(
        functools.partial(finish_kernel, devices, 1.0 / math.sqrt(people * devices)),
        [full, float_of(variants // devices, 2 * columns)],
        [smem] + [anywhere] * (5 + len(others)),
        [anywhere, vmem],
        [
            full_room, full_room, room(variants // devices, 2 * columns), room(variants // devices, 2 * columns),
            room(2 * devices, SUBLANES, columns),
            pltpu.SemaphoreType.DMA((2 * devices + 8,)),
        ],
    )(place, direction, scaled, direction_scores, scaled_scores, sums, *others)
    return (solved, scores)


def solution(mesh):
    return jax.shard_map(
        per_device,
        mesh=mesh,
        in_specs=(
            P(("groups", "samples"), None, None, None),
            P("groups", None),
            P(("groups", "samples")),
            P(("groups", "samples"), "cols"),
            P(("groups", "samples"), "cols"),
        ),
        out_specs=(P(("groups", "samples"), "cols"), P(("groups", "cols", "samples"), None)),
        check_vma=False,
    )
```

```python
import functools
import math

import jax
import jax.numpy as jnp
from jax import lax
from jax.experimental import pallas as pl
from jax.experimental.pallas import tpu as pltpu
from jax.sharding import PartitionSpec as P

VMEM_LIMIT = 40 * 1024 * 1024
SUBLANES = 8


def split(values):
    high = values.astype(jnp.bfloat16)
    low = (values - high.astype(jnp.float32)).astype(jnp.bfloat16)
    return high, low


def product(left, right):
    left_high, left_low = split(left)
    right_high, right_low = split(right)
    dot = functools.partial(jnp.dot, preferred_element_type=jnp.float32)
    return dot(left_high, right_high) + (dot(left_high, right_low) + dot(left_low, right_high))


def on_diagonal(size):
    rows = lax.broadcasted_iota(jnp.int32, (size, size), 0)
    return rows == lax.broadcasted_iota(jnp.int32, (size, size), 1)


def column_sums(values):
    rows, columns = values.shape
    return jnp.sum(values.reshape(rows // SUBLANES, SUBLANES, columns), axis=0)


class Copies:
    def __init__(self, semaphores):
        self.semaphores = semaphores
        self.count = 0

    def start(self, source, target):
        copy = pltpu.make_async_copy(source, target, self.semaphores.at[self.count])
        self.count += 1
        copy.start()
        return copy


def wait_all(copies):
    for copy in copies:
        copy.wait()


def quotient(value, divisor):
    if divisor & (divisor - 1) == 0:
        return lax.shift_right_logical(value, jnp.int32(divisor.bit_length() - 1))
    return lax.div(value, jnp.int32(divisor))


def prepare_kernel(devices, capacity, list_ref, kinship_hbm, variance_hbm, phenotypes_hbm, *refs):
    direction_hbm, diagonal_ref, table_ref = refs[:3]
    outgoing_hbm = refs[3:3 + devices - 1]
    kinship_ref, variance_ref, phenotypes_ref, direction_ref, first_ref, last_ref, semaphores = refs[3 + devices - 1:]
    block_count, positions, tile = kinship_ref.shape[:3]
    copies = Copies(semaphores)
    loads = [copies.start(variance_hbm, variance_ref)]
    for row in range(block_count):
        block = pl.ds(row * tile, tile)
        loads.append(copies.start(kinship_hbm.at[row], kinship_ref.at[row]))
        loads.append(copies.start(phenotypes_hbm.at[block], phenotypes_ref.at[block]))
    me = lax.axis_index("samples")
    spare = jnp.where(me == 0, 1, 0)
    top = block_count * block_count
    for j in range(devices):
        first_ref[j] = jnp.int32(top)
        last_ref[j] = jnp.int32(-1)
    entries = []
    for row in range(block_count):
        for position in range(positions - 1):
            listed = list_ref[position, me * block_count + row]
            live = listed >= 0
            safe = jnp.maximum(listed, 0)
            other = quotient(safe, block_count)
            far_block = safe - other * block_count
            key = jnp.where(me < other, row * block_count + far_block, far_block * block_count + row)
            first_ref[other] = jnp.minimum(first_ref[other], jnp.where(live, key, top))
            last_ref[other] = jnp.maximum(last_ref[other], jnp.where(live, key, -1))
            entries.append((live, other, key))
    for entry, (live, other, key) in enumerate(entries):
        first, last = first_ref[other], last_ref[other]
        handled = jnp.where(me < other, first, last)
        weight = jnp.where(first == last, 1, 2)
        table_ref[0, entry] = jnp.where(live, other, spare)
        table_ref[1, entry] = jnp.where(live & (key != first), capacity - 1, 0)
        table_ref[2, entry] = jnp.where(live & (key == handled), weight, 0)

    def mine(key, other):
        lower = quotient(jnp.clip(key, 0, top - 1), block_count)
        higher = jnp.clip(key, 0, top - 1) - lower * block_count
        return jnp.where((key >= 0) & (key < top), jnp.where(me < other, lower, higher), 0)

    blocks = []
    for k in range(1, devices):
        other = me ^ k
        blocks.append((mine(first_ref[other], other), mine(last_ref[other], other)))
        table_ref[3, k] = jnp.where(me < other, blocks[-1][1], blocks[-1][0])
    stores = []
    diagonal_mask = on_diagonal(tile)
    loads[0].wait()
    for row in range(block_count):
        wait_all(loads[1 + 2 * row:3 + 2 * row])
        block = pl.ds(row * tile, tile)
        total = jnp.where(diagonal_mask, variance_ref[row:row + 1, :], kinship_ref[row, 0])
        for position in range(1, positions):
            total = total + kinship_ref[row, position]
        diagonal = jnp.sum(total, axis=1, keepdims=True)
        diagonal_ref[block, :] = diagonal
        direction_ref[block, :] = phenotypes_ref[block, :] / diagonal
    for k in range(1, devices):
        for slot in range(capacity):
            start = pl.multiple_of(blocks[k - 1][slot] * tile, tile)
            stores.append(copies.start(direction_ref.at[pl.ds(start, tile)], outgoing_hbm[k - 1].at[slot]))
    stores.append(copies.start(direction_ref, direction_hbm))
    wait_all(stores)


def apply_kernel(devices, capacity, table_ref, kinship_hbm, direction_hbm, diagonal_ref, phenotypes_hbm,
                 *refs):
    received_hbm, refs = refs[:devices - 1], refs[devices - 1:]
    scaled_hbm, sums_ref = refs[:2]
    outgoing_hbm, refs = refs[2:2 + devices - 1], refs[2 + devices - 1:]
    kinship_ref, direction_ref, phenotypes_ref, received_ref, scaled_ref, mapped_ref, semaphores = refs
    block_count, positions, tile = kinship_ref.shape[:3]
    columns = direction_ref.shape[1]
    me = lax.axis_index("samples")
    copies = Copies(semaphores)
    loads = [
        copies.start(kinship_hbm, kinship_ref),
        copies.start(direction_hbm, direction_ref),
        copies.start(phenotypes_hbm, phenotypes_ref),
    ]
    arrivals = [copies.start(received_hbm[k - 1], received_ref.at[me ^ k]) for k in range(1, devices)]
    wait_all(loads)
    diagonal_mask = on_diagonal(tile)
    norm = jnp.zeros((SUBLANES, columns), jnp.float32)
    cross = jnp.zeros((SUBLANES, columns), jnp.float32)
    for row in range(block_count):
        block = pl.ds(row * tile, tile)
        here = direction_ref[block, :]
        norm = norm + column_sums(here * phenotypes_ref[block, :])
        mapped_ref[block, :] = product(jnp.where(diagonal_mask, 0.0, kinship_ref[row, 0]), here)
    wait_all(arrivals)
    for row in range(block_count):
        block = pl.ds(row * tile, tile)
        mapped = mapped_ref[block, :]
        for position in range(1, positions):
            entry = row * (positions - 1) + position - 1
            there = received_ref[table_ref[0, entry], table_ref[1, entry]]
            mapped = mapped + product(kinship_ref[row, position], there)
        scaled_ref[block, :] = mapped / diagonal_ref[block, :]
        cross = cross + column_sums(direction_ref[block, :] * mapped)
    sums_ref[...] = jnp.zeros_like(sums_ref)
    sums_ref[0:1, :] = jnp.sum(norm, axis=0, keepdims=True)
    sums_ref[1:2, :] = jnp.sum(cross, axis=0, keepdims=True)
    stores = []
    for k in range(1, devices):
        start = pl.multiple_of(table_ref[3, k] * tile, tile)
        stores.append(copies.start(scaled_ref.at[pl.ds(start, tile)], outgoing_hbm[k - 1].at[pl.ds(0, tile)]))
        stores.append(copies.start(sums_ref, outgoing_hbm[k - 1].at[pl.ds(tile, SUBLANES)]))
    stores.append(copies.start(scaled_ref, scaled_hbm))
    wait_all(stores)


def curvature_kernel(devices, capacity, table_ref, kinship_hbm, direction_hbm, diagonal_ref, scaled_hbm,
                     first_sums_ref, *refs):
    received_hbm, refs = refs[:devices - 1], refs[devices - 1:]
    later_hbm, refs = refs[:devices - 1], refs[devices - 1:]
    sums_hbm, kinship_ref, direction_ref, scaled_ref, received_ref, later_ref, all_sums_ref, semaphores = refs
    block_count, positions, tile = kinship_ref.shape[:3]
    columns = direction_ref.shape[1]
    me = lax.axis_index("samples")
    copies = Copies(semaphores)
    loads = [copies.start(later_hbm[k - 1], later_ref.at[me ^ k]) for k in range(1, devices)]
    loads += [
        copies.start(kinship_hbm, kinship_ref),
        copies.start(direction_hbm, direction_ref),
        copies.start(scaled_hbm, scaled_ref),
    ]
    arrivals = [copies.start(received_hbm[k - 1], received_ref.at[me ^ k]) for k in range(1, devices)]
    wait_all(loads)
    first_sums = first_sums_ref[...]
    for k in range(1, devices):
        first_sums = first_sums + later_ref[me ^ k, pl.ds(tile, SUBLANES), :]
    rho = first_sums[1:2, :] / first_sums[0:1, :]
    diagonal_mask = on_diagonal(tile)
    norm = jnp.zeros((SUBLANES, columns), jnp.float32)
    bend = jnp.zeros((SUBLANES, columns), jnp.float32)
    for row in range(block_count):
        block = pl.ds(row * tile, tile)
        here = scaled_ref[block, :] - rho * direction_ref[block, :]
        scaled_ref[block, :] = here
        norm = norm + column_sums(here * here * diagonal_ref[block, :])
        bend = bend + column_sums(here * product(jnp.where(diagonal_mask, 0.0, kinship_ref[row, 0]), here))
    wait_all(arrivals)
    for row in range(block_count):
        mapped = jnp.zeros((tile, columns), jnp.float32)
        for position in range(1, positions):
            entry = row * (positions - 1) + position - 1
            other = table_ref[0, entry]
            weight = table_ref[2, entry].astype(jnp.float32)
            there = weight * (
                later_ref[other, pl.ds(0, tile), :] - rho * received_ref[other, table_ref[1, entry]]
            )
            mapped = mapped + product(kinship_ref[row, position], there)
        bend = bend + column_sums(scaled_ref[pl.ds(row * tile, tile), :] * mapped)
    row_ids = lax.broadcasted_iota(jnp.int32, first_sums.shape, 0)
    sums = jnp.where(row_ids == 2, jnp.sum(norm, axis=0, keepdims=True), first_sums)
    sums = jnp.where(row_ids == 3, jnp.sum(bend, axis=0, keepdims=True), sums)
    for i in range(2 * devices):
        all_sums_ref[i] = sums
    store = copies.start(all_sums_ref, sums_hbm)
    store.wait()


def coefficients(own, shares):
    norm, cross = own[0:1, :], own[1:2, :]
    total = shares[0]
    for other in shares[1:]:
        total = total + other
    later_norm, bend = total[2:3, :], total[3:4, :]
    curve = norm + cross
    ratio = later_norm / curve
    step = jnp.where(later_norm > 0, later_norm / (later_norm + bend - later_norm * ratio), 0.0)
    start = norm / curve
    return start * (1.0 + step * (ratio + cross / norm)), -start * step


def finish_kernel(devices, norm_scale, direction_hbm, scaled_hbm, direction_scores_hbm, scaled_scores_hbm, sums_hbm,
                  *refs):
    (solved_hbm, scores_ref, direction_ref, scaled_ref, direction_scores_ref, scaled_scores_ref, sums_ref,
     semaphores) = refs
    people, columns = direction_ref.shape
    column = lax.axis_index("cols")
    copies = Copies(semaphores)
    arrival = copies.start(sums_hbm, sums_ref)
    loads = [
        copies.start(direction_hbm, direction_ref),
        copies.start(scaled_hbm, scaled_ref),
        copies.start(direction_scores_hbm, direction_scores_ref),
        copies.start(scaled_scores_hbm, scaled_scores_ref),
    ]
    arrival.wait()
    own = [sums_ref[2 * i + column] for i in range(devices)]
    other = [sums_ref[2 * i + 1 - column] for i in range(devices)]
    along, across = coefficients(own[0], own)
    other_along, other_across = coefficients(other[0], other)
    wait_all(loads)
    stores = []
    rows = people // 4
    for part in range(4):
        block = pl.ds(part * rows, rows)
        direction_ref[block, :] = along * direction_ref[block, :] + across * scaled_ref[block, :]
        stores.append(copies.start(direction_ref.at[block], solved_hbm.at[block]))
    for start, first, second, offset in (
        (0, along, across, column * columns),
        (columns, other_along, other_across, (1 - column) * columns),
    ):
        here = pl.ds(start, columns)
        scores_ref[:, pl.ds(pl.multiple_of(offset, columns), columns)] = norm_scale * (
            first * direction_scores_ref[:, here] + second * scaled_scores_ref[:, here]
        )
    wait_all(stores)


def call(kernel, out_shape, in_specs, out_specs, scratch_shapes):
    return pl.pallas_call(
        kernel,
        out_shape=out_shape,
        in_specs=in_specs,
        out_specs=out_specs,
        scratch_shapes=list(scratch_shapes),
        compiler_params=pltpu.CompilerParams(vmem_limit_bytes=VMEM_LIMIT),
    )


def swap(values, axis, devices, step):
    return lax.ppermute(values, axis, [(i, i ^ step) for i in range(devices)])


def share(values, devices):
    me = lax.axis_index("samples")
    rows = values.shape[0] // devices
    values = values.reshape(devices, rows, -1)
    step = 1
    while step < devices:
        bit = (me // step) % 2
        halves = values.reshape(-1, 2, rows, values.shape[-1])
        kept = lax.dynamic_index_in_dim(halves, bit, 1, keepdims=False)
        given = lax.dynamic_index_in_dim(halves, 1 - bit, 1, keepdims=False)
        values = kept + swap(given, "samples", devices, step)
        step *= 2
    return values.reshape(rows, -1)


def per_device(kinship, relatives, variance, phenotypes, dosage):
    devices = lax.axis_size("samples")
    block_count, positions, tile = kinship.shape[:3]
    people, columns = phenotypes.shape
    variants = dosage.shape[1]
    share_rows = variants // devices
    entries = block_count * (positions - 1)
    capacity = -(-entries // (devices - 1))
    assert capacity <= 2
    hbm = pl.BlockSpec(memory_space=pltpu.HBM)
    vmem = pl.BlockSpec(memory_space=pltpu.VMEM)
    smem = pl.BlockSpec(memory_space=pltpu.SMEM)
    float_of = lambda *shape: jax.ShapeDtypeStruct(shape, jnp.float32)
    room = lambda *shape: pltpu.VMEM(shape, jnp.float32)
    full = float_of(people, columns)
    full_room = room(people, columns)
    peers = devices - 1
    direction, diagonal, table, *outgoing = call(
        functools.partial(prepare_kernel, devices, capacity),
        [
            full,
            float_of(people, 1),
            jax.ShapeDtypeStruct((4, max(entries, devices)), jnp.int32),
        ] + [float_of(capacity, tile, columns)] * peers,
        [smem, hbm, hbm, hbm],
        [hbm, vmem, smem] + [hbm] * peers,
        [
            room(*kinship.shape), room(block_count, tile), full_room, full_room,
            pltpu.SMEM((devices,), jnp.int32), pltpu.SMEM((devices,), jnp.int32),
            pltpu.SemaphoreType.DMA((2 * block_count + capacity * peers + 2,)),
        ],
    )(relatives.T, kinship, variance.reshape(block_count, tile), phenotypes)

    def exchange(blocks):
        return [swap(blocks[k - 1], "samples", devices, k) for k in range(1, devices)]

    both_dosages = jnp.concatenate(
        [values.reshape(people, devices, share_rows) for values in (dosage, swap(dosage, "cols", 2, 1))], axis=2
    ).reshape(people, 2 * variants)

    def variant_sums(values):
        partial = lax.dot_general(
            both_dosages, values, (((0,), (0,)), ((), ())), precision=lax.Precision.HIGH,
            preferred_element_type=jnp.float32,
        )
        total = share(partial, devices)
        return jnp.concatenate([total[:share_rows], swap(total[share_rows:], "cols", 2, 1)], axis=1)

    received = exchange(outgoing)
    direction_scores = variant_sums(direction)
    received, direction_scores = lax.optimization_barrier((received, direction_scores))
    scaled, first_sums, *outgoing = call(
        functools.partial(apply_kernel, devices, capacity),
        [full, float_of(SUBLANES, columns)] + [float_of(tile + SUBLANES, columns)] * peers,
        [smem, hbm, hbm, vmem, hbm] + [hbm] * peers,
        [hbm, vmem] + [hbm] * peers,
        [
            room(*kinship.shape), full_room, full_room, room(devices, capacity, tile, columns), full_room, full_room,
            pltpu.SemaphoreType.DMA((3 * peers + 4,)),
        ],
    )(table, kinship, direction, diagonal, phenotypes, *received)
    later = exchange(outgoing)
    scaled_scores = variant_sums(scaled)
    sums = call(
        functools.partial(curvature_kernel, devices, capacity),
        float_of(2 * devices, SUBLANES, columns),
        [smem, hbm, hbm, vmem, hbm, vmem] + [hbm] * (2 * peers),
        hbm,
        [
            room(*kinship.shape), full_room, full_room, room(devices, capacity, tile, columns),
            room(devices, tile + SUBLANES, columns), room(2 * devices, SUBLANES, columns),
            pltpu.SemaphoreType.DMA((2 * peers + 4,)),
        ],
    )(table, kinship, direction, diagonal, scaled, first_sums, *received, *later)
    all_sums = lax.all_to_all(sums, ("samples", "cols"), split_axis=0, concat_axis=0, tiled=True)
    solved, scores = call(
        functools.partial(finish_kernel, devices, 1.0 / math.sqrt(people * devices)),
        [full, float_of(share_rows, 2 * columns)],
        [hbm] * 5,
        [hbm, vmem],
        [
            full_room, full_room, room(share_rows, 2 * columns), room(share_rows, 2 * columns),
            room(2 * devices, SUBLANES, columns),
            pltpu.SemaphoreType.DMA((9,)),
        ],
    )(direction, scaled, direction_scores, scaled_scores, all_sums)
    return (solved, scores)


def solution(mesh):
    return jax.shard_map(
        per_device,
        mesh=mesh,
        in_specs=(
            P(("groups", "samples"), None, None, None),
            P("groups", None),
            P(("groups", "samples")),
            P(("groups", "samples"), "cols"),
            P(("groups", "samples"), "cols"),
        ),
        out_specs=(P(("groups", "samples"), "cols"), P(("groups", "cols", "samples"), None)),
        check_vma=False,
    )
```

```python
import functools
import math

import jax
import jax.numpy as jnp
from jax import lax
from jax.experimental import pallas as pl
from jax.experimental.pallas import tpu as pltpu
from jax.sharding import PartitionSpec as P

VMEM_LIMIT = 60 * 1024 * 1024
SUBLANES = 8


def split(values):
    high = values.astype(jnp.bfloat16)
    low = (values - high.astype(jnp.float32)).astype(jnp.bfloat16)
    return high, low


def product(left, right):
    left_high, left_low = split(left)
    right_high, right_low = split(right)
    dot = functools.partial(jnp.dot, preferred_element_type=jnp.float32)
    return dot(left_high, right_high) + (dot(left_high, right_low) + dot(left_low, right_high))


def on_diagonal(size):
    rows = lax.broadcasted_iota(jnp.int32, (size, size), 0)
    return rows == lax.broadcasted_iota(jnp.int32, (size, size), 1)


def column_sums(values):
    rows, columns = values.shape
    return jnp.sum(values.reshape(rows // SUBLANES, SUBLANES, columns), axis=0)


class Copies:
    def __init__(self, semaphores):
        self.semaphores = semaphores
        self.count = 0

    def start(self, source, target):
        copy = pltpu.make_async_copy(source, target, self.semaphores.at[self.count])
        self.count += 1
        copy.start()
        return copy


def wait_all(copies):
    for copy in copies:
        copy.wait()


def quotient(value, divisor):
    if divisor & (divisor - 1) == 0:
        return lax.shift_right_logical(value, jnp.int32(divisor.bit_length() - 1))
    return lax.div(value, jnp.int32(divisor))


def prepare_kernel(devices, capacity, list_ref, kinship_hbm, variance_hbm, phenotypes_hbm, *refs):
    (direction_hbm, diagonal_ref, table_ref, outgoing_hbm, kinship_ref, variance_ref, phenotypes_ref, direction_ref,
     first_ref, last_ref, semaphores) = refs
    block_count, positions, tile = kinship_ref.shape[:3]
    copies = Copies(semaphores)
    loads = [copies.start(variance_hbm, variance_ref)]
    for row in range(block_count):
        block = pl.ds(row * tile, tile)
        loads.append(copies.start(kinship_hbm.at[row], kinship_ref.at[row]))
        loads.append(copies.start(phenotypes_hbm.at[block], phenotypes_ref.at[block]))
    me = lax.axis_index("samples")
    spare = jnp.where(me == 0, 1, 0)
    top = block_count * block_count
    for j in range(devices):
        first_ref[j] = jnp.int32(top)
        last_ref[j] = jnp.int32(-1)
    entries = []
    for row in range(block_count):
        for position in range(positions - 1):
            listed = list_ref[position, me * block_count + row]
            live = listed >= 0
            safe = jnp.maximum(listed, 0)
            other = quotient(safe, block_count)
            far_block = safe - other * block_count
            key = jnp.where(me < other, row * block_count + far_block, far_block * block_count + row)
            first_ref[other] = jnp.minimum(first_ref[other], jnp.where(live, key, top))
            last_ref[other] = jnp.maximum(last_ref[other], jnp.where(live, key, -1))
            entries.append((live, other, key))
    for entry, (live, other, key) in enumerate(entries):
        first, last = first_ref[other], last_ref[other]
        handled = jnp.where(me < other, first, last)
        weight = jnp.where(first == last, 1, 2)
        table_ref[0, entry] = jnp.where(live, other, spare)
        table_ref[1, entry] = jnp.where(live & (key != first), capacity - 1, 0)
        table_ref[2, entry] = jnp.where(live & (key == handled), weight, 0)

    def mine(key, other):
        lower = quotient(jnp.clip(key, 0, top - 1), block_count)
        higher = jnp.clip(key, 0, top - 1) - lower * block_count
        return jnp.where((key >= 0) & (key < top), jnp.where(me < other, lower, higher), 0)

    blocks = []
    for other in range(devices):
        blocks.append((mine(first_ref[other], other), mine(last_ref[other], other)))
        table_ref[3, other] = jnp.where(me < other, blocks[-1][1], blocks[-1][0])
    stores = []
    diagonal_mask = on_diagonal(tile)
    loads[0].wait()
    for row in range(block_count):
        wait_all(loads[1 + 2 * row:3 + 2 * row])
        block = pl.ds(row * tile, tile)
        total = jnp.where(diagonal_mask, variance_ref[row:row + 1, :], kinship_ref[row, 0])
        for position in range(1, positions):
            total = total + kinship_ref[row, position]
        diagonal = jnp.sum(total, axis=1, keepdims=True)
        diagonal_ref[block, :] = diagonal
        direction_ref[block, :] = phenotypes_ref[block, :] / diagonal
    for other in range(devices):
        for slot in range(capacity):
            start = pl.multiple_of(blocks[other][slot] * tile, tile)
            stores.append(copies.start(direction_ref.at[pl.ds(start, tile)], outgoing_hbm.at[other, slot]))
    stores.append(copies.start(direction_ref, direction_hbm))
    wait_all(stores)


def apply_kernel(devices, table_ref, kinship_hbm, direction_hbm, diagonal_ref, phenotypes_hbm, received_hbm,
                 scaled_hbm, outgoing_hbm, sums_ref, kinship_ref, direction_ref, phenotypes_ref, received_ref,
                 scaled_ref, mapped_ref, semaphores):
    block_count, positions, tile = kinship_ref.shape[:3]
    columns = direction_ref.shape[1]
    copies = Copies(semaphores)
    loads = [
        copies.start(kinship_hbm, kinship_ref),
        copies.start(direction_hbm, direction_ref),
        copies.start(phenotypes_hbm, phenotypes_ref),
    ]
    arrivals = [copies.start(received_hbm, received_ref)]
    wait_all(loads)
    diagonal_mask = on_diagonal(tile)
    norm = jnp.zeros((SUBLANES, columns), jnp.float32)
    cross = jnp.zeros((SUBLANES, columns), jnp.float32)
    for row in range(block_count):
        block = pl.ds(row * tile, tile)
        here = direction_ref[block, :]
        norm = norm + column_sums(here * phenotypes_ref[block, :])
        mapped_ref[block, :] = product(jnp.where(diagonal_mask, 0.0, kinship_ref[row, 0]), here)
    wait_all(arrivals)
    for row in range(block_count):
        block = pl.ds(row * tile, tile)
        mapped = mapped_ref[block, :]
        for position in range(1, positions):
            entry = row * (positions - 1) + position - 1
            there = received_ref[table_ref[0, entry], table_ref[1, entry]]
            mapped = mapped + product(kinship_ref[row, position], there)
        scaled_ref[block, :] = mapped / diagonal_ref[block, :]
        cross = cross + column_sums(direction_ref[block, :] * mapped)
    sums_ref[...] = jnp.zeros_like(sums_ref)
    sums_ref[0:1, :] = jnp.sum(norm, axis=0, keepdims=True)
    sums_ref[1:2, :] = jnp.sum(cross, axis=0, keepdims=True)
    stores = []
    for other in range(devices):
        start = pl.multiple_of(table_ref[3, other] * tile, tile)
        stores.append(copies.start(scaled_ref.at[pl.ds(start, tile)], outgoing_hbm.at[other, pl.ds(0, tile)]))
        stores.append(copies.start(sums_ref, outgoing_hbm.at[other, pl.ds(tile, SUBLANES)]))
    stores.append(copies.start(scaled_ref, scaled_hbm))
    wait_all(stores)


def curvature_kernel(devices, table_ref, kinship_hbm, direction_hbm, diagonal_ref, scaled_hbm, received_hbm,
                     later_hbm, sums_ref, kinship_ref, direction_ref, scaled_ref, received_ref, later_ref, semaphores):
    block_count, positions, tile = kinship_ref.shape[:3]
    columns = direction_ref.shape[1]
    copies = Copies(semaphores)
    loads = [
        copies.start(later_hbm, later_ref),
        copies.start(kinship_hbm, kinship_ref),
        copies.start(direction_hbm, direction_ref),
        copies.start(scaled_hbm, scaled_ref),
    ]
    arrivals = [copies.start(received_hbm, received_ref)]
    wait_all(loads)
    first_sums = later_ref[0, pl.ds(tile, SUBLANES), :]
    for other in range(1, devices):
        first_sums = first_sums + later_ref[other, pl.ds(tile, SUBLANES), :]
    rho = first_sums[1:2, :] / first_sums[0:1, :]
    diagonal_mask = on_diagonal(tile)
    norm = jnp.zeros((SUBLANES, columns), jnp.float32)
    bend = jnp.zeros((SUBLANES, columns), jnp.float32)
    for row in range(block_count):
        block = pl.ds(row * tile, tile)
        here = scaled_ref[block, :] - rho * direction_ref[block, :]
        scaled_ref[block, :] = here
        norm = norm + column_sums(here * here * diagonal_ref[block, :])
        bend = bend + column_sums(here * product(jnp.where(diagonal_mask, 0.0, kinship_ref[row, 0]), here))
    wait_all(arrivals)
    for row in range(block_count):
        mapped = jnp.zeros((tile, columns), jnp.float32)
        for position in range(1, positions):
            entry = row * (positions - 1) + position - 1
            other = table_ref[0, entry]
            weight = table_ref[2, entry].astype(jnp.float32)
            there = weight * (
                later_ref[other, pl.ds(0, tile), :] - rho * received_ref[other, table_ref[1, entry]]
            )
            mapped = mapped + product(kinship_ref[row, position], there)
        bend = bend + column_sums(scaled_ref[pl.ds(row * tile, tile), :] * mapped)
    row_ids = lax.broadcasted_iota(jnp.int32, first_sums.shape, 0)
    sums = jnp.where(row_ids == 2, jnp.sum(norm, axis=0, keepdims=True), first_sums)
    sums_ref[...] = jnp.where(row_ids == 3, jnp.sum(bend, axis=0, keepdims=True), sums)


def coefficients(sums):
    norm, cross, later_norm, bend = (sums[i:i + 1, :] for i in range(4))
    curve = norm + cross
    ratio = later_norm / curve
    step = jnp.where(later_norm > 0, later_norm / (later_norm + bend - later_norm * ratio), 0.0)
    start = norm / curve
    return start * (1.0 + step * (ratio + cross / norm)), -start * step


def finish_kernel(norm_scale, direction_hbm, scaled_hbm, direction_scores_hbm, scaled_scores_hbm, sums_hbm,
                  *refs):
    (solved_hbm, scores_ref, direction_ref, scaled_ref, direction_scores_ref, scaled_scores_ref, sums_ref,
     semaphores) = refs
    people, columns = direction_ref.shape
    column = lax.axis_index("cols")
    copies = Copies(semaphores)
    arrival = copies.start(sums_hbm, sums_ref)
    loads = [
        copies.start(direction_hbm, direction_ref),
        copies.start(scaled_hbm, scaled_ref),
        copies.start(direction_scores_hbm, direction_scores_ref),
        copies.start(scaled_scores_hbm, scaled_scores_ref),
    ]
    arrival.wait()
    along, across = coefficients(sums_ref[0])
    other_along, other_across = coefficients(sums_ref[1])
    wait_all(loads)
    stores = []
    rows = people // 4
    for part in range(4):
        block = pl.ds(part * rows, rows)
        direction_ref[block, :] = along * direction_ref[block, :] + across * scaled_ref[block, :]
        stores.append(copies.start(direction_ref.at[block], solved_hbm.at[block]))
    for start, first, second, offset in (
        (0, along, across, column * columns),
        (columns, other_along, other_across, (1 - column) * columns),
    ):
        here = pl.ds(start, columns)
        scores_ref[:, pl.ds(pl.multiple_of(offset, columns), columns)] = norm_scale * (
            first * direction_scores_ref[:, here] + second * scaled_scores_ref[:, here]
        )
    wait_all(stores)


def call(kernel, out_shape, in_specs, out_specs, scratch_shapes):
    return pl.pallas_call(
        kernel,
        out_shape=out_shape,
        in_specs=in_specs,
        out_specs=out_specs,
        scratch_shapes=list(scratch_shapes),
        compiler_params=pltpu.CompilerParams(vmem_limit_bytes=VMEM_LIMIT),
    )


def swap(values, axis, devices, step):
    return lax.ppermute(values, axis, [(i, i ^ step) for i in range(devices)])


def share(values, devices):
    me = lax.axis_index("samples")
    rows = values.shape[0] // devices
    values = values.reshape(devices, rows, -1)
    step = 1
    while step < devices:
        bit = (me // step) % 2
        halves = values.reshape(-1, 2, rows, values.shape[-1])
        kept = lax.dynamic_index_in_dim(halves, bit, 1, keepdims=False)
        given = lax.dynamic_index_in_dim(halves, 1 - bit, 1, keepdims=False)
        values = kept + swap(given, "samples", devices, step)
        step *= 2
    return values.reshape(rows, -1)


def total_sums(sums, devices):
    both = jnp.stack([sums, swap(sums, "cols", 2, 1)])
    is_share = (jnp.arange(SUBLANES) // 2 == 1)[None, :, None]
    step = 1
    while step < devices:
        both = both + jnp.where(is_share, swap(both, "samples", devices, step), 0.0)
        step *= 2
    return both


def per_device(kinship, relatives, variance, phenotypes, dosage):
    devices = lax.axis_size("samples")
    block_count, positions, tile = kinship.shape[:3]
    people, columns = phenotypes.shape
    variants = dosage.shape[1]
    share_rows = variants // devices
    entries = block_count * (positions - 1)
    capacity = -(-entries // (devices - 1))
    assert capacity <= 2
    hbm = pl.BlockSpec(memory_space=pltpu.HBM)
    vmem = pl.BlockSpec(memory_space=pltpu.VMEM)
    smem = pl.BlockSpec(memory_space=pltpu.SMEM)
    float_of = lambda *shape: jax.ShapeDtypeStruct(shape, jnp.float32)
    room = lambda *shape: pltpu.VMEM(shape, jnp.float32)
    full = float_of(people, columns)
    full_room = room(people, columns)
    direction, diagonal, table, outgoing = call(
        functools.partial(prepare_kernel, devices, capacity),
        [
            full,
            float_of(people, 1),
            jax.ShapeDtypeStruct((4, max(entries, devices)), jnp.int32),
            float_of(devices, capacity, tile, columns),
        ],
        [smem, hbm, hbm, hbm],
        [hbm, vmem, smem, hbm],
        [
            room(*kinship.shape), room(block_count, tile), full_room, full_room,
            pltpu.SMEM((devices,), jnp.int32), pltpu.SMEM((devices,), jnp.int32),
            pltpu.SemaphoreType.DMA((2 * block_count + capacity * devices + 2,)),
        ],
    )(relatives.T, kinship, variance.reshape(block_count, tile), phenotypes)

    def exchange(blocks):
        return lax.all_to_all(blocks, "samples", split_axis=0, concat_axis=0, tiled=True)

    both_dosages = jnp.concatenate(
        [values.reshape(people, devices, share_rows) for values in (dosage, swap(dosage, "cols", 2, 1))], axis=2
    ).reshape(people, 2 * variants)

    def variant_sums(values):
        partial = lax.dot_general(
            both_dosages, values, (((0,), (0,)), ((), ())), precision=lax.Precision.HIGH,
            preferred_element_type=jnp.float32,
        )
        total = share(partial, devices)
        return jnp.concatenate([total[:share_rows], swap(total[share_rows:], "cols", 2, 1)], axis=1)

    received = exchange(outgoing)
    direction_scores = variant_sums(direction)
    received, direction_scores = lax.optimization_barrier((received, direction_scores))
    scaled, outgoing = call(
        functools.partial(apply_kernel, devices),
        [full, float_of(devices, tile + SUBLANES, columns)],
        [smem, hbm, hbm, vmem, hbm, hbm],
        [hbm, hbm],
        [
            room(SUBLANES, columns),
            room(*kinship.shape), full_room, full_room, room(devices, capacity, tile, columns), full_room, full_room,
            pltpu.SemaphoreType.DMA((2 * devices + 5,)),
        ],
    )(table, kinship, direction, diagonal, phenotypes, received)
    later = exchange(outgoing)
    scaled_scores = variant_sums(scaled)
    sums = call(
        functools.partial(curvature_kernel, devices),
        float_of(SUBLANES, columns),
        [smem, hbm, hbm, vmem, hbm, hbm, hbm],
        vmem,
        [
            room(*kinship.shape), full_room, full_room, room(devices, capacity, tile, columns),
            room(devices, tile + SUBLANES, columns),
            pltpu.SemaphoreType.DMA((5,)),
        ],
    )(table, kinship, direction, diagonal, scaled, received, later)
    solved, scores = call(
        functools.partial(finish_kernel, 1.0 / math.sqrt(people * devices)),
        [full, float_of(share_rows, 2 * columns)],
        [hbm] * 5,
        [hbm, vmem],
        [
            full_room, full_room, room(share_rows, 2 * columns), room(share_rows, 2 * columns),
            room(2, SUBLANES, columns),
            pltpu.SemaphoreType.DMA((9,)),
        ],
    )(direction, scaled, direction_scores, scaled_scores, total_sums(sums, devices))
    return (solved, scores)


def solution(mesh):
    return jax.shard_map(
        per_device,
        mesh=mesh,
        in_specs=(
            P(("groups", "samples"), None, None, None),
            P("groups", None),
            P(("groups", "samples")),
            P(("groups", "samples"), "cols"),
            P(("groups", "samples"), "cols"),
        ),
        out_specs=(P(("groups", "samples"), "cols"), P(("groups", "cols", "samples"), None)),
        check_vma=False,
    )
```

```python
import functools
import math

import jax
import jax.numpy as jnp
from jax import lax
from jax.experimental import pallas as pl
from jax.experimental.pallas import tpu as pltpu
from jax.sharding import PartitionSpec as P

VMEM_LIMIT = 60 * 1024 * 1024
SUBLANES = 8


def split(values):
    high = values.astype(jnp.bfloat16)
    low = (values - high.astype(jnp.float32)).astype(jnp.bfloat16)
    return high, low


def dot(left, right):
    return jnp.dot(left, right, preferred_element_type=jnp.float32)


def on_diagonal(size):
    rows = lax.broadcasted_iota(jnp.int32, (size, size), 0)
    return rows == lax.broadcasted_iota(jnp.int32, (size, size), 1)


def split_tiles(kinship_ref, high_ref, low_ref):
    block_count, positions, tile = kinship_ref.shape[:3]
    diagonal_mask = on_diagonal(tile)
    for row in range(block_count):
        for position in range(positions):
            values = kinship_ref[row, position]
            if position == 0:
                values = jnp.where(diagonal_mask, 0.0, values)
            high, low = split(values)
            high_ref[row, :, pl.ds(position * tile, tile)] = high
            low_ref[row, :, pl.ds(position * tile, tile)] = low


def product(high, low, blocks):
    parts = [split(block) for block in blocks]
    blocks_high = jnp.concatenate([part[0] for part in parts], axis=0)
    blocks_low = jnp.concatenate([part[1] for part in parts], axis=0)
    return dot(high, blocks_high) + (dot(low, blocks_high) + dot(high, blocks_low))


def column_sums(values):
    rows, columns = values.shape
    return jnp.sum(values.reshape(rows // SUBLANES, SUBLANES, columns), axis=0)


class Copies:
    def __init__(self, semaphores):
        self.semaphores = semaphores
        self.count = 0

    def start(self, source, target):
        copy = pltpu.make_async_copy(source, target, self.semaphores.at[self.count])
        self.count += 1
        copy.start()
        return copy


def wait_all(copies):
    for copy in copies:
        copy.wait()


def quotient(value, divisor):
    if divisor & (divisor - 1) == 0:
        return lax.shift_right_logical(value, jnp.int32(divisor.bit_length() - 1))
    return lax.div(value, jnp.int32(divisor))


def prepare_kernel(devices, capacity, list_ref, kinship_hbm, variance_hbm, phenotypes_hbm, *refs):
    (direction_hbm, diagonal_ref, table_ref, outgoing_hbm, kinship_ref, variance_ref, phenotypes_ref, direction_ref,
     first_ref, last_ref, semaphores) = refs
    block_count, positions, tile = kinship_ref.shape[:3]
    copies = Copies(semaphores)
    loads = [copies.start(variance_hbm, variance_ref)]
    for row in range(block_count):
        block = pl.ds(row * tile, tile)
        loads.append(copies.start(kinship_hbm.at[row], kinship_ref.at[row]))
        loads.append(copies.start(phenotypes_hbm.at[block], phenotypes_ref.at[block]))
    me = lax.axis_index("samples")
    spare = jnp.where(me == 0, 1, 0)
    top = block_count * block_count
    for j in range(devices):
        first_ref[j] = jnp.int32(top)
        last_ref[j] = jnp.int32(-1)
    entries = []
    for row in range(block_count):
        for position in range(positions - 1):
            listed = list_ref[position, me * block_count + row]
            live = listed >= 0
            safe = jnp.maximum(listed, 0)
            other = quotient(safe, block_count)
            far_block = safe - other * block_count
            key = jnp.where(me < other, row * block_count + far_block, far_block * block_count + row)
            first_ref[other] = jnp.minimum(first_ref[other], jnp.where(live, key, top))
            last_ref[other] = jnp.maximum(last_ref[other], jnp.where(live, key, -1))
            entries.append((live, other, key))
    for entry, (live, other, key) in enumerate(entries):
        first, last = first_ref[other], last_ref[other]
        handled = jnp.where(me < other, first, last)
        weight = jnp.where(first == last, 1, 2)
        table_ref[0, entry] = jnp.where(live, other, spare)
        table_ref[1, entry] = jnp.where(live & (key != first), capacity - 1, 0)
        table_ref[2, entry] = jnp.where(live & (key == handled), weight, 0)

    def mine(key, other):
        lower = quotient(jnp.clip(key, 0, top - 1), block_count)
        higher = jnp.clip(key, 0, top - 1) - lower * block_count
        return jnp.where((key >= 0) & (key < top), jnp.where(me < other, lower, higher), 0)

    blocks = []
    for other in range(devices):
        blocks.append((mine(first_ref[other], other), mine(last_ref[other], other)))
        table_ref[3, other] = jnp.where(me < other, blocks[-1][1], blocks[-1][0])
    stores = []
    diagonal_mask = on_diagonal(tile)
    loads[0].wait()
    for row in range(block_count):
        wait_all(loads[1 + 2 * row:3 + 2 * row])
        block = pl.ds(row * tile, tile)
        total = jnp.where(diagonal_mask, variance_ref[row:row + 1, :], kinship_ref[row, 0])
        for position in range(1, positions):
            total = total + kinship_ref[row, position]
        diagonal = jnp.sum(total, axis=1, keepdims=True)
        diagonal_ref[block, :] = diagonal
        direction_ref[block, :] = phenotypes_ref[block, :] * (1.0 / diagonal)
    for other in range(devices):
        for slot in range(capacity):
            start = pl.multiple_of(blocks[other][slot] * tile, tile)
            stores.append(copies.start(direction_ref.at[pl.ds(start, tile)], outgoing_hbm.at[other, slot]))
    stores.append(copies.start(direction_ref, direction_hbm))
    wait_all(stores)


def apply_kernel(devices, table_ref, kinship_hbm, direction_hbm, diagonal_ref, phenotypes_hbm, received_hbm,
                 scaled_hbm, outgoing_hbm, sums_ref, kinship_ref, direction_ref, phenotypes_ref, received_ref,
                 scaled_ref, high_ref, low_ref, semaphores):
    block_count, positions, tile = kinship_ref.shape[:3]
    columns = direction_ref.shape[1]
    copies = Copies(semaphores)
    tiles = copies.start(kinship_hbm, kinship_ref)
    arrival = copies.start(received_hbm, received_ref)
    loads = [copies.start(direction_hbm, direction_ref), copies.start(phenotypes_hbm, phenotypes_ref)]
    norm = jnp.zeros((SUBLANES, columns), jnp.float32)
    cross = jnp.zeros((SUBLANES, columns), jnp.float32)
    tiles.wait()
    split_tiles(kinship_ref, high_ref, low_ref)
    wait_all(loads)
    arrival.wait()
    for row in range(block_count):
        block = pl.ds(row * tile, tile)
        here = direction_ref[block, :]
        blocks = [here]
        for position in range(positions - 1):
            entry = row * (positions - 1) + position
            blocks.append(received_ref[table_ref[0, entry], table_ref[1, entry]])
        mapped = product(high_ref[row], low_ref[row], blocks)
        scaled_ref[block, :] = mapped * (1.0 / diagonal_ref[block, :])
        norm = norm + column_sums(here * phenotypes_ref[block, :])
        cross = cross + column_sums(here * mapped)
    sums_ref[...] = jnp.zeros_like(sums_ref)
    sums_ref[0:1, :] = jnp.sum(norm, axis=0, keepdims=True)
    sums_ref[1:2, :] = jnp.sum(cross, axis=0, keepdims=True)
    stores = []
    for other in range(devices):
        start = pl.multiple_of(table_ref[3, other] * tile, tile)
        stores.append(copies.start(scaled_ref.at[pl.ds(start, tile)], outgoing_hbm.at[other, pl.ds(0, tile)]))
        stores.append(copies.start(sums_ref, outgoing_hbm.at[other, pl.ds(tile, SUBLANES)]))
    stores.append(copies.start(scaled_ref, scaled_hbm))
    wait_all(stores)


def curvature_kernel(devices, table_ref, kinship_hbm, direction_hbm, diagonal_ref, scaled_hbm, received_hbm,
                     later_hbm, sums_hbm, kinship_ref, direction_ref, scaled_ref, received_ref, later_ref, high_ref,
                     low_ref, sums_ref, semaphores):
    block_count, positions, tile = kinship_ref.shape[:3]
    columns = direction_ref.shape[1]
    copies = Copies(semaphores)
    tiles = copies.start(kinship_hbm, kinship_ref)
    loads = [
        copies.start(later_hbm, later_ref),
        copies.start(direction_hbm, direction_ref),
        copies.start(scaled_hbm, scaled_ref),
        copies.start(received_hbm, received_ref),
    ]
    tiles.wait()
    split_tiles(kinship_ref, high_ref, low_ref)
    wait_all(loads)
    first_sums = later_ref[0, pl.ds(tile, SUBLANES), :]
    for other in range(1, devices):
        first_sums = first_sums + later_ref[other, pl.ds(tile, SUBLANES), :]
    rho = first_sums[1:2, :] / first_sums[0:1, :]
    norm = jnp.zeros((SUBLANES, columns), jnp.float32)
    bend = jnp.zeros((SUBLANES, columns), jnp.float32)
    for row in range(block_count):
        block = pl.ds(row * tile, tile)
        here = scaled_ref[block, :] - rho * direction_ref[block, :]
        blocks = [here]
        for position in range(positions - 1):
            entry = row * (positions - 1) + position
            other = table_ref[0, entry]
            weight = table_ref[2, entry].astype(jnp.float32)
            blocks.append(weight * (
                later_ref[other, pl.ds(0, tile), :] - rho * received_ref[other, table_ref[1, entry]]
            ))
        mapped = product(high_ref[row], low_ref[row], blocks)
        norm = norm + column_sums(here * here * diagonal_ref[block, :])
        bend = bend + column_sums(here * mapped)
    row_ids = lax.broadcasted_iota(jnp.int32, first_sums.shape, 0)
    sums = jnp.where(row_ids == 2, jnp.sum(norm, axis=0, keepdims=True), first_sums)
    sums = jnp.where(row_ids == 3, jnp.sum(bend, axis=0, keepdims=True), sums)
    for i in range(2 * devices):
        sums_ref[i] = sums
    store = copies.start(sums_ref, sums_hbm)
    store.wait()


def coefficients(sums, shared):
    norm, cross = sums[0:1, :], sums[1:2, :]
    later_norm, bend = shared[2:3, :], shared[3:4, :]
    curve = norm + cross
    ratio = later_norm / curve
    step = jnp.where(later_norm > 0, later_norm / (later_norm + bend - later_norm * ratio), 0.0)
    start = norm / curve
    return start * (1.0 + step * (ratio + cross / norm)), -start * step


def finish_kernel(devices, norm_scale, direction_hbm, scaled_hbm, direction_scores_hbm, scaled_scores_hbm,
                  swapped_hbm, sums_hbm, solved_hbm, scores_ref, direction_ref, scaled_ref, direction_scores_ref,
                  scaled_scores_ref, swapped_ref, sums_ref, semaphores):
    people, columns = direction_ref.shape
    rows = scores_ref.shape[0]
    column = lax.axis_index("cols")
    copies = Copies(semaphores)
    arrival = copies.start(sums_hbm, sums_ref)
    vectors = [copies.start(direction_hbm, direction_ref), copies.start(scaled_hbm, scaled_ref)]
    shares = [
        copies.start(direction_scores_hbm.at[pl.ds(0, rows)], direction_scores_ref),
        copies.start(scaled_scores_hbm.at[pl.ds(0, rows)], scaled_scores_ref),
        copies.start(swapped_hbm, swapped_ref),
    ]

    def total(which):
        sums = sums_ref[which]
        shared = sums
        for i in range(1, devices):
            shared = shared + sums_ref[2 * i + which]
        return sums, shared

    arrival.wait()
    along, across = coefficients(*total(column))
    other_along, other_across = coefficients(*total(1 - column))
    wait_all(vectors)
    stores = []
    part_rows = people // 4
    for part in range(4):
        block = pl.ds(part * part_rows, part_rows)
        direction_ref[block, :] = along * direction_ref[block, :] + across * scaled_ref[block, :]
        stores.append(copies.start(direction_ref.at[block], solved_hbm.at[block]))
    wait_all(shares)
    own = pl.multiple_of(column * columns, columns)
    other = pl.multiple_of((1 - column) * columns, columns)
    scores_ref[:, pl.ds(own, columns)] = norm_scale * (
        along * direction_scores_ref[...] + across * scaled_scores_ref[...]
    )
    scores_ref[:, pl.ds(other, columns)] = norm_scale * (
        other_along * swapped_ref[pl.ds(0, rows), :] + other_across * swapped_ref[pl.ds(rows, rows), :]
    )
    wait_all(stores)


def call(kernel, out_shape, in_specs, out_specs, scratch_shapes):
    return pl.pallas_call(
        kernel,
        out_shape=out_shape,
        in_specs=in_specs,
        out_specs=out_specs,
        scratch_shapes=list(scratch_shapes),
        compiler_params=pltpu.CompilerParams(vmem_limit_bytes=VMEM_LIMIT),
    )


def swap(values, axis, devices, step):
    return lax.ppermute(values, axis, [(i, i ^ step) for i in range(devices)])


def halve(values, devices, step):
    bit = (lax.axis_index("samples") // step) % 2
    halves = values.reshape(-1, 2, *values.shape[1:])
    kept = lax.dynamic_index_in_dim(halves, bit, 1, keepdims=False)
    given = lax.dynamic_index_in_dim(halves, 1 - bit, 1, keepdims=False)
    return kept, swap(given, "samples", devices, step)


def halve_all(values, devices, steps):
    for step in steps:
        values = sum(halve(values, devices, step))
    return values


def per_device(kinship, relatives, variance, phenotypes, dosage):
    devices = lax.axis_size("samples")
    block_count, positions, tile = kinship.shape[:3]
    people, columns = phenotypes.shape
    variants = dosage.shape[1]
    share_rows = variants // devices
    entries = block_count * (positions - 1)
    capacity = -(-entries // (devices - 1))
    assert capacity <= 2
    hbm = pl.BlockSpec(memory_space=pltpu.HBM)
    vmem = pl.BlockSpec(memory_space=pltpu.VMEM)
    smem = pl.BlockSpec(memory_space=pltpu.SMEM)
    float_of = lambda *shape: jax.ShapeDtypeStruct(shape, jnp.float32)
    room = lambda *shape: pltpu.VMEM(shape, jnp.float32)
    full = float_of(people, columns)
    full_room = room(people, columns)
    tiles_room = pltpu.VMEM((block_count, tile, positions * tile), jnp.bfloat16)
    direction, diagonal, table, outgoing = call(
        functools.partial(prepare_kernel, devices, capacity),
        [
            full,
            float_of(people, 1),
            jax.ShapeDtypeStruct((4, max(entries, devices)), jnp.int32),
            float_of(devices, capacity, tile, columns),
        ],
        [smem, hbm, hbm, hbm],
        [hbm, vmem, smem, hbm],
        [
            room(*kinship.shape), room(block_count, tile), full_room, full_room,
            pltpu.SMEM((devices,), jnp.int32), pltpu.SMEM((devices,), jnp.int32),
            pltpu.SemaphoreType.DMA((2 * block_count + capacity * devices + 2,)),
        ],
    )(relatives.T, kinship, variance.reshape(block_count, tile), phenotypes)

    def exchange(blocks):
        return lax.all_to_all(blocks, "samples", split_axis=0, concat_axis=0, tiled=True)

    both_dosages = jnp.concatenate(
        [values.reshape(people, devices, share_rows) for values in (dosage, swap(dosage, "cols", 2, 1))], axis=2
    ).reshape(people, 2 * variants)

    def variant_products(values):
        partial = lax.dot_general(
            both_dosages, values, (((0,), (0,)), ((), ())), precision=lax.Precision.HIGH,
            preferred_element_type=jnp.float32,
        )
        return partial.reshape(devices, 2 * share_rows, columns)

    steps = [2 ** i for i in range(devices.bit_length() - 1)]
    received = exchange(outgoing)
    direction_scores = halve_all(variant_products(direction), devices, steps[:1])
    received, direction_scores = lax.optimization_barrier((received, direction_scores))
    scaled, outgoing = call(
        functools.partial(apply_kernel, devices),
        [full, float_of(devices, tile + SUBLANES, columns)],
        [smem, hbm, hbm, vmem, hbm, hbm],
        [hbm, hbm],
        [
            room(SUBLANES, columns),
            room(*kinship.shape), full_room, full_room, room(devices, capacity, tile, columns), full_room,
            tiles_room, tiles_room,
            pltpu.SemaphoreType.DMA((2 * devices + 5,)),
        ],
    )(table, kinship, direction, diagonal, phenotypes, received)
    later = exchange(outgoing)
    scaled, direction_scores = lax.optimization_barrier((scaled, direction_scores))
    scaled_scores = halve_all(variant_products(scaled), devices, steps[:1])
    direction_scores = halve_all(direction_scores, devices, steps[1:2])
    later, scaled_scores, direction_scores = lax.optimization_barrier((later, scaled_scores, direction_scores))
    direction_kept, direction_given = halve(direction_scores, devices, steps[2])
    scaled_kept, scaled_given = halve(scaled_scores, devices, steps[1])
    sums = call(
        functools.partial(curvature_kernel, devices),
        float_of(2 * devices, SUBLANES, columns),
        [smem, hbm, hbm, vmem, hbm, hbm, hbm],
        hbm,
        [
            room(*kinship.shape), full_room, full_room, room(devices, capacity, tile, columns),
            room(devices, tile + SUBLANES, columns), tiles_room, tiles_room,
            room(2 * devices, SUBLANES, columns),
            pltpu.SemaphoreType.DMA((6,)),
        ],
    )(table, kinship, direction, diagonal, scaled, received, later)
    sums, direction_kept, scaled_kept = lax.optimization_barrier((sums, direction_kept, scaled_kept))
    all_sums = lax.all_to_all(sums, ("samples", "cols"), split_axis=0, concat_axis=0, tiled=True)
    direction_scores = halve_all(direction_kept + direction_given, devices, steps[3:])[0]
    scaled_scores = halve_all(scaled_kept + scaled_given, devices, steps[2:])[0]
    swapped = swap(jnp.concatenate([direction_scores[share_rows:], scaled_scores[share_rows:]]), "cols", 2, 1)
    solved, scores = call(
        functools.partial(finish_kernel, devices, 1.0 / math.sqrt(people * devices)),
        [full, float_of(share_rows, 2 * columns)],
        [hbm] * 6,
        [hbm, vmem],
        [
            full_room, full_room, room(share_rows, columns), room(share_rows, columns),
            room(2 * share_rows, columns), room(2 * devices, SUBLANES, columns),
            pltpu.SemaphoreType.DMA((10,)),
        ],
    )(direction, scaled, direction_scores, scaled_scores, swapped, all_sums)
    return (solved, scores)


def solution(mesh):
    return jax.shard_map(
        per_device,
        mesh=mesh,
        in_specs=(
            P(("groups", "samples"), None, None, None),
            P("groups", None),
            P(("groups", "samples")),
            P(("groups", "samples"), "cols"),
            P(("groups", "samples"), "cols"),
        ),
        out_specs=(P(("groups", "samples"), "cols"), P(("groups", "cols", "samples"), None)),
        check_vma=False,
    )
```

```python
import functools
import math

import jax
import jax.numpy as jnp
from jax import lax
from jax.experimental import pallas as pl
from jax.experimental.pallas import tpu as pltpu
from jax.sharding import PartitionSpec as P

VMEM_LIMIT = 60 * 1024 * 1024
SUBLANES = 8


def split(values):
    high = values.astype(jnp.bfloat16)
    low = (values - high.astype(jnp.float32)).astype(jnp.bfloat16)
    return high, low


def dot(left, right):
    return jnp.dot(left, right, preferred_element_type=jnp.float32)


def on_diagonal(size):
    rows = lax.broadcasted_iota(jnp.int32, (size, size), 0)
    return rows == lax.broadcasted_iota(jnp.int32, (size, size), 1)


def split_tiles(kinship_ref, high_ref, low_ref):
    block_count, positions, tile = kinship_ref.shape[:3]
    diagonal_mask = on_diagonal(tile)
    for row in range(block_count):
        for position in range(positions):
            values = kinship_ref[row, position]
            if position == 0:
                values = jnp.where(diagonal_mask, 0.0, values)
            high, low = split(values)
            high_ref[row, :, pl.ds(position * tile, tile)] = high
            low_ref[row, :, pl.ds(position * tile, tile)] = low


def product(high, low, blocks):
    parts = [split(block) for block in blocks]
    blocks_high = jnp.concatenate([part[0] for part in parts], axis=0)
    blocks_low = jnp.concatenate([part[1] for part in parts], axis=0)
    return dot(high, blocks_high) + (dot(low, blocks_high) + dot(high, blocks_low))


def column_sums(values):
    rows, columns = values.shape
    return jnp.sum(values.reshape(rows // SUBLANES, SUBLANES, columns), axis=0)


class Copies:
    def __init__(self, semaphores):
        self.semaphores = semaphores
        self.count = 0

    def start(self, source, target):
        copy = pltpu.make_async_copy(source, target, self.semaphores.at[self.count])
        self.count += 1
        copy.start()
        return copy


def wait_all(copies):
    for copy in copies:
        copy.wait()


def quotient(value, divisor):
    if divisor & (divisor - 1) == 0:
        return lax.shift_right_logical(value, jnp.int32(divisor.bit_length() - 1))
    return lax.div(value, jnp.int32(divisor))


def prepare_kernel(devices, capacity, list_ref, kinship_hbm, variance_hbm, phenotypes_hbm, direction_hbm, left_hbm,
                   right_hbm, diagonal_ref, table_ref, forward_ref, outgoing_hbm, kinship_ref, variance_ref,
                   phenotypes_ref, direction_ref, first_ref, last_ref, semaphores):
    block_count, positions, tile = kinship_ref.shape[:3]
    columns = direction_ref.shape[1]
    half = devices // 2
    copies = Copies(semaphores)
    loads = [copies.start(variance_hbm, variance_ref)]
    for row in range(block_count):
        block = pl.ds(row * tile, tile)
        loads.append(copies.start(kinship_hbm.at[row], kinship_ref.at[row]))
        loads.append(copies.start(phenotypes_hbm.at[block], phenotypes_ref.at[block]))
    me = lax.axis_index("samples")
    partner = me ^ half
    base = me & half
    spare = me ^ 1
    top = block_count * block_count

    def collect(device):
        for j in range(devices):
            first_ref[j] = jnp.int32(top)
            last_ref[j] = jnp.int32(-1)
        found = []
        for row in range(block_count):
            for position in range(positions - 1):
                listed = list_ref[position, device * block_count + row]
                live = listed >= 0
                safe = jnp.maximum(listed, 0)
                other = quotient(safe, block_count)
                far_block = safe - other * block_count
                key = jnp.where(device < other, row * block_count + far_block, far_block * block_count + row)
                first_ref[other] = jnp.minimum(first_ref[other], jnp.where(live, key, top))
                last_ref[other] = jnp.maximum(last_ref[other], jnp.where(live, key, -1))
                found.append((live, other, far_block, key))
        return found

    def blocks_for(device, other):
        blocks = []
        for key in (first_ref[other], last_ref[other]):
            safe = jnp.clip(key, 0, top - 1)
            lower = quotient(safe, block_count)
            higher = safe - lower * block_count
            blocks.append(jnp.where(key == safe, jnp.where(device < other, lower, higher), 0))
        return blocks

    collect(partner)
    for i in range(half):
        blocks = blocks_for(partner, base + i)
        for slot in range(capacity):
            forward_ref[slot, i] = blocks[slot]
    for entry, (live, other, far_block, key) in enumerate(collect(me)):
        first, last = first_ref[other], last_ref[other]
        handled = jnp.where(me < other, first, last)
        weight = jnp.where(first == last, 1, 2)
        slot = jnp.where(key == first, 0, capacity - 1)
        place = jnp.where(other == partner, devices * capacity + far_block, other * capacity + slot)
        table_ref[0, entry] = jnp.where(live, place, spare * capacity)
        table_ref[1, entry] = jnp.where(live, other, spare)
        table_ref[2, entry] = jnp.where(live & (key == handled), weight, 0)
    for other in range(devices):
        blocks = blocks_for(me, other)
        table_ref[3, other] = jnp.where(me < other, blocks[1], blocks[0])
    near = [blocks_for(me, base + i) for i in range(half)]
    stores = []
    diagonal_mask = on_diagonal(tile)
    loads[0].wait()
    for row in range(block_count):
        wait_all(loads[1 + 2 * row:3 + 2 * row])
        block = pl.ds(row * tile, tile)
        total = jnp.where(diagonal_mask, variance_ref[row:row + 1, :], kinship_ref[row, 0])
        for position in range(1, positions):
            total = total + kinship_ref[row, position]
        diagonal = jnp.sum(total, axis=1, keepdims=True)
        diagonal_ref[block, :] = diagonal
        direction_ref[block, :] = phenotypes_ref[block, :] * (1.0 / diagonal)
        stores.append(copies.start(direction_ref.at[block, pl.ds(0, columns // 2)], left_hbm.at[row]))
        stores.append(copies.start(direction_ref.at[block, pl.ds(columns // 2, columns // 2)], right_hbm.at[row]))
        stores.append(copies.start(direction_ref.at[block], direction_hbm.at[block]))
    for i in range(half):
        for slot in range(capacity):
            start = pl.multiple_of(near[i][slot] * tile, tile)
            stores.append(copies.start(direction_ref.at[pl.ds(start, tile)], outgoing_hbm.at[i * capacity + slot]))
    wait_all(stores)


def forward_kernel(forward_ref, partner_hbm, outgoing_hbm, semaphores):
    capacity, half = forward_ref.shape
    copies = Copies(semaphores)
    stores = []
    for i in range(half):
        for slot in range(capacity):
            stores.append(copies.start(partner_hbm.at[forward_ref[slot, i]], outgoing_hbm.at[i * capacity + slot]))
    wait_all(stores)


def load_received(copies, devices, capacity, near_hbm, far_hbm, partner_hbm, received_ref):
    half = devices // 2
    base = lax.axis_index("samples") & half
    width = received_ref.shape[2] // 2
    count = half * capacity
    loads = [copies.start(near_hbm, received_ref.at[pl.ds(base * capacity, count)])]
    for side in range(2):
        lanes = pl.ds(side * width, width)
        loads.append(copies.start(
            far_hbm[side], received_ref.at[pl.ds((half - base) * capacity, count), :, lanes]
        ))
        loads.append(copies.start(
            partner_hbm[side], received_ref.at[pl.ds(devices * capacity, partner_hbm[side].shape[0]), :, lanes]
        ))
    return loads


def apply_kernel(devices, capacity, table_ref, kinship_hbm, direction_hbm, diagonal_ref, phenotypes_hbm, near_hbm,
                 far_left_hbm, far_right_hbm, partner_left_hbm, partner_right_hbm, scaled_hbm, outgoing_hbm, sums_ref, kinship_ref, direction_ref, phenotypes_ref, received_ref,
                 scaled_ref, high_ref, low_ref, semaphores):
    block_count, positions, tile = kinship_ref.shape[:3]
    columns = direction_ref.shape[1]
    copies = Copies(semaphores)
    tiles = copies.start(kinship_hbm, kinship_ref)
    arrivals = load_received(
        copies, devices, capacity, near_hbm, (far_left_hbm, far_right_hbm), (partner_left_hbm, partner_right_hbm),
        received_ref,
    )
    loads = [copies.start(direction_hbm, direction_ref), copies.start(phenotypes_hbm, phenotypes_ref)]
    norm = jnp.zeros((SUBLANES, columns), jnp.float32)
    cross = jnp.zeros((SUBLANES, columns), jnp.float32)
    tiles.wait()
    split_tiles(kinship_ref, high_ref, low_ref)
    wait_all(loads)
    wait_all(arrivals)
    for row in range(block_count):
        block = pl.ds(row * tile, tile)
        here = direction_ref[block, :]
        blocks = [here]
        for position in range(positions - 1):
            entry = row * (positions - 1) + position
            blocks.append(received_ref[table_ref[0, entry]])
        mapped = product(high_ref[row], low_ref[row], blocks)
        scaled_ref[block, :] = mapped * (1.0 / diagonal_ref[block, :])
        norm = norm + column_sums(here * phenotypes_ref[block, :])
        cross = cross + column_sums(here * mapped)
    sums_ref[...] = jnp.zeros_like(sums_ref)
    sums_ref[0:1, :] = jnp.sum(norm, axis=0, keepdims=True)
    sums_ref[1:2, :] = jnp.sum(cross, axis=0, keepdims=True)
    stores = []
    for other in range(devices):
        start = pl.multiple_of(table_ref[3, other] * tile, tile)
        stores.append(copies.start(scaled_ref.at[pl.ds(start, tile)], outgoing_hbm.at[other, pl.ds(0, tile)]))
        stores.append(copies.start(sums_ref, outgoing_hbm.at[other, pl.ds(tile, SUBLANES)]))
    stores.append(copies.start(scaled_ref, scaled_hbm))
    wait_all(stores)


def curvature_kernel(devices, capacity, table_ref, kinship_hbm, direction_hbm, diagonal_ref, scaled_hbm, near_hbm,
                     far_left_hbm, far_right_hbm, partner_left_hbm, partner_right_hbm, later_hbm, sums_hbm, kinship_ref, direction_ref, scaled_ref, received_ref, later_ref, high_ref,
                     low_ref, sums_ref, semaphores):
    block_count, positions, tile = kinship_ref.shape[:3]
    columns = direction_ref.shape[1]
    copies = Copies(semaphores)
    tiles = copies.start(kinship_hbm, kinship_ref)
    loads = [
        copies.start(later_hbm, later_ref),
        copies.start(direction_hbm, direction_ref),
        copies.start(scaled_hbm, scaled_ref),
    ]
    loads += load_received(
        copies, devices, capacity, near_hbm, (far_left_hbm, far_right_hbm), (partner_left_hbm, partner_right_hbm),
        received_ref,
    )
    tiles.wait()
    split_tiles(kinship_ref, high_ref, low_ref)
    wait_all(loads)
    first_sums = later_ref[0, pl.ds(tile, SUBLANES), :]
    for other in range(1, devices):
        first_sums = first_sums + later_ref[other, pl.ds(tile, SUBLANES), :]
    rho = first_sums[1:2, :] / first_sums[0:1, :]
    norm = jnp.zeros((SUBLANES, columns), jnp.float32)
    bend = jnp.zeros((SUBLANES, columns), jnp.float32)
    for row in range(block_count):
        block = pl.ds(row * tile, tile)
        here = scaled_ref[block, :] - rho * direction_ref[block, :]
        blocks = [here]
        for position in range(positions - 1):
            entry = row * (positions - 1) + position
            weight = table_ref[2, entry].astype(jnp.float32)
            there = later_ref[table_ref[1, entry], pl.ds(0, tile), :]
            blocks.append(weight * (there - rho * received_ref[table_ref[0, entry]]))
        mapped = product(high_ref[row], low_ref[row], blocks)
        norm = norm + column_sums(here * here * diagonal_ref[block, :])
        bend = bend + column_sums(here * mapped)
    row_ids = lax.broadcasted_iota(jnp.int32, first_sums.shape, 0)
    sums = jnp.where(row_ids == 2, jnp.sum(norm, axis=0, keepdims=True), first_sums)
    sums = jnp.where(row_ids == 3, jnp.sum(bend, axis=0, keepdims=True), sums)
    for i in range(2 * devices):
        sums_ref[i] = sums
    store = copies.start(sums_ref, sums_hbm)
    store.wait()


def coefficients(sums, shared):
    norm, cross = sums[0:1, :], sums[1:2, :]
    later_norm, bend = shared[2:3, :], shared[3:4, :]
    curve = norm + cross
    ratio = later_norm / curve
    step = jnp.where(later_norm > 0, later_norm / (later_norm + bend - later_norm * ratio), 0.0)
    start = norm / curve
    return start * (1.0 + step * (ratio + cross / norm)), -start * step


def finish_kernel(devices, norm_scale, direction_hbm, scaled_hbm, direction_scores_hbm, scaled_scores_hbm,
                  swapped_hbm, sums_hbm, solved_hbm, scores_ref, direction_ref, scaled_ref, direction_scores_ref,
                  scaled_scores_ref, swapped_ref, sums_ref, semaphores):
    people, columns = direction_ref.shape
    rows = scores_ref.shape[0]
    column = lax.axis_index("cols")
    copies = Copies(semaphores)
    arrival = copies.start(sums_hbm, sums_ref)
    vectors = [copies.start(direction_hbm, direction_ref), copies.start(scaled_hbm, scaled_ref)]
    shares = [
        copies.start(direction_scores_hbm.at[pl.ds(0, rows)], direction_scores_ref),
        copies.start(scaled_scores_hbm.at[pl.ds(0, rows)], scaled_scores_ref),
        copies.start(swapped_hbm, swapped_ref),
    ]

    def total(which):
        sums = sums_ref[which]
        shared = sums
        for i in range(1, devices):
            shared = shared + sums_ref[2 * i + which]
        return sums, shared

    arrival.wait()
    along, across = coefficients(*total(column))
    other_along, other_across = coefficients(*total(1 - column))
    wait_all(vectors)
    stores = []
    part_rows = people // 4
    for part in range(4):
        block = pl.ds(part * part_rows, part_rows)
        direction_ref[block, :] = along * direction_ref[block, :] + across * scaled_ref[block, :]
        stores.append(copies.start(direction_ref.at[block], solved_hbm.at[block]))
    wait_all(shares)
    own = pl.multiple_of(column * columns, columns)
    other = pl.multiple_of((1 - column) * columns, columns)
    scores_ref[:, pl.ds(own, columns)] = norm_scale * (
        along * direction_scores_ref[...] + across * scaled_scores_ref[...]
    )
    scores_ref[:, pl.ds(other, columns)] = norm_scale * (
        other_along * swapped_ref[pl.ds(0, rows), :] + other_across * swapped_ref[pl.ds(rows, rows), :]
    )
    wait_all(stores)


def call(kernel, out_shape, in_specs, out_specs, scratch_shapes):
    return pl.pallas_call(
        kernel,
        out_shape=out_shape,
        in_specs=in_specs,
        out_specs=out_specs,
        scratch_shapes=list(scratch_shapes),
        compiler_params=pltpu.CompilerParams(vmem_limit_bytes=VMEM_LIMIT),
    )


def swap(values, axis, devices, step):
    return lax.ppermute(values, axis, [(i, i ^ step) for i in range(devices)])


def halve(values, devices, step):
    bit = (lax.axis_index("samples") // step) % 2
    halves = values.reshape(-1, 2, *values.shape[1:])
    kept = lax.dynamic_index_in_dim(halves, bit, 1, keepdims=False)
    given = lax.dynamic_index_in_dim(halves, 1 - bit, 1, keepdims=False)
    return kept, swap(given, "samples", devices, step)


def halve_all(values, devices, steps):
    for step in steps:
        values = sum(halve(values, devices, step))
    return values


def per_device(kinship, relatives, variance, phenotypes, dosage):
    devices = lax.axis_size("samples")
    block_count, positions, tile = kinship.shape[:3]
    people, columns = phenotypes.shape
    variants = dosage.shape[1]
    share_rows = variants // devices
    entries = block_count * (positions - 1)
    capacity = -(-entries // (devices - 1))
    assert capacity <= 2
    hbm = pl.BlockSpec(memory_space=pltpu.HBM)
    vmem = pl.BlockSpec(memory_space=pltpu.VMEM)
    smem = pl.BlockSpec(memory_space=pltpu.SMEM)
    float_of = lambda *shape: jax.ShapeDtypeStruct(shape, jnp.float32)
    room = lambda *shape: pltpu.VMEM(shape, jnp.float32)
    full = float_of(people, columns)
    full_room = room(people, columns)
    tiles_room = pltpu.VMEM((block_count, tile, positions * tile), jnp.bfloat16)
    half = devices // 2
    side = float_of(block_count, tile, columns // 2)
    direction, left, right, diagonal, table, forward, outgoing = call(
        functools.partial(prepare_kernel, devices, capacity),
        [
            full, side, side,
            float_of(people, 1),
            jax.ShapeDtypeStruct((4, max(entries, devices)), jnp.int32),
            jax.ShapeDtypeStruct((capacity, half), jnp.int32),
            float_of(half * capacity, tile, columns),
        ],
        [smem, hbm, hbm, hbm],
        [hbm, hbm, hbm, vmem, smem, smem, hbm],
        [
            room(*kinship.shape), room(block_count, tile), full_room, full_room,
            pltpu.SMEM((devices,), jnp.int32), pltpu.SMEM((devices,), jnp.int32),
            pltpu.SemaphoreType.DMA((5 * block_count + capacity * half + 1,)),
        ],
    )(relatives.T, kinship, variance.reshape(block_count, tile), phenotypes)

    def exchange(blocks, groups=None):
        return lax.all_to_all(
            blocks, "samples", split_axis=0, concat_axis=0, axis_index_groups=groups, tiled=True
        )

    halves = [list(range(half)), list(range(half, devices))]

    def hand_on(partner_blocks):
        return exchange(call(
            forward_kernel,
            float_of(half * capacity, tile, columns // 2),
            [smem, hbm],
            hbm,
            [pltpu.SemaphoreType.DMA((half * capacity,))],
        )(forward, partner_blocks), halves)

    both_dosages = jnp.concatenate(
        [values.reshape(people, devices, share_rows) for values in (dosage, swap(dosage, "cols", 2, 1))], axis=2
    ).reshape(people, 2 * variants)

    def variant_products(values):
        partial = lax.dot_general(
            both_dosages, values, (((0,), (0,)), ((), ())), precision=lax.Precision.HIGH,
            preferred_element_type=jnp.float32,
        )
        return partial.reshape(devices, 2 * share_rows, columns)

    steps = [2 ** i for i in range(devices.bit_length() - 1)]
    partners = [swap(blocks, "samples", devices, half) for blocks in (left, right)]
    near = exchange(outgoing, halves)
    received = [near] + [hand_on(blocks) for blocks in partners] + partners
    direction_scores = halve_all(variant_products(direction), devices, steps[:1])
    received, direction_scores = lax.optimization_barrier((received, direction_scores))
    scaled, outgoing = call(
        functools.partial(apply_kernel, devices, capacity),
        [full, float_of(devices, tile + SUBLANES, columns)],
        [smem, hbm, hbm, vmem] + [hbm] * 6,
        [hbm, hbm],
        [
            room(SUBLANES, columns),
            room(*kinship.shape), full_room, full_room, room(devices * capacity + block_count, tile, columns), full_room,
            tiles_room, tiles_room,
            pltpu.SemaphoreType.DMA((2 * devices + 9,)),
        ],
    )(table, kinship, direction, diagonal, phenotypes, *received)
    later = exchange(outgoing)
    scaled, direction_scores = lax.optimization_barrier((scaled, direction_scores))
    scaled_scores = halve_all(variant_products(scaled), devices, steps[:1])
    direction_scores = halve_all(direction_scores, devices, steps[1:2])
    later, scaled_scores, direction_scores = lax.optimization_barrier((later, scaled_scores, direction_scores))
    direction_kept, direction_given = halve(direction_scores, devices, steps[2])
    scaled_kept, scaled_given = halve(scaled_scores, devices, steps[1])
    sums = call(
        functools.partial(curvature_kernel, devices, capacity),
        float_of(2 * devices, SUBLANES, columns),
        [smem, hbm, hbm, vmem] + [hbm] * 7,
        hbm,
        [
            room(*kinship.shape), full_room, full_room, room(devices * capacity + block_count, tile, columns),
            room(devices, tile + SUBLANES, columns), tiles_room, tiles_room,
            room(2 * devices, SUBLANES, columns),
            pltpu.SemaphoreType.DMA((10,)),
        ],
    )(table, kinship, direction, diagonal, scaled, *received, later)
    sums, direction_kept, scaled_kept = lax.optimization_barrier((sums, direction_kept, scaled_kept))
    all_sums = lax.all_to_all(sums, ("samples", "cols"), split_axis=0, concat_axis=0, tiled=True)
    direction_scores = halve_all(direction_kept + direction_given, devices, steps[3:])[0]
    scaled_scores = halve_all(scaled_kept + scaled_given, devices, steps[2:])[0]
    swapped = swap(jnp.concatenate([direction_scores[share_rows:], scaled_scores[share_rows:]]), "cols", 2, 1)
    solved, scores = call(
        functools.partial(finish_kernel, devices, 1.0 / math.sqrt(people * devices)),
        [full, float_of(share_rows, 2 * columns)],
        [hbm] * 6,
        [hbm, vmem],
        [
            full_room, full_room, room(share_rows, columns), room(share_rows, columns),
            room(2 * share_rows, columns), room(2 * devices, SUBLANES, columns),
            pltpu.SemaphoreType.DMA((10,)),
        ],
    )(direction, scaled, direction_scores, scaled_scores, swapped, all_sums)
    return (solved, scores)


def solution(mesh):
    return jax.shard_map(
        per_device,
        mesh=mesh,
        in_specs=(
            P(("groups", "samples"), None, None, None),
            P("groups", None),
            P(("groups", "samples")),
            P(("groups", "samples"), "cols"),
            P(("groups", "samples"), "cols"),
        ),
        out_specs=(P(("groups", "samples"), "cols"), P(("groups", "cols", "samples"), None)),
        check_vma=False,
    )
```

```python
import functools
import math

import jax
import jax.numpy as jnp
from jax import lax
from jax.experimental import pallas as pl
from jax.experimental.pallas import tpu as pltpu
from jax.sharding import PartitionSpec as P

VMEM_LIMIT = 60 * 1024 * 1024
SUBLANES = 8


def split(values):
    high = values.astype(jnp.bfloat16)
    low = (values - high.astype(jnp.float32)).astype(jnp.bfloat16)
    return high, low


def dot(left, right):
    return jnp.dot(left, right, preferred_element_type=jnp.float32)


def on_diagonal(size):
    rows = lax.broadcasted_iota(jnp.int32, (size, size), 0)
    return rows == lax.broadcasted_iota(jnp.int32, (size, size), 1)


def split_tiles(kinship_ref, high_ref, low_ref):
    block_count, positions, tile = kinship_ref.shape[:3]
    diagonal_mask = on_diagonal(tile)
    for row in range(block_count):
        for position in range(positions):
            values = kinship_ref[row, position]
            if position == 0:
                values = jnp.where(diagonal_mask, 0.0, values)
            high, low = split(values)
            high_ref[row, :, pl.ds(position * tile, tile)] = high
            low_ref[row, :, pl.ds(position * tile, tile)] = low


def product(high, low, blocks):
    parts = [split(block) for block in blocks]
    blocks_high = jnp.concatenate([part[0] for part in parts], axis=0)
    blocks_low = jnp.concatenate([part[1] for part in parts], axis=0)
    return dot(high, blocks_high) + (dot(low, blocks_high) + dot(high, blocks_low))


def column_sums(values):
    rows, columns = values.shape
    return jnp.sum(values.reshape(rows // SUBLANES, SUBLANES, columns), axis=0)


class Copies:
    def __init__(self, semaphores):
        self.semaphores = semaphores
        self.count = 0

    def start(self, source, target):
        copy = pltpu.make_async_copy(source, target, self.semaphores.at[self.count])
        self.count += 1
        copy.start()
        return copy


def wait_all(copies):
    for copy in copies:
        copy.wait()


def quotient(value, divisor):
    if divisor & (divisor - 1) == 0:
        return lax.shift_right_logical(value, jnp.int32(divisor.bit_length() - 1))
    return lax.div(value, jnp.int32(divisor))


def prepare_kernel(devices, capacity, list_ref, kinship_hbm, variance_hbm, phenotypes_hbm, direction_hbm, diagonal_ref,
                   table_ref, forward_ref, outgoing_hbm, kinship_ref, variance_ref, phenotypes_ref, direction_ref,
                   first_ref, last_ref, semaphores):
    block_count, positions, tile = kinship_ref.shape[:3]
    half = devices // 2
    copies = Copies(semaphores)
    loads = [copies.start(variance_hbm, variance_ref)]
    for row in range(block_count):
        block = pl.ds(row * tile, tile)
        loads.append(copies.start(kinship_hbm.at[row], kinship_ref.at[row]))
        loads.append(copies.start(phenotypes_hbm.at[block], phenotypes_ref.at[block]))
    me = lax.axis_index("samples")
    partner = me ^ half
    base = me & half
    spare = me ^ 1
    top = block_count * block_count

    def collect(device):
        for j in range(devices):
            first_ref[j] = jnp.int32(top)
            last_ref[j] = jnp.int32(-1)
        found = []
        for row in range(block_count):
            for position in range(positions - 1):
                listed = list_ref[position, device * block_count + row]
                live = listed >= 0
                safe = jnp.maximum(listed, 0)
                other = quotient(safe, block_count)
                far_block = safe - other * block_count
                key = jnp.where(device < other, row * block_count + far_block, far_block * block_count + row)
                first_ref[other] = jnp.minimum(first_ref[other], jnp.where(live, key, top))
                last_ref[other] = jnp.maximum(last_ref[other], jnp.where(live, key, -1))
                found.append((live, other, far_block, key))
        return found

    def blocks_for(device, other):
        blocks = []
        for key in (first_ref[other], last_ref[other]):
            safe = jnp.clip(key, 0, top - 1)
            lower = quotient(safe, block_count)
            higher = safe - lower * block_count
            blocks.append(jnp.where(key == safe, jnp.where(device < other, lower, higher), 0))
        return blocks

    collect(partner)
    for i in range(half):
        blocks = blocks_for(partner, base + i)
        for slot in range(capacity):
            forward_ref[slot, i] = blocks[slot]
    for entry, (live, other, far_block, key) in enumerate(collect(me)):
        first, last = first_ref[other], last_ref[other]
        handled = jnp.where(me < other, first, last)
        weight = jnp.where(first == last, 1, 2)
        slot = jnp.where(key == first, 0, capacity - 1)
        place = jnp.where(other == partner, devices * capacity + far_block, other * capacity + slot)
        table_ref[0, entry] = jnp.where(live, place, spare * capacity)
        table_ref[1, entry] = jnp.where(live, other, spare)
        table_ref[2, entry] = jnp.where(live & (key == handled), weight, 0)
    for other in range(devices):
        blocks = blocks_for(me, other)
        table_ref[3, other] = jnp.where(me < other, blocks[1], blocks[0])
    near = [blocks_for(me, base + i) for i in range(half)]
    stores = []
    diagonal_mask = on_diagonal(tile)
    loads[0].wait()
    for row in range(block_count):
        wait_all(loads[1 + 2 * row:3 + 2 * row])
        block = pl.ds(row * tile, tile)
        total = jnp.where(diagonal_mask, variance_ref[row:row + 1, :], kinship_ref[row, 0])
        for position in range(1, positions):
            total = total + kinship_ref[row, position]
        diagonal = jnp.sum(total, axis=1, keepdims=True)
        diagonal_ref[block, :] = diagonal
        direction_ref[block, :] = phenotypes_ref[block, :] * (1.0 / diagonal)
        stores.append(copies.start(direction_ref.at[block], direction_hbm.at[block]))
    for i in range(half):
        for slot in range(capacity):
            start = pl.multiple_of(near[i][slot] * tile, tile)
            stores.append(copies.start(direction_ref.at[pl.ds(start, tile)], outgoing_hbm.at[i * capacity + slot]))
    wait_all(stores)


def forward_kernel(forward_ref, partner_hbm, outgoing_hbm, partner_ref, semaphores):
    capacity, half = forward_ref.shape
    tile = outgoing_hbm.shape[1]
    copies = Copies(semaphores)
    copies.start(partner_hbm, partner_ref).wait()
    stores = []
    for i in range(half):
        for slot in range(capacity):
            start = pl.multiple_of(forward_ref[slot, i] * tile, tile)
            stores.append(copies.start(partner_ref.at[pl.ds(start, tile)], outgoing_hbm.at[i * capacity + slot]))
    wait_all(stores)


def load_received(copies, devices, capacity, near_hbm, far_hbm, partner_hbm, received_ref):
    half = devices // 2
    base = lax.axis_index("samples") & half
    count = half * capacity
    return [
        copies.start(near_hbm, received_ref.at[pl.ds(base * capacity, count)]),
        copies.start(far_hbm, received_ref.at[pl.ds((half - base) * capacity, count)]),
        copies.start(partner_hbm, received_ref.at[pl.ds(devices * capacity, partner_hbm.shape[0])]),
    ]


def apply_kernel(devices, capacity, table_ref, kinship_hbm, direction_hbm, diagonal_ref, phenotypes_hbm, near_hbm,
                 far_hbm, partner_hbm, scaled_hbm, outgoing_hbm, sums_ref, kinship_ref, direction_ref, phenotypes_ref, received_ref,
                 scaled_ref, high_ref, low_ref, semaphores):
    block_count, positions, tile = kinship_ref.shape[:3]
    columns = direction_ref.shape[1]
    copies = Copies(semaphores)
    tiles = copies.start(kinship_hbm, kinship_ref)
    arrivals = load_received(copies, devices, capacity, near_hbm, far_hbm, partner_hbm, received_ref)
    loads = [copies.start(direction_hbm, direction_ref), copies.start(phenotypes_hbm, phenotypes_ref)]
    norm = jnp.zeros((SUBLANES, columns), jnp.float32)
    cross = jnp.zeros((SUBLANES, columns), jnp.float32)
    tiles.wait()
    split_tiles(kinship_ref, high_ref, low_ref)
    wait_all(loads)
    wait_all(arrivals)
    for row in range(block_count):
        block = pl.ds(row * tile, tile)
        here = direction_ref[block, :]
        blocks = [here]
        for position in range(positions - 1):
            entry = row * (positions - 1) + position
            blocks.append(received_ref[table_ref[0, entry]])
        mapped = product(high_ref[row], low_ref[row], blocks)
        scaled_ref[block, :] = mapped * (1.0 / diagonal_ref[block, :])
        norm = norm + column_sums(here * phenotypes_ref[block, :])
        cross = cross + column_sums(here * mapped)
    sums_ref[...] = jnp.zeros_like(sums_ref)
    sums_ref[0:1, :] = jnp.sum(norm, axis=0, keepdims=True)
    sums_ref[1:2, :] = jnp.sum(cross, axis=0, keepdims=True)
    stores = []
    for other in range(devices):
        start = pl.multiple_of(table_ref[3, other] * tile, tile)
        stores.append(copies.start(scaled_ref.at[pl.ds(start, tile)], outgoing_hbm.at[other, pl.ds(0, tile)]))
        stores.append(copies.start(sums_ref, outgoing_hbm.at[other, pl.ds(tile, SUBLANES)]))
    stores.append(copies.start(scaled_ref, scaled_hbm))
    wait_all(stores)


def curvature_kernel(devices, capacity, table_ref, kinship_hbm, direction_hbm, diagonal_ref, scaled_hbm, near_hbm,
                     far_hbm, partner_hbm, later_hbm, sums_hbm, kinship_ref, direction_ref, scaled_ref, received_ref, later_ref, high_ref,
                     low_ref, sums_ref, semaphores):
    block_count, positions, tile = kinship_ref.shape[:3]
    columns = direction_ref.shape[1]
    copies = Copies(semaphores)
    tiles = copies.start(kinship_hbm, kinship_ref)
    loads = [
        copies.start(later_hbm, later_ref),
        copies.start(direction_hbm, direction_ref),
        copies.start(scaled_hbm, scaled_ref),
    ]
    loads += load_received(copies, devices, capacity, near_hbm, far_hbm, partner_hbm, received_ref)
    tiles.wait()
    split_tiles(kinship_ref, high_ref, low_ref)
    wait_all(loads)
    first_sums = later_ref[0, pl.ds(tile, SUBLANES), :]
    for other in range(1, devices):
        first_sums = first_sums + later_ref[other, pl.ds(tile, SUBLANES), :]
    rho = first_sums[1:2, :] / first_sums[0:1, :]
    norm = jnp.zeros((SUBLANES, columns), jnp.float32)
    bend = jnp.zeros((SUBLANES, columns), jnp.float32)
    for row in range(block_count):
        block = pl.ds(row * tile, tile)
        here = scaled_ref[block, :] - rho * direction_ref[block, :]
        blocks = [here]
        for position in range(positions - 1):
            entry = row * (positions - 1) + position
            weight = table_ref[2, entry].astype(jnp.float32)
            there = later_ref[table_ref[1, entry], pl.ds(0, tile), :]
            blocks.append(weight * (there - rho * received_ref[table_ref[0, entry]]))
        mapped = product(high_ref[row], low_ref[row], blocks)
        norm = norm + column_sums(here * here * diagonal_ref[block, :])
        bend = bend + column_sums(here * mapped)
    row_ids = lax.broadcasted_iota(jnp.int32, first_sums.shape, 0)
    sums = jnp.where(row_ids == 2, jnp.sum(norm, axis=0, keepdims=True), first_sums)
    sums = jnp.where(row_ids == 3, jnp.sum(bend, axis=0, keepdims=True), sums)
    for i in range(2 * devices):
        sums_ref[i] = sums
    store = copies.start(sums_ref, sums_hbm)
    store.wait()


def coefficients(sums, shared):
    norm, cross = sums[0:1, :], sums[1:2, :]
    later_norm, bend = shared[2:3, :], shared[3:4, :]
    curve = norm + cross
    ratio = later_norm / curve
    step = jnp.where(later_norm > 0, later_norm / (later_norm + bend - later_norm * ratio), 0.0)
    start = norm / curve
    return start * (1.0 + step * (ratio + cross / norm)), -start * step


def finish_kernel(devices, norm_scale, direction_hbm, scaled_hbm, direction_scores_hbm, scaled_scores_hbm,
                  swapped_hbm, sums_hbm, solved_hbm, scores_ref, direction_ref, scaled_ref, direction_scores_ref,
                  scaled_scores_ref, swapped_ref, sums_ref, semaphores):
    people, columns = direction_ref.shape
    rows = scores_ref.shape[0]
    column = lax.axis_index("cols")
    copies = Copies(semaphores)
    arrival = copies.start(sums_hbm, sums_ref)
    vectors = [copies.start(direction_hbm, direction_ref), copies.start(scaled_hbm, scaled_ref)]
    shares = [
        copies.start(direction_scores_hbm.at[pl.ds(0, rows)], direction_scores_ref),
        copies.start(scaled_scores_hbm.at[pl.ds(0, rows)], scaled_scores_ref),
        copies.start(swapped_hbm, swapped_ref),
    ]

    def total(which):
        sums = sums_ref[which]
        shared = sums
        for i in range(1, devices):
            shared = shared + sums_ref[2 * i + which]
        return sums, shared

    arrival.wait()
    along, across = coefficients(*total(column))
    other_along, other_across = coefficients(*total(1 - column))
    wait_all(vectors)
    stores = []
    part_rows = people // 4
    for part in range(4):
        block = pl.ds(part * part_rows, part_rows)
        direction_ref[block, :] = along * direction_ref[block, :] + across * scaled_ref[block, :]
        stores.append(copies.start(direction_ref.at[block], solved_hbm.at[block]))
    wait_all(shares)
    own = pl.multiple_of(column * columns, columns)
    other = pl.multiple_of((1 - column) * columns, columns)
    scores_ref[:, pl.ds(own, columns)] = norm_scale * (
        along * direction_scores_ref[...] + across * scaled_scores_ref[...]
    )
    scores_ref[:, pl.ds(other, columns)] = norm_scale * (
        other_along * swapped_ref[pl.ds(0, rows), :] + other_across * swapped_ref[pl.ds(rows, rows), :]
    )
    wait_all(stores)


def call(kernel, out_shape, in_specs, out_specs, scratch_shapes):
    return pl.pallas_call(
        kernel,
        out_shape=out_shape,
        in_specs=in_specs,
        out_specs=out_specs,
        scratch_shapes=list(scratch_shapes),
        compiler_params=pltpu.CompilerParams(vmem_limit_bytes=VMEM_LIMIT),
    )


def swap(values, axis, devices, step):
    return lax.ppermute(values, axis, [(i, i ^ step) for i in range(devices)])


def halve(values, devices, step):
    bit = (lax.axis_index("samples") // step) % 2
    halves = values.reshape(-1, 2, *values.shape[1:])
    kept = lax.dynamic_index_in_dim(halves, bit, 1, keepdims=False)
    given = lax.dynamic_index_in_dim(halves, 1 - bit, 1, keepdims=False)
    return kept, swap(given, "samples", devices, step)


def halve_all(values, devices, steps):
    for step in steps:
        values = sum(halve(values, devices, step))
    return values


def per_device(kinship, relatives, variance, phenotypes, dosage):
    devices = lax.axis_size("samples")
    block_count, positions, tile = kinship.shape[:3]
    people, columns = phenotypes.shape
    variants = dosage.shape[1]
    share_rows = variants // devices
    entries = block_count * (positions - 1)
    capacity = -(-entries // (devices - 1))
    assert capacity <= 2
    hbm = pl.BlockSpec(memory_space=pltpu.HBM)
    vmem = pl.BlockSpec(memory_space=pltpu.VMEM)
    smem = pl.BlockSpec(memory_space=pltpu.SMEM)
    float_of = lambda *shape: jax.ShapeDtypeStruct(shape, jnp.float32)
    room = lambda *shape: pltpu.VMEM(shape, jnp.float32)
    full = float_of(people, columns)
    full_room = room(people, columns)
    tiles_room = pltpu.VMEM((block_count, tile, positions * tile), jnp.bfloat16)
    half = devices // 2
    direction, diagonal, table, forward, outgoing = call(
        functools.partial(prepare_kernel, devices, capacity),
        [
            full,
            float_of(people, 1),
            jax.ShapeDtypeStruct((4, max(entries, devices)), jnp.int32),
            jax.ShapeDtypeStruct((capacity, half), jnp.int32),
            float_of(half * capacity, tile, columns),
        ],
        [smem, hbm, hbm, hbm],
        [hbm, vmem, smem, smem, hbm],
        [
            room(*kinship.shape), room(block_count, tile), full_room, full_room,
            pltpu.SMEM((devices,), jnp.int32), pltpu.SMEM((devices,), jnp.int32),
            pltpu.SemaphoreType.DMA((3 * block_count + capacity * half + 1,)),
        ],
    )(relatives.T, kinship, variance.reshape(block_count, tile), phenotypes)

    def exchange(blocks, groups=None):
        return lax.all_to_all(
            blocks, "samples", split_axis=0, concat_axis=0, axis_index_groups=groups, tiled=True
        )

    halves = [list(range(half)), list(range(half, devices))]

    both_dosages = jnp.concatenate(
        [values.reshape(people, devices, share_rows) for values in (dosage, swap(dosage, "cols", 2, 1))], axis=2
    ).reshape(people, 2 * variants)

    def variant_products(values):
        partial = lax.dot_general(
            both_dosages, values, (((0,), (0,)), ((), ())), precision=lax.Precision.HIGH,
            preferred_element_type=jnp.float32,
        )
        return partial.reshape(devices, 2 * share_rows, columns)

    steps = [2 ** i for i in range(devices.bit_length() - 1)]
    partner = swap(direction, "samples", devices, half)
    near = exchange(outgoing, halves)
    partner, near = lax.optimization_barrier((partner, near))
    far = exchange(call(
        forward_kernel,
        float_of(half * capacity, tile, columns),
        [smem, hbm],
        hbm,
        [full_room, pltpu.SemaphoreType.DMA((half * capacity + 1,))],
    )(forward, partner), halves)
    received = [near, far, partner.reshape(block_count, tile, columns)]
    direction_scores = halve_all(variant_products(direction), devices, steps[:1])
    received, direction_scores = lax.optimization_barrier((received, direction_scores))
    scaled, outgoing = call(
        functools.partial(apply_kernel, devices, capacity),
        [full, float_of(devices, tile + SUBLANES, columns)],
        [smem, hbm, hbm, vmem] + [hbm] * 4,
        [hbm, hbm],
        [
            room(SUBLANES, columns),
            room(*kinship.shape), full_room, full_room, room(devices * capacity + block_count, tile, columns), full_room,
            tiles_room, tiles_room,
            pltpu.SemaphoreType.DMA((2 * devices + 9,)),
        ],
    )(table, kinship, direction, diagonal, phenotypes, *received)
    later = exchange(outgoing)
    scaled, direction_scores = lax.optimization_barrier((scaled, direction_scores))
    scaled_scores = halve_all(variant_products(scaled), devices, steps[:1])
    direction_scores = halve_all(direction_scores, devices, steps[1:2])
    later, scaled_scores, direction_scores = lax.optimization_barrier((later, scaled_scores, direction_scores))
    direction_kept, direction_given = halve(direction_scores, devices, steps[2])
    scaled_kept, scaled_given = halve(scaled_scores, devices, steps[1])
    sums = call(
        functools.partial(curvature_kernel, devices, capacity),
        float_of(2 * devices, SUBLANES, columns),
        [smem, hbm, hbm, vmem] + [hbm] * 5,
        hbm,
        [
            room(*kinship.shape), full_room, full_room, room(devices * capacity + block_count, tile, columns),
            room(devices, tile + SUBLANES, columns), tiles_room, tiles_room,
            room(2 * devices, SUBLANES, columns),
            pltpu.SemaphoreType.DMA((10,)),
        ],
    )(table, kinship, direction, diagonal, scaled, *received, later)
    sums, direction_kept, scaled_kept = lax.optimization_barrier((sums, direction_kept, scaled_kept))
    direction_scores = halve_all(direction_kept + direction_given, devices, steps[3:])[0]
    scaled_kept, scaled_given = halve(scaled_kept + scaled_given, devices, steps[2])
    sums, scaled_kept, direction_scores = lax.optimization_barrier((sums, scaled_kept, direction_scores))
    all_sums = lax.all_to_all(sums, ("samples", "cols"), split_axis=0, concat_axis=0, tiled=True)
    scaled_scores = halve_all(scaled_kept + scaled_given, devices, steps[3:])[0]
    swapped = swap(jnp.concatenate([direction_scores[share_rows:], scaled_scores[share_rows:]]), "cols", 2, 1)
    solved, scores = call(
        functools.partial(finish_kernel, devices, 1.0 / math.sqrt(people * devices)),
        [full, float_of(share_rows, 2 * columns)],
        [hbm] * 6,
        [hbm, vmem],
        [
            full_room, full_room, room(share_rows, columns), room(share_rows, columns),
            room(2 * share_rows, columns), room(2 * devices, SUBLANES, columns),
            pltpu.SemaphoreType.DMA((10,)),
        ],
    )(direction, scaled, direction_scores, scaled_scores, swapped, all_sums)
    return (solved, scores)


def solution(mesh):
    return jax.shard_map(
        per_device,
        mesh=mesh,
        in_specs=(
            P(("groups", "samples"), None, None, None),
            P("groups", None),
            P(("groups", "samples")),
            P(("groups", "samples"), "cols"),
            P(("groups", "samples"), "cols"),
        ),
        out_specs=(P(("groups", "samples"), "cols"), P(("groups", "cols", "samples"), None)),
        check_vma=False,
    )
```

```python
import functools
import math

import jax
import jax.numpy as jnp
from jax import lax
from jax.experimental import pallas as pl
from jax.experimental.pallas import tpu as pltpu
from jax.sharding import PartitionSpec as P

VMEM_LIMIT = 60 * 1024 * 1024
SUBLANES = 8


def split(values):
    high = values.astype(jnp.bfloat16)
    low = (values - high.astype(jnp.float32)).astype(jnp.bfloat16)
    return high, low


def dot(left, right):
    return jnp.dot(left, right, preferred_element_type=jnp.float32)


def on_diagonal(size):
    rows = lax.broadcasted_iota(jnp.int32, (size, size), 0)
    return rows == lax.broadcasted_iota(jnp.int32, (size, size), 1)


def split_tiles(kinship_ref, high_ref, low_ref):
    block_count, positions, tile = kinship_ref.shape[:3]
    diagonal_mask = on_diagonal(tile)
    for row in range(block_count):
        for position in range(positions):
            values = kinship_ref[row, position]
            if position == 0:
                values = jnp.where(diagonal_mask, 0.0, values)
            high, low = split(values)
            high_ref[row, :, pl.ds(position * tile, tile)] = high
            low_ref[row, :, pl.ds(position * tile, tile)] = low


def product(high, low, blocks):
    parts = [split(block) for block in blocks]
    blocks_high = jnp.concatenate([part[0] for part in parts], axis=0)
    blocks_low = jnp.concatenate([part[1] for part in parts], axis=0)
    return dot(high, blocks_high) + (dot(low, blocks_high) + dot(high, blocks_low))


def column_sums(values):
    rows, columns = values.shape
    return jnp.sum(values.reshape(rows // SUBLANES, SUBLANES, columns), axis=0)


class Copies:
    def __init__(self, semaphores):
        self.semaphores = semaphores
        self.count = 0

    def start(self, source, target):
        copy = pltpu.make_async_copy(source, target, self.semaphores.at[self.count])
        self.count += 1
        copy.start()
        return copy


def wait_all(copies):
    for copy in copies:
        copy.wait()


def quotient(value, divisor):
    if divisor & (divisor - 1) == 0:
        return lax.shift_right_logical(value, jnp.int32(divisor.bit_length() - 1))
    return lax.div(value, jnp.int32(divisor))


def prepare_kernel(devices, capacity, list_ref, kinship_hbm, variance_hbm, phenotypes_hbm, direction_hbm, diagonal_ref,
                   table_ref, forward_ref, *refs):
    half = devices // 2
    outgoing_hbm, refs = refs[:half - 1], refs[half - 1:]
    kinship_ref, variance_ref, phenotypes_ref, direction_ref, first_ref, last_ref, semaphores = refs
    block_count, positions, tile = kinship_ref.shape[:3]
    copies = Copies(semaphores)
    loads = [copies.start(variance_hbm, variance_ref)]
    for row in range(block_count):
        block = pl.ds(row * tile, tile)
        loads.append(copies.start(kinship_hbm.at[row], kinship_ref.at[row]))
        loads.append(copies.start(phenotypes_hbm.at[block], phenotypes_ref.at[block]))
    me = lax.axis_index("samples")
    partner = me ^ half
    spare = me ^ 1
    top = block_count * block_count

    def collect(device):
        for j in range(devices):
            first_ref[j] = jnp.int32(top)
            last_ref[j] = jnp.int32(-1)
        found = []
        for row in range(block_count):
            for position in range(positions - 1):
                listed = list_ref[position, device * block_count + row]
                live = listed >= 0
                safe = jnp.maximum(listed, 0)
                other = quotient(safe, block_count)
                far_block = safe - other * block_count
                key = jnp.where(device < other, row * block_count + far_block, far_block * block_count + row)
                first_ref[other] = jnp.minimum(first_ref[other], jnp.where(live, key, top))
                last_ref[other] = jnp.maximum(last_ref[other], jnp.where(live, key, -1))
                found.append((live, other, far_block, key))
        return found

    def blocks_for(device, other):
        blocks = []
        for key in (first_ref[other], last_ref[other]):
            safe = jnp.clip(key, 0, top - 1)
            lower = quotient(safe, block_count)
            higher = safe - lower * block_count
            blocks.append(jnp.where(key == safe, jnp.where(device < other, lower, higher), 0))
        return blocks

    collect(partner)
    for k in range(1, half):
        blocks = blocks_for(partner, me ^ k)
        for slot in range(capacity):
            forward_ref[slot, k] = blocks[slot]
    for entry, (live, other, far_block, key) in enumerate(collect(me)):
        first, last = first_ref[other], last_ref[other]
        handled = jnp.where(me < other, first, last)
        weight = jnp.where(first == last, 1, 2)
        slot = jnp.where(key == first, 0, capacity - 1)
        place = jnp.where(other == partner, devices * capacity + far_block, other * capacity + slot)
        table_ref[0, entry] = jnp.where(live, place, spare * capacity)
        table_ref[1, entry] = jnp.where(live, other, spare)
        table_ref[2, entry] = jnp.where(live & (key == handled), weight, 0)
    for other in range(devices):
        blocks = blocks_for(me, other)
        table_ref[3, other] = jnp.where(me < other, blocks[1], blocks[0])
    near = [blocks_for(me, me ^ k) for k in range(1, half)]
    stores = []
    diagonal_mask = on_diagonal(tile)
    loads[0].wait()
    for row in range(block_count):
        wait_all(loads[1 + 2 * row:3 + 2 * row])
        block = pl.ds(row * tile, tile)
        total = jnp.where(diagonal_mask, variance_ref[row:row + 1, :], kinship_ref[row, 0])
        for position in range(1, positions):
            total = total + kinship_ref[row, position]
        diagonal = jnp.sum(total, axis=1, keepdims=True)
        diagonal_ref[block, :] = diagonal
        direction_ref[block, :] = phenotypes_ref[block, :] * (1.0 / diagonal)
        stores.append(copies.start(direction_ref.at[block], direction_hbm.at[block]))
    for k in range(1, half):
        for slot in range(capacity):
            start = pl.multiple_of(near[k - 1][slot] * tile, tile)
            stores.append(copies.start(direction_ref.at[pl.ds(start, tile)], outgoing_hbm[k - 1].at[slot]))
    wait_all(stores)


def forward_kernel(forward_ref, *refs):
    capacity, half = forward_ref.shape
    partner_hbm = refs[half - 1]
    outgoing_hbm, (partner_ref, semaphores) = refs[-1 - half:-2], refs[-2:]
    tile = outgoing_hbm[0].shape[1]
    copies = Copies(semaphores)
    copies.start(partner_hbm, partner_ref).wait()
    stores = []
    for k in range(1, half):
        for slot in range(capacity):
            start = pl.multiple_of(forward_ref[slot, k] * tile, tile)
            stores.append(copies.start(partner_ref.at[pl.ds(start, tile)], outgoing_hbm[k - 1].at[slot]))
    wait_all(stores)


def load_received(copies, devices, capacity, received_hbm, received_ref):
    half = devices // 2
    me = lax.axis_index("samples")
    near_hbm, far_hbm, partner_hbm = received_hbm[:half - 1], received_hbm[half - 1:-1], received_hbm[-1]
    loads = [copies.start(partner_hbm, received_ref.at[pl.ds(devices * capacity, partner_hbm.shape[0])])]
    for k in range(1, half):
        mate = me ^ k
        loads.append(copies.start(near_hbm[k - 1], received_ref.at[pl.ds(mate * capacity, capacity)]))
        loads.append(copies.start(far_hbm[k - 1], received_ref.at[pl.ds((mate ^ half) * capacity, capacity)]))
    return loads


def apply_kernel(devices, capacity, table_ref, kinship_hbm, direction_hbm, diagonal_ref, phenotypes_hbm, *refs):
    received_hbm, refs = refs[:devices - 1], refs[devices - 1:]
    (scaled_hbm, outgoing_hbm, sums_ref, kinship_ref, direction_ref, phenotypes_ref, received_ref, scaled_ref, high_ref,
     low_ref, semaphores) = refs
    block_count, positions, tile = kinship_ref.shape[:3]
    columns = direction_ref.shape[1]
    copies = Copies(semaphores)
    tiles = copies.start(kinship_hbm, kinship_ref)
    arrivals = load_received(copies, devices, capacity, received_hbm, received_ref)
    loads = [copies.start(direction_hbm, direction_ref), copies.start(phenotypes_hbm, phenotypes_ref)]
    norm = jnp.zeros((SUBLANES, columns), jnp.float32)
    cross = jnp.zeros((SUBLANES, columns), jnp.float32)
    tiles.wait()
    split_tiles(kinship_ref, high_ref, low_ref)
    wait_all(loads)
    wait_all(arrivals)
    for row in range(block_count):
        block = pl.ds(row * tile, tile)
        here = direction_ref[block, :]
        blocks = [here]
        for position in range(positions - 1):
            entry = row * (positions - 1) + position
            blocks.append(received_ref[table_ref[0, entry]])
        mapped = product(high_ref[row], low_ref[row], blocks)
        scaled_ref[block, :] = mapped * (1.0 / diagonal_ref[block, :])
        norm = norm + column_sums(here * phenotypes_ref[block, :])
        cross = cross + column_sums(here * mapped)
    sums_ref[...] = jnp.zeros_like(sums_ref)
    sums_ref[0:1, :] = jnp.sum(norm, axis=0, keepdims=True)
    sums_ref[1:2, :] = jnp.sum(cross, axis=0, keepdims=True)
    stores = []
    for other in range(devices):
        start = pl.multiple_of(table_ref[3, other] * tile, tile)
        stores.append(copies.start(scaled_ref.at[pl.ds(start, tile)], outgoing_hbm.at[other, pl.ds(0, tile)]))
        stores.append(copies.start(sums_ref, outgoing_hbm.at[other, pl.ds(tile, SUBLANES)]))
    stores.append(copies.start(scaled_ref, scaled_hbm))
    wait_all(stores)


def curvature_kernel(devices, capacity, table_ref, kinship_hbm, direction_hbm, diagonal_ref, scaled_hbm, later_hbm,
                     *refs):
    received_hbm = refs[:devices - 1]
    (sums_hbm, kinship_ref, direction_ref, scaled_ref, received_ref, later_ref, high_ref, low_ref, sums_ref,
     semaphores) = refs[-10:]
    block_count, positions, tile = kinship_ref.shape[:3]
    columns = direction_ref.shape[1]
    copies = Copies(semaphores)
    tiles = copies.start(kinship_hbm, kinship_ref)
    loads = [
        copies.start(later_hbm, later_ref),
        copies.start(direction_hbm, direction_ref),
        copies.start(scaled_hbm, scaled_ref),
    ]
    loads += load_received(copies, devices, capacity, received_hbm, received_ref)
    tiles.wait()
    split_tiles(kinship_ref, high_ref, low_ref)
    wait_all(loads)
    first_sums = later_ref[0, pl.ds(tile, SUBLANES), :]
    for other in range(1, devices):
        first_sums = first_sums + later_ref[other, pl.ds(tile, SUBLANES), :]
    rho = first_sums[1:2, :] / first_sums[0:1, :]
    norm = jnp.zeros((SUBLANES, columns), jnp.float32)
    bend = jnp.zeros((SUBLANES, columns), jnp.float32)
    for row in range(block_count):
        block = pl.ds(row * tile, tile)
        here = scaled_ref[block, :] - rho * direction_ref[block, :]
        blocks = [here]
        for position in range(positions - 1):
            entry = row * (positions - 1) + position
            weight = table_ref[2, entry].astype(jnp.float32)
            there = later_ref[table_ref[1, entry], pl.ds(0, tile), :]
            blocks.append(weight * (there - rho * received_ref[table_ref[0, entry]]))
        mapped = product(high_ref[row], low_ref[row], blocks)
        norm = norm + column_sums(here * here * diagonal_ref[block, :])
        bend = bend + column_sums(here * mapped)
    row_ids = lax.broadcasted_iota(jnp.int32, first_sums.shape, 0)
    sums = jnp.where(row_ids == 2, jnp.sum(norm, axis=0, keepdims=True), first_sums)
    sums = jnp.where(row_ids == 3, jnp.sum(bend, axis=0, keepdims=True), sums)
    for i in range(2 * devices):
        sums_ref[i] = sums
    store = copies.start(sums_ref, sums_hbm)
    store.wait()


def coefficients(sums, shared):
    norm, cross = sums[0:1, :], sums[1:2, :]
    later_norm, bend = shared[2:3, :], shared[3:4, :]
    curve = norm + cross
    ratio = later_norm / curve
    step = jnp.where(later_norm > 0, later_norm / (later_norm + bend - later_norm * ratio), 0.0)
    start = norm / curve
    return start * (1.0 + step * (ratio + cross / norm)), -start * step


def finish_kernel(devices, norm_scale, direction_hbm, scaled_hbm, direction_scores_hbm, scaled_scores_hbm,
                  swapped_hbm, sums_hbm, solved_hbm, scores_ref, direction_ref, scaled_ref, direction_scores_ref,
                  scaled_scores_ref, swapped_ref, sums_ref, semaphores):
    people, columns = direction_ref.shape
    rows = scores_ref.shape[0]
    column = lax.axis_index("cols")
    copies = Copies(semaphores)
    arrival = copies.start(sums_hbm, sums_ref)
    vectors = [copies.start(direction_hbm, direction_ref), copies.start(scaled_hbm, scaled_ref)]
    shares = [
        copies.start(direction_scores_hbm.at[pl.ds(0, rows)], direction_scores_ref),
        copies.start(scaled_scores_hbm.at[pl.ds(0, rows)], scaled_scores_ref),
        copies.start(swapped_hbm, swapped_ref),
    ]

    def total(which):
        sums = sums_ref[which]
        shared = sums
        for i in range(1, devices):
            shared = shared + sums_ref[2 * i + which]
        return sums, shared

    arrival.wait()
    along, across = coefficients(*total(column))
    other_along, other_across = coefficients(*total(1 - column))
    wait_all(vectors)
    stores = []
    part_rows = people // 4
    for part in range(4):
        block = pl.ds(part * part_rows, part_rows)
        direction_ref[block, :] = along * direction_ref[block, :] + across * scaled_ref[block, :]
        stores.append(copies.start(direction_ref.at[block], solved_hbm.at[block]))
    wait_all(shares)
    own = pl.multiple_of(column * columns, columns)
    other = pl.multiple_of((1 - column) * columns, columns)
    scores_ref[:, pl.ds(own, columns)] = norm_scale * (
        along * direction_scores_ref[...] + across * scaled_scores_ref[...]
    )
    scores_ref[:, pl.ds(other, columns)] = norm_scale * (
        other_along * swapped_ref[pl.ds(0, rows), :] + other_across * swapped_ref[pl.ds(rows, rows), :]
    )
    wait_all(stores)


def call(kernel, out_shape, in_specs, out_specs, scratch_shapes):
    return pl.pallas_call(
        kernel,
        out_shape=out_shape,
        in_specs=in_specs,
        out_specs=out_specs,
        scratch_shapes=list(scratch_shapes),
        compiler_params=pltpu.CompilerParams(vmem_limit_bytes=VMEM_LIMIT),
    )


def swap(values, axis, devices, step):
    return lax.ppermute(values, axis, [(i, i ^ step) for i in range(devices)])


def after(value, *others):
    return lax.optimization_barrier((value, *others))[0]


def per_device(kinship, relatives, variance, phenotypes, dosage):
    devices = lax.axis_size("samples")
    block_count, positions, tile = kinship.shape[:3]
    people, columns = phenotypes.shape
    variants = dosage.shape[1]
    share_rows = variants // devices
    entries = block_count * (positions - 1)
    capacity = -(-entries // (devices - 1))
    assert capacity <= 2
    hbm = pl.BlockSpec(memory_space=pltpu.HBM)
    anywhere = pl.BlockSpec(memory_space=pl.ANY)
    vmem = pl.BlockSpec(memory_space=pltpu.VMEM)
    smem = pl.BlockSpec(memory_space=pltpu.SMEM)
    float_of = lambda *shape: jax.ShapeDtypeStruct(shape, jnp.float32)
    room = lambda *shape: pltpu.VMEM(shape, jnp.float32)
    full = float_of(people, columns)
    full_room = room(people, columns)
    tiles_room = pltpu.VMEM((block_count, tile, positions * tile), jnp.bfloat16)
    half = devices // 2
    near_by = list(range(1, half))
    direction, diagonal, table, forward, *outgoing = call(
        functools.partial(prepare_kernel, devices, capacity),
        [
            full,
            float_of(people, 1),
            jax.ShapeDtypeStruct((4, max(entries, devices)), jnp.int32),
            jax.ShapeDtypeStruct((capacity, half), jnp.int32),
        ] + [float_of(capacity, tile, columns)] * (half - 1),
        [smem, hbm, hbm, hbm],
        [hbm, vmem, smem, smem] + [hbm] * (half - 1),
        [
            room(*kinship.shape), room(block_count, tile), full_room, full_room,
            pltpu.SMEM((devices,), jnp.int32), pltpu.SMEM((devices,), jnp.int32),
            pltpu.SemaphoreType.DMA((3 * block_count + capacity * (half - 1) + 1,)),
        ],
    )(relatives.T, kinship, variance.reshape(block_count, tile), phenotypes)

    def to_mates(blocks):
        return [swap(block, "samples", devices, k) for k, block in zip(near_by, blocks)]

    me = lax.axis_index("samples")
    dosage = after(dosage, direction)
    other_dosage = swap(dosage, "cols", 2, 1)
    dosages = [values.reshape(people, devices, share_rows) for values in (dosage, other_dosage)]
    fourth = devices // 4
    grouped = [
        jnp.concatenate([
            lax.dynamic_index_in_dim(values, me ^ (4 * j + k), 1, keepdims=False)
            for j in range(fourth) for values in dosages
        ], axis=1)
        for k in range(4)
    ]

    def variant_products(values):
        return [
            lax.dot_general(
                group, values, (((0,), (0,)), ((), ())), precision=lax.Precision.HIGH,
                preferred_element_type=jnp.float32,
            ).reshape(fourth, 2 * share_rows, columns)
            for group in grouped
        ]

    def neighbour_shares(products):
        return [swap(products[k], "samples", devices, k) for k in range(1, 4)]

    def over_the_middle(values):
        return values[:fourth // 2], swap(values[fourth // 2:], "samples", devices, half)

    def remaining(values):
        step = half // 2
        while values.shape[0] > 1:
            count = values.shape[0] // 2
            values = values[:count] + swap(values[count:], "samples", devices, step)
            step //= 2
        return values[0]

    near = to_mates(after(outgoing, other_dosage))
    partner = swap(direction, "samples", devices, half)
    direction_products = variant_products(direction)
    direction_shares = neighbour_shares(direction_products)
    far = to_mates(call(
        forward_kernel,
        [float_of(capacity, tile, columns)] * (half - 1),
        [smem] + [anywhere] * (half + 4),
        [hbm] * (half - 1),
        [full_room, pltpu.SemaphoreType.DMA((capacity * (half - 1) + 1,))],
    )(forward, *near, partner, *direction_products))
    received = near + far + [partner.reshape(block_count, tile, columns)]
    scaled, outgoing = call(
        functools.partial(apply_kernel, devices, capacity),
        [full, float_of(devices, tile + SUBLANES, columns)],
        [smem, hbm, hbm, vmem, hbm] + [anywhere] * (devices - 1),
        [hbm, hbm],
        [
            room(SUBLANES, columns),
            room(*kinship.shape), full_room, full_room, room(devices * capacity + block_count, tile, columns),
            full_room, tiles_room, tiles_room,
            pltpu.SemaphoreType.DMA((3 * devices + 5,)),
        ],
    )(table, kinship, direction, diagonal, phenotypes, *received)
    later = lax.all_to_all(outgoing, "samples", split_axis=0, concat_axis=0, tiled=True)
    scaled_products = variant_products(scaled)
    scaled_sum = scaled_products[0] + sum(neighbour_shares(scaled_products))
    direction_sum = after(direction_products[0], scaled) + sum(direction_shares)
    scaled_kept, scaled_taken = over_the_middle(scaled_sum)
    direction_kept, direction_taken = over_the_middle(direction_sum)
    sums = call(
        functools.partial(curvature_kernel, devices, capacity),
        float_of(2 * devices, SUBLANES, columns),
        [smem, hbm, hbm, vmem, hbm, hbm] + [anywhere] * devices,
        hbm,
        [
            room(*kinship.shape), full_room, full_room, room(devices * capacity + block_count, tile, columns),
            room(devices, tile + SUBLANES, columns), tiles_room, tiles_room,
            room(2 * devices, SUBLANES, columns),
            pltpu.SemaphoreType.DMA((2 * devices + 5,)),
        ],
    )(table, kinship, direction, diagonal, scaled, later, *received, scaled_sum)
    all_sums = lax.all_to_all(sums, ("samples", "cols"), split_axis=0, concat_axis=0, tiled=True)
    direction_scores = remaining(after(direction_kept, sums) + direction_taken)
    scaled_scores = remaining(after(scaled_kept, sums) + scaled_taken)
    swapped = swap(jnp.concatenate([direction_scores[share_rows:], scaled_scores[share_rows:]]), "cols", 2, 1)
    solved, scores = call(
        functools.partial(finish_kernel, devices, 1.0 / math.sqrt(people * devices)),
        [full, float_of(share_rows, 2 * columns)],
        [hbm, hbm] + [anywhere] * 4,
        [hbm, vmem],
        [
            full_room, full_room, room(share_rows, columns), room(share_rows, columns),
            room(2 * share_rows, columns), room(2 * devices, SUBLANES, columns),
            pltpu.SemaphoreType.DMA((10,)),
        ],
    )(direction, scaled, direction_scores, scaled_scores, swapped, all_sums)
    return (solved, scores)


def solution(mesh):
    return jax.shard_map(
        per_device,
        mesh=mesh,
        in_specs=(
            P(("groups", "samples"), None, None, None),
            P("groups", None),
            P(("groups", "samples")),
            P(("groups", "samples"), "cols"),
            P(("groups", "samples"), "cols"),
        ),
        out_specs=(P(("groups", "samples"), "cols"), P(("groups", "cols", "samples"), None)),
        check_vma=False,
    )
```

```python
import functools
import math

import jax
import jax.numpy as jnp
from jax import lax
from jax.experimental import pallas as pl
from jax.experimental.layout import Layout, with_layout_constraint
from jax.experimental.pallas import tpu as pltpu
from jax.sharding import PartitionSpec as P

VMEM_LIMIT = 24 * 1024 * 1024
SUBLANES = 8


def split(values):
    high = values.astype(jnp.bfloat16)
    low = (values - high.astype(jnp.float32)).astype(jnp.bfloat16)
    return high, low


def dot(left, right):
    return jnp.dot(left, right, preferred_element_type=jnp.float32)


def on_diagonal(size):
    rows = lax.broadcasted_iota(jnp.int32, (size, size), 0)
    return rows == lax.broadcasted_iota(jnp.int32, (size, size), 1)


def split_tiles(kinship_ref, high_ref, low_ref):
    block_count, positions, tile = kinship_ref.shape[:3]
    diagonal_mask = on_diagonal(tile)
    for row in range(block_count):
        for position in range(positions):
            values = kinship_ref[row, position]
            if position == 0:
                values = jnp.where(diagonal_mask, 0.0, values)
            high, low = split(values)
            high_ref[row, :, pl.ds(position * tile, tile)] = high
            low_ref[row, :, pl.ds(position * tile, tile)] = low


def product(high, low, blocks):
    parts = [split(block) for block in blocks]
    blocks_high = jnp.concatenate([part[0] for part in parts], axis=0)
    blocks_low = jnp.concatenate([part[1] for part in parts], axis=0)
    return dot(high, blocks_high) + (dot(low, blocks_high) + dot(high, blocks_low))


def column_sums(values):
    rows, columns = values.shape
    return jnp.sum(values.reshape(rows // SUBLANES, SUBLANES, columns), axis=0)


class Copies:
    def __init__(self, semaphores):
        self.semaphores = semaphores
        self.count = 0

    def start(self, source, target):
        copy = pltpu.make_async_copy(source, target, self.semaphores.at[self.count])
        self.count += 1
        copy.start()
        return copy


def wait_all(copies):
    for copy in copies:
        copy.wait()


def quotient(value, divisor):
    if divisor & (divisor - 1) == 0:
        return lax.shift_right_logical(value, jnp.int32(divisor.bit_length() - 1))
    return lax.div(value, jnp.int32(divisor))


def direction_kernel(kinship_ref, variance_ref, phenotypes_ref, direction_ref, diagonal_ref, sums_ref):
    block_count, positions, tile = kinship_ref.shape[:3]
    norm = jnp.zeros((SUBLANES, direction_ref.shape[1]), jnp.float32)
    diagonal_mask = on_diagonal(tile)
    for row in range(block_count):
        block = pl.ds(row * tile, tile)
        total = jnp.where(diagonal_mask, variance_ref[row:row + 1, :], kinship_ref[row, 0])
        for position in range(1, positions):
            total = total + kinship_ref[row, position]
        diagonal = jnp.sum(total, axis=1, keepdims=True)
        diagonal_ref[block, :] = diagonal
        here = phenotypes_ref[block, :] * (1.0 / diagonal)
        direction_ref[block, :] = here
        norm = norm + column_sums(here * phenotypes_ref[block, :])
    row_ids = lax.broadcasted_iota(jnp.int32, norm.shape, 0)
    sums_ref[...] = jnp.where(row_ids == 0, jnp.sum(norm, axis=0, keepdims=True), 0.0)


def route_kernel(devices, capacity, list_ref, kinship_ref, direction_ref, table_ref, forward_ref, high_ref, low_ref,
                 *refs):
    half = devices // 2
    outgoing_refs, (first_ref, last_ref) = refs[:half - 1], refs[half - 1:]
    block_count, positions, tile = kinship_ref.shape[:3]
    split_tiles(kinship_ref, high_ref, low_ref)
    me = lax.axis_index("samples")
    partner = me ^ half
    spare = me ^ 1
    top = block_count * block_count

    def collect(device):
        for j in range(devices):
            first_ref[j] = jnp.int32(top)
            last_ref[j] = jnp.int32(-1)
        found = []
        for row in range(block_count):
            for position in range(positions - 1):
                listed = list_ref[position, device * block_count + row]
                live = listed >= 0
                safe = jnp.maximum(listed, 0)
                other = quotient(safe, block_count)
                far_block = safe - other * block_count
                key = jnp.where(device < other, row * block_count + far_block, far_block * block_count + row)
                first_ref[other] = jnp.minimum(first_ref[other], jnp.where(live, key, top))
                last_ref[other] = jnp.maximum(last_ref[other], jnp.where(live, key, -1))
                found.append((live, other, far_block, key))
        return found

    def blocks_for(device, other):
        blocks = []
        for key in (first_ref[other], last_ref[other]):
            safe = jnp.clip(key, 0, top - 1)
            lower = quotient(safe, block_count)
            higher = safe - lower * block_count
            blocks.append(jnp.where(key == safe, jnp.where(device < other, lower, higher), 0))
        return blocks

    collect(partner)
    for k in range(1, half):
        blocks = blocks_for(partner, me ^ k)
        for slot in range(capacity):
            forward_ref[slot, k] = blocks[slot]
    for entry, (live, other, far_block, key) in enumerate(collect(me)):
        first, last = first_ref[other], last_ref[other]
        handled = jnp.where(me < other, first, last)
        weight = jnp.where(first == last, 1, 2)
        slot = jnp.where(key == first, 0, capacity - 1)
        place = jnp.where(other == partner, devices * capacity + far_block, other * capacity + slot)
        table_ref[0, entry] = jnp.where(live, place, spare * capacity)
        table_ref[1, entry] = jnp.where(live, other, spare)
        table_ref[2, entry] = jnp.where(live & (key == handled), weight, 0)
    for other in range(devices):
        blocks = blocks_for(me, other)
        table_ref[3, other] = jnp.where(me < other, blocks[1], blocks[0])
    near = [blocks_for(me, me ^ k) for k in range(1, half)]
    for k in range(1, half):
        for slot in range(capacity):
            start = pl.multiple_of(near[k - 1][slot] * tile, tile)
            outgoing_refs[k - 1][slot] = direction_ref[pl.ds(start, tile), :]


def forward_kernel(forward_ref, partner_ref, *refs):
    capacity, half = forward_ref.shape
    outgoing_refs = refs[1 - half:]
    tile = outgoing_refs[0].shape[1]
    for k in range(1, half):
        for slot in range(capacity):
            start = pl.multiple_of(forward_ref[slot, k] * tile, tile)
            outgoing_refs[k - 1][slot] = partner_ref[pl.ds(start, tile), :]


def gather_received(devices, capacity, received_refs, gathered_ref):
    half = devices // 2
    me = lax.axis_index("samples")
    near_refs, far_refs, partner_ref = received_refs[:half - 1], received_refs[half - 1:-1], received_refs[-1]
    gathered_ref[pl.ds(devices * capacity, partner_ref.shape[0])] = partner_ref[...]
    for k in range(1, half):
        mate = me ^ k
        gathered_ref[pl.ds(mate * capacity, capacity)] = near_refs[k - 1][...]
        gathered_ref[pl.ds((mate ^ half) * capacity, capacity)] = far_refs[k - 1][...]


def apply_kernel(devices, capacity, table_ref, high_ref, low_ref, direction_ref, diagonal_ref, norm_ref, *refs):
    received_refs = refs[:devices - 1]
    scaled_ref, sums_ref, gathered_ref, *outgoing_refs = refs[-2 - devices:]
    gather_received(devices, capacity, received_refs, gathered_ref)
    block_count, tile, depth = high_ref.shape
    others = depth // tile - 1
    cross = jnp.zeros(sums_ref.shape, jnp.float32)
    for row in range(block_count):
        block = pl.ds(row * tile, tile)
        here = direction_ref[block, :]
        blocks = [here] + [gathered_ref[table_ref[0, row * others + i]] for i in range(others)]
        mapped = product(high_ref[row], low_ref[row], blocks)
        scaled_ref[block, :] = mapped * (1.0 / diagonal_ref[block, :])
        cross = cross + column_sums(here * mapped)
    row_ids = lax.broadcasted_iota(jnp.int32, cross.shape, 0)
    sums = jnp.where(row_ids == 1, jnp.sum(cross, axis=0, keepdims=True), norm_ref[...])
    sums_ref[...] = sums
    me = lax.axis_index("samples")
    for k in range(1, devices):
        start = pl.multiple_of(table_ref[3, me ^ k] * tile, tile)
        outgoing_refs[k - 1][pl.ds(0, tile), :] = scaled_ref[pl.ds(start, tile), :]
        outgoing_refs[k - 1][pl.ds(tile, SUBLANES), :] = sums


def curvature_kernel(devices, table_ref, high_ref, low_ref, direction_ref, diagonal_ref, scaled_ref, own_sums_ref,
                     gathered_ref, *refs):
    later_refs = refs[:devices - 1]
    sums_hbm, later_ref, sums_ref, semaphores = refs[-4:]
    block_count, tile, depth = high_ref.shape
    others = depth // tile - 1
    me = lax.axis_index("samples")
    first_sums = own_sums_ref[...]
    for k in range(1, devices):
        later_ref[me ^ k] = later_refs[k - 1][pl.ds(0, tile), :]
        first_sums = first_sums + later_refs[k - 1][pl.ds(tile, SUBLANES), :]
    rho = first_sums[1:2, :] / first_sums[0:1, :]
    norm = jnp.zeros(first_sums.shape, jnp.float32)
    bend = jnp.zeros(first_sums.shape, jnp.float32)
    for row in range(block_count):
        block = pl.ds(row * tile, tile)
        here = scaled_ref[block, :] - rho * direction_ref[block, :]
        blocks = [here]
        for i in range(others):
            entry = row * others + i
            weight = table_ref[2, entry].astype(jnp.float32)
            blocks.append(weight * (later_ref[table_ref[1, entry]] - rho * gathered_ref[table_ref[0, entry]]))
        mapped = product(high_ref[row], low_ref[row], blocks)
        norm = norm + column_sums(here * here * diagonal_ref[block, :])
        bend = bend + column_sums(here * mapped)
    row_ids = lax.broadcasted_iota(jnp.int32, first_sums.shape, 0)
    sums = jnp.where(row_ids == 2, jnp.sum(norm, axis=0, keepdims=True), first_sums)
    sums = jnp.where(row_ids == 3, jnp.sum(bend, axis=0, keepdims=True), sums)
    for i in range(2 * devices):
        sums_ref[i] = sums
    Copies(semaphores).start(sums_ref, sums_hbm).wait()


def coefficients(sums, shared):
    norm, cross = sums[0:1, :], sums[1:2, :]
    later_norm, bend = shared[2:3, :], shared[3:4, :]
    curve = norm + cross
    ratio = later_norm / curve
    step = jnp.where(later_norm > 0, later_norm / (later_norm + bend - later_norm * ratio), 0.0)
    start = norm / curve
    return start * (1.0 + step * (ratio + cross / norm)), -start * step


def finish_kernel(devices, norm_scale, direction_ref, scaled_ref, direction_scores_ref, scaled_scores_ref, swapped_ref,
                  sums_ref, solved_hbm, scores_ref, solved_ref, semaphores):
    people, columns = direction_ref.shape
    rows = scores_ref.shape[0]
    column = lax.axis_index("cols")
    copies = Copies(semaphores)

    def total(which):
        sums = sums_ref[which]
        shared = sums
        for i in range(1, devices):
            shared = shared + sums_ref[2 * i + which]
        return sums, shared

    along, across = coefficients(*total(column))
    other_along, other_across = coefficients(*total(1 - column))
    stores = []
    part_rows = people // 4
    for part in range(4):
        block = pl.ds(part * part_rows, part_rows)
        solved_ref[block, :] = along * direction_ref[block, :] + across * scaled_ref[block, :]
        stores.append(copies.start(solved_ref.at[block], solved_hbm.at[block]))
    own = pl.multiple_of(column * columns, columns)
    other = pl.multiple_of((1 - column) * columns, columns)
    here = pl.ds(0, rows)
    scores_ref[:, pl.ds(own, columns)] = norm_scale * (
        along * direction_scores_ref[here, :] + across * scaled_scores_ref[here, :]
    )
    scores_ref[:, pl.ds(other, columns)] = norm_scale * (
        other_along * swapped_ref[here, :] + other_across * swapped_ref[pl.ds(rows, rows), :]
    )
    wait_all(stores)


def call(kernel, out_shape, in_specs, out_specs, scratch_shapes=()):
    return pl.pallas_call(
        kernel,
        out_shape=out_shape,
        in_specs=in_specs,
        out_specs=out_specs,
        scratch_shapes=list(scratch_shapes),
        compiler_params=pltpu.CompilerParams(vmem_limit_bytes=VMEM_LIMIT),
    )


def swap(values, axis, devices, step):
    return lax.ppermute(values, axis, [(i, i ^ step) for i in range(devices)])


def after(value, *others):
    return lax.optimization_barrier((value, *others))[0]


def per_device(kinship, relatives, variance, phenotypes, dosage):
    devices = lax.axis_size("samples")
    block_count, positions, tile = kinship.shape[:3]
    people, columns = phenotypes.shape
    variants = dosage.shape[1]
    share_rows = variants // devices
    entries = block_count * (positions - 1)
    capacity = -(-entries // (devices - 1))
    assert capacity <= 2
    hbm = pl.BlockSpec(memory_space=pltpu.HBM)
    anywhere = pl.BlockSpec(memory_space=pl.ANY)
    vmem = pl.BlockSpec(memory_space=pltpu.VMEM)
    smem = pl.BlockSpec(memory_space=pltpu.SMEM)
    float_of = lambda *shape: jax.ShapeDtypeStruct(shape, jnp.float32)
    room = lambda *shape: pltpu.VMEM(shape, jnp.float32)
    full = float_of(people, columns)
    full_room = room(people, columns)
    half = devices // 2
    near_by = list(range(1, half))
    direction, diagonal, norm = call(
        direction_kernel,
        [full, float_of(people, 1), float_of(SUBLANES, columns)],
        [vmem] * 3,
        [vmem] * 3,
    )(kinship, variance.reshape(block_count, tile), phenotypes)
    tiles = jax.ShapeDtypeStruct((block_count, tile, positions * tile), jnp.bfloat16)
    table, forward, high, low, *outgoing = call(
        functools.partial(route_kernel, devices, capacity),
        [
            jax.ShapeDtypeStruct((4, max(entries, devices)), jnp.int32),
            jax.ShapeDtypeStruct((capacity, half), jnp.int32),
            tiles, tiles,
        ] + [float_of(capacity, tile, columns)] * (half - 1),
        [smem, vmem, vmem],
        [smem, smem] + [vmem] * (half + 1),
        [pltpu.SMEM((devices,), jnp.int32), pltpu.SMEM((devices,), jnp.int32)],
    )(relatives.T, kinship, direction)

    def to_mates(blocks):
        return [swap(block, "samples", devices, k) for k, block in zip(near_by, blocks)]

    me = lax.axis_index("samples")
    dosage = after(dosage, table)
    other_dosage = with_layout_constraint(swap(dosage, "cols", 2, 1), Layout((0, 1)))
    dosages = [values.reshape(people, devices, share_rows) for values in (dosage, other_dosage)]
    bits = half.bit_length() - 1
    even = [sum(((i >> b) & 1) << (bits - b) for b in range(bits)) for i in range(half)]
    steps = [2 << i for i in range(bits)]
    grouped = [
        jnp.concatenate([
            lax.dynamic_index_in_dim(values, me ^ k ^ odd, 1, keepdims=False)
            for k in even for values in dosages
        ], axis=1)
        for odd in range(2)
    ]

    def variant_products(values):
        return [
            lax.dot_general(
                group, values, (((0,), (0,)), ((), ())), precision=lax.Precision.HIGH,
                preferred_element_type=jnp.float32,
            ).reshape(half, 2 * share_rows, columns)
            for group in grouped
        ]

    def halved(values, step):
        count = values.shape[0] // 2
        return values[:count], swap(values[count:], "samples", devices, step)

    partner = swap(direction, "samples", devices, half)
    near = to_mates(outgoing)
    direction_even, direction_odd = variant_products(direction)
    direction_share = swap(direction_odd, "samples", devices, 1)
    far = to_mates(call(
        forward_kernel,
        [float_of(capacity, tile, columns)] * (half - 1),
        [smem, vmem] + [anywhere] * (half + 1),
        [vmem] * (half - 1),
    )(forward, partner, *near, direction_even, direction_odd))
    received = near + far + [partner.reshape(block_count, tile, columns)]
    scaled, own_sums, gathered, *outgoing = call(
        functools.partial(apply_kernel, devices, capacity),
        [full, float_of(SUBLANES, columns), float_of(devices * capacity + block_count, tile, columns)]
        + [float_of(tile + SUBLANES, columns)] * (devices - 1),
        [smem] + [vmem] * (devices + 4) + [anywhere],
        [vmem] * (devices + 2),
    )(table, high, low, direction, diagonal, norm, *received, direction_share)
    order = [k for k in range(half, devices)] + near_by
    sent = {k: swap(outgoing[k - 1], "samples", devices, k) for k in order}
    later = [sent[k] for k in range(1, devices)]
    scaled_even, scaled_odd = variant_products(scaled)
    scaled_sum = scaled_even + swap(scaled_odd, "samples", devices, 1)
    direction_sum = after(direction_even, scaled) + direction_share
    for step in steps[:-1]:
        direction_kept, direction_taken = halved(direction_sum, step)
        direction_sum = direction_kept + direction_taken
    direction_kept, direction_taken = halved(direction_sum, steps[-1])
    scaled_kept, scaled_taken = halved(scaled_sum, steps[0])
    sums = call(
        functools.partial(curvature_kernel, devices),
        float_of(2 * devices, SUBLANES, columns),
        [smem] + [vmem] * (devices + 6) + [anywhere],
        hbm,
        [room(devices, tile, columns), room(2 * devices, SUBLANES, columns), pltpu.SemaphoreType.DMA((1,))],
    )(table, high, low, direction, diagonal, scaled, own_sums, gathered, *later, scaled_sum)
    scaled_sum = after(scaled_kept, sums) + scaled_taken
    for step in steps[1:-1]:
        scaled_kept, scaled_taken = halved(scaled_sum, step)
        scaled_sum = scaled_kept + scaled_taken
    scaled_kept, scaled_taken = halved(scaled_sum, steps[-1])
    all_sums = lax.all_to_all(
        after(sums, scaled_kept), ("samples", "cols"), split_axis=0, concat_axis=0, tiled=True
    )
    direction_scores = (after(direction_kept, sums) + direction_taken)[0]
    scaled_scores = (scaled_kept + scaled_taken)[0]
    swapped = swap(jnp.concatenate([direction_scores[share_rows:], scaled_scores[share_rows:]]), "cols", 2, 1)
    solved, scores = call(
        functools.partial(finish_kernel, devices, 1.0 / math.sqrt(people * devices)),
        [full, float_of(share_rows, 2 * columns)],
        [vmem] * 6,
        [hbm, vmem],
        [full_room, pltpu.SemaphoreType.DMA((4,))],
    )(direction, scaled, direction_scores, scaled_scores, swapped, all_sums)
    return (solved, scores)


def solution(mesh):
    return jax.shard_map(
        per_device,
        mesh=mesh,
        in_specs=(
            P(("groups", "samples"), None, None, None),
            P("groups", None),
            P(("groups", "samples")),
            P(("groups", "samples"), "cols"),
            P(("groups", "samples"), "cols"),
        ),
        out_specs=(P(("groups", "samples"), "cols"), P(("groups", "cols", "samples"), None)),
        check_vma=False,
    )
```

```python
import functools
import math

import jax
import jax.numpy as jnp
from jax import lax
from jax.experimental import pallas as pl
from jax.experimental.layout import Layout, with_layout_constraint
from jax.experimental.pallas import tpu as pltpu
from jax.sharding import PartitionSpec as P

VMEM_LIMIT = 24 * 1024 * 1024
LARGE_VMEM = 56 * 1024 * 1024
SUBLANES = 8


def split(values):
    high = values.astype(jnp.bfloat16)
    low = (values - high.astype(jnp.float32)).astype(jnp.bfloat16)
    return high, low


def dot(left, right):
    return jnp.dot(left, right, preferred_element_type=jnp.float32)


def on_diagonal(size):
    rows = lax.broadcasted_iota(jnp.int32, (size, size), 0)
    return rows == lax.broadcasted_iota(jnp.int32, (size, size), 1)


def split_tiles(kinship_ref, high_ref, low_ref):
    block_count, positions, tile = kinship_ref.shape[:3]
    diagonal_mask = on_diagonal(tile)
    for row in range(block_count):
        for position in range(positions):
            values = kinship_ref[row, position]
            if position == 0:
                values = jnp.where(diagonal_mask, 0.0, values)
            high, low = split(values)
            high_ref[row, :, pl.ds(position * tile, tile)] = high
            low_ref[row, :, pl.ds(position * tile, tile)] = low


def product(high, low, blocks):
    parts = [split(block) for block in blocks]
    blocks_high = jnp.concatenate([part[0] for part in parts], axis=0)
    blocks_low = jnp.concatenate([part[1] for part in parts], axis=0)
    return dot(high, blocks_high) + (dot(low, blocks_high) + dot(high, blocks_low))


def column_sums(values):
    rows, columns = values.shape
    return jnp.sum(values.reshape(rows // SUBLANES, SUBLANES, columns), axis=0)


class Copies:
    def __init__(self, semaphores):
        self.semaphores = semaphores
        self.count = 0

    def start(self, source, target):
        copy = pltpu.make_async_copy(source, target, self.semaphores.at[self.count])
        self.count += 1
        copy.start()
        return copy


def wait_all(copies):
    for copy in copies:
        copy.wait()


def quotient(value, divisor):
    if divisor & (divisor - 1) == 0:
        return lax.shift_right_logical(value, jnp.int32(divisor.bit_length() - 1))
    return lax.div(value, jnp.int32(divisor))


def direction_kernel(kinship_ref, variance_ref, phenotypes_ref, direction_ref, diagonal_ref, sums_ref):
    block_count, positions, tile = kinship_ref.shape[:3]
    norm = jnp.zeros((SUBLANES, direction_ref.shape[1]), jnp.float32)
    diagonal_mask = on_diagonal(tile)
    for row in range(block_count):
        block = pl.ds(row * tile, tile)
        total = jnp.where(diagonal_mask, variance_ref[row:row + 1, :], kinship_ref[row, 0])
        for position in range(1, positions):
            total = total + kinship_ref[row, position]
        diagonal = jnp.sum(total, axis=1, keepdims=True)
        diagonal_ref[block, :] = diagonal
        here = phenotypes_ref[block, :] * (1.0 / diagonal)
        direction_ref[block, :] = here
        norm = norm + column_sums(here * phenotypes_ref[block, :])
    row_ids = lax.broadcasted_iota(jnp.int32, norm.shape, 0)
    sums_ref[...] = jnp.where(row_ids == 0, jnp.sum(norm, axis=0, keepdims=True), 0.0)


def route_kernel(devices, capacity, list_ref, kinship_ref, direction_ref, gate_ref, table_ref, forward_ref, high_ref,
                 low_ref, *refs):
    half = devices // 2
    outgoing_refs, (first_ref, last_ref) = refs[:half - 1], refs[half - 1:]
    block_count, positions, tile = kinship_ref.shape[:3]
    split_tiles(kinship_ref, high_ref, low_ref)
    me = lax.axis_index("samples")
    partner = me ^ half
    spare = me ^ 1
    top = block_count * block_count

    def collect(device):
        for j in range(devices):
            first_ref[j] = jnp.int32(top)
            last_ref[j] = jnp.int32(-1)
        found = []
        for row in range(block_count):
            for position in range(positions - 1):
                listed = list_ref[position, device * block_count + row]
                live = listed >= 0
                safe = jnp.maximum(listed, 0)
                other = quotient(safe, block_count)
                far_block = safe - other * block_count
                key = jnp.where(device < other, row * block_count + far_block, far_block * block_count + row)
                first_ref[other] = jnp.minimum(first_ref[other], jnp.where(live, key, top))
                last_ref[other] = jnp.maximum(last_ref[other], jnp.where(live, key, -1))
                found.append((live, other, far_block, key))
        return found

    def blocks_for(device, other):
        blocks = []
        for key in (first_ref[other], last_ref[other]):
            safe = jnp.clip(key, 0, top - 1)
            lower = quotient(safe, block_count)
            higher = safe - lower * block_count
            blocks.append(jnp.where(key == safe, jnp.where(device < other, lower, higher), 0))
        return blocks

    collect(partner)
    for k in range(1, half):
        blocks = blocks_for(partner, me ^ k)
        for slot in range(capacity):
            forward_ref[slot, k] = blocks[slot]
    for entry, (live, other, far_block, key) in enumerate(collect(me)):
        first, last = first_ref[other], last_ref[other]
        handled = jnp.where(me < other, first, last)
        weight = jnp.where(first == last, 1, 2)
        slot = jnp.where(key == first, 0, capacity - 1)
        place = jnp.where(other == partner, devices * capacity + far_block, other * capacity + slot)
        table_ref[0, entry] = jnp.where(live, place, spare * capacity)
        table_ref[1, entry] = jnp.where(live, other, spare)
        table_ref[2, entry] = jnp.where(live & (key == handled), weight, 0)
    for other in range(devices):
        blocks = blocks_for(me, other)
        table_ref[3, other] = jnp.where(me < other, blocks[1], blocks[0])
    near = [blocks_for(me, me ^ k) for k in range(1, half)]
    for k in range(1, half):
        for slot in range(capacity):
            start = pl.multiple_of(near[k - 1][slot] * tile, tile)
            outgoing_refs[k - 1][slot] = direction_ref[pl.ds(start, tile), :]


def forward_kernel(forward_ref, partner_ref, *refs):
    capacity, half = forward_ref.shape
    outgoing_refs = refs[1 - half:]
    tile = outgoing_refs[0].shape[1]
    for k in range(1, half):
        for slot in range(capacity):
            start = pl.multiple_of(forward_ref[slot, k] * tile, tile)
            outgoing_refs[k - 1][slot] = partner_ref[pl.ds(start, tile), :]


def gather_received(devices, capacity, received_refs, gathered_ref):
    half = devices // 2
    me = lax.axis_index("samples")
    near_refs, far_refs, partner_ref = received_refs[:half - 1], received_refs[half - 1:-1], received_refs[-1]
    gathered_ref[pl.ds(devices * capacity, partner_ref.shape[0])] = partner_ref[...]
    for k in range(1, half):
        mate = me ^ k
        gathered_ref[pl.ds(mate * capacity, capacity)] = near_refs[k - 1][...]
        gathered_ref[pl.ds((mate ^ half) * capacity, capacity)] = far_refs[k - 1][...]


def apply_kernel(devices, capacity, table_ref, high_ref, low_ref, direction_ref, diagonal_ref, norm_ref, *refs):
    received_refs = refs[:devices - 1]
    scaled_ref, sums_ref, gathered_ref, outgoing_ref = refs[-4:]
    gather_received(devices, capacity, received_refs, gathered_ref)
    block_count, tile, depth = high_ref.shape
    others = depth // tile - 1
    cross = jnp.zeros(sums_ref.shape, jnp.float32)
    for row in range(block_count):
        block = pl.ds(row * tile, tile)
        here = direction_ref[block, :]
        blocks = [here] + [gathered_ref[table_ref[0, row * others + i]] for i in range(others)]
        mapped = product(high_ref[row], low_ref[row], blocks)
        scaled_ref[block, :] = mapped * (1.0 / diagonal_ref[block, :])
        cross = cross + column_sums(here * mapped)
    row_ids = lax.broadcasted_iota(jnp.int32, cross.shape, 0)
    sums = jnp.where(row_ids == 1, jnp.sum(cross, axis=0, keepdims=True), norm_ref[...])
    sums_ref[...] = sums
    for other in range(devices):
        start = pl.multiple_of(table_ref[3, other] * tile, tile)
        outgoing_ref[other, pl.ds(0, tile), :] = scaled_ref[pl.ds(start, tile), :]
        outgoing_ref[other, pl.ds(tile, SUBLANES), :] = sums


def curvature_kernel(devices, table_ref, high_ref, low_ref, direction_ref, diagonal_ref, scaled_ref, gathered_ref,
                     later_ref, *refs):
    sums_ref = refs[-1]
    block_count, tile, depth = high_ref.shape
    others = depth // tile - 1
    first_sums = later_ref[0, pl.ds(tile, SUBLANES), :]
    for other in range(1, devices):
        first_sums = first_sums + later_ref[other, pl.ds(tile, SUBLANES), :]
    rho = first_sums[1:2, :] / first_sums[0:1, :]
    norm = jnp.zeros(first_sums.shape, jnp.float32)
    bend = jnp.zeros(first_sums.shape, jnp.float32)
    for row in range(block_count):
        block = pl.ds(row * tile, tile)
        here = scaled_ref[block, :] - rho * direction_ref[block, :]
        blocks = [here]
        for i in range(others):
            entry = row * others + i
            weight = table_ref[2, entry].astype(jnp.float32)
            there = later_ref[table_ref[1, entry], pl.ds(0, tile), :]
            blocks.append(weight * (there - rho * gathered_ref[table_ref[0, entry]]))
        mapped = product(high_ref[row], low_ref[row], blocks)
        norm = norm + column_sums(here * here * diagonal_ref[block, :])
        bend = bend + column_sums(here * mapped)
    row_ids = lax.broadcasted_iota(jnp.int32, first_sums.shape, 0)
    sums = jnp.where(row_ids == 2, jnp.sum(norm, axis=0, keepdims=True), first_sums)
    sums_ref[...] = jnp.where(row_ids == 3, jnp.sum(bend, axis=0, keepdims=True), sums)


def add_kernel(sums_ref, kept_ref, taken_ref, all_sums_ref, near_ref, far_ref):
    count = near_ref.shape[0]
    near_ref[...] = kept_ref[pl.ds(0, count)] + taken_ref[pl.ds(0, count)]
    far_ref[...] = kept_ref[pl.ds(count, count)] + taken_ref[pl.ds(count, count)]
    for i in range(all_sums_ref.shape[0]):
        all_sums_ref[i] = sums_ref[...]


def group_kernel(order, own_ref, other_ref, high_ref, low_ref):
    rows = own_ref.shape[0] // (2 * len(order))
    me = lax.axis_index("samples")
    for odd in range(2):
        for i, distance in enumerate(order):
            start = pl.multiple_of((me ^ distance ^ odd) * rows, rows)
            for j, dosage_ref in enumerate((own_ref, other_ref)):
                high, low = split(dosage_ref[pl.ds(start, rows), :])
                here = pl.ds((2 * i + j) * rows, rows)
                high_ref[odd, here, :] = high
                low_ref[odd, here, :] = low


def score_kernel(high_ref, low_ref, values_ref, even_ref, odd_ref):
    count, rows = even_ref.shape[:2]
    for odd, out_ref in enumerate((even_ref, odd_ref)):
        for i in range(0, count, 4):
            here = pl.ds(i * rows, 4 * rows)
            total = product(high_ref[odd, here, :], low_ref[odd, here, :], [values_ref[...]])
            out_ref[pl.ds(i, 4)] = total.reshape(4, rows, -1)


def coefficients(sums, shared):
    norm, cross = sums[0:1, :], sums[1:2, :]
    later_norm, bend = shared[2:3, :], shared[3:4, :]
    curve = norm + cross
    ratio = later_norm / curve
    step = jnp.where(later_norm > 0, later_norm / (later_norm + bend - later_norm * ratio), 0.0)
    start = norm / curve
    return start * (1.0 + step * (ratio + cross / norm)), -start * step


def finish_kernel(devices, norm_scale, direction_ref, scaled_ref, direction_scores_ref, scaled_scores_ref, swapped_ref,
                  sums_ref, solved_hbm, scores_ref, solved_ref, semaphores):
    people, columns = direction_ref.shape
    rows = scores_ref.shape[0]
    column = lax.axis_index("cols")
    copies = Copies(semaphores)

    def total(which):
        sums = sums_ref[which]
        shared = sums
        for i in range(1, devices):
            shared = shared + sums_ref[2 * i + which]
        return sums, shared

    along, across = coefficients(*total(column))
    other_along, other_across = coefficients(*total(1 - column))
    stores = []
    part_rows = people // 4
    for part in range(4):
        block = pl.ds(part * part_rows, part_rows)
        solved_ref[block, :] = along * direction_ref[block, :] + across * scaled_ref[block, :]
        stores.append(copies.start(solved_ref.at[block], solved_hbm.at[block]))
    own = pl.multiple_of(column * columns, columns)
    other = pl.multiple_of((1 - column) * columns, columns)
    here = pl.ds(0, rows)
    scores_ref[:, pl.ds(own, columns)] = norm_scale * (
        along * direction_scores_ref[here, :] + across * scaled_scores_ref[here, :]
    )
    scores_ref[:, pl.ds(other, columns)] = norm_scale * (
        other_along * swapped_ref[here, :] + other_across * swapped_ref[pl.ds(rows, rows), :]
    )
    wait_all(stores)


def call(kernel, out_shape, in_specs, out_specs, scratch_shapes=(), limit=VMEM_LIMIT):
    return pl.pallas_call(
        kernel,
        out_shape=out_shape,
        in_specs=in_specs,
        out_specs=out_specs,
        scratch_shapes=list(scratch_shapes),
        compiler_params=pltpu.CompilerParams(vmem_limit_bytes=limit),
    )


def swap(values, axis, devices, step):
    return lax.ppermute(values, axis, [(i, i ^ step) for i in range(devices)])


def after(value, *others):
    return lax.optimization_barrier((value, *others))[0]


def per_device(kinship, relatives, variance, phenotypes, dosage):
    devices = lax.axis_size("samples")
    block_count, positions, tile = kinship.shape[:3]
    people, columns = phenotypes.shape
    variants = dosage.shape[1]
    share_rows = variants // devices
    entries = block_count * (positions - 1)
    capacity = -(-entries // (devices - 1))
    assert capacity <= 2
    hbm = pl.BlockSpec(memory_space=pltpu.HBM)
    anywhere = pl.BlockSpec(memory_space=pl.ANY)
    vmem = pl.BlockSpec(memory_space=pltpu.VMEM)
    smem = pl.BlockSpec(memory_space=pltpu.SMEM)
    float_of = lambda *shape: jax.ShapeDtypeStruct(shape, jnp.float32)
    room = lambda *shape: pltpu.VMEM(shape, jnp.float32)
    full = float_of(people, columns)
    full_room = room(people, columns)
    half = devices // 2
    near_by = list(range(1, half))
    direction, diagonal, norm = call(
        direction_kernel,
        [full, float_of(people, 1), float_of(SUBLANES, columns)],
        [vmem] * 3,
        [vmem] * 3,
    )(kinship, variance.reshape(block_count, tile), phenotypes)
    def to_mates(blocks):
        return [swap(block, "samples", devices, k) for k, block in zip(near_by, blocks)]

    bits = half.bit_length() - 1
    even = [sum(((i >> b) & 1) << (bits - b) for b in range(bits)) for i in range(half)]
    steps = [2 << i for i in range(bits)]
    other_dosage = with_layout_constraint(swap(after(dosage, direction), "cols", 2, 1), Layout((0, 1)))
    tiles = jax.ShapeDtypeStruct((block_count, tile, positions * tile), jnp.bfloat16)
    table, forward, high, low, *outgoing = call(
        functools.partial(route_kernel, devices, capacity),
        [
            jax.ShapeDtypeStruct((4, max(entries, devices)), jnp.int32),
            jax.ShapeDtypeStruct((capacity, half), jnp.int32),
            tiles, tiles,
        ] + [float_of(capacity, tile, columns)] * (half - 1),
        [smem, vmem, vmem, anywhere],
        [smem, smem] + [vmem] * (half + 1),
        [pltpu.SMEM((devices,), jnp.int32), pltpu.SMEM((devices,), jnp.int32)],
    )(relatives.T, kinship, direction, other_dosage)


    parts = jax.ShapeDtypeStruct((2, variants, people), jnp.bfloat16)
    large = VMEM_LIMIT if variants <= people else LARGE_VMEM
    grouped = call(
        functools.partial(group_kernel, even), [parts] * 2, [vmem] * 2, [vmem] * 2, limit=large
    )(after(dosage, table).T, other_dosage.T)

    def variant_products(values):
        return call(
            score_kernel, [float_of(half, 2 * share_rows, columns)] * 2, [vmem] * 3, [vmem] * 2, limit=large
        )(*grouped, values)

    def halved(values, step):
        count = values.shape[0] // 2
        return values[:count], swap(values[count:], "samples", devices, step)

    partner = swap(direction, "samples", devices, half)
    near = to_mates(outgoing)
    direction_even, direction_odd = variant_products(direction)
    direction_share = swap(direction_odd, "samples", devices, 1)
    far = to_mates(call(
        forward_kernel,
        [float_of(capacity, tile, columns)] * (half - 1),
        [smem, vmem] + [anywhere] * (half + 1),
        [vmem] * (half - 1),
    )(forward, partner, *near, direction_even, direction_odd))
    received = near + far + [partner.reshape(block_count, tile, columns)]
    scaled, sums, gathered, outgoing = call(
        functools.partial(apply_kernel, devices, capacity),
        [
            full, float_of(SUBLANES, columns), float_of(devices * capacity + block_count, tile, columns),
            float_of(devices, tile + SUBLANES, columns),
        ],
        [smem] + [vmem] * (devices + 4) + [anywhere],
        [vmem] * 4,
    )(table, high, low, direction, diagonal, norm, *received, direction_share)
    later = lax.all_to_all(outgoing, "samples", split_axis=0, concat_axis=0, tiled=True)
    scaled_even, scaled_odd = variant_products(scaled)
    scaled_sum = scaled_even + swap(scaled_odd, "samples", devices, 1)
    direction_sum = after(direction_even, scaled) + direction_share
    for step in steps[:-1]:
        direction_kept, direction_taken = halved(direction_sum, step)
        direction_sum = direction_kept + direction_taken
    direction_kept, direction_taken = halved(direction_sum, steps[-1])
    scaled_kept, scaled_taken = halved(scaled_sum, steps[0])
    sums = call(
        functools.partial(curvature_kernel, devices),
        float_of(SUBLANES, columns),
        [smem] + [vmem] * 7 + [anywhere] * 2,
        vmem,
    )(table, high, low, direction, diagonal, scaled, gathered, later, scaled_sum, direction_sum)
    half_sum = float_of(scaled_kept.shape[0] // 2, 2 * share_rows, columns)
    all_sums, scaled_kept, scaled_given = call(
        add_kernel, [float_of(2 * devices, SUBLANES, columns), half_sum, half_sum], [vmem] * 3, [vmem] * 3
    )(sums, scaled_kept, scaled_taken)
    all_sums = lax.all_to_all(all_sums, ("samples", "cols"), split_axis=0, concat_axis=0, tiled=True)
    scaled_sum = scaled_kept + swap(scaled_given, "samples", devices, steps[1])
    for step in steps[2:]:
        scaled_kept, scaled_taken = halved(scaled_sum, step)
        scaled_sum = scaled_kept + scaled_taken
    direction_scores = (after(direction_kept, sums) + direction_taken)[0]
    scaled_scores = scaled_sum[0]
    swapped = swap(jnp.concatenate([direction_scores[share_rows:], scaled_scores[share_rows:]]), "cols", 2, 1)
    solved, scores = call(
        functools.partial(finish_kernel, devices, 1.0 / math.sqrt(people * devices)),
        [full, float_of(share_rows, 2 * columns)],
        [vmem] * 6,
        [hbm, vmem],
        [full_room, pltpu.SemaphoreType.DMA((4,))],
    )(direction, scaled, direction_scores, scaled_scores, swapped, all_sums)
    return (solved, scores)


def solution(mesh):
    return jax.shard_map(
        per_device,
        mesh=mesh,
        in_specs=(
            P(("groups", "samples"), None, None, None),
            P("groups", None),
            P(("groups", "samples")),
            P(("groups", "samples"), "cols"),
            P(("groups", "samples"), "cols"),
        ),
        out_specs=(P(("groups", "samples"), "cols"), P(("groups", "cols", "samples"), None)),
        check_vma=False,
    )
```

```python
import functools
import math

import jax
import jax.numpy as jnp
from jax import lax
from jax.experimental import pallas as pl
from jax.experimental.layout import Layout, with_layout_constraint
from jax.experimental.pallas import tpu as pltpu
from jax.sharding import PartitionSpec as P

VMEM_LIMIT = 24 * 1024 * 1024
LARGE_VMEM = 56 * 1024 * 1024
SUBLANES = 8


def split(values):
    high = values.astype(jnp.bfloat16)
    low = (values - high.astype(jnp.float32)).astype(jnp.bfloat16)
    return high, low


def dot(left, right):
    return jnp.dot(left, right, preferred_element_type=jnp.float32)


def on_diagonal(size):
    rows = lax.broadcasted_iota(jnp.int32, (size, size), 0)
    return rows == lax.broadcasted_iota(jnp.int32, (size, size), 1)


def split_tiles(kinship_ref, high_ref, low_ref):
    block_count, positions, tile = kinship_ref.shape[:3]
    diagonal_mask = on_diagonal(tile)
    for row in range(block_count):
        for position in range(positions):
            values = kinship_ref[row, position]
            if position == 0:
                values = jnp.where(diagonal_mask, 0.0, values)
            high, low = split(values)
            high_ref[row, :, pl.ds(position * tile, tile)] = high
            low_ref[row, :, pl.ds(position * tile, tile)] = low


def product(high, low, blocks):
    parts = [split(block) for block in blocks]
    blocks_high = jnp.concatenate([part[0] for part in parts], axis=0)
    blocks_low = jnp.concatenate([part[1] for part in parts], axis=0)
    return dot(high, blocks_high) + (dot(low, blocks_high) + dot(high, blocks_low))


def column_sums(values):
    rows, columns = values.shape
    return jnp.sum(values.reshape(rows // SUBLANES, SUBLANES, columns), axis=0)


class Copies:
    def __init__(self, semaphores):
        self.semaphores = semaphores
        self.count = 0

    def start(self, source, target):
        copy = pltpu.make_async_copy(source, target, self.semaphores.at[self.count])
        self.count += 1
        copy.start()
        return copy


def wait_all(copies):
    for copy in copies:
        copy.wait()


def quotient(value, divisor):
    if divisor & (divisor - 1) == 0:
        return lax.shift_right_logical(value, jnp.int32(divisor.bit_length() - 1))
    return lax.div(value, jnp.int32(divisor))


def direction_kernel(kinship_ref, variance_ref, phenotypes_ref, direction_ref, diagonal_ref, sums_ref):
    block_count, positions, tile = kinship_ref.shape[:3]
    norm = jnp.zeros((SUBLANES, direction_ref.shape[1]), jnp.float32)
    diagonal_mask = on_diagonal(tile)
    for row in range(block_count):
        block = pl.ds(row * tile, tile)
        total = jnp.where(diagonal_mask, variance_ref[row:row + 1, :], kinship_ref[row, 0])
        for position in range(1, positions):
            total = total + kinship_ref[row, position]
        diagonal = jnp.sum(total, axis=1, keepdims=True)
        diagonal_ref[block, :] = diagonal
        here = phenotypes_ref[block, :] * (1.0 / diagonal)
        direction_ref[block, :] = here
        norm = norm + column_sums(here * phenotypes_ref[block, :])
    row_ids = lax.broadcasted_iota(jnp.int32, norm.shape, 0)
    sums_ref[...] = jnp.where(row_ids == 0, jnp.sum(norm, axis=0, keepdims=True), 0.0)


def route_kernel(devices, capacity, list_ref, kinship_ref, direction_ref, gate_ref, table_ref, forward_ref, high_ref,
                 low_ref, *refs):
    half = devices // 2
    outgoing_refs, (first_ref, last_ref) = refs[:half - 1], refs[half - 1:]
    block_count, positions, tile = kinship_ref.shape[:3]
    split_tiles(kinship_ref, high_ref, low_ref)
    me = lax.axis_index("samples")
    partner = me ^ half
    spare = me ^ 1
    top = block_count * block_count

    def collect(device):
        for j in range(devices):
            first_ref[j] = jnp.int32(top)
            last_ref[j] = jnp.int32(-1)
        found = []
        for row in range(block_count):
            for position in range(positions - 1):
                listed = list_ref[position, device * block_count + row]
                live = listed >= 0
                safe = jnp.maximum(listed, 0)
                other = quotient(safe, block_count)
                far_block = safe - other * block_count
                key = jnp.where(device < other, row * block_count + far_block, far_block * block_count + row)
                first_ref[other] = jnp.minimum(first_ref[other], jnp.where(live, key, top))
                last_ref[other] = jnp.maximum(last_ref[other], jnp.where(live, key, -1))
                found.append((live, other, far_block, key))
        return found

    def blocks_for(device, other):
        blocks = []
        for key in (first_ref[other], last_ref[other]):
            safe = jnp.clip(key, 0, top - 1)
            lower = quotient(safe, block_count)
            higher = safe - lower * block_count
            blocks.append(jnp.where(key == safe, jnp.where(device < other, lower, higher), 0))
        return blocks

    collect(partner)
    for k in range(1, half):
        blocks = blocks_for(partner, me ^ k)
        for slot in range(capacity):
            forward_ref[slot, k] = blocks[slot]
    for entry, (live, other, far_block, key) in enumerate(collect(me)):
        first, last = first_ref[other], last_ref[other]
        handled = jnp.where(me < other, first, last)
        weight = jnp.where(first == last, 1, 2)
        slot = jnp.where(key == first, 0, capacity - 1)
        place = jnp.where(other == partner, devices * capacity + far_block, other * capacity + slot)
        table_ref[0, entry] = jnp.where(live, place, spare * capacity)
        table_ref[1, entry] = jnp.where(live, other, spare)
        table_ref[2, entry] = jnp.where(live & (key == handled), weight, 0)
    for other in range(devices):
        blocks = blocks_for(me, other)
        table_ref[3, other] = jnp.where(me < other, blocks[1], blocks[0])
    near = [blocks_for(me, me ^ k) for k in range(1, half)]
    for k in range(1, half):
        for slot in range(capacity):
            start = pl.multiple_of(near[k - 1][slot] * tile, tile)
            outgoing_refs[k - 1][slot] = direction_ref[pl.ds(start, tile), :]


def forward_kernel(forward_ref, partner_ref, *refs):
    capacity, half = forward_ref.shape
    outgoing_refs = refs[1 - half:]
    tile = outgoing_refs[0].shape[1]
    for k in range(1, half):
        for slot in range(capacity):
            start = pl.multiple_of(forward_ref[slot, k] * tile, tile)
            outgoing_refs[k - 1][slot] = partner_ref[pl.ds(start, tile), :]


def gather_received(devices, capacity, received_refs, gathered_ref):
    half = devices // 2
    me = lax.axis_index("samples")
    near_refs, far_refs, partner_ref = received_refs[:half - 1], received_refs[half - 1:-1], received_refs[-1]
    gathered_ref[pl.ds(devices * capacity, partner_ref.shape[0])] = partner_ref[...]
    for k in range(1, half):
        mate = me ^ k
        gathered_ref[pl.ds(mate * capacity, capacity)] = near_refs[k - 1][...]
        gathered_ref[pl.ds((mate ^ half) * capacity, capacity)] = far_refs[k - 1][...]


def score_products(high_ref, low_ref, values, even_ref, odd_ref):
    count, rows = even_ref.shape[:2]
    for odd, out_ref in enumerate((even_ref, odd_ref)):
        for i in range(0, count, 4):
            here = pl.ds(i * rows, 4 * rows)
            total = product(high_ref[odd, here, :], low_ref[odd, here, :], [values])
            out_ref[pl.ds(i, 4)] = total.reshape(4, rows, -1)


def score_kernel(order, high_ref, low_ref, values_ref, out_ref):
    rows = out_ref.shape[1]
    me = lax.axis_index("samples")
    for odd in range(2):
        for i in range(0, len(order), 4):
            here = pl.ds(i * rows, 4 * rows)
            total = product(high_ref[odd, here, :], low_ref[odd, here, :], [values_ref[...]])
            for j in range(4):
                out_ref[me ^ order[i + j] ^ odd] = total[j * rows:(j + 1) * rows]


def apply_kernel(devices, capacity, table_ref, high_ref, low_ref, direction_ref, diagonal_ref, norm_ref,
                 dosage_high_ref, dosage_low_ref, *refs):
    received_refs = refs[:devices - 1]
    scaled_ref, sums_ref, gathered_ref, even_ref, odd_ref, *outgoing_refs = refs[-4 - devices:]
    gather_received(devices, capacity, received_refs, gathered_ref)
    block_count, tile, depth = high_ref.shape
    others = depth // tile - 1
    cross = jnp.zeros(sums_ref.shape, jnp.float32)
    for row in range(block_count):
        block = pl.ds(row * tile, tile)
        here = direction_ref[block, :]
        blocks = [here] + [gathered_ref[table_ref[0, row * others + i]] for i in range(others)]
        mapped = product(high_ref[row], low_ref[row], blocks)
        scaled_ref[block, :] = mapped * (1.0 / diagonal_ref[block, :])
        cross = cross + column_sums(here * mapped)
    row_ids = lax.broadcasted_iota(jnp.int32, cross.shape, 0)
    sums = jnp.where(row_ids == 1, jnp.sum(cross, axis=0, keepdims=True), norm_ref[...])
    sums_ref[...] = sums
    me = lax.axis_index("samples")
    for k in range(1, devices):
        start = pl.multiple_of(table_ref[3, me ^ k] * tile, tile)
        outgoing_refs[k - 1][pl.ds(0, tile), :] = scaled_ref[pl.ds(start, tile), :]
        outgoing_refs[k - 1][pl.ds(tile, SUBLANES), :] = sums
    score_products(dosage_high_ref, dosage_low_ref, scaled_ref[...], even_ref, odd_ref)


def curvature_kernel(order, table_ref, high_ref, low_ref, direction_ref, diagonal_ref, scaled_ref, own_sums_ref,
                     gathered_ref, *refs):
    later_refs, (first_sums_ref, sums_ref, later_ref) = refs[:len(order)], refs[-3:]
    block_count, tile, depth = high_ref.shape
    others = depth // tile - 1
    me = lax.axis_index("samples")
    first_sums = own_sums_ref[...]
    for distance, arrived_ref in zip(order, later_refs):
        later_ref[me ^ distance] = arrived_ref[pl.ds(0, tile), :]
        first_sums = first_sums + arrived_ref[pl.ds(tile, SUBLANES), :]
    rho = first_sums[1:2, :] / first_sums[0:1, :]
    norm = jnp.zeros(first_sums.shape, jnp.float32)
    bend = jnp.zeros(first_sums.shape, jnp.float32)
    for row in range(block_count):
        block = pl.ds(row * tile, tile)
        here = scaled_ref[block, :] - rho * direction_ref[block, :]
        blocks = [here]
        for i in range(others):
            entry = row * others + i
            weight = table_ref[2, entry].astype(jnp.float32)
            blocks.append(weight * (later_ref[table_ref[1, entry]] - rho * gathered_ref[table_ref[0, entry]]))
        mapped = product(high_ref[row], low_ref[row], blocks)
        norm = norm + column_sums(here * here * diagonal_ref[block, :])
        bend = bend + column_sums(here * mapped)
    row_ids = lax.broadcasted_iota(jnp.int32, first_sums.shape, 0)
    sums = jnp.where(row_ids == 2, jnp.sum(norm, axis=0, keepdims=True), 0.0)
    sums_ref[...] = jnp.where(row_ids == 3, jnp.sum(bend, axis=0, keepdims=True), sums)
    first_sums_ref[...] = first_sums


def add_kernel(kept_ref, taken_ref, *refs):
    near_ref, far_ref = refs[-2:]
    count = near_ref.shape[0]
    near_ref[...] = kept_ref[pl.ds(0, count)] + taken_ref[pl.ds(0, count)]
    far_ref[...] = kept_ref[pl.ds(count, count)] + taken_ref[pl.ds(count, count)]


def last_add_kernel(kept_ref, taken_ref, own_ref, other_ref):
    rows = own_ref.shape[0]
    own_ref[...] = kept_ref[0, pl.ds(0, rows), :] + taken_ref[0, pl.ds(0, rows), :]
    other_ref[...] = kept_ref[0, pl.ds(rows, rows), :] + taken_ref[0, pl.ds(rows, rows), :]


def group_kernel(order, own_ref, other_ref, high_ref, low_ref):
    rows = own_ref.shape[0] // (2 * len(order))
    me = lax.axis_index("samples")
    for odd in range(2):
        for i, distance in enumerate(order):
            start = pl.multiple_of((me ^ distance ^ odd) * rows, rows)
            for j, dosage_ref in enumerate((own_ref, other_ref)):
                high, low = split(dosage_ref[pl.ds(start, rows), :])
                here = pl.ds((2 * i + j) * rows, rows)
                high_ref[odd, here, :] = high
                low_ref[odd, here, :] = low


def coefficients(sums):
    norm, cross, later_norm, bend = (sums[i:i + 1, :] for i in range(4))
    curve = norm + cross
    ratio = later_norm / curve
    step = jnp.where(later_norm > 0, later_norm / (later_norm + bend - later_norm * ratio), 0.0)
    start = norm / curve
    return start * (1.0 + step * (ratio + cross / norm)), -start * step


def finish_kernel(norm_scale, direction_ref, scaled_ref, direction_scores_ref, own_scores_ref, swapped_ref,
                  other_scores_ref, sums_ref, other_sums_ref, solved_hbm, scores_ref, solved_ref, semaphores):
    people, columns = direction_ref.shape
    rows = scores_ref.shape[0]
    column = lax.axis_index("cols")
    copies = Copies(semaphores)
    along, across = coefficients(sums_ref[...])
    other_along, other_across = coefficients(other_sums_ref[...])
    stores = []
    part_rows = people // 4
    for part in range(4):
        block = pl.ds(part * part_rows, part_rows)
        solved_ref[block, :] = along * direction_ref[block, :] + across * scaled_ref[block, :]
        stores.append(copies.start(solved_ref.at[block], solved_hbm.at[block]))
    own = pl.multiple_of(column * columns, columns)
    other = pl.multiple_of((1 - column) * columns, columns)
    scores_ref[:, pl.ds(own, columns)] = norm_scale * (
        along * direction_scores_ref[pl.ds(0, rows), :] + across * own_scores_ref[...]
    )
    scores_ref[:, pl.ds(other, columns)] = norm_scale * (
        other_along * swapped_ref[...] + other_across * other_scores_ref[...]
    )
    wait_all(stores)


def call(kernel, out_shape, in_specs, out_specs, scratch_shapes=(), limit=VMEM_LIMIT):
    return pl.pallas_call(
        kernel,
        out_shape=out_shape,
        in_specs=in_specs,
        out_specs=out_specs,
        scratch_shapes=list(scratch_shapes),
        compiler_params=pltpu.CompilerParams(vmem_limit_bytes=limit),
    )


def swap(values, axis, devices, step):
    return lax.ppermute(values, axis, [(i, i ^ step) for i in range(devices)])


def after(value, *others):
    return lax.optimization_barrier((value, *others))[0]


def per_device(kinship, relatives, variance, phenotypes, dosage):
    devices = lax.axis_size("samples")
    block_count, positions, tile = kinship.shape[:3]
    people, columns = phenotypes.shape
    variants = dosage.shape[1]
    share_rows = variants // devices
    entries = block_count * (positions - 1)
    capacity = -(-entries // (devices - 1))
    assert capacity <= 2
    hbm = pl.BlockSpec(memory_space=pltpu.HBM)
    anywhere = pl.BlockSpec(memory_space=pl.ANY)
    vmem = pl.BlockSpec(memory_space=pltpu.VMEM)
    smem = pl.BlockSpec(memory_space=pltpu.SMEM)
    float_of = lambda *shape: jax.ShapeDtypeStruct(shape, jnp.float32)
    room = lambda *shape: pltpu.VMEM(shape, jnp.float32)
    full = float_of(people, columns)
    full_room = room(people, columns)
    half = devices // 2
    near_by = list(range(1, half))
    direction, diagonal, norm = call(
        direction_kernel,
        [full, float_of(people, 1), float_of(SUBLANES, columns)],
        [vmem] * 3,
        [vmem] * 3,
    )(kinship, variance.reshape(block_count, tile), phenotypes)
    def to_mates(blocks):
        return [swap(block, "samples", devices, k) for k, block in zip(near_by, blocks)]

    bits = half.bit_length() - 1
    even = [sum(((i >> b) & 1) << (bits - b) for b in range(bits)) for i in range(half)]
    steps = [2 << i for i in range(bits)]
    other_dosage = with_layout_constraint(swap(after(dosage, direction), "cols", 2, 1), Layout((0, 1)))
    tiles = jax.ShapeDtypeStruct((block_count, tile, positions * tile), jnp.bfloat16)
    table, forward, high, low, *outgoing = call(
        functools.partial(route_kernel, devices, capacity),
        [
            jax.ShapeDtypeStruct((4, max(entries, devices)), jnp.int32),
            jax.ShapeDtypeStruct((capacity, half), jnp.int32),
            tiles, tiles,
        ] + [float_of(capacity, tile, columns)] * (half - 1),
        [smem, vmem, vmem, anywhere],
        [smem, smem] + [vmem] * (half + 1),
        [pltpu.SMEM((devices,), jnp.int32), pltpu.SMEM((devices,), jnp.int32)],
    )(relatives.T, kinship, direction, other_dosage)


    parts = jax.ShapeDtypeStruct((2, variants, people), jnp.bfloat16)
    large = VMEM_LIMIT if variants <= people else LARGE_VMEM
    grouped = call(
        functools.partial(group_kernel, even), [parts] * 2, [vmem] * 2, [vmem] * 2, limit=large
    )(after(dosage, table).T, other_dosage.T)

    products = float_of(half, 2 * share_rows, columns)

    partner = swap(direction, "samples", devices, half)
    near = to_mates(outgoing)
    direction_products = call(
        functools.partial(score_kernel, even), float_of(devices, 2 * share_rows, columns), [vmem] * 3, vmem, limit=large
    )(*grouped, direction)
    direction_scores = lax.psum_scatter(
        direction_products.reshape(2 * variants, columns), "samples", scatter_dimension=0, tiled=True
    )
    far = to_mates(call(
        forward_kernel,
        [float_of(capacity, tile, columns)] * (half - 1),
        [smem, vmem] + [anywhere] * half,
        [vmem] * (half - 1),
    )(forward, partner, *near, direction_products))
    received = near + far + [partner.reshape(block_count, tile, columns)]
    scaled, own_sums, gathered, scaled_even, scaled_odd, *outgoing = call(
        functools.partial(apply_kernel, devices, capacity),
        [
            full, float_of(SUBLANES, columns), float_of(devices * capacity + block_count, tile, columns),
            products, products,
        ] + [float_of(tile + SUBLANES, columns)] * (devices - 1),
        [smem] + [vmem] * (devices + 6),
        [vmem] * (devices + 4),
        limit=large,
    )(table, high, low, direction, diagonal, norm, *grouped, *received)
    scaled_share = swap(scaled_odd, "samples", devices, 1)
    order = [k for k in range(half, devices)] + near_by
    later = [swap(outgoing[k - 1], "samples", devices, k) for k in order]
    rows = float_of(half // 2, 2 * share_rows, columns)
    kept, given = call(add_kernel, [rows] * 2, [vmem] * 2, [vmem] * 2)(scaled_even, scaled_share)
    taken = swap(given, "samples", devices, steps[0])
    first_sums, sums = call(
        functools.partial(curvature_kernel, order),
        [float_of(SUBLANES, columns)] * 2,
        [smem] + [vmem] * (devices + 6) + [anywhere],
        [vmem] * 2,
        [room(devices, tile, columns)],
    )(table, high, low, direction, diagonal, scaled, own_sums, gathered, *later, given)
    for step in steps[1:]:
        rows = float_of(kept.shape[0] // 2, 2 * share_rows, columns)
        kept, given = call(
            add_kernel, [rows] * 2, [vmem] * 2 + [anywhere], [vmem] * 2
        )(kept, taken, sums)
        taken = swap(given, "samples", devices, step)
    for step in [1] + steps:
        sums = sums + swap(sums, "samples", devices, step)
    sums = sums + first_sums
    rows = float_of(share_rows, columns)
    own_scores, other_scores = call(last_add_kernel, [rows] * 2, [vmem] * 2, [vmem] * 2)(kept, taken)
    solved, scores = call(
        functools.partial(finish_kernel, 1.0 / math.sqrt(people * devices)),
        [full, float_of(share_rows, 2 * columns)],
        [vmem] * 8,
        [hbm, vmem],
        [full_room, pltpu.SemaphoreType.DMA((4,))],
    )(
        direction, scaled, direction_scores, own_scores,
        *(swap(rows, "cols", 2, 1) for rows in (direction_scores[share_rows:], other_scores)),
        sums, swap(sums, "cols", 2, 1),
    )
    return (solved, scores)


def solution(mesh):
    return jax.shard_map(
        per_device,
        mesh=mesh,
        in_specs=(
            P(("groups", "samples"), None, None, None),
            P("groups", None),
            P(("groups", "samples")),
            P(("groups", "samples"), "cols"),
            P(("groups", "samples"), "cols"),
        ),
        out_specs=(P(("groups", "samples"), "cols"), P(("groups", "cols", "samples"), None)),
        check_vma=False,
    )
```

```python
import functools
import math

import jax
import jax.numpy as jnp
from jax import lax
from jax.experimental import pallas as pl
from jax.experimental.layout import Layout, with_layout_constraint
from jax.experimental.pallas import tpu as pltpu
from jax.sharding import PartitionSpec as P

VMEM_LIMIT = 24 * 1024 * 1024
LARGE_VMEM = 56 * 1024 * 1024
SUBLANES = 8


def split(values):
    high = values.astype(jnp.bfloat16)
    low = (values - high.astype(jnp.float32)).astype(jnp.bfloat16)
    return high, low


def dot(left, right):
    return jnp.dot(left, right, preferred_element_type=jnp.float32)


def on_diagonal(size):
    rows = lax.broadcasted_iota(jnp.int32, (size, size), 0)
    return rows == lax.broadcasted_iota(jnp.int32, (size, size), 1)


def split_tiles(kinship_ref, high_ref, low_ref):
    block_count, positions, tile = kinship_ref.shape[:3]
    diagonal_mask = on_diagonal(tile)
    for row in range(block_count):
        for position in range(positions):
            values = kinship_ref[row, position]
            if position == 0:
                values = jnp.where(diagonal_mask, 0.0, values)
            high, low = split(values)
            high_ref[row, :, pl.ds(position * tile, tile)] = high
            low_ref[row, :, pl.ds(position * tile, tile)] = low


def product(high, low, blocks):
    parts = [split(block) for block in blocks]
    blocks_high = jnp.concatenate([part[0] for part in parts], axis=0)
    blocks_low = jnp.concatenate([part[1] for part in parts], axis=0)
    return dot(high, blocks_high) + (dot(low, blocks_high) + dot(high, blocks_low))


def column_sums(values):
    rows, columns = values.shape
    return jnp.sum(values.reshape(rows // SUBLANES, SUBLANES, columns), axis=0)


class Copies:
    def __init__(self, semaphores):
        self.semaphores = semaphores
        self.count = 0

    def start(self, source, target):
        copy = pltpu.make_async_copy(source, target, self.semaphores.at[self.count])
        self.count += 1
        copy.start()
        return copy


def wait_all(copies):
    for copy in copies:
        copy.wait()


def quotient(value, divisor):
    if divisor & (divisor - 1) == 0:
        return lax.shift_right_logical(value, jnp.int32(divisor.bit_length() - 1))
    return lax.div(value, jnp.int32(divisor))


def direction_kernel(kinship_ref, variance_ref, phenotypes_ref, direction_ref, diagonal_ref, sums_ref):
    block_count, positions, tile = kinship_ref.shape[:3]
    norm = jnp.zeros((SUBLANES, direction_ref.shape[1]), jnp.float32)
    diagonal_mask = on_diagonal(tile)
    for row in range(block_count):
        block = pl.ds(row * tile, tile)
        total = jnp.where(diagonal_mask, variance_ref[row:row + 1, :], kinship_ref[row, 0])
        for position in range(1, positions):
            total = total + kinship_ref[row, position]
        diagonal = jnp.sum(total, axis=1, keepdims=True)
        diagonal_ref[block, :] = diagonal
        here = phenotypes_ref[block, :] * (1.0 / diagonal)
        direction_ref[block, :] = here
        norm = norm + column_sums(here * phenotypes_ref[block, :])
    row_ids = lax.broadcasted_iota(jnp.int32, norm.shape, 0)
    sums_ref[...] = jnp.where(row_ids == 0, jnp.sum(norm, axis=0, keepdims=True), 0.0)


def route_kernel(devices, capacity, list_ref, kinship_ref, direction_ref, gate_ref, table_ref, forward_ref, high_ref,
                 low_ref, *refs):
    half = devices // 2
    outgoing_refs, (first_ref, last_ref) = refs[:half - 1], refs[half - 1:]
    block_count, positions, tile = kinship_ref.shape[:3]
    split_tiles(kinship_ref, high_ref, low_ref)
    me = lax.axis_index("samples")
    partner = me ^ half
    spare = me ^ 1
    top = block_count * block_count

    def collect(device):
        for j in range(devices):
            first_ref[j] = jnp.int32(top)
            last_ref[j] = jnp.int32(-1)
        found = []
        for row in range(block_count):
            for position in range(positions - 1):
                listed = list_ref[position, device * block_count + row]
                live = listed >= 0
                safe = jnp.maximum(listed, 0)
                other = quotient(safe, block_count)
                far_block = safe - other * block_count
                key = jnp.where(device < other, row * block_count + far_block, far_block * block_count + row)
                first_ref[other] = jnp.minimum(first_ref[other], jnp.where(live, key, top))
                last_ref[other] = jnp.maximum(last_ref[other], jnp.where(live, key, -1))
                found.append((live, other, far_block, key))
        return found

    def blocks_for(device, other):
        blocks = []
        for key in (first_ref[other], last_ref[other]):
            safe = jnp.clip(key, 0, top - 1)
            lower = quotient(safe, block_count)
            higher = safe - lower * block_count
            blocks.append(jnp.where(key == safe, jnp.where(device < other, lower, higher), 0))
        return blocks

    collect(partner)
    for k in range(1, half):
        blocks = blocks_for(partner, me ^ k)
        for slot in range(capacity):
            forward_ref[slot, k] = blocks[slot]
    for entry, (live, other, far_block, key) in enumerate(collect(me)):
        first, last = first_ref[other], last_ref[other]
        handled = jnp.where(me < other, first, last)
        weight = jnp.where(first == last, 1, 2)
        slot = jnp.where(key == first, 0, capacity - 1)
        place = jnp.where(other == partner, devices * capacity + far_block, other * capacity + slot)
        table_ref[0, entry] = jnp.where(live, place, spare * capacity)
        table_ref[1, entry] = jnp.where(live, other, spare)
        table_ref[2, entry] = jnp.where(live & (key == handled), weight, 0)
    for other in range(devices):
        blocks = blocks_for(me, other)
        table_ref[3, other] = jnp.where(me < other, blocks[1], blocks[0])
    near = [blocks_for(me, me ^ k) for k in range(1, half)]
    for k in range(1, half):
        for slot in range(capacity):
            start = pl.multiple_of(near[k - 1][slot] * tile, tile)
            outgoing_refs[k - 1][slot] = direction_ref[pl.ds(start, tile), :]


def forward_kernel(forward_ref, partner_ref, *refs):
    capacity, half = forward_ref.shape
    outgoing_refs = refs[1 - half:]
    tile = outgoing_refs[0].shape[1]
    for k in range(1, half):
        for slot in range(capacity):
            start = pl.multiple_of(forward_ref[slot, k] * tile, tile)
            outgoing_refs[k - 1][slot] = partner_ref[pl.ds(start, tile), :]


def gather_received(devices, capacity, received_refs, gathered_ref):
    half = devices // 2
    me = lax.axis_index("samples")
    near_refs, far_refs, partner_ref = received_refs[:half - 1], received_refs[half - 1:-1], received_refs[-1]
    gathered_ref[pl.ds(devices * capacity, partner_ref.shape[0])] = partner_ref[...]
    for k in range(1, half):
        mate = me ^ k
        gathered_ref[pl.ds(mate * capacity, capacity)] = near_refs[k - 1][...]
        gathered_ref[pl.ds((mate ^ half) * capacity, capacity)] = far_refs[k - 1][...]


def score_products(high_ref, low_ref, values, even_ref, odd_ref):
    count, rows = even_ref.shape[:2]
    for odd, out_ref in enumerate((even_ref, odd_ref)):
        for i in range(0, count, 4):
            here = pl.ds(i * rows, 4 * rows)
            total = product(high_ref[odd, here, :], low_ref[odd, here, :], [values])
            out_ref[pl.ds(i, 4)] = total.reshape(4, rows, -1)


def score_kernel(high_ref, low_ref, values_ref, even_ref, odd_ref):
    score_products(high_ref, low_ref, values_ref[...], even_ref, odd_ref)


def apply_kernel(devices, capacity, table_ref, high_ref, low_ref, direction_ref, diagonal_ref, norm_ref,
                 dosage_high_ref, dosage_low_ref, *refs):
    received_refs = refs[:devices - 1]
    scaled_ref, handled_ref, outgoing_ref, even_ref, odd_ref, gathered_ref = refs[-6:]
    gather_received(devices, capacity, received_refs, gathered_ref)
    block_count, tile, depth = high_ref.shape
    others = depth // tile - 1
    cross = jnp.zeros(norm_ref.shape, jnp.float32)
    for row in range(block_count):
        block = pl.ds(row * tile, tile)
        here = direction_ref[block, :]
        blocks = [gathered_ref[table_ref[0, row * others + i]] for i in range(others)]
        weights = [table_ref[2, row * others + i].astype(jnp.float32) for i in range(others)]
        mapped = product(high_ref[row], low_ref[row], [here] + blocks)
        far = pl.ds(tile, depth - tile)
        handled_ref[block, :] = product(
            high_ref[row, :, far], low_ref[row, :, far], [weight * there for weight, there in zip(weights, blocks)]
        )
        scaled_ref[block, :] = mapped * (1.0 / diagonal_ref[block, :])
        cross = cross + column_sums(here * mapped)
    row_ids = lax.broadcasted_iota(jnp.int32, cross.shape, 0)
    sums = jnp.where(row_ids == 1, jnp.sum(cross, axis=0, keepdims=True), norm_ref[...])
    for other in range(devices):
        start = pl.multiple_of(table_ref[3, other] * tile, tile)
        outgoing_ref[other, pl.ds(0, tile), :] = scaled_ref[pl.ds(start, tile), :]
        outgoing_ref[other, pl.ds(tile, SUBLANES), :] = sums
    score_products(dosage_high_ref, dosage_low_ref, scaled_ref[...], even_ref, odd_ref)


def curvature_kernel(devices, table_ref, high_ref, low_ref, direction_ref, diagonal_ref, scaled_ref, handled_ref,
                     later_ref, *refs):
    sums_ref = refs[-1]
    block_count, tile, depth = high_ref.shape
    others = depth // tile - 1
    first_sums = later_ref[0, pl.ds(tile, SUBLANES), :]
    for other in range(1, devices):
        first_sums = first_sums + later_ref[other, pl.ds(tile, SUBLANES), :]
    rho = first_sums[1:2, :] / first_sums[0:1, :]
    norm = jnp.zeros(first_sums.shape, jnp.float32)
    bend = jnp.zeros(first_sums.shape, jnp.float32)
    for row in range(block_count):
        block = pl.ds(row * tile, tile)
        here = scaled_ref[block, :] - rho * direction_ref[block, :]
        blocks = [here]
        for i in range(others):
            entry = row * others + i
            weight = table_ref[2, entry].astype(jnp.float32)
            blocks.append(weight * later_ref[table_ref[1, entry], pl.ds(0, tile), :])
        mapped = product(high_ref[row], low_ref[row], blocks) - rho * handled_ref[block, :]
        norm = norm + column_sums(here * here * diagonal_ref[block, :])
        bend = bend + column_sums(here * mapped)
    row_ids = lax.broadcasted_iota(jnp.int32, first_sums.shape, 0)
    sums = jnp.where(row_ids == 2, jnp.sum(norm, axis=0, keepdims=True), first_sums)
    sums = jnp.where(row_ids == 3, jnp.sum(bend, axis=0, keepdims=True), sums)
    for i in range(2 * devices):
        sums_ref[i] = sums


def add_kernel(kept_ref, taken_ref, near_ref, far_ref):
    count = near_ref.shape[0]
    near_ref[...] = kept_ref[pl.ds(0, count)] + taken_ref[pl.ds(0, count)]
    far_ref[...] = kept_ref[pl.ds(count, count)] + taken_ref[pl.ds(count, count)]


def last_add_kernel(first_kept_ref, first_taken_ref, second_kept_ref, second_taken_ref, gate_ref, own_ref, other_ref):
    rows = own_ref.shape[1]
    for i, (kept_ref, taken_ref) in enumerate(
        ((first_kept_ref, first_taken_ref), (second_kept_ref, second_taken_ref))
    ):
        own_ref[i] = kept_ref[0, pl.ds(0, rows), :] + taken_ref[0, pl.ds(0, rows), :]
        other_ref[i] = kept_ref[0, pl.ds(rows, rows), :] + taken_ref[0, pl.ds(rows, rows), :]


def group_kernel(order, own_ref, other_ref, high_ref, low_ref):
    rows = own_ref.shape[0] // (2 * len(order))
    me = lax.axis_index("samples")
    for odd in range(2):
        for i, distance in enumerate(order):
            start = pl.multiple_of((me ^ distance ^ odd) * rows, rows)
            for j, dosage_ref in enumerate((own_ref, other_ref)):
                high, low = split(dosage_ref[pl.ds(start, rows), :])
                here = pl.ds((2 * i + j) * rows, rows)
                high_ref[odd, here, :] = high
                low_ref[odd, here, :] = low


def coefficients(sums, shared):
    norm, cross = sums[0:1, :], sums[1:2, :]
    later_norm, bend = shared[2:3, :], shared[3:4, :]
    curve = norm + cross
    ratio = later_norm / curve
    step = jnp.where(later_norm > 0, later_norm / (later_norm + bend - later_norm * ratio), 0.0)
    start = norm / curve
    return start * (1.0 + step * (ratio + cross / norm)), -start * step


def finish_kernel(devices, norm_scale, direction_ref, scaled_ref, own_scores_ref, other_scores_ref, sums_ref, solved_hbm,
                  scores_ref, solved_ref, semaphores):
    people, columns = direction_ref.shape
    column = lax.axis_index("cols")
    copies = Copies(semaphores)

    def total(which):
        sums = sums_ref[which]
        shared = sums
        for i in range(1, devices):
            shared = shared + sums_ref[2 * i + which]
        return sums, shared

    along, across = coefficients(*total(column))
    other_along, other_across = coefficients(*total(1 - column))
    stores = []
    part_rows = people // 4
    for part in range(4):
        block = pl.ds(part * part_rows, part_rows)
        solved_ref[block, :] = along * direction_ref[block, :] + across * scaled_ref[block, :]
        stores.append(copies.start(solved_ref.at[block], solved_hbm.at[block]))
    own = pl.multiple_of(column * columns, columns)
    other = pl.multiple_of((1 - column) * columns, columns)
    scores_ref[:, pl.ds(own, columns)] = norm_scale * (
        along * own_scores_ref[0] + across * own_scores_ref[1]
    )
    scores_ref[:, pl.ds(other, columns)] = norm_scale * (
        other_along * other_scores_ref[0] + other_across * other_scores_ref[1]
    )
    wait_all(stores)


def call(kernel, out_shape, in_specs, out_specs, scratch_shapes=(), limit=VMEM_LIMIT):
    return pl.pallas_call(
        kernel,
        out_shape=out_shape,
        in_specs=in_specs,
        out_specs=out_specs,
        scratch_shapes=list(scratch_shapes),
        compiler_params=pltpu.CompilerParams(vmem_limit_bytes=limit),
    )


def swap(values, axis, devices, step):
    return lax.ppermute(values, axis, [(i, i ^ step) for i in range(devices)])


def after(value, *others):
    return lax.optimization_barrier((value, *others))[0]


def per_device(kinship, relatives, variance, phenotypes, dosage):
    devices = lax.axis_size("samples")
    block_count, positions, tile = kinship.shape[:3]
    people, columns = phenotypes.shape
    variants = dosage.shape[1]
    share_rows = variants // devices
    entries = block_count * (positions - 1)
    capacity = -(-entries // (devices - 1))
    assert capacity <= 2
    hbm = pl.BlockSpec(memory_space=pltpu.HBM)
    anywhere = pl.BlockSpec(memory_space=pl.ANY)
    vmem = pl.BlockSpec(memory_space=pltpu.VMEM)
    smem = pl.BlockSpec(memory_space=pltpu.SMEM)
    float_of = lambda *shape: jax.ShapeDtypeStruct(shape, jnp.float32)
    room = lambda *shape: pltpu.VMEM(shape, jnp.float32)
    full = float_of(people, columns)
    full_room = room(people, columns)
    half = devices // 2
    near_by = list(range(1, half))
    direction, diagonal, norm = call(
        direction_kernel,
        [full, float_of(people, 1), float_of(SUBLANES, columns)],
        [vmem] * 3,
        [vmem] * 3,
    )(kinship, variance.reshape(block_count, tile), phenotypes)
    def to_mates(blocks):
        return [swap(block, "samples", devices, k) for k, block in zip(near_by, blocks)]

    bits = half.bit_length() - 1
    even = [sum(((i >> b) & 1) << (bits - b) for b in range(bits)) for i in range(half)]
    steps = [2 << i for i in range(bits)]
    other_dosage = with_layout_constraint(swap(after(dosage, direction), "cols", 2, 1), Layout((0, 1)))
    tiles = jax.ShapeDtypeStruct((block_count, tile, positions * tile), jnp.bfloat16)
    table, forward, high, low, *outgoing = call(
        functools.partial(route_kernel, devices, capacity),
        [
            jax.ShapeDtypeStruct((4, max(entries, devices)), jnp.int32),
            jax.ShapeDtypeStruct((capacity, half), jnp.int32),
            tiles, tiles,
        ] + [float_of(capacity, tile, columns)] * (half - 1),
        [smem, vmem, vmem, anywhere],
        [smem, smem] + [vmem] * (half + 1),
        [pltpu.SMEM((devices,), jnp.int32), pltpu.SMEM((devices,), jnp.int32)],
    )(relatives.T, kinship, direction, other_dosage)


    parts = jax.ShapeDtypeStruct((2, variants, people), jnp.bfloat16)
    large = VMEM_LIMIT if variants <= people else LARGE_VMEM
    grouped = call(
        functools.partial(group_kernel, even), [parts] * 2, [vmem] * 2, [vmem] * 2, limit=large
    )(after(dosage, table).T, other_dosage.T)

    products = float_of(half, 2 * share_rows, columns)

    def add_step(kept, taken):
        rows = float_of(kept.shape[0] // 2, 2 * share_rows, columns)
        return call(add_kernel, [rows] * 2, [vmem] * 2, [vmem] * 2)(kept, taken)

    partner = swap(direction, "samples", devices, half)
    near = to_mates(outgoing)
    direction_even, direction_odd = call(
        score_kernel, [products] * 2, [vmem] * 3, [vmem] * 2, limit=large
    )(*grouped, direction)
    direction_share = swap(direction_odd, "samples", devices, 1)
    far = to_mates(call(
        forward_kernel,
        [float_of(capacity, tile, columns)] * (half - 1),
        [smem, vmem] + [anywhere] * (half + 1),
        [vmem] * (half - 1),
    )(forward, partner, *near, direction_even, direction_odd))
    received = near + far + [partner.reshape(block_count, tile, columns)]
    scaled, handled, outgoing, scaled_even, scaled_odd = call(
        functools.partial(apply_kernel, devices, capacity),
        [full, full, float_of(devices, tile + SUBLANES, columns), products, products],
        [smem] + [vmem] * (devices + 6) + [anywhere],
        [vmem] * 5,
        [room(devices * capacity + block_count, tile, columns)],
        limit=large,
    )(table, high, low, direction, diagonal, norm, *grouped, *received, direction_share)
    later = lax.all_to_all(outgoing, "samples", split_axis=0, concat_axis=0, tiled=True)
    scaled_share = swap(scaled_odd, "samples", devices, 1)
    direction_kept, direction_given = add_step(direction_even, direction_share)
    scaled_kept, scaled_given = add_step(scaled_even, scaled_share)
    for step in steps[:-1]:
        direction_taken = swap(after(direction_given, scaled), "samples", devices, step)
        direction_kept, direction_given = add_step(direction_kept, direction_taken)
        scaled_taken = swap(scaled_given, "samples", devices, step)
        scaled_kept, scaled_given = add_step(scaled_kept, scaled_taken)
    direction_taken = swap(direction_given, "samples", devices, steps[-1])
    scaled_taken = swap(scaled_given, "samples", devices, steps[-1])
    sums = call(
        functools.partial(curvature_kernel, devices),
        float_of(2 * devices, SUBLANES, columns),
        [smem] + [vmem] * 7 + [anywhere] * 2,
        vmem,
    )(table, high, low, direction, diagonal, scaled, handled, later, direction_given, scaled_given)
    all_sums = lax.all_to_all(sums, ("samples", "cols"), split_axis=0, concat_axis=0, tiled=True)
    rows = float_of(2, share_rows, columns)
    own_scores, other_scores = call(
        last_add_kernel, [rows] * 2, [vmem] * 4 + [anywhere], [vmem] * 2
    )(direction_kept, direction_taken, scaled_kept, scaled_taken, sums)
    solved, scores = call(
        functools.partial(finish_kernel, devices, 1.0 / math.sqrt(people * devices)),
        [full, float_of(share_rows, 2 * columns)],
        [vmem] * 5,
        [hbm, vmem],
        [full_room, pltpu.SemaphoreType.DMA((4,))],
    )(direction, scaled, own_scores, swap(other_scores, "cols", 2, 1), all_sums)
    return (solved, scores)


def solution(mesh):
    return jax.shard_map(
        per_device,
        mesh=mesh,
        in_specs=(
            P(("groups", "samples"), None, None, None),
            P("groups", None),
            P(("groups", "samples")),
            P(("groups", "samples"), "cols"),
            P(("groups", "samples"), "cols"),
        ),
        out_specs=(P(("groups", "samples"), "cols"), P(("groups", "cols", "samples"), None)),
        check_vma=False,
    )
```

```python
import functools
import math

import jax
import jax.numpy as jnp
from jax import lax
from jax.experimental import pallas as pl
from jax.experimental.layout import Layout, with_layout_constraint
from jax.experimental.pallas import tpu as pltpu
from jax.sharding import PartitionSpec as P

VMEM_LIMIT = 24 * 1024 * 1024
LARGE_VMEM = 56 * 1024 * 1024
SUBLANES = 8


def split(values):
    high = values.astype(jnp.bfloat16)
    low = (values - high.astype(jnp.float32)).astype(jnp.bfloat16)
    return high, low


def dot(left, right):
    return jnp.dot(left, right, preferred_element_type=jnp.float32)


def on_diagonal(size):
    rows = lax.broadcasted_iota(jnp.int32, (size, size), 0)
    return rows == lax.broadcasted_iota(jnp.int32, (size, size), 1)


def split_tiles(kinship_ref, high_ref, low_ref):
    block_count, positions, tile = kinship_ref.shape[:3]
    diagonal_mask = on_diagonal(tile)
    for row in range(block_count):
        for position in range(positions):
            values = kinship_ref[row, position]
            if position == 0:
                values = jnp.where(diagonal_mask, 0.0, values)
            high, low = split(values)
            high_ref[row, :, pl.ds(position * tile, tile)] = high
            low_ref[row, :, pl.ds(position * tile, tile)] = low


def product(high, low, blocks):
    parts = [split(block) for block in blocks]
    blocks_high = jnp.concatenate([part[0] for part in parts], axis=0)
    blocks_low = jnp.concatenate([part[1] for part in parts], axis=0)
    return dot(high, blocks_high) + (dot(low, blocks_high) + dot(high, blocks_low))


def column_sums(values):
    rows, columns = values.shape
    return jnp.sum(values.reshape(rows // SUBLANES, SUBLANES, columns), axis=0)


class Copies:
    def __init__(self, semaphores):
        self.semaphores = semaphores
        self.count = 0

    def start(self, source, target):
        copy = pltpu.make_async_copy(source, target, self.semaphores.at[self.count])
        self.count += 1
        copy.start()
        return copy


def wait_all(copies):
    for copy in copies:
        copy.wait()


def quotient(value, divisor):
    if divisor & (divisor - 1) == 0:
        return lax.shift_right_logical(value, jnp.int32(divisor.bit_length() - 1))
    return lax.div(value, jnp.int32(divisor))


def direction_kernel(kinship_hbm, variance_hbm, phenotypes_hbm, direction_ref, direction_hbm, diagonal_hbm, sums_ref,
                     kinship_ref, variance_ref, phenotypes_ref, diagonal_ref, semaphores):
    block_count, positions, tile = kinship_ref.shape[:3]
    copies = Copies(semaphores)
    loads = [copies.start(variance_hbm, variance_ref)]
    for row in range(block_count):
        block = pl.ds(row * tile, tile)
        loads.append(copies.start(kinship_hbm.at[row], kinship_ref.at[row]))
        loads.append(copies.start(phenotypes_hbm.at[block], phenotypes_ref.at[block]))
    stores = []
    norm = jnp.zeros((SUBLANES, direction_ref.shape[1]), jnp.float32)
    diagonal_mask = on_diagonal(tile)
    loads[0].wait()
    for row in range(block_count):
        wait_all(loads[1 + 2 * row:3 + 2 * row])
        block = pl.ds(row * tile, tile)
        total = jnp.where(diagonal_mask, variance_ref[row:row + 1, :], kinship_ref[row, 0])
        for position in range(1, positions):
            total = total + kinship_ref[row, position]
        diagonal = jnp.sum(total, axis=1, keepdims=True)
        diagonal_ref[block, :] = diagonal
        here = phenotypes_ref[block, :] * (1.0 / diagonal)
        direction_ref[block, :] = here
        norm = norm + column_sums(here * phenotypes_ref[block, :])
        stores.append(copies.start(direction_ref.at[block], direction_hbm.at[block]))
    stores.append(copies.start(diagonal_ref, diagonal_hbm))
    row_ids = lax.broadcasted_iota(jnp.int32, norm.shape, 0)
    sums_ref[...] = jnp.where(row_ids == 0, jnp.sum(norm, axis=0, keepdims=True), 0.0)
    wait_all(stores)


def route_kernel(devices, capacity, list_ref, kinship_hbm, direction_ref, gate_ref, table_ref, forward_ref, high_hbm,
                 low_hbm, *refs):
    half = devices // 2
    outgoing_refs, refs = refs[:half - 1], refs[half - 1:]
    first_ref, last_ref, kinship_ref, high_ref, low_ref, semaphores = refs
    copies = Copies(semaphores)
    load = copies.start(kinship_hbm, kinship_ref)
    block_count, positions, tile = kinship_ref.shape[:3]
    me = lax.axis_index("samples")
    partner = me ^ half
    spare = me ^ 1
    top = block_count * block_count

    def collect(device):
        for j in range(devices):
            first_ref[j] = jnp.int32(top)
            last_ref[j] = jnp.int32(-1)
        found = []
        for row in range(block_count):
            for position in range(positions - 1):
                listed = list_ref[position, device * block_count + row]
                live = listed >= 0
                safe = jnp.maximum(listed, 0)
                other = quotient(safe, block_count)
                far_block = safe - other * block_count
                key = jnp.where(device < other, row * block_count + far_block, far_block * block_count + row)
                first_ref[other] = jnp.minimum(first_ref[other], jnp.where(live, key, top))
                last_ref[other] = jnp.maximum(last_ref[other], jnp.where(live, key, -1))
                found.append((live, other, far_block, key))
        return found

    def blocks_for(device, other):
        blocks = []
        for key in (first_ref[other], last_ref[other]):
            safe = jnp.clip(key, 0, top - 1)
            lower = quotient(safe, block_count)
            higher = safe - lower * block_count
            blocks.append(jnp.where(key == safe, jnp.where(device < other, lower, higher), 0))
        return blocks

    collect(partner)
    for k in range(1, half):
        blocks = blocks_for(partner, me ^ k)
        for slot in range(capacity):
            forward_ref[slot, k] = blocks[slot]
    for entry, (live, other, far_block, key) in enumerate(collect(me)):
        first, last = first_ref[other], last_ref[other]
        handled = jnp.where(me < other, first, last)
        weight = jnp.where(first == last, 1, 2)
        slot = jnp.where(key == first, 0, capacity - 1)
        place = jnp.where(other == partner, devices * capacity + far_block, other * capacity + slot)
        table_ref[0, entry] = jnp.where(live, place, spare * capacity)
        table_ref[1, entry] = jnp.where(live, other, spare)
        table_ref[2, entry] = jnp.where(live & (key == handled), weight, 0)
    for other in range(devices):
        blocks = blocks_for(me, other)
        table_ref[3, other] = jnp.where(me < other, blocks[1], blocks[0])
    near = [blocks_for(me, me ^ k) for k in range(1, half)]
    load.wait()
    split_tiles(kinship_ref, high_ref, low_ref)
    stores = [copies.start(high_ref, high_hbm), copies.start(low_ref, low_hbm)]
    for k in range(1, half):
        for slot in range(capacity):
            start = pl.multiple_of(near[k - 1][slot] * tile, tile)
            outgoing_refs[k - 1][slot] = direction_ref[pl.ds(start, tile), :]
    wait_all(stores)


def forward_kernel(forward_ref, partner_ref, *refs):
    capacity, half = forward_ref.shape
    outgoing_refs = refs[1 - half:]
    tile = outgoing_refs[0].shape[1]
    for k in range(1, half):
        for slot in range(capacity):
            start = pl.multiple_of(forward_ref[slot, k] * tile, tile)
            outgoing_refs[k - 1][slot] = partner_ref[pl.ds(start, tile), :]


def gather_received(devices, capacity, received_refs, gathered_ref):
    half = devices // 2
    me = lax.axis_index("samples")
    near_refs, far_refs, partner_ref = received_refs[:half - 1], received_refs[half - 1:-1], received_refs[-1]
    gathered_ref[pl.ds(devices * capacity, partner_ref.shape[0])] = partner_ref[...]
    for k in range(1, half):
        mate = me ^ k
        gathered_ref[pl.ds(mate * capacity, capacity)] = near_refs[k - 1][...]
        gathered_ref[pl.ds((mate ^ half) * capacity, capacity)] = far_refs[k - 1][...]


def score_products(high_ref, low_ref, values, even_ref, odd_ref):
    count, rows = even_ref.shape[:2]
    for odd, out_ref in enumerate((even_ref, odd_ref)):
        for i in range(0, count, 4):
            here = pl.ds(i * rows, 4 * rows)
            total = product(high_ref[odd, here, :], low_ref[odd, here, :], [values])
            out_ref[pl.ds(i, 4)] = total.reshape(4, rows, -1)


def score_kernel(high_ref, low_ref, values_ref, even_ref, odd_ref):
    score_products(high_ref, low_ref, values_ref[...], even_ref, odd_ref)


def apply_kernel(devices, capacity, table_ref, high_hbm, low_hbm, diagonal_hbm, direction_ref, norm_ref, dosage_high_ref,
                 dosage_low_ref, *refs):
    received_refs = refs[:devices - 1]
    (scaled_hbm, handled_hbm, outgoing_hbm, even_ref, odd_ref, gathered_ref, high_ref, low_ref, diagonal_ref, scaled_ref,
     handled_ref, sums_ref, semaphores) = refs[-13:]
    copies = Copies(semaphores)
    loads = [
        copies.start(high_hbm, high_ref), copies.start(low_hbm, low_ref), copies.start(diagonal_hbm, diagonal_ref)
    ]
    gather_received(devices, capacity, received_refs, gathered_ref)
    wait_all(loads)
    block_count, tile, depth = high_ref.shape
    others = depth // tile - 1
    cross = jnp.zeros(norm_ref.shape, jnp.float32)
    for row in range(block_count):
        block = pl.ds(row * tile, tile)
        here = direction_ref[block, :]
        blocks = [here] + [gathered_ref[table_ref[0, row * others + i]] for i in range(others)]
        mapped = product(high_ref[row], low_ref[row], blocks)
        scaled_ref[block, :] = mapped * (1.0 / diagonal_ref[block, :])
        cross = cross + column_sums(here * mapped)
    row_ids = lax.broadcasted_iota(jnp.int32, cross.shape, 0)
    sums_ref[...] = jnp.where(row_ids == 1, jnp.sum(cross, axis=0, keepdims=True), norm_ref[...])
    stores = [copies.start(scaled_ref, scaled_hbm)]
    for other in range(devices):
        start = pl.multiple_of(table_ref[3, other] * tile, tile)
        stores.append(copies.start(scaled_ref.at[pl.ds(start, tile)], outgoing_hbm.at[other, pl.ds(0, tile)]))
        stores.append(copies.start(sums_ref, outgoing_hbm.at[other, pl.ds(tile, SUBLANES)]))
    score_products(dosage_high_ref, dosage_low_ref, scaled_ref[...], even_ref, odd_ref)
    far = pl.ds(tile, depth - tile)
    for row in range(block_count):
        blocks = []
        for i in range(others):
            weight = table_ref[2, row * others + i].astype(jnp.float32)
            blocks.append(weight * gathered_ref[table_ref[0, row * others + i]])
        handled_ref[pl.ds(row * tile, tile), :] = product(high_ref[row, :, far], low_ref[row, :, far], blocks)
    stores.append(copies.start(handled_ref, handled_hbm))
    wait_all(stores)


def curvature_kernel(devices, table_ref, high_hbm, low_hbm, direction_hbm, diagonal_hbm, scaled_hbm, handled_hbm,
                     later_hbm, *refs):
    (sums_hbm, sums_ref, high_ref, low_ref, direction_ref, diagonal_ref, scaled_ref, handled_ref, later_ref,
     semaphores) = refs[-10:]
    block_count, tile, depth = high_ref.shape
    copies = Copies(semaphores)
    wait_all([copies.start(source, target) for source, target in (
        (later_hbm, later_ref), (scaled_hbm, scaled_ref), (direction_hbm, direction_ref), (high_hbm, high_ref),
        (low_hbm, low_ref), (handled_hbm, handled_ref), (diagonal_hbm, diagonal_ref),
    )])
    others = depth // tile - 1
    first_sums = later_ref[0, pl.ds(tile, SUBLANES), :]
    for other in range(1, devices):
        first_sums = first_sums + later_ref[other, pl.ds(tile, SUBLANES), :]
    rho = first_sums[1:2, :] / first_sums[0:1, :]
    norm = jnp.zeros(first_sums.shape, jnp.float32)
    bend = jnp.zeros(first_sums.shape, jnp.float32)
    for row in range(block_count):
        block = pl.ds(row * tile, tile)
        here = scaled_ref[block, :] - rho * direction_ref[block, :]
        blocks = [here]
        for i in range(others):
            entry = row * others + i
            weight = table_ref[2, entry].astype(jnp.float32)
            blocks.append(weight * later_ref[table_ref[1, entry], pl.ds(0, tile), :])
        mapped = product(high_ref[row], low_ref[row], blocks) - rho * handled_ref[block, :]
        norm = norm + column_sums(here * here * diagonal_ref[block, :])
        bend = bend + column_sums(here * mapped)
    row_ids = lax.broadcasted_iota(jnp.int32, first_sums.shape, 0)
    sums = jnp.where(row_ids == 2, jnp.sum(norm, axis=0, keepdims=True), first_sums)
    sums = jnp.where(row_ids == 3, jnp.sum(bend, axis=0, keepdims=True), sums)
    for i in range(2 * devices):
        sums_ref[i] = sums
    copies.start(sums_ref, sums_hbm).wait()


def add_kernel(kept_ref, taken_ref, near_ref, far_ref):
    count = near_ref.shape[0]
    near_ref[...] = kept_ref[pl.ds(0, count)] + taken_ref[pl.ds(0, count)]
    far_ref[...] = kept_ref[pl.ds(count, count)] + taken_ref[pl.ds(count, count)]


def last_add_kernel(first_kept_ref, first_taken_ref, second_kept_ref, second_taken_ref, own_ref, other_ref):
    rows = own_ref.shape[1]
    for i, (kept_ref, taken_ref) in enumerate(
        ((first_kept_ref, first_taken_ref), (second_kept_ref, second_taken_ref))
    ):
        own_ref[i] = kept_ref[0, pl.ds(0, rows), :] + taken_ref[0, pl.ds(0, rows), :]
        other_ref[i] = kept_ref[0, pl.ds(rows, rows), :] + taken_ref[0, pl.ds(rows, rows), :]


def group_kernel(order, own_ref, other_ref, high_ref, low_ref):
    rows = own_ref.shape[0] // (2 * len(order))
    me = lax.axis_index("samples")
    for odd in range(2):
        for i, distance in enumerate(order):
            start = pl.multiple_of((me ^ distance ^ odd) * rows, rows)
            for j, dosage_ref in enumerate((own_ref, other_ref)):
                high, low = split(dosage_ref[pl.ds(start, rows), :])
                here = pl.ds((2 * i + j) * rows, rows)
                high_ref[odd, here, :] = high
                low_ref[odd, here, :] = low


def coefficients(sums, shared):
    norm, cross = sums[0:1, :], sums[1:2, :]
    later_norm, bend = shared[2:3, :], shared[3:4, :]
    curve = norm + cross
    ratio = later_norm / curve
    step = jnp.where(later_norm > 0, later_norm / (later_norm + bend - later_norm * ratio), 0.0)
    start = norm / curve
    return start * (1.0 + step * (ratio + cross / norm)), -start * step


def finish_kernel(devices, norm_scale, direction_hbm, scaled_hbm, own_scores_ref, other_scores_ref, sums_ref, solved_hbm,
                  scores_ref, direction_ref, scaled_ref, semaphores):
    people, columns = direction_ref.shape
    column = lax.axis_index("cols")
    copies = Copies(semaphores)
    loads = [copies.start(direction_hbm, direction_ref), copies.start(scaled_hbm, scaled_ref)]

    def total(which):
        sums = sums_ref[which]
        shared = sums
        for i in range(1, devices):
            shared = shared + sums_ref[2 * i + which]
        return sums, shared

    along, across = coefficients(*total(column))
    other_along, other_across = coefficients(*total(1 - column))
    wait_all(loads)
    stores = []
    part_rows = people // 4
    for part in range(4):
        block = pl.ds(part * part_rows, part_rows)
        direction_ref[block, :] = along * direction_ref[block, :] + across * scaled_ref[block, :]
        stores.append(copies.start(direction_ref.at[block], solved_hbm.at[block]))
    own = pl.multiple_of(column * columns, columns)
    other = pl.multiple_of((1 - column) * columns, columns)
    scores_ref[:, pl.ds(own, columns)] = norm_scale * (
        along * own_scores_ref[0] + across * own_scores_ref[1]
    )
    scores_ref[:, pl.ds(other, columns)] = norm_scale * (
        other_along * other_scores_ref[0] + other_across * other_scores_ref[1]
    )
    wait_all(stores)


def call(kernel, out_shape, in_specs, out_specs, scratch_shapes=(), limit=VMEM_LIMIT):
    return pl.pallas_call(
        kernel,
        out_shape=out_shape,
        in_specs=in_specs,
        out_specs=out_specs,
        scratch_shapes=list(scratch_shapes),
        compiler_params=pltpu.CompilerParams(vmem_limit_bytes=limit),
    )


def swap(values, axis, devices, step):
    return lax.ppermute(values, axis, [(i, i ^ step) for i in range(devices)])


def after(value, *others):
    return lax.optimization_barrier((value, *others))[0]


def per_device(kinship, relatives, variance, phenotypes, dosage):
    devices = lax.axis_size("samples")
    block_count, positions, tile = kinship.shape[:3]
    people, columns = phenotypes.shape
    variants = dosage.shape[1]
    share_rows = variants // devices
    entries = block_count * (positions - 1)
    capacity = -(-entries // (devices - 1))
    assert capacity <= 2
    hbm = pl.BlockSpec(memory_space=pltpu.HBM)
    anywhere = pl.BlockSpec(memory_space=pl.ANY)
    vmem = pl.BlockSpec(memory_space=pltpu.VMEM)
    smem = pl.BlockSpec(memory_space=pltpu.SMEM)
    float_of = lambda *shape: jax.ShapeDtypeStruct(shape, jnp.float32)
    room = lambda *shape: pltpu.VMEM(shape, jnp.float32)
    full = float_of(people, columns)
    full_room = room(people, columns)
    half = devices // 2
    near_by = list(range(1, half))
    kinship = pltpu.with_memory_space_constraint(kinship, pltpu.HBM)
    tiles_room = pltpu.VMEM((block_count, tile, positions * tile), jnp.bfloat16)
    tiles_out = pltpu.HBM((block_count, tile, positions * tile), jnp.bfloat16)
    full_out = pltpu.HBM((people, columns), jnp.float32)
    direction, direction_kept_hbm, diagonal, norm = call(
        direction_kernel,
        [full, full_out, pltpu.HBM((people, 1), jnp.float32), float_of(SUBLANES, columns)],
        [hbm] * 3,
        [vmem, hbm, hbm, vmem],
        [
            room(*kinship.shape), room(block_count, tile), full_room, room(people, 1),
            pltpu.SemaphoreType.DMA((3 * block_count + 2,)),
        ],
    )(
        kinship,
        pltpu.with_memory_space_constraint(variance.reshape(block_count, tile), pltpu.HBM),
        pltpu.with_memory_space_constraint(phenotypes, pltpu.HBM),
    )
    def to_mates(blocks):
        return [swap(block, "samples", devices, k) for k, block in zip(near_by, blocks)]

    bits = half.bit_length() - 1
    even = [sum(((i >> b) & 1) << (bits - b) for b in range(bits)) for i in range(half)]
    steps = [2 << i for i in range(bits)]
    other_dosage = with_layout_constraint(swap(after(dosage, direction), "cols", 2, 1), Layout((0, 1)))
    table, forward, high, low, *outgoing = call(
        functools.partial(route_kernel, devices, capacity),
        [
            jax.ShapeDtypeStruct((4, max(entries, devices)), jnp.int32),
            jax.ShapeDtypeStruct((capacity, half), jnp.int32),
            tiles_out, tiles_out,
        ] + [float_of(capacity, tile, columns)] * (half - 1),
        [smem, hbm, vmem, anywhere],
        [smem, smem, hbm, hbm] + [vmem] * (half - 1),
        [
            pltpu.SMEM((devices,), jnp.int32), pltpu.SMEM((devices,), jnp.int32),
            room(*kinship.shape), tiles_room, tiles_room, pltpu.SemaphoreType.DMA((3,)),
        ],
    )(relatives.T, kinship, direction, other_dosage)


    parts = jax.ShapeDtypeStruct((2, variants, people), jnp.bfloat16)
    large = VMEM_LIMIT if variants <= people else LARGE_VMEM
    grouped = call(
        functools.partial(group_kernel, even), [parts] * 2, [vmem] * 2, [vmem] * 2, limit=large
    )(after(dosage, table).T, other_dosage.T)

    products = float_of(half, 2 * share_rows, columns)

    def add_step(kept, taken):
        rows = float_of(kept.shape[0] // 2, 2 * share_rows, columns)
        return call(add_kernel, [rows] * 2, [vmem] * 2, [vmem] * 2)(kept, taken)

    partner = swap(direction, "samples", devices, half)
    near = to_mates(outgoing)
    direction_even, direction_odd = call(
        score_kernel, [products] * 2, [vmem] * 3, [vmem] * 2, limit=large
    )(*grouped, direction)
    direction_share = swap(direction_odd, "samples", devices, 1)
    far = to_mates(call(
        forward_kernel,
        [float_of(capacity, tile, columns)] * (half - 1),
        [smem, vmem] + [anywhere] * (half + 1),
        [vmem] * (half - 1),
    )(forward, partner, *near, direction_even, direction_odd))
    received = near + far + [partner.reshape(block_count, tile, columns)]
    scaled, handled, outgoing, scaled_even, scaled_odd = call(
        functools.partial(apply_kernel, devices, capacity),
        [
            full_out, full_out, pltpu.HBM((devices, tile + SUBLANES, columns), jnp.float32), products, products,
        ],
        [smem, hbm, hbm, hbm] + [vmem] * (devices + 3) + [anywhere],
        [hbm, hbm, hbm, vmem, vmem],
        [
            room(devices * capacity + block_count, tile, columns), tiles_room, tiles_room, room(people, 1), full_room,
            full_room, room(SUBLANES, columns), pltpu.SemaphoreType.DMA((2 * devices + 5,)),
        ],
        limit=large,
    )(table, high, low, diagonal, direction, norm, *grouped, *received, direction_share)
    later = lax.all_to_all(outgoing, "samples", split_axis=0, concat_axis=0, tiled=True)
    scaled_share = swap(scaled_odd, "samples", devices, 1)
    direction_kept, direction_given = add_step(direction_even, direction_share)
    scaled_kept, scaled_given = add_step(scaled_even, scaled_share)
    for step in steps[:-1]:
        direction_taken = swap(after(direction_given, scaled), "samples", devices, step)
        direction_kept, direction_given = add_step(direction_kept, direction_taken)
        scaled_taken = swap(scaled_given, "samples", devices, step)
        scaled_kept, scaled_given = add_step(scaled_kept, scaled_taken)
    direction_taken = swap(direction_given, "samples", devices, steps[-1])
    scaled_taken = swap(scaled_given, "samples", devices, steps[-1])
    rows = float_of(2, share_rows, columns)
    own_scores, other_scores = call(
        last_add_kernel, [rows] * 2, [vmem] * 4, [vmem] * 2
    )(direction_kept, direction_taken, scaled_kept, scaled_taken)
    other_scores = swap(other_scores, "cols", 2, 1)
    sums = call(
        functools.partial(curvature_kernel, devices),
        pltpu.HBM((2 * devices, SUBLANES, columns), jnp.float32),
        [smem] + [hbm] * 6 + [anywhere] * 2,
        hbm,
        [
            room(2 * devices, SUBLANES, columns), tiles_room, tiles_room, full_room, room(people, 1), full_room,
            full_room, room(devices, tile + SUBLANES, columns), pltpu.SemaphoreType.DMA((8,)),
        ],
    )(table, high, low, direction_kept_hbm, diagonal, scaled, handled, later, other_scores)
    all_sums = lax.all_to_all(sums, ("samples", "cols"), split_axis=0, concat_axis=0, tiled=True)
    solved, scores = call(
        functools.partial(finish_kernel, devices, 1.0 / math.sqrt(people * devices)),
        [full, float_of(share_rows, 2 * columns)],
        [hbm, hbm, vmem, vmem, vmem],
        [hbm, vmem],
        [full_room, full_room, pltpu.SemaphoreType.DMA((6,))],
    )(direction_kept_hbm, scaled, own_scores, other_scores, all_sums)
    return (solved, scores)


def solution(mesh):
    return jax.shard_map(
        per_device,
        mesh=mesh,
        in_specs=(
            P(("groups", "samples"), None, None, None),
            P("groups", None),
            P(("groups", "samples")),
            P(("groups", "samples"), "cols"),
            P(("groups", "samples"), "cols"),
        ),
        out_specs=(P(("groups", "samples"), "cols"), P(("groups", "cols", "samples"), None)),
        check_vma=False,
    )
```

```python
import functools
import math

import jax
import jax.numpy as jnp
from jax import lax
from jax.experimental import pallas as pl
from jax.experimental.layout import Layout, with_layout_constraint
from jax.experimental.pallas import tpu as pltpu
from jax.sharding import PartitionSpec as P

VMEM_LIMIT = 24 * 1024 * 1024
LARGE_VMEM = 56 * 1024 * 1024
SUBLANES = 8


def split(values):
    high = values.astype(jnp.bfloat16)
    low = (values - high.astype(jnp.float32)).astype(jnp.bfloat16)
    return high, low


def dot(left, right):
    return jnp.dot(left, right, preferred_element_type=jnp.float32)


def on_diagonal(size):
    rows = lax.broadcasted_iota(jnp.int32, (size, size), 0)
    return rows == lax.broadcasted_iota(jnp.int32, (size, size), 1)


def split_tiles(kinship_ref, high_ref, low_ref):
    block_count, positions, tile = kinship_ref.shape[:3]
    diagonal_mask = on_diagonal(tile)
    for row in range(block_count):
        for position in range(positions):
            values = kinship_ref[row, position]
            if position == 0:
                values = jnp.where(diagonal_mask, 0.0, values)
            high, low = split(values)
            high_ref[row, :, pl.ds(position * tile, tile)] = high
            low_ref[row, :, pl.ds(position * tile, tile)] = low


def product(high, low, blocks):
    parts = [split(block) for block in blocks]
    blocks_high = jnp.concatenate([part[0] for part in parts], axis=0)
    blocks_low = jnp.concatenate([part[1] for part in parts], axis=0)
    return dot(high, blocks_high) + (dot(low, blocks_high) + dot(high, blocks_low))


def column_sums(values):
    rows, columns = values.shape
    return jnp.sum(values.reshape(rows // SUBLANES, SUBLANES, columns), axis=0)


class Copies:
    def __init__(self, semaphores):
        self.semaphores = semaphores
        self.count = 0

    def start(self, source, target):
        copy = pltpu.make_async_copy(source, target, self.semaphores.at[self.count])
        self.count += 1
        copy.start()
        return copy


def wait_all(copies):
    for copy in copies:
        copy.wait()


def quotient(value, divisor):
    if divisor & (divisor - 1) == 0:
        return lax.shift_right_logical(value, jnp.int32(divisor.bit_length() - 1))
    return lax.div(value, jnp.int32(divisor))


def direction_kernel(kinship_hbm, variance_hbm, phenotypes_hbm, direction_ref, direction_hbm, diagonal_hbm, sums_ref,
                     kinship_ref, variance_ref, phenotypes_ref, diagonal_ref, semaphores):
    block_count, positions, tile = kinship_ref.shape[:3]
    copies = Copies(semaphores)
    loads = [copies.start(variance_hbm, variance_ref)]
    for row in range(block_count):
        block = pl.ds(row * tile, tile)
        loads.append(copies.start(kinship_hbm.at[row], kinship_ref.at[row]))
        loads.append(copies.start(phenotypes_hbm.at[block], phenotypes_ref.at[block]))
    stores = []
    norm = jnp.zeros((SUBLANES, direction_ref.shape[1]), jnp.float32)
    diagonal_mask = on_diagonal(tile)
    loads[0].wait()
    for row in range(block_count):
        wait_all(loads[1 + 2 * row:3 + 2 * row])
        block = pl.ds(row * tile, tile)
        total = jnp.where(diagonal_mask, variance_ref[row:row + 1, :], kinship_ref[row, 0])
        for position in range(1, positions):
            total = total + kinship_ref[row, position]
        diagonal = jnp.sum(total, axis=1, keepdims=True)
        diagonal_ref[block, :] = diagonal
        here = phenotypes_ref[block, :] * (1.0 / diagonal)
        direction_ref[block, :] = here
        norm = norm + column_sums(here * phenotypes_ref[block, :])
        stores.append(copies.start(direction_ref.at[block], direction_hbm.at[block]))
    stores.append(copies.start(diagonal_ref, diagonal_hbm))
    row_ids = lax.broadcasted_iota(jnp.int32, norm.shape, 0)
    sums_ref[...] = jnp.where(row_ids == 0, jnp.sum(norm, axis=0, keepdims=True), 0.0)
    wait_all(stores)


def route_kernel(devices, capacity, list_ref, kinship_hbm, direction_ref, gate_ref, table_ref, forward_ref, high_hbm,
                 low_hbm, *refs):
    half = devices // 2
    outgoing_refs, refs = refs[:half - 1], refs[half - 1:]
    first_ref, last_ref, kinship_ref, high_ref, low_ref, semaphores = refs
    copies = Copies(semaphores)
    load = copies.start(kinship_hbm, kinship_ref)
    block_count, positions, tile = kinship_ref.shape[:3]
    me = lax.axis_index("samples")
    partner = me ^ half
    spare = me ^ 1
    top = block_count * block_count

    def collect(device):
        for j in range(devices):
            first_ref[j] = jnp.int32(top)
            last_ref[j] = jnp.int32(-1)
        found = []
        for row in range(block_count):
            for position in range(positions - 1):
                listed = list_ref[position, device * block_count + row]
                live = listed >= 0
                safe = jnp.maximum(listed, 0)
                other = quotient(safe, block_count)
                far_block = safe - other * block_count
                key = jnp.where(device < other, row * block_count + far_block, far_block * block_count + row)
                first_ref[other] = jnp.minimum(first_ref[other], jnp.where(live, key, top))
                last_ref[other] = jnp.maximum(last_ref[other], jnp.where(live, key, -1))
                found.append((live, other, far_block, key))
        return found

    def blocks_for(device, other):
        blocks = []
        for key in (first_ref[other], last_ref[other]):
            safe = jnp.clip(key, 0, top - 1)
            lower = quotient(safe, block_count)
            higher = safe - lower * block_count
            blocks.append(jnp.where(key == safe, jnp.where(device < other, lower, higher), 0))
        return blocks

    collect(partner)
    for k in range(1, half):
        blocks = blocks_for(partner, me ^ k)
        for slot in range(capacity):
            forward_ref[slot, k] = blocks[slot]
    for entry, (live, other, far_block, key) in enumerate(collect(me)):
        first, last = first_ref[other], last_ref[other]
        handled = jnp.where(me < other, first, last)
        weight = jnp.where(first == last, 1, 2)
        slot = jnp.where(key == first, 0, capacity - 1)
        place = jnp.where(other == partner, devices * capacity + far_block, other * capacity + slot)
        table_ref[0, entry] = jnp.where(live, place, spare * capacity)
        table_ref[1, entry] = jnp.where(live, other, spare)
        table_ref[2, entry] = jnp.where(live & (key == handled), weight, 0)
    for other in range(devices):
        blocks = blocks_for(me, other)
        table_ref[3, other] = jnp.where(me < other, blocks[1], blocks[0])
    near = [blocks_for(me, me ^ k) for k in range(1, half)]
    load.wait()
    split_tiles(kinship_ref, high_ref, low_ref)
    stores = [copies.start(high_ref, high_hbm), copies.start(low_ref, low_hbm)]
    for k in range(1, half):
        for slot in range(capacity):
            start = pl.multiple_of(near[k - 1][slot] * tile, tile)
            outgoing_refs[k - 1][slot] = direction_ref[pl.ds(start, tile), :]
    wait_all(stores)


def forward_kernel(forward_ref, partner_ref, *refs):
    capacity, half = forward_ref.shape
    outgoing_refs = refs[1 - half:]
    tile = outgoing_refs[0].shape[1]
    for k in range(1, half):
        for slot in range(capacity):
            start = pl.multiple_of(forward_ref[slot, k] * tile, tile)
            outgoing_refs[k - 1][slot] = partner_ref[pl.ds(start, tile), :]


def gather_received(devices, capacity, received_refs, gathered_ref):
    half = devices // 2
    me = lax.axis_index("samples")
    near_refs, far_refs, partner_ref = received_refs[:half - 1], received_refs[half - 1:-1], received_refs[-1]
    gathered_ref[pl.ds(devices * capacity, partner_ref.shape[0])] = partner_ref[...]
    for k in range(1, half):
        mate = me ^ k
        gathered_ref[pl.ds(mate * capacity, capacity)] = near_refs[k - 1][...]
        gathered_ref[pl.ds((mate ^ half) * capacity, capacity)] = far_refs[k - 1][...]


def score_products(high_ref, low_ref, values, even_ref, odd_ref):
    count, rows = even_ref.shape[:2]
    for odd, out_ref in enumerate((even_ref, odd_ref)):
        for i in range(0, count, 4):
            here = pl.ds(i * rows, 4 * rows)
            total = product(high_ref[odd, here, :], low_ref[odd, here, :], [values])
            out_ref[pl.ds(i, 4)] = total.reshape(4, rows, -1)


def score_kernel(high_ref, low_ref, values_ref, even_ref, odd_ref):
    score_products(high_ref, low_ref, values_ref[...], even_ref, odd_ref)


def apply_kernel(devices, capacity, table_ref, high_hbm, low_hbm, diagonal_hbm, direction_ref, norm_ref, dosage_high_ref,
                 dosage_low_ref, *refs):
    received_refs = refs[:devices - 1]
    (scaled_hbm, handled_hbm, outgoing_hbm, even_hbm, odd_hbm, gathered_ref, high_ref, low_ref, diagonal_ref, scaled_ref,
     handled_ref, sums_ref, even_ref, odd_ref, semaphores) = refs[-15:]
    copies = Copies(semaphores)
    loads = [
        copies.start(high_hbm, high_ref), copies.start(low_hbm, low_ref), copies.start(diagonal_hbm, diagonal_ref)
    ]
    gather_received(devices, capacity, received_refs, gathered_ref)
    wait_all(loads)
    block_count, tile, depth = high_ref.shape
    others = depth // tile - 1
    cross = jnp.zeros(norm_ref.shape, jnp.float32)
    for row in range(block_count):
        block = pl.ds(row * tile, tile)
        here = direction_ref[block, :]
        blocks = [here] + [gathered_ref[table_ref[0, row * others + i]] for i in range(others)]
        mapped = product(high_ref[row], low_ref[row], blocks)
        scaled_ref[block, :] = mapped * (1.0 / diagonal_ref[block, :])
        cross = cross + column_sums(here * mapped)
    row_ids = lax.broadcasted_iota(jnp.int32, cross.shape, 0)
    sums_ref[...] = jnp.where(row_ids == 1, jnp.sum(cross, axis=0, keepdims=True), norm_ref[...])
    stores = [copies.start(scaled_ref, scaled_hbm)]
    for other in range(devices):
        start = pl.multiple_of(table_ref[3, other] * tile, tile)
        stores.append(copies.start(scaled_ref.at[pl.ds(start, tile)], outgoing_hbm.at[other, pl.ds(0, tile)]))
        stores.append(copies.start(sums_ref, outgoing_hbm.at[other, pl.ds(tile, SUBLANES)]))
    score_products(dosage_high_ref, dosage_low_ref, scaled_ref[...], even_ref, odd_ref)
    stores += [copies.start(odd_ref, odd_hbm), copies.start(even_ref, even_hbm)]
    far = pl.ds(tile, depth - tile)
    for row in range(block_count):
        blocks = []
        for i in range(others):
            weight = table_ref[2, row * others + i].astype(jnp.float32)
            blocks.append(weight * gathered_ref[table_ref[0, row * others + i]])
        handled_ref[pl.ds(row * tile, tile), :] = product(high_ref[row, :, far], low_ref[row, :, far], blocks)
    stores.append(copies.start(handled_ref, handled_hbm))
    wait_all(stores)


def curvature_kernel(devices, table_ref, high_hbm, low_hbm, direction_hbm, diagonal_hbm, scaled_hbm, handled_hbm,
                     later_hbm, *refs):
    (sums_ref, high_ref, low_ref, direction_ref, diagonal_ref, scaled_ref, handled_ref, later_ref,
     semaphores) = refs[-9:]
    block_count, tile, depth = high_ref.shape
    copies = Copies(semaphores)
    wait_all([copies.start(source, target) for source, target in (
        (later_hbm, later_ref), (scaled_hbm, scaled_ref), (direction_hbm, direction_ref), (high_hbm, high_ref),
        (low_hbm, low_ref), (handled_hbm, handled_ref), (diagonal_hbm, diagonal_ref),
    )])
    others = depth // tile - 1
    first_sums = later_ref[0, pl.ds(tile, SUBLANES), :]
    for other in range(1, devices):
        first_sums = first_sums + later_ref[other, pl.ds(tile, SUBLANES), :]
    rho = first_sums[1:2, :] / first_sums[0:1, :]
    norm = jnp.zeros(first_sums.shape, jnp.float32)
    bend = jnp.zeros(first_sums.shape, jnp.float32)
    for row in range(block_count):
        block = pl.ds(row * tile, tile)
        here = scaled_ref[block, :] - rho * direction_ref[block, :]
        blocks = [here]
        for i in range(others):
            entry = row * others + i
            weight = table_ref[2, entry].astype(jnp.float32)
            blocks.append(weight * later_ref[table_ref[1, entry], pl.ds(0, tile), :])
        mapped = product(high_ref[row], low_ref[row], blocks) - rho * handled_ref[block, :]
        norm = norm + column_sums(here * here * diagonal_ref[block, :])
        bend = bend + column_sums(here * mapped)
    row_ids = lax.broadcasted_iota(jnp.int32, first_sums.shape, 0)
    sums = jnp.where(row_ids == 2, jnp.sum(norm, axis=0, keepdims=True), first_sums)
    sums = jnp.where(row_ids == 3, jnp.sum(bend, axis=0, keepdims=True), sums)
    for i in range(2 * devices):
        sums_ref[i] = sums


def add_kernel(kept_ref, taken_ref, near_ref, far_ref):
    count = near_ref.shape[0]
    near_ref[...] = kept_ref[pl.ds(0, count)] + taken_ref[pl.ds(0, count)]
    far_ref[...] = kept_ref[pl.ds(count, count)] + taken_ref[pl.ds(count, count)]


def gated_add_kernel(kept_ref, taken_ref, sums_ref, near_ref, far_ref, sums_hbm, semaphores):
    store = Copies(semaphores).start(sums_ref, sums_hbm)
    add_kernel(kept_ref, taken_ref, near_ref, far_ref)
    store.wait()


def last_add_kernel(first_kept_ref, first_taken_ref, second_kept_ref, second_taken_ref, own_ref, other_ref):
    rows = own_ref.shape[1]
    for i, (kept_ref, taken_ref) in enumerate(
        ((first_kept_ref, first_taken_ref), (second_kept_ref, second_taken_ref))
    ):
        own_ref[i] = kept_ref[0, pl.ds(0, rows), :] + taken_ref[0, pl.ds(0, rows), :]
        other_ref[i] = kept_ref[0, pl.ds(rows, rows), :] + taken_ref[0, pl.ds(rows, rows), :]


def group_kernel(order, own_ref, other_ref, high_ref, low_ref):
    rows = own_ref.shape[0] // (2 * len(order))
    me = lax.axis_index("samples")
    for odd in range(2):
        for i, distance in enumerate(order):
            start = pl.multiple_of((me ^ distance ^ odd) * rows, rows)
            for j, dosage_ref in enumerate((own_ref, other_ref)):
                high, low = split(dosage_ref[pl.ds(start, rows), :])
                here = pl.ds((2 * i + j) * rows, rows)
                high_ref[odd, here, :] = high
                low_ref[odd, here, :] = low


def coefficients(sums, shared):
    norm, cross = sums[0:1, :], sums[1:2, :]
    later_norm, bend = shared[2:3, :], shared[3:4, :]
    curve = norm + cross
    ratio = later_norm / curve
    step = jnp.where(later_norm > 0, later_norm / (later_norm + bend - later_norm * ratio), 0.0)
    start = norm / curve
    return start * (1.0 + step * (ratio + cross / norm)), -start * step


def finish_kernel(devices, norm_scale, direction_hbm, scaled_hbm, own_scores_ref, other_scores_ref, sums_ref, solved_hbm,
                  scores_ref, direction_ref, scaled_ref, semaphores):
    people, columns = direction_ref.shape
    column = lax.axis_index("cols")
    copies = Copies(semaphores)
    loads = [copies.start(direction_hbm, direction_ref), copies.start(scaled_hbm, scaled_ref)]

    def total(which):
        sums = sums_ref[which]
        shared = sums
        for i in range(1, devices):
            shared = shared + sums_ref[2 * i + which]
        return sums, shared

    along, across = coefficients(*total(column))
    other_along, other_across = coefficients(*total(1 - column))
    wait_all(loads)
    stores = []
    part_rows = people // 4
    for part in range(4):
        block = pl.ds(part * part_rows, part_rows)
        direction_ref[block, :] = along * direction_ref[block, :] + across * scaled_ref[block, :]
        stores.append(copies.start(direction_ref.at[block], solved_hbm.at[block]))
    own = pl.multiple_of(column * columns, columns)
    other = pl.multiple_of((1 - column) * columns, columns)
    scores_ref[:, pl.ds(own, columns)] = norm_scale * (
        along * own_scores_ref[0] + across * own_scores_ref[1]
    )
    scores_ref[:, pl.ds(other, columns)] = norm_scale * (
        other_along * other_scores_ref[0] + other_across * other_scores_ref[1]
    )
    wait_all(stores)


def call(kernel, out_shape, in_specs, out_specs, scratch_shapes=(), limit=VMEM_LIMIT):
    return pl.pallas_call(
        kernel,
        out_shape=out_shape,
        in_specs=in_specs,
        out_specs=out_specs,
        scratch_shapes=list(scratch_shapes),
        compiler_params=pltpu.CompilerParams(vmem_limit_bytes=limit),
    )


def swap(values, axis, devices, step):
    return lax.ppermute(values, axis, [(i, i ^ step) for i in range(devices)])


def after(value, *others):
    return lax.optimization_barrier((value, *others))[0]


def per_device(kinship, relatives, variance, phenotypes, dosage):
    devices = lax.axis_size("samples")
    block_count, positions, tile = kinship.shape[:3]
    people, columns = phenotypes.shape
    variants = dosage.shape[1]
    share_rows = variants // devices
    entries = block_count * (positions - 1)
    capacity = -(-entries // (devices - 1))
    assert capacity <= 2
    hbm = pl.BlockSpec(memory_space=pltpu.HBM)
    anywhere = pl.BlockSpec(memory_space=pl.ANY)
    vmem = pl.BlockSpec(memory_space=pltpu.VMEM)
    smem = pl.BlockSpec(memory_space=pltpu.SMEM)
    float_of = lambda *shape: jax.ShapeDtypeStruct(shape, jnp.float32)
    room = lambda *shape: pltpu.VMEM(shape, jnp.float32)
    full = float_of(people, columns)
    full_room = room(people, columns)
    half = devices // 2
    near_by = list(range(1, half))
    kinship = pltpu.with_memory_space_constraint(kinship, pltpu.HBM)
    tiles_room = pltpu.VMEM((block_count, tile, positions * tile), jnp.bfloat16)
    tiles_out = pltpu.HBM((block_count, tile, positions * tile), jnp.bfloat16)
    full_out = pltpu.HBM((people, columns), jnp.float32)
    direction, direction_kept_hbm, diagonal, norm = call(
        direction_kernel,
        [full, full_out, pltpu.HBM((people, 1), jnp.float32), float_of(SUBLANES, columns)],
        [hbm] * 3,
        [vmem, hbm, hbm, vmem],
        [
            room(*kinship.shape), room(block_count, tile), full_room, room(people, 1),
            pltpu.SemaphoreType.DMA((3 * block_count + 2,)),
        ],
    )(
        kinship,
        pltpu.with_memory_space_constraint(variance.reshape(block_count, tile), pltpu.HBM),
        pltpu.with_memory_space_constraint(phenotypes, pltpu.HBM),
    )
    def to_mates(blocks):
        return [swap(block, "samples", devices, k) for k, block in zip(near_by, blocks)]

    bits = half.bit_length() - 1
    even = [sum(((i >> b) & 1) << (bits - b) for b in range(bits)) for i in range(half)]
    steps = [2 << i for i in range(bits)]
    other_dosage = with_layout_constraint(swap(after(dosage, direction), "cols", 2, 1), Layout((0, 1)))
    table, forward, high, low, *outgoing = call(
        functools.partial(route_kernel, devices, capacity),
        [
            jax.ShapeDtypeStruct((4, max(entries, devices)), jnp.int32),
            jax.ShapeDtypeStruct((capacity, half), jnp.int32),
            tiles_out, tiles_out,
        ] + [float_of(capacity, tile, columns)] * (half - 1),
        [smem, hbm, vmem, anywhere],
        [smem, smem, hbm, hbm] + [vmem] * (half - 1),
        [
            pltpu.SMEM((devices,), jnp.int32), pltpu.SMEM((devices,), jnp.int32),
            room(*kinship.shape), tiles_room, tiles_room, pltpu.SemaphoreType.DMA((3,)),
        ],
    )(relatives.T, kinship, direction, other_dosage)


    parts = jax.ShapeDtypeStruct((2, variants, people), jnp.bfloat16)
    large = VMEM_LIMIT if variants <= people else LARGE_VMEM
    grouped = call(
        functools.partial(group_kernel, even), [parts] * 2, [vmem] * 2, [vmem] * 2, limit=large
    )(after(dosage, table).T, other_dosage.T)

    products = float_of(half, 2 * share_rows, columns)

    def add_step(kept, taken):
        rows = float_of(kept.shape[0] // 2, 2 * share_rows, columns)
        return call(add_kernel, [rows] * 2, [vmem] * 2, [vmem] * 2)(kept, taken)

    partner = swap(direction, "samples", devices, half)
    near = to_mates(outgoing)
    direction_even, direction_odd = call(
        score_kernel, [products] * 2, [vmem] * 3, [vmem] * 2, limit=large
    )(*grouped, direction)
    direction_share = swap(direction_odd, "samples", devices, 1)
    far = to_mates(call(
        forward_kernel,
        [float_of(capacity, tile, columns)] * (half - 1),
        [smem, vmem] + [anywhere] * (half + 1),
        [vmem] * (half - 1),
    )(forward, partner, *near, direction_even, direction_odd))
    received = near + far + [partner.reshape(block_count, tile, columns)]
    scaled, handled, outgoing, scaled_even, scaled_odd = call(
        functools.partial(apply_kernel, devices, capacity),
        [
            full_out, full_out, pltpu.HBM((devices, tile + SUBLANES, columns), jnp.float32),
            pltpu.HBM(products.shape, jnp.float32), pltpu.HBM(products.shape, jnp.float32),
        ],
        [smem, hbm, hbm, hbm] + [vmem] * (devices + 3) + [anywhere],
        [hbm] * 5,
        [
            room(devices * capacity + block_count, tile, columns), tiles_room, tiles_room, room(people, 1), full_room,
            full_room, room(SUBLANES, columns), room(*products.shape), room(*products.shape),
            pltpu.SemaphoreType.DMA((2 * devices + 7,)),
        ],
        limit=large,
    )(table, high, low, diagonal, direction, norm, *grouped, *received, direction_share)
    later = lax.all_to_all(outgoing, "samples", split_axis=0, concat_axis=0, tiled=True)
    scaled_share = swap(scaled_odd, "samples", devices, 1)
    direction_kept, direction_given = add_step(direction_even, direction_share)
    scaled_kept, scaled_given = add_step(scaled_even, scaled_share)
    for step in steps[:-1]:
        direction_taken = swap(after(direction_given, scaled), "samples", devices, step)
        direction_kept, direction_given = add_step(direction_kept, direction_taken)
    direction_taken = swap(direction_given, "samples", devices, steps[-1])
    scaled_taken = swap(scaled_given, "samples", devices, steps[0])
    at_home = lambda *arrays: [pltpu.with_memory_space_constraint(array, pltpu.HBM) for array in arrays]
    sums = call(
        functools.partial(curvature_kernel, devices),
        float_of(2 * devices, SUBLANES, columns),
        [smem] + [hbm] * 6 + [anywhere] * 3,
        vmem,
        [
            tiles_room, tiles_room, full_room, room(people, 1), full_room, full_room,
            room(devices, tile + SUBLANES, columns), pltpu.SemaphoreType.DMA((7,)),
        ],
    )(
        table, *at_home(high, low, direction_kept_hbm, diagonal, scaled, handled), later, scaled_given, direction_given
    )
    scaled_kept, scaled_given, sums = call(
        gated_add_kernel, [float_of(scaled_kept.shape[0] // 2, 2 * share_rows, columns)] * 2
        + [pltpu.HBM(sums.shape, jnp.float32)], [vmem] * 3, [vmem, vmem, hbm], [pltpu.SemaphoreType.DMA((1,))]
    )(scaled_kept, scaled_taken, sums)
    sums, scaled_given = lax.optimization_barrier((sums, scaled_given))
    for step in steps[1:-1]:
        scaled_kept, scaled_given = add_step(scaled_kept, swap(scaled_given, "samples", devices, step))
    scaled_taken = swap(scaled_given, "samples", devices, steps[-1])
    all_sums = lax.all_to_all(sums, ("samples", "cols"), split_axis=0, concat_axis=0, tiled=True)
    rows = float_of(2, share_rows, columns)
    own_scores, other_scores = call(
        last_add_kernel, [rows] * 2, [vmem] * 4, [vmem] * 2
    )(direction_kept, direction_taken, scaled_kept, scaled_taken)
    other_scores = swap(other_scores, "cols", 2, 1)
    solved, scores = call(
        functools.partial(finish_kernel, devices, 1.0 / math.sqrt(people * devices)),
        [full, float_of(share_rows, 2 * columns)],
        [hbm, hbm, vmem, vmem, vmem],
        [hbm, vmem],
        [full_room, full_room, pltpu.SemaphoreType.DMA((6,))],
    )(*at_home(direction_kept_hbm, scaled), own_scores, other_scores, all_sums)
    return (solved, scores)


def solution(mesh):
    return jax.shard_map(
        per_device,
        mesh=mesh,
        in_specs=(
            P(("groups", "samples"), None, None, None),
            P("groups", None),
            P(("groups", "samples")),
            P(("groups", "samples"), "cols"),
            P(("groups", "samples"), "cols"),
        ),
        out_specs=(P(("groups", "samples"), "cols"), P(("groups", "cols", "samples"), None)),
        check_vma=False,
    )
```

```python
import functools
import math

import jax
import jax.numpy as jnp
from jax import lax
from jax.experimental import pallas as pl
from jax.experimental.layout import Layout, with_layout_constraint
from jax.experimental.pallas import tpu as pltpu
from jax.sharding import PartitionSpec as P

VMEM_LIMIT = 24 * 1024 * 1024
LARGE_VMEM = 56 * 1024 * 1024
SUBLANES = 8


def split(values):
    high = values.astype(jnp.bfloat16)
    low = (values - high.astype(jnp.float32)).astype(jnp.bfloat16)
    return high, low


def dot(left, right):
    return jnp.dot(left, right, preferred_element_type=jnp.float32)


def on_diagonal(size):
    rows = lax.broadcasted_iota(jnp.int32, (size, size), 0)
    return rows == lax.broadcasted_iota(jnp.int32, (size, size), 1)


def split_tiles(kinship_ref, high_ref, low_ref):
    block_count, positions, tile = kinship_ref.shape[:3]
    diagonal_mask = on_diagonal(tile)
    for row in range(block_count):
        for position in range(positions):
            values = kinship_ref[row, position]
            if position == 0:
                values = jnp.where(diagonal_mask, 0.0, values)
            high, low = split(values)
            high_ref[row, :, pl.ds(position * tile, tile)] = high
            low_ref[row, :, pl.ds(position * tile, tile)] = low


def product(high, low, blocks):
    parts = [split(block) for block in blocks]
    blocks_high = jnp.concatenate([part[0] for part in parts], axis=0)
    blocks_low = jnp.concatenate([part[1] for part in parts], axis=0)
    return dot(high, blocks_high) + (dot(low, blocks_high) + dot(high, blocks_low))


def column_sums(values):
    rows, columns = values.shape
    return jnp.sum(values.reshape(rows // SUBLANES, SUBLANES, columns), axis=0)


class Copies:
    def __init__(self, semaphores):
        self.semaphores = semaphores
        self.count = 0

    def start(self, source, target):
        copy = pltpu.make_async_copy(source, target, self.semaphores.at[self.count])
        self.count += 1
        copy.start()
        return copy


def wait_all(copies):
    for copy in copies:
        copy.wait()


def quotient(value, divisor):
    if divisor & (divisor - 1) == 0:
        return lax.shift_right_logical(value, jnp.int32(divisor.bit_length() - 1))
    return lax.div(value, jnp.int32(divisor))


def direction_kernel(kinship_hbm, variance_hbm, phenotypes_hbm, direction_ref, direction_hbm, diagonal_hbm, sums_ref,
                     kinship_ref, variance_ref, phenotypes_ref, diagonal_ref, semaphores):
    block_count, positions, tile = kinship_ref.shape[:3]
    copies = Copies(semaphores)
    loads = [copies.start(variance_hbm, variance_ref)]
    for row in range(block_count):
        block = pl.ds(row * tile, tile)
        loads.append(copies.start(kinship_hbm.at[row], kinship_ref.at[row]))
        loads.append(copies.start(phenotypes_hbm.at[block], phenotypes_ref.at[block]))
    stores = []
    norm = jnp.zeros((SUBLANES, direction_ref.shape[1]), jnp.float32)
    diagonal_mask = on_diagonal(tile)
    loads[0].wait()
    for row in range(block_count):
        wait_all(loads[1 + 2 * row:3 + 2 * row])
        block = pl.ds(row * tile, tile)
        total = jnp.where(diagonal_mask, variance_ref[row:row + 1, :], kinship_ref[row, 0])
        for position in range(1, positions):
            total = total + kinship_ref[row, position]
        diagonal = jnp.sum(total, axis=1, keepdims=True)
        diagonal_ref[block, :] = diagonal
        here = phenotypes_ref[block, :] * (1.0 / diagonal)
        direction_ref[block, :] = here
        norm = norm + column_sums(here * phenotypes_ref[block, :])
        stores.append(copies.start(direction_ref.at[block], direction_hbm.at[block]))
    stores.append(copies.start(diagonal_ref, diagonal_hbm))
    row_ids = lax.broadcasted_iota(jnp.int32, norm.shape, 0)
    sums_ref[...] = jnp.where(row_ids == 0, jnp.sum(norm, axis=0, keepdims=True), 0.0)
    wait_all(stores)


def tiles_kernel(kinship_hbm, high_hbm, low_hbm, kinship_ref, high_ref, low_ref, semaphores):
    copies = Copies(semaphores)
    copies.start(kinship_hbm, kinship_ref).wait()
    split_tiles(kinship_ref, high_ref, low_ref)
    wait_all([copies.start(high_ref, high_hbm), copies.start(low_ref, low_hbm)])


def route_kernel(devices, capacity, block_count, list_ref, direction_ref, gate_ref, table_ref, forward_ref, *refs):
    half = devices // 2
    outgoing_refs, (first_ref, last_ref) = refs[:half - 1], refs[half - 1:]
    positions = list_ref.shape[0] + 1
    tile = direction_ref.shape[0] // block_count
    me = lax.axis_index("samples")
    partner = me ^ half
    spare = me ^ 1
    top = block_count * block_count

    def collect(device):
        for j in range(devices):
            first_ref[j] = jnp.int32(top)
            last_ref[j] = jnp.int32(-1)
        found = []
        for row in range(block_count):
            for position in range(positions - 1):
                listed = list_ref[position, device * block_count + row]
                live = listed >= 0
                safe = jnp.maximum(listed, 0)
                other = quotient(safe, block_count)
                far_block = safe - other * block_count
                key = jnp.where(device < other, row * block_count + far_block, far_block * block_count + row)
                first_ref[other] = jnp.minimum(first_ref[other], jnp.where(live, key, top))
                last_ref[other] = jnp.maximum(last_ref[other], jnp.where(live, key, -1))
                found.append((live, other, far_block, key))
        return found

    def blocks_for(device, other):
        blocks = []
        for key in (first_ref[other], last_ref[other]):
            safe = jnp.clip(key, 0, top - 1)
            lower = quotient(safe, block_count)
            higher = safe - lower * block_count
            blocks.append(jnp.where(key == safe, jnp.where(device < other, lower, higher), 0))
        return blocks

    collect(partner)
    for k in range(1, half):
        blocks = blocks_for(partner, me ^ k)
        for slot in range(capacity):
            forward_ref[slot, k] = blocks[slot]
    for entry, (live, other, far_block, key) in enumerate(collect(me)):
        first, last = first_ref[other], last_ref[other]
        handled = jnp.where(me < other, first, last)
        weight = jnp.where(first == last, 1, 2)
        slot = jnp.where(key == first, 0, capacity - 1)
        place = jnp.where(other == partner, devices * capacity + far_block, other * capacity + slot)
        table_ref[0, entry] = jnp.where(live, place, spare * capacity)
        table_ref[1, entry] = jnp.where(live, other, spare)
        table_ref[2, entry] = jnp.where(live & (key == handled), weight, 0)
    for other in range(devices):
        blocks = blocks_for(me, other)
        table_ref[3, other] = jnp.where(me < other, blocks[1], blocks[0])
    near = [blocks_for(me, me ^ k) for k in range(1, half)]
    for k in range(1, half):
        for slot in range(capacity):
            start = pl.multiple_of(near[k - 1][slot] * tile, tile)
            outgoing_refs[k - 1][slot] = direction_ref[pl.ds(start, tile), :]


def forward_kernel(forward_ref, partner_ref, *refs):
    capacity, half = forward_ref.shape
    outgoing_refs = refs[1 - half:]
    tile = outgoing_refs[0].shape[1]
    for k in range(1, half):
        for slot in range(capacity):
            start = pl.multiple_of(forward_ref[slot, k] * tile, tile)
            outgoing_refs[k - 1][slot] = partner_ref[pl.ds(start, tile), :]


def gather_received(devices, capacity, received_refs, gathered_ref):
    half = devices // 2
    me = lax.axis_index("samples")
    near_refs, far_refs, partner_ref = received_refs[:half - 1], received_refs[half - 1:-1], received_refs[-1]
    gathered_ref[pl.ds(devices * capacity, partner_ref.shape[0])] = partner_ref[...]
    for i in range(half - 1):
        mate = me ^ (half - 1 - i)
        gathered_ref[pl.ds(mate * capacity, capacity)] = near_refs[i][...]
        gathered_ref[pl.ds((mate ^ half) * capacity, capacity)] = far_refs[i][...]


def score_products(high_ref, low_ref, values, even_ref, odd_ref):
    count, rows = even_ref.shape[:2]
    for odd, out_ref in enumerate((even_ref, odd_ref)):
        for i in range(0, count, 4):
            here = pl.ds(i * rows, 4 * rows)
            total = product(high_ref[odd, here, :], low_ref[odd, here, :], [values])
            out_ref[pl.ds(i, 4)] = total.reshape(4, rows, -1)


def score_kernel(high_ref, low_ref, values_ref, even_ref, odd_ref):
    score_products(high_ref, low_ref, values_ref[...], even_ref, odd_ref)


def apply_kernel(devices, capacity, table_ref, high_hbm, low_hbm, diagonal_hbm, direction_ref, norm_ref, *refs):
    received_refs = refs[:devices - 1]
    (scaled_ref, scaled_hbm, handled_hbm, outgoing_hbm, gathered_ref, high_ref, low_ref, diagonal_ref, handled_ref,
     sums_ref, semaphores) = refs[-11:]
    copies = Copies(semaphores)
    loads = [
        copies.start(high_hbm, high_ref), copies.start(low_hbm, low_ref), copies.start(diagonal_hbm, diagonal_ref)
    ]
    gather_received(devices, capacity, received_refs, gathered_ref)
    wait_all(loads)
    block_count, tile, depth = high_ref.shape
    others = depth // tile - 1
    cross = jnp.zeros(norm_ref.shape, jnp.float32)
    for row in range(block_count):
        block = pl.ds(row * tile, tile)
        here = direction_ref[block, :]
        blocks = [here] + [gathered_ref[table_ref[0, row * others + i]] for i in range(others)]
        mapped = product(high_ref[row], low_ref[row], blocks)
        scaled_ref[block, :] = mapped * (1.0 / diagonal_ref[block, :])
        cross = cross + column_sums(here * mapped)
    row_ids = lax.broadcasted_iota(jnp.int32, cross.shape, 0)
    sums_ref[...] = jnp.where(row_ids == 1, jnp.sum(cross, axis=0, keepdims=True), norm_ref[...])
    stores = []
    for other in range(devices):
        start = pl.multiple_of(table_ref[3, other] * tile, tile)
        stores.append(copies.start(scaled_ref.at[pl.ds(start, tile)], outgoing_hbm.at[other, pl.ds(0, tile)]))
        stores.append(copies.start(sums_ref, outgoing_hbm.at[other, pl.ds(tile, SUBLANES)]))
    stores.append(copies.start(scaled_ref, scaled_hbm))
    far = pl.ds(tile, depth - tile)
    for row in range(block_count):
        blocks = []
        for i in range(others):
            weight = table_ref[2, row * others + i].astype(jnp.float32)
            blocks.append(weight * gathered_ref[table_ref[0, row * others + i]])
        handled_ref[pl.ds(row * tile, tile), :] = product(high_ref[row, :, far], low_ref[row, :, far], blocks)
    stores.append(copies.start(handled_ref, handled_hbm))
    wait_all(stores)


def curvature_kernel(devices, table_ref, high_hbm, low_hbm, direction_hbm, diagonal_hbm, scaled_hbm, handled_hbm,
                     later_hbm, *refs):
    (sums_hbm, sums_ref, high_ref, low_ref, direction_ref, diagonal_ref, scaled_ref, handled_ref, later_ref,
     semaphores) = refs[-10:]
    block_count, tile, depth = high_ref.shape
    copies = Copies(semaphores)
    wait_all([copies.start(source, target) for source, target in (
        (later_hbm, later_ref), (scaled_hbm, scaled_ref), (direction_hbm, direction_ref), (high_hbm, high_ref),
        (low_hbm, low_ref), (handled_hbm, handled_ref), (diagonal_hbm, diagonal_ref),
    )])
    others = depth // tile - 1
    first_sums = later_ref[0, pl.ds(tile, SUBLANES), :]
    for other in range(1, devices):
        first_sums = first_sums + later_ref[other, pl.ds(tile, SUBLANES), :]
    rho = first_sums[1:2, :] / first_sums[0:1, :]
    norm = jnp.zeros(first_sums.shape, jnp.float32)
    bend = jnp.zeros(first_sums.shape, jnp.float32)
    for row in range(block_count):
        block = pl.ds(row * tile, tile)
        here = scaled_ref[block, :] - rho * direction_ref[block, :]
        blocks = [here]
        for i in range(others):
            entry = row * others + i
            weight = table_ref[2, entry].astype(jnp.float32)
            blocks.append(weight * later_ref[table_ref[1, entry], pl.ds(0, tile), :])
        mapped = product(high_ref[row], low_ref[row], blocks) - rho * handled_ref[block, :]
        norm = norm + column_sums(here * here * diagonal_ref[block, :])
        bend = bend + column_sums(here * mapped)
    row_ids = lax.broadcasted_iota(jnp.int32, first_sums.shape, 0)
    sums = jnp.where(row_ids == 2, jnp.sum(norm, axis=0, keepdims=True), first_sums)
    sums = jnp.where(row_ids == 3, jnp.sum(bend, axis=0, keepdims=True), sums)
    for i in range(2 * devices):
        sums_ref[i] = sums
    copies.start(sums_ref, sums_hbm).wait()


def add_kernel(kept_ref, taken_ref, *refs):
    near_ref, far_ref = refs[-2:]
    count = near_ref.shape[0]
    near_ref[...] = kept_ref[pl.ds(0, count)] + taken_ref[pl.ds(0, count)]
    far_ref[...] = kept_ref[pl.ds(count, count)] + taken_ref[pl.ds(count, count)]


def last_add_kernel(first_kept_ref, first_taken_ref, second_kept_ref, second_taken_ref, own_ref, other_ref):
    rows = own_ref.shape[1]
    for i, (kept_ref, taken_ref) in enumerate(
        ((first_kept_ref, first_taken_ref), (second_kept_ref, second_taken_ref))
    ):
        own_ref[i] = kept_ref[0, pl.ds(0, rows), :] + taken_ref[0, pl.ds(0, rows), :]
        other_ref[i] = kept_ref[0, pl.ds(rows, rows), :] + taken_ref[0, pl.ds(rows, rows), :]


def group_kernel(order, own_ref, other_ref, high_ref, low_ref):
    rows = own_ref.shape[0] // (2 * len(order))
    me = lax.axis_index("samples")
    for odd in range(2):
        for i, distance in enumerate(order):
            start = pl.multiple_of((me ^ distance ^ odd) * rows, rows)
            for j, dosage_ref in enumerate((own_ref, other_ref)):
                high, low = split(dosage_ref[pl.ds(start, rows), :])
                here = pl.ds((2 * i + j) * rows, rows)
                high_ref[odd, here, :] = high
                low_ref[odd, here, :] = low


def coefficients(sums, shared):
    norm, cross = sums[0:1, :], sums[1:2, :]
    later_norm, bend = shared[2:3, :], shared[3:4, :]
    curve = norm + cross
    ratio = later_norm / curve
    step = jnp.where(later_norm > 0, later_norm / (later_norm + bend - later_norm * ratio), 0.0)
    start = norm / curve
    return start * (1.0 + step * (ratio + cross / norm)), -start * step


def solved_kernel(devices, direction_hbm, scaled_hbm, sums_ref, solved_hbm, factors_ref, direction_ref, scaled_ref,
                  semaphores):
    people, columns = direction_ref.shape
    column = lax.axis_index("cols")
    copies = Copies(semaphores)
    loads = [copies.start(direction_hbm, direction_ref), copies.start(scaled_hbm, scaled_ref)]

    def total(which):
        sums = sums_ref[which]
        shared = sums
        for i in range(1, devices):
            shared = shared + sums_ref[2 * i + which]
        return sums, shared

    along, across = coefficients(*total(column))
    factors = jnp.concatenate([along, across, *coefficients(*total(1 - column))], axis=0)
    factors_ref[...] = jnp.concatenate([factors, factors], axis=0)
    wait_all(loads)
    stores = []
    part_rows = people // 4
    for part in range(4):
        block = pl.ds(part * part_rows, part_rows)
        direction_ref[block, :] = along * direction_ref[block, :] + across * scaled_ref[block, :]
        stores.append(copies.start(direction_ref.at[block], solved_hbm.at[block]))
    wait_all(stores)


def scores_kernel(norm_scale, factors_ref, own_ref, other_ref, scores_ref):
    columns = own_ref.shape[2]
    column = lax.axis_index("cols")
    for which, rows_ref, place in ((0, own_ref, column), (2, other_ref, 1 - column)):
        along, across = factors_ref[which:which + 1, :], factors_ref[which + 1:which + 2, :]
        here = pl.ds(pl.multiple_of(place * columns, columns), columns)
        scores_ref[:, here] = norm_scale * (along * rows_ref[0] + across * rows_ref[1])


def call(kernel, out_shape, in_specs, out_specs, scratch_shapes=(), limit=VMEM_LIMIT):
    return pl.pallas_call(
        kernel,
        out_shape=out_shape,
        in_specs=in_specs,
        out_specs=out_specs,
        scratch_shapes=list(scratch_shapes),
        compiler_params=pltpu.CompilerParams(vmem_limit_bytes=limit),
    )


def swap(values, axis, devices, step):
    return lax.ppermute(values, axis, [(i, i ^ step) for i in range(devices)])


def after(value, *others):
    return lax.optimization_barrier((value, *others))[0]


def per_device(kinship, relatives, variance, phenotypes, dosage):
    devices = lax.axis_size("samples")
    block_count, positions, tile = kinship.shape[:3]
    people, columns = phenotypes.shape
    variants = dosage.shape[1]
    share_rows = variants // devices
    entries = block_count * (positions - 1)
    capacity = -(-entries // (devices - 1))
    assert capacity <= 2
    hbm = pl.BlockSpec(memory_space=pltpu.HBM)
    anywhere = pl.BlockSpec(memory_space=pl.ANY)
    vmem = pl.BlockSpec(memory_space=pltpu.VMEM)
    smem = pl.BlockSpec(memory_space=pltpu.SMEM)
    float_of = lambda *shape: jax.ShapeDtypeStruct(shape, jnp.float32)
    room = lambda *shape: pltpu.VMEM(shape, jnp.float32)
    full = float_of(people, columns)
    full_room = room(people, columns)
    half = devices // 2
    near_by = list(range(half - 1, 0, -1))
    at_home = lambda *arrays: [pltpu.with_memory_space_constraint(array, pltpu.HBM) for array in arrays]
    kinship, = at_home(kinship)
    tiles_room = pltpu.VMEM((block_count, tile, positions * tile), jnp.bfloat16)
    tiles_out = pltpu.HBM((block_count, tile, positions * tile), jnp.bfloat16)
    full_out = pltpu.HBM((people, columns), jnp.float32)
    direction, direction_kept_hbm, diagonal, norm = call(
        direction_kernel,
        [full, full_out, pltpu.HBM((people, 1), jnp.float32), float_of(SUBLANES, columns)],
        [hbm] * 3,
        [vmem, hbm, hbm, vmem],
        [
            room(*kinship.shape), room(block_count, tile), full_room, room(people, 1),
            pltpu.SemaphoreType.DMA((3 * block_count + 2,)),
        ],
    )(
        kinship, *at_home(variance.reshape(block_count, tile), phenotypes)
    )
    def to_mates(blocks):
        return [swap(blocks[k - 1], "samples", devices, k) for k in near_by]

    bits = half.bit_length() - 1
    even = [sum(((i >> b) & 1) << (bits - b) for b in range(bits)) for i in range(half)]
    steps = [2 << i for i in range(bits)]
    other_dosage = with_layout_constraint(swap(after(dosage, direction), "cols", 2, 1), Layout((0, 1)))
    table, forward, *outgoing = call(
        functools.partial(route_kernel, devices, capacity, block_count),
        [
            jax.ShapeDtypeStruct((4, max(entries, devices)), jnp.int32),
            jax.ShapeDtypeStruct((capacity, half), jnp.int32),
        ] + [float_of(capacity, tile, columns)] * (half - 1),
        [smem, vmem, anywhere],
        [smem, smem] + [vmem] * (half - 1),
        [pltpu.SMEM((devices,), jnp.int32), pltpu.SMEM((devices,), jnp.int32)],
    )(relatives.T, direction, other_dosage)
    high, low = call(
        tiles_kernel, [tiles_out] * 2, [hbm], [hbm] * 2,
        [room(*kinship.shape), tiles_room, tiles_room, pltpu.SemaphoreType.DMA((3,))],
    )(kinship)

    parts = jax.ShapeDtypeStruct((2, variants, people), jnp.bfloat16)
    large = VMEM_LIMIT if variants <= people else LARGE_VMEM
    grouped = call(
        functools.partial(group_kernel, even), [parts] * 2, [vmem] * 2, [vmem] * 2, limit=large
    )(after(dosage, table).T, other_dosage.T)

    products = float_of(half, 2 * share_rows, columns)

    def add_step(kept, taken, *gates):
        rows = float_of(kept.shape[0] // 2, 2 * share_rows, columns)
        return call(
            add_kernel, [rows] * 2, [vmem] * 2 + [hbm] * len(gates), [vmem] * 2
        )(kept, taken, *at_home(*gates))

    partner = swap(direction, "samples", devices, half)
    near = to_mates(outgoing)
    direction_even, direction_odd = call(
        score_kernel, [products] * 2, [vmem] * 3, [vmem] * 2, limit=large
    )(*grouped, direction)
    direction_share = swap(direction_odd, "samples", devices, 1)
    far = to_mates(call(
        forward_kernel,
        [float_of(capacity, tile, columns)] * (half - 1),
        [smem, vmem] + [anywhere] * (half + 1) + [hbm] * 2,
        [vmem] * (half - 1),
    )(forward, partner, *near, direction_even, direction_odd, *at_home(high, low)))
    received = near + far + [partner.reshape(block_count, tile, columns)]
    scaled_here, scaled, handled, outgoing = call(
        functools.partial(apply_kernel, devices, capacity),
        [full, full_out, full_out, pltpu.HBM((devices, tile + SUBLANES, columns), jnp.float32)],
        [smem, hbm, hbm, hbm] + [vmem] * (devices + 1) + [anywhere],
        [vmem] + [hbm] * 3,
        [
            room(devices * capacity + block_count, tile, columns), tiles_room, tiles_room, room(people, 1),
            full_room, room(SUBLANES, columns), pltpu.SemaphoreType.DMA((2 * devices + 5,)),
        ],
        limit=large,
    )(table, *at_home(high, low, diagonal), direction, norm, *received, direction_share)
    scaled_even, scaled_odd = call(
        score_kernel, [products] * 2, [vmem] * 3, [vmem] * 2, limit=large
    )(*grouped, scaled_here)
    later = lax.all_to_all(outgoing, "samples", split_axis=0, concat_axis=0, tiled=True)
    scaled_share = swap(scaled_odd, "samples", devices, 1)
    direction_kept, direction_given = add_step(direction_even, direction_share)
    scaled_kept, scaled_given = add_step(scaled_even, scaled_share)
    for step in steps[:-1]:
        direction_taken = swap(after(direction_given, scaled), "samples", devices, step)
        direction_kept, direction_given = add_step(direction_kept, direction_taken)
    direction_taken = swap(direction_given, "samples", devices, steps[-1])
    scaled_taken = swap(scaled_given, "samples", devices, steps[0])
    sums = call(
        functools.partial(curvature_kernel, devices),
        pltpu.HBM((2 * devices, SUBLANES, columns), jnp.float32),
        [smem] + [hbm] * 6 + [anywhere] * 3,
        hbm,
        [
            room(2 * devices, SUBLANES, columns), tiles_room, tiles_room, full_room, room(people, 1), full_room,
            full_room, room(devices, tile + SUBLANES, columns), pltpu.SemaphoreType.DMA((8,)),
        ],
    )(
        table, *at_home(high, low, direction_kept_hbm, diagonal, scaled, handled), later, scaled_given, direction_given
    )
    all_sums = lax.all_to_all(sums, ("samples", "cols"), split_axis=0, concat_axis=0, tiled=True)
    for step in steps[1:]:
        scaled_kept, scaled_given = add_step(scaled_kept, scaled_taken, sums)
        scaled_taken = swap(scaled_given, "samples", devices, step)
    rows = float_of(2, share_rows, columns)
    own_scores, other_scores = call(
        last_add_kernel, [rows] * 2, [vmem] * 4, [vmem] * 2
    )(direction_kept, direction_taken, scaled_kept, scaled_taken)
    solved, factors = call(
        functools.partial(solved_kernel, devices),
        [full, float_of(SUBLANES, columns)],
        [hbm, hbm, vmem],
        [hbm, vmem],
        [full_room, full_room, pltpu.SemaphoreType.DMA((6,))],
    )(*at_home(direction_kept_hbm, scaled), all_sums)
    scores = call(
        functools.partial(scores_kernel, 1.0 / math.sqrt(people * devices)),
        float_of(share_rows, 2 * columns), [vmem] * 3, vmem,
    )(factors, own_scores, swap(other_scores, "cols", 2, 1))
    return (solved, scores)


def solution(mesh):
    return jax.shard_map(
        per_device,
        mesh=mesh,
        in_specs=(
            P(("groups", "samples"), None, None, None),
            P("groups", None),
            P(("groups", "samples")),
            P(("groups", "samples"), "cols"),
            P(("groups", "samples"), "cols"),
        ),
        out_specs=(P(("groups", "samples"), "cols"), P(("groups", "cols", "samples"), None)),
        check_vma=False,
    )
```

```python
import functools
import math

import jax
import jax.numpy as jnp
from jax import lax
from jax.experimental import pallas as pl
from jax.experimental.layout import Layout, with_layout_constraint
from jax.experimental.pallas import tpu as pltpu
from jax.sharding import PartitionSpec as P

VMEM_LIMIT = 24 * 1024 * 1024
LARGE_VMEM = 56 * 1024 * 1024
SUBLANES = 8


def split(values):
    high = values.astype(jnp.bfloat16)
    low = (values - high.astype(jnp.float32)).astype(jnp.bfloat16)
    return high, low


def dot(left, right):
    return jnp.dot(left, right, preferred_element_type=jnp.float32)


def on_diagonal(size):
    rows = lax.broadcasted_iota(jnp.int32, (size, size), 0)
    return rows == lax.broadcasted_iota(jnp.int32, (size, size), 1)


def split_tiles(kinship_ref, stacked_ref):
    block_count, positions, tile = kinship_ref.shape[:3]
    diagonal_mask = on_diagonal(tile)
    for row in range(block_count):
        for position in range(positions):
            values = kinship_ref[row, position]
            if position == 0:
                values = jnp.where(diagonal_mask, 0.0, values)
            high, low = split(values)
            here = pl.ds(position * tile, tile)
            stacked_ref[row, pl.ds(0, tile), here] = high
            stacked_ref[row, pl.ds(tile, tile), here] = low


def tile_product(stacked, blocks):
    tile = stacked.shape[0] // 2
    parts = [split(block) for block in blocks]
    blocks_high = jnp.concatenate([part[0] for part in parts], axis=0)
    blocks_low = jnp.concatenate([part[1] for part in parts], axis=0)
    both = dot(stacked, blocks_high)
    return both[:tile] + (both[tile:] + dot(stacked[:tile], blocks_low))


def product(high, low, blocks):
    parts = [split(block) for block in blocks]
    blocks_high = jnp.concatenate([part[0] for part in parts], axis=0)
    blocks_low = jnp.concatenate([part[1] for part in parts], axis=0)
    return dot(high, blocks_high) + (dot(low, blocks_high) + dot(high, blocks_low))


def column_sums(values):
    rows, columns = values.shape
    return jnp.sum(values.reshape(rows // SUBLANES, SUBLANES, columns), axis=0)


class Copies:
    def __init__(self, semaphores):
        self.semaphores = semaphores
        self.count = 0

    def start(self, source, target):
        copy = pltpu.make_async_copy(source, target, self.semaphores.at[self.count])
        self.count += 1
        copy.start()
        return copy


def wait_all(copies):
    for copy in copies:
        copy.wait()


def quotient(value, divisor):
    if divisor & (divisor - 1) == 0:
        return lax.shift_right_logical(value, jnp.int32(divisor.bit_length() - 1))
    return lax.div(value, jnp.int32(divisor))


def direction_kernel(kinship_hbm, variance_hbm, phenotypes_hbm, direction_ref, direction_hbm, diagonal_hbm, sums_ref,
                     kinship_ref, variance_ref, phenotypes_ref, diagonal_ref, semaphores):
    block_count, positions, tile = kinship_ref.shape[:3]
    copies = Copies(semaphores)
    loads = [copies.start(variance_hbm, variance_ref)]
    for row in range(block_count):
        block = pl.ds(row * tile, tile)
        loads.append(copies.start(kinship_hbm.at[row], kinship_ref.at[row]))
        loads.append(copies.start(phenotypes_hbm.at[block], phenotypes_ref.at[block]))
    stores = []
    norm = jnp.zeros((SUBLANES, direction_ref.shape[1]), jnp.float32)
    diagonal_mask = on_diagonal(tile)
    loads[0].wait()
    for row in range(block_count):
        wait_all(loads[1 + 2 * row:3 + 2 * row])
        block = pl.ds(row * tile, tile)
        total = jnp.where(diagonal_mask, variance_ref[row:row + 1, :], kinship_ref[row, 0])
        for position in range(1, positions):
            total = total + kinship_ref[row, position]
        diagonal = jnp.sum(total, axis=1, keepdims=True)
        diagonal_ref[block, :] = diagonal
        here = phenotypes_ref[block, :] * (1.0 / diagonal)
        direction_ref[block, :] = here
        norm = norm + column_sums(here * phenotypes_ref[block, :])
        stores.append(copies.start(direction_ref.at[block], direction_hbm.at[block]))
    stores.append(copies.start(diagonal_ref, diagonal_hbm))
    row_ids = lax.broadcasted_iota(jnp.int32, norm.shape, 0)
    sums_ref[...] = jnp.where(row_ids == 0, jnp.sum(norm, axis=0, keepdims=True), 0.0)
    wait_all(stores)


def tiles_kernel(kinship_hbm, stacked_hbm, kinship_ref, stacked_ref, semaphores):
    copies = Copies(semaphores)
    copies.start(kinship_hbm, kinship_ref).wait()
    split_tiles(kinship_ref, stacked_ref)
    copies.start(stacked_ref, stacked_hbm).wait()


def route_kernel(devices, capacity, block_count, list_ref, direction_ref, gate_ref, table_ref, forward_ref, *refs):
    half = devices // 2
    outgoing_refs, (first_ref, last_ref) = refs[:half - 1], refs[half - 1:]
    positions = list_ref.shape[0] + 1
    tile = direction_ref.shape[0] // block_count
    me = lax.axis_index("samples")
    partner = me ^ half
    spare = me ^ 1
    top = block_count * block_count

    def collect(device):
        for j in range(devices):
            first_ref[j] = jnp.int32(top)
            last_ref[j] = jnp.int32(-1)
        found = []
        for row in range(block_count):
            for position in range(positions - 1):
                listed = list_ref[position, device * block_count + row]
                live = listed >= 0
                safe = jnp.maximum(listed, 0)
                other = quotient(safe, block_count)
                far_block = safe - other * block_count
                key = jnp.where(device < other, row * block_count + far_block, far_block * block_count + row)
                first_ref[other] = jnp.minimum(first_ref[other], jnp.where(live, key, top))
                last_ref[other] = jnp.maximum(last_ref[other], jnp.where(live, key, -1))
                found.append((live, other, far_block, key))
        return found

    def blocks_for(device, other):
        blocks = []
        for key in (first_ref[other], last_ref[other]):
            safe = jnp.clip(key, 0, top - 1)
            lower = quotient(safe, block_count)
            higher = safe - lower * block_count
            blocks.append(jnp.where(key == safe, jnp.where(device < other, lower, higher), 0))
        return blocks

    collect(partner)
    for k in range(1, half):
        blocks = blocks_for(partner, me ^ k)
        for slot in range(capacity):
            forward_ref[slot, k] = blocks[slot]
    for entry, (live, other, far_block, key) in enumerate(collect(me)):
        first, last = first_ref[other], last_ref[other]
        handled = jnp.where(me < other, first, last)
        weight = jnp.where(first == last, 1, 2)
        slot = jnp.where(key == first, 0, capacity - 1)
        place = jnp.where(other == partner, devices * capacity + far_block, other * capacity + slot)
        table_ref[0, entry] = jnp.where(live, place, spare * capacity)
        table_ref[1, entry] = jnp.where(live, other, spare)
        table_ref[2, entry] = jnp.where(live & (key == handled), weight, 0)
    for other in range(devices):
        blocks = blocks_for(me, other)
        table_ref[3, other] = jnp.where(me < other, blocks[1], blocks[0])
    near = [blocks_for(me, me ^ k) for k in range(1, half)]
    for k in range(1, half):
        for slot in range(capacity):
            start = pl.multiple_of(near[k - 1][slot] * tile, tile)
            outgoing_refs[k - 1][slot] = direction_ref[pl.ds(start, tile), :]


def forward_kernel(forward_ref, partner_ref, *refs):
    capacity, half = forward_ref.shape
    outgoing_refs = refs[1 - half:]
    tile = outgoing_refs[0].shape[1]
    for k in range(1, half):
        for slot in range(capacity):
            start = pl.multiple_of(forward_ref[slot, k] * tile, tile)
            outgoing_refs[k - 1][slot] = partner_ref[pl.ds(start, tile), :]


def gather_received(devices, capacity, received_refs, gathered_ref):
    half = devices // 2
    me = lax.axis_index("samples")
    near_refs, far_refs, partner_ref = received_refs[:half - 1], received_refs[half - 1:-1], received_refs[-1]
    gathered_ref[pl.ds(devices * capacity, partner_ref.shape[0])] = partner_ref[...]
    for i in range(half - 1):
        mate = me ^ (half - 1 - i)
        gathered_ref[pl.ds(mate * capacity, capacity)] = near_refs[i][...]
        gathered_ref[pl.ds((mate ^ half) * capacity, capacity)] = far_refs[i][...]


def score_products(high_ref, low_ref, values, even_ref, odd_ref):
    count, rows = even_ref.shape[:2]
    for odd, out_ref in enumerate((even_ref, odd_ref)):
        for i in range(0, count, 4):
            here = pl.ds(i * rows, 4 * rows)
            total = product(high_ref[odd, here, :], low_ref[odd, here, :], [values])
            out_ref[pl.ds(i, 4)] = total.reshape(4, rows, -1)


def score_kernel(high_ref, low_ref, values_ref, even_ref, odd_ref):
    score_products(high_ref, low_ref, values_ref[...], even_ref, odd_ref)


def apply_kernel(devices, capacity, table_ref, stacked_hbm, diagonal_hbm, direction_ref, norm_ref, dosage_high_ref,
                 dosage_low_ref, *refs):
    received_refs = refs[:devices - 1]
    (scaled_hbm, handled_hbm, outgoing_hbm, even_hbm, odd_hbm, gathered_ref, stacked_ref, diagonal_ref, scaled_ref,
     handled_ref, sums_ref, even_ref, odd_ref, semaphores) = refs[-14:]
    copies = Copies(semaphores)
    loads = [copies.start(stacked_hbm, stacked_ref), copies.start(diagonal_hbm, diagonal_ref)]
    gather_received(devices, capacity, received_refs, gathered_ref)
    wait_all(loads)
    block_count, tile, depth = stacked_ref.shape[0], stacked_ref.shape[1] // 2, stacked_ref.shape[2]
    others = depth // tile - 1
    cross = jnp.zeros(norm_ref.shape, jnp.float32)
    for row in range(block_count):
        block = pl.ds(row * tile, tile)
        here = direction_ref[block, :]
        mapped = tile_product(stacked_ref[row, :, pl.ds(0, tile)], [here])
        handled = jnp.zeros_like(mapped)
        for i in range(others):
            entry = row * others + i
            there = gathered_ref[table_ref[0, entry]]
            term = tile_product(stacked_ref[row, :, pl.ds((1 + i) * tile, tile)], [there])
            mapped = mapped + term
            handled = handled + table_ref[2, entry].astype(jnp.float32) * term
        handled_ref[block, :] = handled
        scaled_ref[block, :] = mapped * (1.0 / diagonal_ref[block, :])
        cross = cross + column_sums(here * mapped)
    row_ids = lax.broadcasted_iota(jnp.int32, cross.shape, 0)
    sums_ref[...] = jnp.where(row_ids == 1, jnp.sum(cross, axis=0, keepdims=True), norm_ref[...])
    stores = []
    for other in range(devices):
        start = pl.multiple_of(table_ref[3, other] * tile, tile)
        stores.append(copies.start(scaled_ref.at[pl.ds(start, tile)], outgoing_hbm.at[other, pl.ds(0, tile)]))
        stores.append(copies.start(sums_ref, outgoing_hbm.at[other, pl.ds(tile, SUBLANES)]))
    stores += [copies.start(scaled_ref, scaled_hbm), copies.start(handled_ref, handled_hbm)]
    score_products(dosage_high_ref, dosage_low_ref, scaled_ref[...], even_ref, odd_ref)
    stores += [copies.start(odd_ref, odd_hbm), copies.start(even_ref, even_hbm)]
    wait_all(stores)


def curvature_kernel(devices, table_ref, stacked_hbm, direction_hbm, diagonal_hbm, scaled_hbm, handled_hbm, later_hbm,
                     *refs):
    (sums_hbm, sums_ref, stacked_ref, direction_ref, diagonal_ref, scaled_ref, handled_ref, later_ref,
     semaphores) = refs[-9:]
    block_count, tile, depth = stacked_ref.shape[0], stacked_ref.shape[1] // 2, stacked_ref.shape[2]
    others = depth // tile - 1
    copies = Copies(semaphores)
    arrival = copies.start(later_hbm, later_ref)
    loads = []
    for row in range(block_count):
        block = pl.ds(row * tile, tile)
        loads.append([copies.start(stacked_hbm.at[row], stacked_ref.at[row])] + [
            copies.start(source.at[block], target.at[block]) for source, target in (
                (scaled_hbm, scaled_ref), (direction_hbm, direction_ref), (handled_hbm, handled_ref),
                (diagonal_hbm, diagonal_ref),
            )
        ])
    arrival.wait()
    first_sums = later_ref[0, pl.ds(tile, SUBLANES), :]
    for other in range(1, devices):
        first_sums = first_sums + later_ref[other, pl.ds(tile, SUBLANES), :]
    rho = first_sums[1:2, :] / first_sums[0:1, :]
    norm = jnp.zeros(first_sums.shape, jnp.float32)
    bend = jnp.zeros(first_sums.shape, jnp.float32)
    for row in range(block_count):
        wait_all(loads[row])
        block = pl.ds(row * tile, tile)
        here = scaled_ref[block, :] - rho * direction_ref[block, :]
        blocks = [here]
        for i in range(others):
            entry = row * others + i
            weight = table_ref[2, entry].astype(jnp.float32)
            blocks.append(weight * later_ref[table_ref[1, entry], pl.ds(0, tile), :])
        mapped = tile_product(stacked_ref[row], blocks) - rho * handled_ref[block, :]
        norm = norm + column_sums(here * here * diagonal_ref[block, :])
        bend = bend + column_sums(here * mapped)
    row_ids = lax.broadcasted_iota(jnp.int32, first_sums.shape, 0)
    sums = jnp.where(row_ids == 2, jnp.sum(norm, axis=0, keepdims=True), first_sums)
    sums = jnp.where(row_ids == 3, jnp.sum(bend, axis=0, keepdims=True), sums)
    for i in range(2 * devices):
        sums_ref[i] = sums
    copies.start(sums_ref, sums_hbm).wait()


def add_kernel(kept_ref, taken_ref, *refs):
    near_ref, far_ref = refs[-2:]
    count = near_ref.shape[0]
    near_ref[...] = kept_ref[pl.ds(0, count)] + taken_ref[pl.ds(0, count)]
    far_ref[...] = kept_ref[pl.ds(count, count)] + taken_ref[pl.ds(count, count)]


def last_add_kernel(first_kept_ref, first_taken_ref, second_kept_ref, second_taken_ref, own_ref, other_ref):
    rows = own_ref.shape[1]
    for i, (kept_ref, taken_ref) in enumerate(
        ((first_kept_ref, first_taken_ref), (second_kept_ref, second_taken_ref))
    ):
        own_ref[i] = kept_ref[0, pl.ds(0, rows), :] + taken_ref[0, pl.ds(0, rows), :]
        other_ref[i] = kept_ref[0, pl.ds(rows, rows), :] + taken_ref[0, pl.ds(rows, rows), :]


def group_kernel(order, own_ref, other_ref, high_ref, low_ref):
    rows = own_ref.shape[0] // (2 * len(order))
    me = lax.axis_index("samples")
    for odd in range(2):
        for i, distance in enumerate(order):
            start = pl.multiple_of((me ^ distance ^ odd) * rows, rows)
            for j, dosage_ref in enumerate((own_ref, other_ref)):
                high, low = split(dosage_ref[pl.ds(start, rows), :])
                here = pl.ds((2 * i + j) * rows, rows)
                high_ref[odd, here, :] = high
                low_ref[odd, here, :] = low


def coefficients(sums, shared):
    norm, cross = sums[0:1, :], sums[1:2, :]
    later_norm, bend = shared[2:3, :], shared[3:4, :]
    curve = norm + cross
    ratio = later_norm / curve
    step = jnp.where(later_norm > 0, later_norm / (later_norm + bend - later_norm * ratio), 0.0)
    start = norm / curve
    return start * (1.0 + step * (ratio + cross / norm)), -start * step


def solved_kernel(devices, direction_hbm, scaled_hbm, sums_ref, solved_hbm, factors_ref, direction_ref, scaled_ref,
                  semaphores):
    people, columns = direction_ref.shape
    column = lax.axis_index("cols")
    copies = Copies(semaphores)
    loads = [copies.start(direction_hbm, direction_ref), copies.start(scaled_hbm, scaled_ref)]

    def total(which):
        sums = sums_ref[which]
        shared = sums
        for i in range(1, devices):
            shared = shared + sums_ref[2 * i + which]
        return sums, shared

    along, across = coefficients(*total(column))
    factors = jnp.concatenate([along, across, *coefficients(*total(1 - column))], axis=0)
    factors_ref[...] = jnp.concatenate([factors, factors], axis=0)
    wait_all(loads)
    stores = []
    part_rows = people // 4
    for part in range(4):
        block = pl.ds(part * part_rows, part_rows)
        direction_ref[block, :] = along * direction_ref[block, :] + across * scaled_ref[block, :]
        stores.append(copies.start(direction_ref.at[block], solved_hbm.at[block]))
    wait_all(stores)


def scores_kernel(norm_scale, factors_ref, own_ref, other_ref, scores_ref):
    columns = own_ref.shape[2]
    column = lax.axis_index("cols")
    for which, rows_ref, place in ((0, own_ref, column), (2, other_ref, 1 - column)):
        along, across = factors_ref[which:which + 1, :], factors_ref[which + 1:which + 2, :]
        here = pl.ds(pl.multiple_of(place * columns, columns), columns)
        scores_ref[:, here] = norm_scale * (along * rows_ref[0] + across * rows_ref[1])


def call(kernel, out_shape, in_specs, out_specs, scratch_shapes=(), limit=VMEM_LIMIT):
    return pl.pallas_call(
        kernel,
        out_shape=out_shape,
        in_specs=in_specs,
        out_specs=out_specs,
        scratch_shapes=list(scratch_shapes),
        compiler_params=pltpu.CompilerParams(vmem_limit_bytes=limit),
    )


def swap(values, axis, devices, step):
    return lax.ppermute(values, axis, [(i, i ^ step) for i in range(devices)])


def after(value, *others):
    return lax.optimization_barrier((value, *others))[0]


def per_device(kinship, relatives, variance, phenotypes, dosage):
    devices = lax.axis_size("samples")
    block_count, positions, tile = kinship.shape[:3]
    people, columns = phenotypes.shape
    variants = dosage.shape[1]
    share_rows = variants // devices
    entries = block_count * (positions - 1)
    capacity = -(-entries // (devices - 1))
    assert capacity <= 2
    hbm = pl.BlockSpec(memory_space=pltpu.HBM)
    anywhere = pl.BlockSpec(memory_space=pl.ANY)
    vmem = pl.BlockSpec(memory_space=pltpu.VMEM)
    smem = pl.BlockSpec(memory_space=pltpu.SMEM)
    float_of = lambda *shape: jax.ShapeDtypeStruct(shape, jnp.float32)
    room = lambda *shape: pltpu.VMEM(shape, jnp.float32)
    full = float_of(people, columns)
    full_room = room(people, columns)
    half = devices // 2
    near_by = list(range(half - 1, 0, -1))
    at_home = lambda *arrays: [pltpu.with_memory_space_constraint(array, pltpu.HBM) for array in arrays]
    kinship, = at_home(kinship)
    tiles_room = pltpu.VMEM((block_count, 2 * tile, positions * tile), jnp.bfloat16)
    tiles_out = pltpu.HBM((block_count, 2 * tile, positions * tile), jnp.bfloat16)
    full_out = pltpu.HBM((people, columns), jnp.float32)
    direction, direction_kept_hbm, diagonal, norm = call(
        direction_kernel,
        [full, full_out, pltpu.HBM((people, 1), jnp.float32), float_of(SUBLANES, columns)],
        [hbm] * 3,
        [vmem, hbm, hbm, vmem],
        [
            room(*kinship.shape), room(block_count, tile), full_room, room(people, 1),
            pltpu.SemaphoreType.DMA((3 * block_count + 2,)),
        ],
    )(
        kinship, *at_home(variance.reshape(block_count, tile), phenotypes)
    )
    def to_mates(blocks):
        return [swap(blocks[k - 1], "samples", devices, k) for k in near_by]

    bits = half.bit_length() - 1
    even = [sum(((i >> b) & 1) << (bits - b) for b in range(bits)) for i in range(half)]
    steps = [2 << i for i in range(bits)]
    other_dosage = with_layout_constraint(swap(after(dosage, direction), "cols", 2, 1), Layout((0, 1)))
    table, forward, *outgoing = call(
        functools.partial(route_kernel, devices, capacity, block_count),
        [
            jax.ShapeDtypeStruct((4, max(entries, devices)), jnp.int32),
            jax.ShapeDtypeStruct((capacity, half), jnp.int32),
        ] + [float_of(capacity, tile, columns)] * (half - 1),
        [smem, vmem, anywhere],
        [smem, smem] + [vmem] * (half - 1),
        [pltpu.SMEM((devices,), jnp.int32), pltpu.SMEM((devices,), jnp.int32)],
    )(relatives.T, direction, other_dosage)
    stacked = call(
        tiles_kernel, tiles_out, [hbm], hbm,
        [room(*kinship.shape), tiles_room, pltpu.SemaphoreType.DMA((2,))],
    )(kinship)

    parts = jax.ShapeDtypeStruct((2, variants, people), jnp.bfloat16)
    large = VMEM_LIMIT if variants <= people else LARGE_VMEM
    grouped = call(
        functools.partial(group_kernel, even), [parts] * 2, [vmem] * 2, [vmem] * 2, limit=large
    )(after(dosage, table).T, other_dosage.T)

    products = float_of(half, 2 * share_rows, columns)

    def add_step(kept, taken, *gates):
        rows = float_of(kept.shape[0] // 2, 2 * share_rows, columns)
        return call(
            add_kernel, [rows] * 2, [vmem] * 2 + [hbm] * len(gates), [vmem] * 2
        )(kept, taken, *gates)

    partner = swap(direction, "samples", devices, half)
    near = to_mates(outgoing)
    direction_even, direction_odd = call(
        score_kernel, [products] * 2, [vmem] * 3, [vmem] * 2, limit=large
    )(*grouped, direction)
    direction_share = swap(direction_odd, "samples", devices, 1)
    far = to_mates(call(
        forward_kernel,
        [float_of(capacity, tile, columns)] * (half - 1),
        [smem, vmem] + [anywhere] * (half + 1) + [hbm],
        [vmem] * (half - 1),
    )(forward, partner, *near, direction_even, direction_odd, *at_home(stacked)))
    received = near + far + [partner.reshape(block_count, tile, columns)]
    products_out = pltpu.HBM(products.shape, jnp.float32)
    scaled, handled, outgoing, scaled_even, scaled_odd = call(
        functools.partial(apply_kernel, devices, capacity),
        [
            full_out, full_out, pltpu.HBM((devices, tile + SUBLANES, columns), jnp.float32), products_out, products_out,
        ],
        [smem, hbm, hbm] + [vmem] * (devices + 3) + [anywhere],
        [hbm] * 5,
        [
            room(devices * capacity + block_count, tile, columns), tiles_room, room(people, 1), full_room, full_room,
            room(SUBLANES, columns), room(*products.shape), room(*products.shape),
            pltpu.SemaphoreType.DMA((2 * devices + 6,)),
        ],
        limit=large,
    )(table, *at_home(stacked, diagonal), direction, norm, *grouped, *received, direction_share)
    later = lax.all_to_all(outgoing, "samples", split_axis=0, concat_axis=0, tiled=True)
    scaled_share = swap(scaled_odd, "samples", devices, 1)
    direction_kept, direction_given = add_step(direction_even, direction_share)
    for step in steps[:-1]:
        direction_taken = swap(after(direction_given, scaled), "samples", devices, step)
        direction_kept, direction_given = add_step(direction_kept, direction_taken)
    direction_taken = swap(direction_given, "samples", devices, steps[-1])
    scaled_kept, scaled_given = add_step(scaled_even, scaled_share, direction_taken)
    scaled_taken = swap(scaled_given, "samples", devices, steps[0])
    sums = call(
        functools.partial(curvature_kernel, devices),
        pltpu.HBM((2 * devices, SUBLANES, columns), jnp.float32),
        [smem] + [hbm] * 5 + [anywhere] * 2,
        hbm,
        [
            room(2 * devices, SUBLANES, columns), tiles_room, full_room, room(people, 1), full_room, full_room,
            room(devices, tile + SUBLANES, columns), pltpu.SemaphoreType.DMA((5 * block_count + 2,)),
        ],
    )(table, *at_home(stacked, direction_kept_hbm, diagonal, scaled, handled), later, scaled_given)
    all_sums = lax.all_to_all(sums, ("samples", "cols"), split_axis=0, concat_axis=0, tiled=True)
    for step in steps[1:]:
        scaled_kept, scaled_given = add_step(scaled_kept, scaled_taken, *at_home(sums))
        scaled_taken = swap(scaled_given, "samples", devices, step)
    rows = float_of(2, share_rows, columns)
    own_scores, other_scores = call(
        last_add_kernel, [rows] * 2, [vmem] * 4, [vmem] * 2
    )(direction_kept, direction_taken, scaled_kept, scaled_taken)
    solved, factors = call(
        functools.partial(solved_kernel, devices),
        [full, float_of(SUBLANES, columns)],
        [hbm, hbm, vmem],
        [hbm, vmem],
        [full_room, full_room, pltpu.SemaphoreType.DMA((6,))],
    )(*at_home(direction_kept_hbm, scaled), all_sums)
    scores = call(
        functools.partial(scores_kernel, 1.0 / math.sqrt(people * devices)),
        float_of(share_rows, 2 * columns), [vmem] * 3, vmem,
    )(factors, own_scores, swap(other_scores, "cols", 2, 1))
    return (solved, scores)


def solution(mesh):
    return jax.shard_map(
        per_device,
        mesh=mesh,
        in_specs=(
            P(("groups", "samples"), None, None, None),
            P("groups", None),
            P(("groups", "samples")),
            P(("groups", "samples"), "cols"),
            P(("groups", "samples"), "cols"),
        ),
        out_specs=(P(("groups", "samples"), "cols"), P(("groups", "cols", "samples"), None)),
        check_vma=False,
    )
```

```python
import functools
import math

import jax
import jax.numpy as jnp
from jax import lax
from jax.experimental import pallas as pl
from jax.experimental.layout import Layout, with_layout_constraint
from jax.experimental.pallas import tpu as pltpu
from jax.sharding import PartitionSpec as P

VMEM_LIMIT = 24 * 1024 * 1024
LARGE_VMEM = 56 * 1024 * 1024
SUBLANES = 8


def split(values):
    high = values.astype(jnp.bfloat16)
    low = (values - high.astype(jnp.float32)).astype(jnp.bfloat16)
    return high, low


def dot(left, right):
    return jnp.dot(left, right, preferred_element_type=jnp.float32)


def on_diagonal(size):
    rows = lax.broadcasted_iota(jnp.int32, (size, size), 0)
    return rows == lax.broadcasted_iota(jnp.int32, (size, size), 1)


def split_tiles(kinship_ref, high_ref, low_ref):
    block_count, positions, tile = kinship_ref.shape[:3]
    diagonal_mask = on_diagonal(tile)
    for row in range(block_count):
        for position in range(positions):
            values = kinship_ref[row, position]
            if position == 0:
                values = jnp.where(diagonal_mask, 0.0, values)
            high, low = split(values)
            high_ref[row, :, pl.ds(position * tile, tile)] = high
            low_ref[row, :, pl.ds(position * tile, tile)] = low


def product(high, low, blocks):
    parts = [split(block) for block in blocks]
    blocks_high = jnp.concatenate([part[0] for part in parts], axis=0)
    blocks_low = jnp.concatenate([part[1] for part in parts], axis=0)
    return dot(high, blocks_high) + (dot(low, blocks_high) + dot(high, blocks_low))


def column_sums(values):
    rows, columns = values.shape
    return jnp.sum(values.reshape(rows // SUBLANES, SUBLANES, columns), axis=0)


class Copies:
    def __init__(self, semaphores):
        self.semaphores = semaphores
        self.count = 0

    def start(self, source, target):
        copy = pltpu.make_async_copy(source, target, self.semaphores.at[self.count])
        self.count += 1
        copy.start()
        return copy


def wait_all(copies):
    for copy in copies:
        copy.wait()


def quotient(value, divisor):
    if divisor & (divisor - 1) == 0:
        return lax.shift_right_logical(value, jnp.int32(divisor.bit_length() - 1))
    return lax.div(value, jnp.int32(divisor))


def direction_kernel(kinship_hbm, variance_hbm, phenotypes_hbm, direction_ref, direction_hbm, diagonal_hbm, sums_ref,
                     kinship_ref, variance_ref, phenotypes_ref, diagonal_ref, semaphores):
    block_count, positions, tile = kinship_ref.shape[:3]
    copies = Copies(semaphores)
    loads = [copies.start(variance_hbm, variance_ref)]
    for row in range(block_count):
        block = pl.ds(row * tile, tile)
        loads.append(copies.start(kinship_hbm.at[row], kinship_ref.at[row]))
        loads.append(copies.start(phenotypes_hbm.at[block], phenotypes_ref.at[block]))
    stores = []
    norm = jnp.zeros((SUBLANES, direction_ref.shape[1]), jnp.float32)
    diagonal_mask = on_diagonal(tile)
    loads[0].wait()
    for row in range(block_count):
        wait_all(loads[1 + 2 * row:3 + 2 * row])
        block = pl.ds(row * tile, tile)
        total = jnp.where(diagonal_mask, variance_ref[row:row + 1, :], kinship_ref[row, 0])
        for position in range(1, positions):
            total = total + kinship_ref[row, position]
        diagonal = jnp.sum(total, axis=1, keepdims=True)
        diagonal_ref[block, :] = diagonal
        here = phenotypes_ref[block, :] * (1.0 / diagonal)
        direction_ref[block, :] = here
        norm = norm + column_sums(here * phenotypes_ref[block, :])
        stores.append(copies.start(direction_ref.at[block], direction_hbm.at[block]))
    stores.append(copies.start(diagonal_ref, diagonal_hbm))
    row_ids = lax.broadcasted_iota(jnp.int32, norm.shape, 0)
    sums_ref[...] = jnp.where(row_ids == 0, jnp.sum(norm, axis=0, keepdims=True), 0.0)
    wait_all(stores)


def tiles_kernel(kinship_hbm, high_hbm, low_hbm, kinship_ref, high_ref, low_ref, semaphores):
    copies = Copies(semaphores)
    copies.start(kinship_hbm, kinship_ref).wait()
    split_tiles(kinship_ref, high_ref, low_ref)
    wait_all([copies.start(high_ref, high_hbm), copies.start(low_ref, low_hbm)])


def route_kernel(devices, capacity, block_count, list_ref, direction_ref, gate_ref, table_ref, forward_ref, *refs):
    half = devices // 2
    outgoing_refs, (first_ref, last_ref) = refs[:half - 1], refs[half - 1:]
    positions = list_ref.shape[0] + 1
    tile = direction_ref.shape[0] // block_count
    me = lax.axis_index("samples")
    partner = me ^ half
    spare = me ^ 1
    top = block_count * block_count

    def collect(device):
        for j in range(devices):
            first_ref[j] = jnp.int32(top)
            last_ref[j] = jnp.int32(-1)
        found = []
        for row in range(block_count):
            for position in range(positions - 1):
                listed = list_ref[position, device * block_count + row]
                live = listed >= 0
                safe = jnp.maximum(listed, 0)
                other = quotient(safe, block_count)
                far_block = safe - other * block_count
                key = jnp.where(device < other, row * block_count + far_block, far_block * block_count + row)
                first_ref[other] = jnp.minimum(first_ref[other], jnp.where(live, key, top))
                last_ref[other] = jnp.maximum(last_ref[other], jnp.where(live, key, -1))
                found.append((live, other, far_block, key))
        return found

    def blocks_for(device, other):
        blocks = []
        for key in (first_ref[other], last_ref[other]):
            safe = jnp.clip(key, 0, top - 1)
            lower = quotient(safe, block_count)
            higher = safe - lower * block_count
            blocks.append(jnp.where(key == safe, jnp.where(device < other, lower, higher), 0))
        return blocks

    collect(partner)
    for k in range(1, half):
        blocks = blocks_for(partner, me ^ k)
        for slot in range(capacity):
            forward_ref[slot, k] = blocks[slot]
    for entry, (live, other, far_block, key) in enumerate(collect(me)):
        first, last = first_ref[other], last_ref[other]
        handled = jnp.where(me < other, first, last)
        weight = jnp.where(first == last, 1, 2)
        slot = jnp.where(key == first, 0, capacity - 1)
        place = jnp.where(other == partner, devices * capacity + far_block, other * capacity + slot)
        table_ref[0, entry] = jnp.where(live, place, spare * capacity)
        table_ref[1, entry] = jnp.where(live, other, spare)
        table_ref[2, entry] = jnp.where(live & (key == handled), weight, 0)
    for other in range(devices):
        blocks = blocks_for(me, other)
        table_ref[3, other] = jnp.where(me < other, blocks[1], blocks[0])
    near = [blocks_for(me, me ^ k) for k in range(1, half)]
    for k in range(1, half):
        for slot in range(capacity):
            start = pl.multiple_of(near[k - 1][slot] * tile, tile)
            outgoing_refs[k - 1][slot] = direction_ref[pl.ds(start, tile), :]


def forward_kernel(forward_ref, partner_ref, *refs):
    capacity, half = forward_ref.shape
    outgoing_refs = refs[1 - half:]
    tile = outgoing_refs[0].shape[1]
    for k in range(1, half):
        for slot in range(capacity):
            start = pl.multiple_of(forward_ref[slot, k] * tile, tile)
            outgoing_refs[k - 1][slot] = partner_ref[pl.ds(start, tile), :]


def gather_received(devices, capacity, received_refs, gathered_ref):
    half = devices // 2
    me = lax.axis_index("samples")
    near_refs, far_refs, partner_ref = received_refs[:half - 1], received_refs[half - 1:-1], received_refs[-1]
    gathered_ref[pl.ds(devices * capacity, partner_ref.shape[0])] = partner_ref[...]
    for i in range(half - 1):
        mate = me ^ (half - 1 - i)
        gathered_ref[pl.ds(mate * capacity, capacity)] = near_refs[i][...]
        gathered_ref[pl.ds((mate ^ half) * capacity, capacity)] = far_refs[i][...]


def score_products(high_ref, low_ref, values, even_ref, odd_ref):
    count, rows = even_ref.shape[:2]
    for odd, out_ref in enumerate((even_ref, odd_ref)):
        for i in range(0, count, 4):
            here = pl.ds(i * rows, 4 * rows)
            total = product(high_ref[odd, here, :], low_ref[odd, here, :], [values])
            out_ref[pl.ds(i, 4)] = total.reshape(4, rows, -1)


def score_kernel(high_ref, low_ref, values_ref, even_ref, odd_ref):
    score_products(high_ref, low_ref, values_ref[...], even_ref, odd_ref)


def apply_kernel(devices, capacity, table_ref, high_hbm, low_hbm, diagonal_hbm, direction_ref, norm_ref, dosage_high_ref,
                 dosage_low_ref, *refs):
    received_refs = refs[:devices - 1]
    (scaled_hbm, handled_hbm, outgoing_hbm, products_hbm, gathered_ref, high_ref, low_ref, diagonal_ref, scaled_ref,
     handled_ref, sums_ref, even_ref, odd_ref, semaphores) = refs[-14:]
    copies = Copies(semaphores)
    loads = [
        copies.start(high_hbm, high_ref), copies.start(low_hbm, low_ref), copies.start(diagonal_hbm, diagonal_ref)
    ]
    gather_received(devices, capacity, received_refs, gathered_ref)
    wait_all(loads)
    block_count, tile, depth = high_ref.shape
    others = depth // tile - 1
    cross = jnp.zeros(norm_ref.shape, jnp.float32)
    for row in range(block_count):
        block = pl.ds(row * tile, tile)
        here = direction_ref[block, :]
        blocks = [here] + [gathered_ref[table_ref[0, row * others + i]] for i in range(others)]
        mapped = product(high_ref[row], low_ref[row], blocks)
        scaled_ref[block, :] = mapped * (1.0 / diagonal_ref[block, :])
        cross = cross + column_sums(here * mapped)
    row_ids = lax.broadcasted_iota(jnp.int32, cross.shape, 0)
    sums_ref[...] = jnp.where(row_ids == 1, jnp.sum(cross, axis=0, keepdims=True), norm_ref[...])
    stores = [copies.start(scaled_ref, scaled_hbm)]
    for other in range(devices):
        start = pl.multiple_of(table_ref[3, other] * tile, tile)
        stores.append(copies.start(scaled_ref.at[pl.ds(start, tile)], outgoing_hbm.at[other, pl.ds(0, tile)]))
        stores.append(copies.start(sums_ref, outgoing_hbm.at[other, pl.ds(tile, SUBLANES)]))
    score_products(dosage_high_ref, dosage_low_ref, scaled_ref[...], even_ref, odd_ref)
    own_bit = lax.axis_index("samples") & 1
    stores += [copies.start(odd_ref, products_hbm.at[1 - own_bit]), copies.start(even_ref, products_hbm.at[own_bit])]
    far = pl.ds(tile, depth - tile)
    for row in range(block_count):
        blocks = []
        for i in range(others):
            weight = table_ref[2, row * others + i].astype(jnp.float32)
            blocks.append(weight * gathered_ref[table_ref[0, row * others + i]])
        handled_ref[pl.ds(row * tile, tile), :] = product(high_ref[row, :, far], low_ref[row, :, far], blocks)
    stores.append(copies.start(handled_ref, handled_hbm))
    wait_all(stores)


def curvature_kernel(devices, table_ref, high_hbm, low_hbm, direction_hbm, diagonal_hbm, scaled_hbm, handled_hbm,
                     later_hbm, *refs):
    (sums_hbm, sums_ref, high_ref, low_ref, direction_ref, diagonal_ref, scaled_ref, handled_ref, later_ref,
     semaphores) = refs[-10:]
    block_count, tile, depth = high_ref.shape
    copies = Copies(semaphores)
    wait_all([copies.start(source, target) for source, target in (
        (later_hbm, later_ref), (scaled_hbm, scaled_ref), (direction_hbm, direction_ref), (high_hbm, high_ref),
        (low_hbm, low_ref), (handled_hbm, handled_ref), (diagonal_hbm, diagonal_ref),
    )])
    others = depth // tile - 1
    first_sums = later_ref[0, pl.ds(tile, SUBLANES), :]
    for other in range(1, devices):
        first_sums = first_sums + later_ref[other, pl.ds(tile, SUBLANES), :]
    rho = first_sums[1:2, :] / first_sums[0:1, :]
    norm = jnp.zeros(first_sums.shape, jnp.float32)
    bend = jnp.zeros(first_sums.shape, jnp.float32)
    for row in range(block_count):
        block = pl.ds(row * tile, tile)
        here = scaled_ref[block, :] - rho * direction_ref[block, :]
        blocks = [here]
        for i in range(others):
            entry = row * others + i
            weight = table_ref[2, entry].astype(jnp.float32)
            blocks.append(weight * later_ref[table_ref[1, entry], pl.ds(0, tile), :])
        mapped = product(high_ref[row], low_ref[row], blocks) - rho * handled_ref[block, :]
        norm = norm + column_sums(here * here * diagonal_ref[block, :])
        bend = bend + column_sums(here * mapped)
    row_ids = lax.broadcasted_iota(jnp.int32, first_sums.shape, 0)
    sums = jnp.where(row_ids == 2, jnp.sum(norm, axis=0, keepdims=True), first_sums)
    sums = jnp.where(row_ids == 3, jnp.sum(bend, axis=0, keepdims=True), sums)
    for i in range(2 * devices):
        sums_ref[i] = sums
    copies.start(sums_ref, sums_hbm).wait()


def add_kernel(kept_ref, taken_ref, *refs):
    near_ref, far_ref = refs[-2:]
    count = near_ref.shape[0]
    near_ref[...] = kept_ref[pl.ds(0, count)] + taken_ref[pl.ds(0, count)]
    far_ref[...] = kept_ref[pl.ds(count, count)] + taken_ref[pl.ds(count, count)]


def pair_kernel(products_ref, near_ref, far_ref):
    count = near_ref.shape[0]
    near_ref[...] = products_ref[0, pl.ds(0, count)] + products_ref[1, pl.ds(0, count)]
    far_ref[...] = products_ref[0, pl.ds(count, count)] + products_ref[1, pl.ds(count, count)]


def last_add_kernel(first_kept_ref, first_taken_ref, second_kept_ref, second_taken_ref, own_ref, other_ref):
    rows = own_ref.shape[1]
    for i, (kept_ref, taken_ref) in enumerate(
        ((first_kept_ref, first_taken_ref), (second_kept_ref, second_taken_ref))
    ):
        own_ref[i] = kept_ref[0, pl.ds(0, rows), :] + taken_ref[0, pl.ds(0, rows), :]
        other_ref[i] = kept_ref[0, pl.ds(rows, rows), :] + taken_ref[0, pl.ds(rows, rows), :]


def group_kernel(order, own_ref, other_ref, high_ref, low_ref):
    rows = own_ref.shape[0] // (2 * len(order))
    me = lax.axis_index("samples")
    for odd in range(2):
        for i, distance in enumerate(order):
            start = pl.multiple_of((me ^ distance ^ odd) * rows, rows)
            for j, dosage_ref in enumerate((own_ref, other_ref)):
                high, low = split(dosage_ref[pl.ds(start, rows), :])
                here = pl.ds((2 * i + j) * rows, rows)
                high_ref[odd, here, :] = high
                low_ref[odd, here, :] = low


def coefficients(sums, shared):
    norm, cross = sums[0:1, :], sums[1:2, :]
    later_norm, bend = shared[2:3, :], shared[3:4, :]
    curve = norm + cross
    ratio = later_norm / curve
    step = jnp.where(later_norm > 0, later_norm / (later_norm + bend - later_norm * ratio), 0.0)
    start = norm / curve
    return start * (1.0 + step * (ratio + cross / norm)), -start * step


def solved_kernel(devices, direction_hbm, scaled_hbm, sums_ref, solved_hbm, factors_ref, direction_ref, scaled_ref,
                  semaphores):
    people, columns = direction_ref.shape
    column = lax.axis_index("cols")
    copies = Copies(semaphores)
    loads = [copies.start(direction_hbm, direction_ref), copies.start(scaled_hbm, scaled_ref)]

    def total(which):
        sums = sums_ref[which]
        shared = sums
        for i in range(1, devices):
            shared = shared + sums_ref[2 * i + which]
        return sums, shared

    along, across = coefficients(*total(column))
    factors = jnp.concatenate([along, across, *coefficients(*total(1 - column))], axis=0)
    factors_ref[...] = jnp.concatenate([factors, factors], axis=0)
    wait_all(loads)
    stores = []
    part_rows = people // 4
    for part in range(4):
        block = pl.ds(part * part_rows, part_rows)
        direction_ref[block, :] = along * direction_ref[block, :] + across * scaled_ref[block, :]
        stores.append(copies.start(direction_ref.at[block], solved_hbm.at[block]))
    wait_all(stores)


def scores_kernel(norm_scale, factors_ref, own_ref, other_ref, scores_ref):
    columns = own_ref.shape[2]
    column = lax.axis_index("cols")
    for which, rows_ref, place in ((0, own_ref, column), (2, other_ref, 1 - column)):
        along, across = factors_ref[which:which + 1, :], factors_ref[which + 1:which + 2, :]
        here = pl.ds(pl.multiple_of(place * columns, columns), columns)
        scores_ref[:, here] = norm_scale * (along * rows_ref[0] + across * rows_ref[1])


def call(kernel, out_shape, in_specs, out_specs, scratch_shapes=(), limit=VMEM_LIMIT):
    return pl.pallas_call(
        kernel,
        out_shape=out_shape,
        in_specs=in_specs,
        out_specs=out_specs,
        scratch_shapes=list(scratch_shapes),
        compiler_params=pltpu.CompilerParams(vmem_limit_bytes=limit),
    )


def swap(values, axis, devices, step):
    return lax.ppermute(values, axis, [(i, i ^ step) for i in range(devices)])


def after(value, *others):
    return lax.optimization_barrier((value, *others))[0]


def per_device(kinship, relatives, variance, phenotypes, dosage):
    devices = lax.axis_size("samples")
    block_count, positions, tile = kinship.shape[:3]
    people, columns = phenotypes.shape
    variants = dosage.shape[1]
    share_rows = variants // devices
    entries = block_count * (positions - 1)
    capacity = -(-entries // (devices - 1))
    assert capacity <= 2
    hbm = pl.BlockSpec(memory_space=pltpu.HBM)
    anywhere = pl.BlockSpec(memory_space=pl.ANY)
    vmem = pl.BlockSpec(memory_space=pltpu.VMEM)
    smem = pl.BlockSpec(memory_space=pltpu.SMEM)
    float_of = lambda *shape: jax.ShapeDtypeStruct(shape, jnp.float32)
    room = lambda *shape: pltpu.VMEM(shape, jnp.float32)
    full = float_of(people, columns)
    full_room = room(people, columns)
    half = devices // 2
    near_by = list(range(half - 1, 0, -1))
    at_home = lambda *arrays: [pltpu.with_memory_space_constraint(array, pltpu.HBM) for array in arrays]
    kinship, = at_home(kinship)
    tiles_room = pltpu.VMEM((block_count, tile, positions * tile), jnp.bfloat16)
    tiles_out = pltpu.HBM((block_count, tile, positions * tile), jnp.bfloat16)
    full_out = pltpu.HBM((people, columns), jnp.float32)
    direction, direction_kept_hbm, diagonal, norm = call(
        direction_kernel,
        [full, full_out, pltpu.HBM((people, 1), jnp.float32), float_of(SUBLANES, columns)],
        [hbm] * 3,
        [vmem, hbm, hbm, vmem],
        [
            room(*kinship.shape), room(block_count, tile), full_room, room(people, 1),
            pltpu.SemaphoreType.DMA((3 * block_count + 2,)),
        ],
    )(
        kinship, *at_home(variance.reshape(block_count, tile), phenotypes)
    )
    def to_mates(blocks):
        return [swap(blocks[k - 1], "samples", devices, k) for k in near_by]

    bits = half.bit_length() - 1
    even = [sum(((i >> b) & 1) << (bits - b) for b in range(bits)) for i in range(half)]
    steps = [2 << i for i in range(bits)]
    other_dosage = with_layout_constraint(swap(after(dosage, direction), "cols", 2, 1), Layout((0, 1)))
    table, forward, *outgoing = call(
        functools.partial(route_kernel, devices, capacity, block_count),
        [
            jax.ShapeDtypeStruct((4, max(entries, devices)), jnp.int32),
            jax.ShapeDtypeStruct((capacity, half), jnp.int32),
        ] + [float_of(capacity, tile, columns)] * (half - 1),
        [smem, vmem, anywhere],
        [smem, smem] + [vmem] * (half - 1),
        [pltpu.SMEM((devices,), jnp.int32), pltpu.SMEM((devices,), jnp.int32)],
    )(relatives.T, direction, other_dosage)
    high, low = call(
        tiles_kernel, [tiles_out] * 2, [hbm], [hbm] * 2,
        [room(*kinship.shape), tiles_room, tiles_room, pltpu.SemaphoreType.DMA((3,))],
    )(kinship)

    parts = jax.ShapeDtypeStruct((2, variants, people), jnp.bfloat16)
    large = VMEM_LIMIT if variants <= people else LARGE_VMEM
    grouped = call(
        functools.partial(group_kernel, even), [parts] * 2, [vmem] * 2, [vmem] * 2, limit=large
    )(after(dosage, table).T, other_dosage.T)

    products = float_of(half, 2 * share_rows, columns)

    def add_step(kept, taken, *gates):
        rows = float_of(kept.shape[0] // 2, 2 * share_rows, columns)
        return call(
            add_kernel, [rows] * 2, [vmem] * 2 + [hbm] * len(gates), [vmem] * 2
        )(kept, taken, *at_home(*gates))

    partner = swap(direction, "samples", devices, half)
    near = to_mates(outgoing)
    direction_even, direction_odd = call(
        score_kernel, [products] * 2, [vmem] * 3, [vmem] * 2, limit=large
    )(*grouped, direction)
    direction_share = swap(direction_odd, "samples", devices, 1)
    far = to_mates(call(
        forward_kernel,
        [float_of(capacity, tile, columns)] * (half - 1),
        [smem, vmem] + [anywhere] * (half + 1) + [hbm] * 2,
        [vmem] * (half - 1),
    )(forward, partner, *near, direction_even, direction_odd, *at_home(high, low)))
    received = near + far + [partner.reshape(block_count, tile, columns)]
    scaled, handled, outgoing, scaled_products = call(
        functools.partial(apply_kernel, devices, capacity),
        [
            full_out, full_out, pltpu.HBM((devices, tile + SUBLANES, columns), jnp.float32),
            pltpu.HBM((2, *products.shape), jnp.float32),
        ],
        [smem, hbm, hbm, hbm] + [vmem] * (devices + 3) + [anywhere],
        [hbm] * 4,
        [
            room(devices * capacity + block_count, tile, columns), tiles_room, tiles_room, room(people, 1), full_room,
            full_room, room(SUBLANES, columns), room(*products.shape), room(*products.shape),
            pltpu.SemaphoreType.DMA((2 * devices + 7,)),
        ],
        limit=large,
    )(table, *at_home(high, low, diagonal), direction, norm, *grouped, *received, direction_share)
    scaled_products = lax.all_to_all(
        scaled_products, "samples", split_axis=0, concat_axis=0, tiled=True,
        axis_index_groups=[[i, i + 1] for i in range(0, devices, 2)],
    )
    later = lax.all_to_all(outgoing, "samples", split_axis=0, concat_axis=0, tiled=True)
    direction_kept, direction_given = add_step(direction_even, direction_share)
    scaled_kept, scaled_given = call(
        pair_kernel, [float_of(half // 2, 2 * share_rows, columns)] * 2, [vmem], [vmem] * 2
    )(scaled_products)
    for step in steps[:-1]:
        direction_taken = swap(after(direction_given, scaled), "samples", devices, step)
        direction_kept, direction_given = add_step(direction_kept, direction_taken)
    direction_taken = swap(direction_given, "samples", devices, steps[-1])
    scaled_taken = swap(scaled_given, "samples", devices, steps[0])
    sums = call(
        functools.partial(curvature_kernel, devices),
        pltpu.HBM((2 * devices, SUBLANES, columns), jnp.float32),
        [smem] + [hbm] * 6 + [anywhere] * 3,
        hbm,
        [
            room(2 * devices, SUBLANES, columns), tiles_room, tiles_room, full_room, room(people, 1), full_room,
            full_room, room(devices, tile + SUBLANES, columns), pltpu.SemaphoreType.DMA((8,)),
        ],
    )(
        table, *at_home(high, low, direction_kept_hbm, diagonal, scaled, handled), later, scaled_given, direction_given
    )
    all_sums = lax.all_to_all(sums, ("samples", "cols"), split_axis=0, concat_axis=0, tiled=True)
    for step in steps[1:]:
        scaled_kept, scaled_given = add_step(scaled_kept, scaled_taken, sums)
        scaled_taken = swap(scaled_given, "samples", devices, step)
    rows = float_of(2, share_rows, columns)
    own_scores, other_scores = call(
        last_add_kernel, [rows] * 2, [vmem] * 4, [vmem] * 2
    )(direction_kept, direction_taken, scaled_kept, scaled_taken)
    solved, factors = call(
        functools.partial(solved_kernel, devices),
        [full, float_of(SUBLANES, columns)],
        [hbm, hbm, vmem],
        [hbm, vmem],
        [full_room, full_room, pltpu.SemaphoreType.DMA((6,))],
    )(*at_home(direction_kept_hbm, scaled), all_sums)
    scores = call(
        functools.partial(scores_kernel, 1.0 / math.sqrt(people * devices)),
        float_of(share_rows, 2 * columns), [vmem] * 3, vmem,
    )(factors, own_scores, swap(other_scores, "cols", 2, 1))
    return (solved, scores)


def solution(mesh):
    return jax.shard_map(
        per_device,
        mesh=mesh,
        in_specs=(
            P(("groups", "samples"), None, None, None),
            P("groups", None),
            P(("groups", "samples")),
            P(("groups", "samples"), "cols"),
            P(("groups", "samples"), "cols"),
        ),
        out_specs=(P(("groups", "samples"), "cols"), P(("groups", "cols", "samples"), None)),
        check_vma=False,
    )
```

```python
import functools
import math

import jax
import jax.numpy as jnp
from jax import lax
from jax.experimental import pallas as pl
from jax.experimental.layout import Layout, with_layout_constraint
from jax.experimental.pallas import tpu as pltpu
from jax.sharding import PartitionSpec as P

VMEM_LIMIT = 24 * 1024 * 1024
LARGE_VMEM = 56 * 1024 * 1024
SUBLANES = 8


def split(values):
    high = values.astype(jnp.bfloat16)
    low = (values - high.astype(jnp.float32)).astype(jnp.bfloat16)
    return high, low


def dot(left, right):
    return jnp.dot(left, right, preferred_element_type=jnp.float32)


def on_diagonal(size):
    rows = lax.broadcasted_iota(jnp.int32, (size, size), 0)
    return rows == lax.broadcasted_iota(jnp.int32, (size, size), 1)


def split_tiles(kinship_ref, high_ref, low_ref):
    block_count, positions, tile = kinship_ref.shape[:3]
    diagonal_mask = on_diagonal(tile)
    for row in range(block_count):
        for position in range(positions):
            values = kinship_ref[row, position]
            if position == 0:
                values = jnp.where(diagonal_mask, 0.0, values)
            high, low = split(values)
            high_ref[row, :, pl.ds(position * tile, tile)] = high
            low_ref[row, :, pl.ds(position * tile, tile)] = low


def product(high, low, blocks):
    parts = [split(block) for block in blocks]
    blocks_high = jnp.concatenate([part[0] for part in parts], axis=0)
    blocks_low = jnp.concatenate([part[1] for part in parts], axis=0)
    return dot(high, blocks_high) + (dot(low, blocks_high) + dot(high, blocks_low))


def column_sums(values):
    rows, columns = values.shape
    return jnp.sum(values.reshape(rows // SUBLANES, SUBLANES, columns), axis=0)


class Copies:
    def __init__(self, semaphores):
        self.semaphores = semaphores
        self.count = 0

    def start(self, source, target):
        copy = pltpu.make_async_copy(source, target, self.semaphores.at[self.count])
        self.count += 1
        copy.start()
        return copy


def wait_all(copies):
    for copy in copies:
        copy.wait()


def quotient(value, divisor):
    if divisor & (divisor - 1) == 0:
        return lax.shift_right_logical(value, jnp.int32(divisor.bit_length() - 1))
    return lax.div(value, jnp.int32(divisor))


def direction_kernel(kinship_hbm, variance_hbm, phenotypes_hbm, direction_ref, direction_hbm, diagonal_hbm, sums_ref,
                     kinship_ref, variance_ref, phenotypes_ref, diagonal_ref, semaphores):
    block_count, positions, tile = kinship_ref.shape[:3]
    copies = Copies(semaphores)
    loads = [copies.start(variance_hbm, variance_ref)]
    for row in range(block_count):
        block = pl.ds(row * tile, tile)
        loads.append(copies.start(kinship_hbm.at[row], kinship_ref.at[row]))
        loads.append(copies.start(phenotypes_hbm.at[block], phenotypes_ref.at[block]))
    stores = []
    norm = jnp.zeros((SUBLANES, direction_ref.shape[1]), jnp.float32)
    diagonal_mask = on_diagonal(tile)
    loads[0].wait()
    for row in range(block_count):
        wait_all(loads[1 + 2 * row:3 + 2 * row])
        block = pl.ds(row * tile, tile)
        total = jnp.where(diagonal_mask, variance_ref[row:row + 1, :], kinship_ref[row, 0])
        for position in range(1, positions):
            total = total + kinship_ref[row, position]
        diagonal = jnp.sum(total, axis=1, keepdims=True)
        diagonal_ref[block, :] = diagonal
        here = phenotypes_ref[block, :] * (1.0 / diagonal)
        direction_ref[block, :] = here
        norm = norm + column_sums(here * phenotypes_ref[block, :])
        stores.append(copies.start(direction_ref.at[block], direction_hbm.at[block]))
    stores.append(copies.start(diagonal_ref, diagonal_hbm))
    row_ids = lax.broadcasted_iota(jnp.int32, norm.shape, 0)
    sums_ref[...] = jnp.where(row_ids == 0, jnp.sum(norm, axis=0, keepdims=True), 0.0)
    wait_all(stores)


def tiles_kernel(kinship_hbm, high_hbm, low_hbm, kinship_ref, high_ref, low_ref, semaphores):
    copies = Copies(semaphores)
    copies.start(kinship_hbm, kinship_ref).wait()
    split_tiles(kinship_ref, high_ref, low_ref)
    wait_all([copies.start(high_ref, high_hbm), copies.start(low_ref, low_hbm)])


def route_kernel(devices, capacity, block_count, list_ref, direction_ref, gate_ref, table_ref, forward_ref, *refs):
    half = devices // 2
    outgoing_refs, (first_ref, last_ref) = refs[:half - 1], refs[half - 1:]
    positions = list_ref.shape[0] + 1
    tile = direction_ref.shape[0] // block_count
    me = lax.axis_index("samples")
    partner = me ^ half
    spare = me ^ 1
    top = block_count * block_count

    def collect(device):
        for j in range(devices):
            first_ref[j] = jnp.int32(top)
            last_ref[j] = jnp.int32(-1)
        found = []
        for row in range(block_count):
            for position in range(positions - 1):
                listed = list_ref[position, device * block_count + row]
                live = listed >= 0
                safe = jnp.maximum(listed, 0)
                other = quotient(safe, block_count)
                far_block = safe - other * block_count
                key = jnp.where(device < other, row * block_count + far_block, far_block * block_count + row)
                first_ref[other] = jnp.minimum(first_ref[other], jnp.where(live, key, top))
                last_ref[other] = jnp.maximum(last_ref[other], jnp.where(live, key, -1))
                found.append((live, other, far_block, key))
        return found

    def blocks_for(device, other):
        blocks = []
        for key in (first_ref[other], last_ref[other]):
            safe = jnp.clip(key, 0, top - 1)
            lower = quotient(safe, block_count)
            higher = safe - lower * block_count
            blocks.append(jnp.where(key == safe, jnp.where(device < other, lower, higher), 0))
        return blocks

    collect(partner)
    for k in range(1, half):
        blocks = blocks_for(partner, me ^ k)
        for slot in range(capacity):
            forward_ref[slot, k] = blocks[slot]
    for entry, (live, other, far_block, key) in enumerate(collect(me)):
        first, last = first_ref[other], last_ref[other]
        handled = jnp.where(me < other, first, last)
        weight = jnp.where(first == last, 1, 2)
        slot = jnp.where(key == first, 0, capacity - 1)
        place = jnp.where(other == partner, devices * capacity + far_block, other * capacity + slot)
        table_ref[0, entry] = jnp.where(live, place, spare * capacity)
        table_ref[1, entry] = jnp.where(live, other, spare)
        table_ref[2, entry] = jnp.where(live & (key == handled), weight, 0)
    for other in range(devices):
        blocks = blocks_for(me, other)
        table_ref[3, other] = jnp.where(me < other, blocks[1], blocks[0])
    near = [blocks_for(me, me ^ k) for k in range(1, half)]
    for k in range(1, half):
        for slot in range(capacity):
            start = pl.multiple_of(near[k - 1][slot] * tile, tile)
            outgoing_refs[k - 1][slot] = direction_ref[pl.ds(start, tile), :]


def forward_kernel(forward_ref, partner_ref, *refs):
    capacity, half = forward_ref.shape
    outgoing_refs = refs[1 - half:]
    tile = outgoing_refs[0].shape[1]
    for k in range(1, half):
        for slot in range(capacity):
            start = pl.multiple_of(forward_ref[slot, k] * tile, tile)
            outgoing_refs[k - 1][slot] = partner_ref[pl.ds(start, tile), :]


def gather_received(devices, capacity, received_refs, gathered_ref):
    half = devices // 2
    me = lax.axis_index("samples")
    near_refs, far_refs, partner_ref = received_refs[:half - 1], received_refs[half - 1:-1], received_refs[-1]
    gathered_ref[pl.ds(devices * capacity, partner_ref.shape[0])] = partner_ref[...]
    for i in range(half - 1):
        mate = me ^ (half - 1 - i)
        gathered_ref[pl.ds(mate * capacity, capacity)] = near_refs[i][...]
        gathered_ref[pl.ds((mate ^ half) * capacity, capacity)] = far_refs[i][...]


def score_products(high_ref, low_ref, values, even_ref, odd_ref):
    count, rows = even_ref.shape[:2]
    for odd, out_ref in enumerate((even_ref, odd_ref)):
        for i in range(0, count, 4):
            here = pl.ds(i * rows, 4 * rows)
            total = product(high_ref[odd, here, :], low_ref[odd, here, :], [values])
            out_ref[pl.ds(i, 4)] = total.reshape(4, rows, -1)


def score_kernel(high_ref, low_ref, values_ref, even_ref, odd_ref):
    score_products(high_ref, low_ref, values_ref[...], even_ref, odd_ref)


def apply_kernel(devices, capacity, table_ref, high_hbm, low_hbm, diagonal_hbm, direction_ref, norm_ref, dosage_high_ref,
                 dosage_low_ref, *refs):
    received_refs = refs[:devices - 1]
    (scaled_hbm, handled_hbm, outgoing_hbm, even_hbm, odd_hbm, gathered_ref, high_ref, low_ref, diagonal_ref, scaled_ref,
     handled_ref, sums_ref, even_ref, odd_ref, semaphores) = refs[-15:]
    copies = Copies(semaphores)
    loads = [
        copies.start(high_hbm, high_ref), copies.start(low_hbm, low_ref), copies.start(diagonal_hbm, diagonal_ref)
    ]
    gather_received(devices, capacity, received_refs, gathered_ref)
    wait_all(loads)
    block_count, tile, depth = high_ref.shape
    others = depth // tile - 1
    cross = jnp.zeros(norm_ref.shape, jnp.float32)
    for row in range(block_count):
        block = pl.ds(row * tile, tile)
        here = direction_ref[block, :]
        blocks = [here] + [gathered_ref[table_ref[0, row * others + i]] for i in range(others)]
        mapped = product(high_ref[row], low_ref[row], blocks)
        scaled_ref[block, :] = mapped * (1.0 / diagonal_ref[block, :])
        cross = cross + column_sums(here * mapped)
    row_ids = lax.broadcasted_iota(jnp.int32, cross.shape, 0)
    sums_ref[...] = jnp.where(row_ids == 1, jnp.sum(cross, axis=0, keepdims=True), norm_ref[...])
    stores = [copies.start(scaled_ref, scaled_hbm)]
    for other in range(devices):
        start = pl.multiple_of(table_ref[3, other] * tile, tile)
        stores.append(copies.start(scaled_ref.at[pl.ds(start, tile)], outgoing_hbm.at[other, pl.ds(0, tile)]))
        stores.append(copies.start(sums_ref, outgoing_hbm.at[other, pl.ds(tile, SUBLANES)]))
    score_products(dosage_high_ref, dosage_low_ref, scaled_ref[...], even_ref, odd_ref)
    stores += [copies.start(odd_ref, odd_hbm), copies.start(even_ref, even_hbm)]
    far = pl.ds(tile, depth - tile)
    for row in range(block_count):
        blocks = []
        for i in range(others):
            weight = table_ref[2, row * others + i].astype(jnp.float32)
            blocks.append(weight * gathered_ref[table_ref[0, row * others + i]])
        handled_ref[pl.ds(row * tile, tile), :] = product(high_ref[row, :, far], low_ref[row, :, far], blocks)
    stores.append(copies.start(handled_ref, handled_hbm))
    wait_all(stores)


def curvature_kernel(devices, table_ref, high_hbm, low_hbm, direction_hbm, diagonal_hbm, scaled_hbm, handled_hbm,
                     later_hbm, *refs):
    (sums_hbm, sums_ref, high_ref, low_ref, direction_ref, diagonal_ref, scaled_ref, handled_ref, later_ref,
     semaphores) = refs[-10:]
    block_count, tile, depth = high_ref.shape
    copies = Copies(semaphores)
    wait_all([copies.start(source, target) for source, target in (
        (later_hbm, later_ref), (scaled_hbm, scaled_ref), (direction_hbm, direction_ref), (high_hbm, high_ref),
        (low_hbm, low_ref), (handled_hbm, handled_ref), (diagonal_hbm, diagonal_ref),
    )])
    others = depth // tile - 1
    first_sums = later_ref[0, pl.ds(tile, SUBLANES), :]
    for other in range(1, devices):
        first_sums = first_sums + later_ref[other, pl.ds(tile, SUBLANES), :]
    rho = first_sums[1:2, :] / first_sums[0:1, :]
    norm = jnp.zeros(first_sums.shape, jnp.float32)
    bend = jnp.zeros(first_sums.shape, jnp.float32)
    for row in range(block_count):
        block = pl.ds(row * tile, tile)
        here = scaled_ref[block, :] - rho * direction_ref[block, :]
        blocks = [here]
        for i in range(others):
            entry = row * others + i
            weight = table_ref[2, entry].astype(jnp.float32)
            blocks.append(weight * later_ref[table_ref[1, entry], pl.ds(0, tile), :])
        mapped = product(high_ref[row], low_ref[row], blocks) - rho * handled_ref[block, :]
        norm = norm + column_sums(here * here * diagonal_ref[block, :])
        bend = bend + column_sums(here * mapped)
    row_ids = lax.broadcasted_iota(jnp.int32, first_sums.shape, 0)
    sums = jnp.where(row_ids == 2, jnp.sum(norm, axis=0, keepdims=True), first_sums)
    sums = jnp.where(row_ids == 3, jnp.sum(bend, axis=0, keepdims=True), sums)
    for i in range(2 * devices):
        sums_ref[i] = sums
    copies.start(sums_ref, sums_hbm).wait()


def add_kernel(kept_ref, taken_ref, near_ref, far_ref):
    count = near_ref.shape[0]
    near_ref[...] = kept_ref[pl.ds(0, count)] + taken_ref[pl.ds(0, count)]
    far_ref[...] = kept_ref[pl.ds(count, count)] + taken_ref[pl.ds(count, count)]


def merge_kernel(first_kept_ref, first_taken_ref, second_kept_ref, second_taken_ref, gate_ref, near_ref, far_ref):
    count = first_kept_ref.shape[0] // 2
    for start, out_ref in ((0, near_ref), (count, far_ref)):
        here = pl.ds(start, count)
        out_ref[pl.ds(0, count)] = first_kept_ref[here] + first_taken_ref[here]
        out_ref[pl.ds(count, count)] = second_kept_ref[here] + second_taken_ref[here]


def add_both_kernel(kept_ref, taken_ref, near_ref, far_ref):
    count = kept_ref.shape[0] // 4
    for start, out_ref in ((0, near_ref), (count, far_ref)):
        for i in range(2):
            here = pl.ds(2 * i * count + start, count)
            out_ref[pl.ds(i * count, count)] = kept_ref[here] + taken_ref[here]


def last_add_kernel(kept_ref, taken_ref, own_ref, other_ref):
    rows = own_ref.shape[1]
    for start, out_ref in ((0, own_ref), (rows, other_ref)):
        here = pl.ds(start, rows)
        out_ref[...] = kept_ref[:, here, :] + taken_ref[:, here, :]


def group_kernel(order, own_ref, other_ref, high_ref, low_ref):
    rows = own_ref.shape[0] // (2 * len(order))
    me = lax.axis_index("samples")
    for odd in range(2):
        for i, distance in enumerate(order):
            start = pl.multiple_of((me ^ distance ^ odd) * rows, rows)
            for j, dosage_ref in enumerate((own_ref, other_ref)):
                high, low = split(dosage_ref[pl.ds(start, rows), :])
                here = pl.ds((2 * i + j) * rows, rows)
                high_ref[odd, here, :] = high
                low_ref[odd, here, :] = low


def coefficients(sums, shared):
    norm, cross = sums[0:1, :], sums[1:2, :]
    later_norm, bend = shared[2:3, :], shared[3:4, :]
    curve = norm + cross
    ratio = later_norm / curve
    step = jnp.where(later_norm > 0, later_norm / (later_norm + bend - later_norm * ratio), 0.0)
    start = norm / curve
    return start * (1.0 + step * (ratio + cross / norm)), -start * step


def solved_kernel(devices, direction_hbm, scaled_hbm, sums_ref, solved_hbm, factors_ref, direction_ref, scaled_ref,
                  semaphores):
    people, columns = direction_ref.shape
    column = lax.axis_index("cols")
    copies = Copies(semaphores)
    loads = [copies.start(direction_hbm, direction_ref), copies.start(scaled_hbm, scaled_ref)]

    def total(which):
        sums = sums_ref[which]
        shared = sums
        for i in range(1, devices):
            shared = shared + sums_ref[2 * i + which]
        return sums, shared

    along, across = coefficients(*total(column))
    factors = jnp.concatenate([along, across, *coefficients(*total(1 - column))], axis=0)
    factors_ref[...] = jnp.concatenate([factors, factors], axis=0)
    wait_all(loads)
    stores = []
    part_rows = people // 4
    for part in range(4):
        block = pl.ds(part * part_rows, part_rows)
        direction_ref[block, :] = along * direction_ref[block, :] + across * scaled_ref[block, :]
        stores.append(copies.start(direction_ref.at[block], solved_hbm.at[block]))
    wait_all(stores)


def scores_kernel(norm_scale, factors_ref, own_ref, other_ref, scores_ref):
    columns = own_ref.shape[2]
    column = lax.axis_index("cols")
    for which, rows_ref, place in ((0, own_ref, column), (2, other_ref, 1 - column)):
        along, across = factors_ref[which:which + 1, :], factors_ref[which + 1:which + 2, :]
        here = pl.ds(pl.multiple_of(place * columns, columns), columns)
        scores_ref[:, here] = norm_scale * (along * rows_ref[0] + across * rows_ref[1])


def call(kernel, out_shape, in_specs, out_specs, scratch_shapes=(), limit=VMEM_LIMIT):
    return pl.pallas_call(
        kernel,
        out_shape=out_shape,
        in_specs=in_specs,
        out_specs=out_specs,
        scratch_shapes=list(scratch_shapes),
        compiler_params=pltpu.CompilerParams(vmem_limit_bytes=limit),
    )


def swap(values, axis, devices, step):
    return lax.ppermute(values, axis, [(i, i ^ step) for i in range(devices)])


def after(value, *others):
    return lax.optimization_barrier((value, *others))[0]


def per_device(kinship, relatives, variance, phenotypes, dosage):
    devices = lax.axis_size("samples")
    block_count, positions, tile = kinship.shape[:3]
    people, columns = phenotypes.shape
    variants = dosage.shape[1]
    share_rows = variants // devices
    entries = block_count * (positions - 1)
    capacity = -(-entries // (devices - 1))
    assert capacity <= 2
    hbm = pl.BlockSpec(memory_space=pltpu.HBM)
    anywhere = pl.BlockSpec(memory_space=pl.ANY)
    vmem = pl.BlockSpec(memory_space=pltpu.VMEM)
    smem = pl.BlockSpec(memory_space=pltpu.SMEM)
    float_of = lambda *shape: jax.ShapeDtypeStruct(shape, jnp.float32)
    room = lambda *shape: pltpu.VMEM(shape, jnp.float32)
    full = float_of(people, columns)
    full_room = room(people, columns)
    half = devices // 2
    near_by = list(range(half - 1, 0, -1))
    at_home = lambda *arrays: [pltpu.with_memory_space_constraint(array, pltpu.HBM) for array in arrays]
    kinship, = at_home(kinship)
    tiles_room = pltpu.VMEM((block_count, tile, positions * tile), jnp.bfloat16)
    tiles_out = pltpu.HBM((block_count, tile, positions * tile), jnp.bfloat16)
    full_out = pltpu.HBM((people, columns), jnp.float32)
    direction, direction_kept_hbm, diagonal, norm = call(
        direction_kernel,
        [full, full_out, pltpu.HBM((people, 1), jnp.float32), float_of(SUBLANES, columns)],
        [hbm] * 3,
        [vmem, hbm, hbm, vmem],
        [
            room(*kinship.shape), room(block_count, tile), full_room, room(people, 1),
            pltpu.SemaphoreType.DMA((3 * block_count + 2,)),
        ],
    )(
        kinship, *at_home(variance.reshape(block_count, tile), phenotypes)
    )
    def to_mates(blocks):
        return [swap(blocks[k - 1], "samples", devices, k) for k in near_by]

    bits = half.bit_length() - 1
    even = [sum(((i >> b) & 1) << (bits - b) for b in range(bits)) for i in range(half)]
    steps = [2 << i for i in range(bits)]
    other_dosage = with_layout_constraint(swap(after(dosage, direction), "cols", 2, 1), Layout((0, 1)))
    table, forward, *outgoing = call(
        functools.partial(route_kernel, devices, capacity, block_count),
        [
            jax.ShapeDtypeStruct((4, max(entries, devices)), jnp.int32),
            jax.ShapeDtypeStruct((capacity, half), jnp.int32),
        ] + [float_of(capacity, tile, columns)] * (half - 1),
        [smem, vmem, anywhere],
        [smem, smem] + [vmem] * (half - 1),
        [pltpu.SMEM((devices,), jnp.int32), pltpu.SMEM((devices,), jnp.int32)],
    )(relatives.T, direction, other_dosage)
    high, low = call(
        tiles_kernel, [tiles_out] * 2, [hbm], [hbm] * 2,
        [room(*kinship.shape), tiles_room, tiles_room, pltpu.SemaphoreType.DMA((3,))],
    )(kinship)

    parts = jax.ShapeDtypeStruct((2, variants, people), jnp.bfloat16)
    large = VMEM_LIMIT if variants <= people else LARGE_VMEM
    grouped = call(
        functools.partial(group_kernel, even), [parts] * 2, [vmem] * 2, [vmem] * 2, limit=large
    )(after(dosage, table).T, other_dosage.T)

    products = float_of(half, 2 * share_rows, columns)

    def add_step(kernel, kept, *taken):
        rows = float_of(kept.shape[0] // 2, 2 * share_rows, columns)
        return call(kernel, [rows] * 2, [vmem] * (1 + len(taken)), [vmem] * 2)(kept, *taken)

    partner = swap(direction, "samples", devices, half)
    near = to_mates(outgoing)
    direction_even, direction_odd = call(
        score_kernel, [products] * 2, [vmem] * 3, [vmem] * 2, limit=large
    )(*grouped, direction)
    direction_share = swap(direction_odd, "samples", devices, 1)
    far = to_mates(call(
        forward_kernel,
        [float_of(capacity, tile, columns)] * (half - 1),
        [smem, vmem] + [anywhere] * (half + 1) + [hbm] * 2,
        [vmem] * (half - 1),
    )(forward, partner, *near, direction_even, direction_odd, *at_home(high, low)))
    received = near + far + [partner.reshape(block_count, tile, columns)]
    products_out = pltpu.HBM(products.shape, jnp.float32)
    scaled, handled, outgoing, scaled_even, scaled_odd = call(
        functools.partial(apply_kernel, devices, capacity),
        [
            full_out, full_out, pltpu.HBM((devices, tile + SUBLANES, columns), jnp.float32), products_out, products_out,
        ],
        [smem, hbm, hbm, hbm] + [vmem] * (devices + 3) + [anywhere],
        [hbm] * 5,
        [
            room(devices * capacity + block_count, tile, columns), tiles_room, tiles_room, room(people, 1), full_room,
            full_room, room(SUBLANES, columns), room(*products.shape), room(*products.shape),
            pltpu.SemaphoreType.DMA((2 * devices + 7,)),
        ],
        limit=large,
    )(table, high, low, diagonal, direction, norm, *grouped, *received, direction_share)
    later = lax.all_to_all(outgoing, "samples", split_axis=0, concat_axis=0, tiled=True)
    scaled_share = swap(scaled_odd, "samples", devices, 1)
    direction_kept, direction_given = add_step(add_kernel, direction_even, direction_share)
    direction_taken = swap(after(direction_given, scaled), "samples", devices, steps[0])
    scaled_kept, scaled_given = add_step(add_kernel, scaled_even, scaled_share)
    scaled_taken = swap(scaled_given, "samples", devices, steps[0])
    sums = call(
        functools.partial(curvature_kernel, devices),
        pltpu.HBM((2 * devices, SUBLANES, columns), jnp.float32),
        [smem] + [hbm] * 6 + [anywhere] * 2,
        hbm,
        [
            room(2 * devices, SUBLANES, columns), tiles_room, tiles_room, full_room, room(people, 1), full_room,
            full_room, room(devices, tile + SUBLANES, columns), pltpu.SemaphoreType.DMA((8,)),
        ],
    )(table, *at_home(high, low, direction_kept_hbm, diagonal, scaled, handled), later, scaled_given)
    all_sums = lax.all_to_all(sums, ("samples", "cols"), split_axis=0, concat_axis=0, tiled=True)
    halves = float_of(scaled_kept.shape[0], 2 * share_rows, columns)
    kept, given = call(
        merge_kernel, [halves] * 2, [vmem] * 4 + [hbm], [vmem] * 2
    )(direction_kept, direction_taken, scaled_kept, scaled_taken, *at_home(sums))
    for step in steps[1:-1]:
        kept, given = add_step(add_both_kernel, kept, swap(given, "samples", devices, step))
    taken = swap(given, "samples", devices, steps[-1])
    rows = float_of(2, share_rows, columns)
    own_scores, other_scores = call(last_add_kernel, [rows] * 2, [vmem] * 2, [vmem] * 2)(kept, taken)
    solved, factors = call(
        functools.partial(solved_kernel, devices),
        [full, float_of(SUBLANES, columns)],
        [hbm, hbm, vmem],
        [hbm, vmem],
        [full_room, full_room, pltpu.SemaphoreType.DMA((6,))],
    )(*at_home(direction_kept_hbm, scaled), all_sums)
    scores = call(
        functools.partial(scores_kernel, 1.0 / math.sqrt(people * devices)),
        float_of(share_rows, 2 * columns), [vmem] * 3, vmem,
    )(factors, own_scores, swap(other_scores, "cols", 2, 1))
    return (solved, scores)


def solution(mesh):
    return jax.shard_map(
        per_device,
        mesh=mesh,
        in_specs=(
            P(("groups", "samples"), None, None, None),
            P("groups", None),
            P(("groups", "samples")),
            P(("groups", "samples"), "cols"),
            P(("groups", "samples"), "cols"),
        ),
        out_specs=(P(("groups", "samples"), "cols"), P(("groups", "cols", "samples"), None)),
        check_vma=False,
    )
```

```python
import functools
import math

import jax
import jax.numpy as jnp
from jax import lax
from jax.experimental import pallas as pl
from jax.experimental.layout import Layout, with_layout_constraint
from jax.experimental.pallas import tpu as pltpu
from jax.sharding import PartitionSpec as P

VMEM_LIMIT = 24 * 1024 * 1024
LARGE_VMEM = 56 * 1024 * 1024
SUBLANES = 8


def split(values):
    high = values.astype(jnp.bfloat16)
    low = (values - high.astype(jnp.float32)).astype(jnp.bfloat16)
    return high, low


def dot(left, right):
    return jnp.dot(left, right, preferred_element_type=jnp.float32)


def on_diagonal(size):
    rows = lax.broadcasted_iota(jnp.int32, (size, size), 0)
    return rows == lax.broadcasted_iota(jnp.int32, (size, size), 1)


def split_tiles(kinship_ref, high_ref, low_ref):
    block_count, positions, tile = kinship_ref.shape[:3]
    diagonal_mask = on_diagonal(tile)
    for row in range(block_count):
        for position in range(positions):
            values = kinship_ref[row, position]
            if position == 0:
                values = jnp.where(diagonal_mask, 0.0, values)
            high, low = split(values)
            high_ref[row, :, pl.ds(position * tile, tile)] = high
            low_ref[row, :, pl.ds(position * tile, tile)] = low


def product(high, low, blocks):
    parts = [split(block) for block in blocks]
    blocks_high = jnp.concatenate([part[0] for part in parts], axis=0)
    blocks_low = jnp.concatenate([part[1] for part in parts], axis=0)
    return dot(high, blocks_high) + (dot(low, blocks_high) + dot(high, blocks_low))


def column_sums(values):
    rows, columns = values.shape
    return jnp.sum(values.reshape(rows // SUBLANES, SUBLANES, columns), axis=0)


class Copies:
    def __init__(self, semaphores):
        self.semaphores = semaphores
        self.count = 0

    def start(self, source, target):
        copy = pltpu.make_async_copy(source, target, self.semaphores.at[self.count])
        self.count += 1
        copy.start()
        return copy


def wait_all(copies):
    for copy in copies:
        copy.wait()


def quotient(value, divisor):
    if divisor & (divisor - 1) == 0:
        return lax.shift_right_logical(value, jnp.int32(divisor.bit_length() - 1))
    return lax.div(value, jnp.int32(divisor))


def direction_kernel(kinship_hbm, variance_hbm, phenotypes_hbm, direction_ref, direction_hbm, diagonal_hbm, sums_ref,
                     kinship_ref, variance_ref, phenotypes_ref, diagonal_ref, semaphores):
    block_count, positions, tile = kinship_ref.shape[:3]
    copies = Copies(semaphores)
    loads = [copies.start(variance_hbm, variance_ref)]
    for row in range(block_count):
        block = pl.ds(row * tile, tile)
        loads.append(copies.start(kinship_hbm.at[row], kinship_ref.at[row]))
        loads.append(copies.start(phenotypes_hbm.at[block], phenotypes_ref.at[block]))
    stores = []
    norm = jnp.zeros((SUBLANES, direction_ref.shape[1]), jnp.float32)
    diagonal_mask = on_diagonal(tile)
    loads[0].wait()
    for row in range(block_count):
        wait_all(loads[1 + 2 * row:3 + 2 * row])
        block = pl.ds(row * tile, tile)
        total = jnp.where(diagonal_mask, variance_ref[row:row + 1, :], kinship_ref[row, 0])
        for position in range(1, positions):
            total = total + kinship_ref[row, position]
        diagonal = jnp.sum(total, axis=1, keepdims=True)
        diagonal_ref[block, :] = diagonal
        here = phenotypes_ref[block, :] * (1.0 / diagonal)
        direction_ref[block, :] = here
        norm = norm + column_sums(here * phenotypes_ref[block, :])
        stores.append(copies.start(direction_ref.at[block], direction_hbm.at[block]))
    stores.append(copies.start(diagonal_ref, diagonal_hbm))
    row_ids = lax.broadcasted_iota(jnp.int32, norm.shape, 0)
    sums_ref[...] = jnp.where(row_ids == 0, jnp.sum(norm, axis=0, keepdims=True), 0.0)
    wait_all(stores)


def tiles_kernel(kinship_hbm, high_hbm, low_hbm, kinship_ref, high_ref, low_ref, semaphores):
    copies = Copies(semaphores)
    copies.start(kinship_hbm, kinship_ref).wait()
    split_tiles(kinship_ref, high_ref, low_ref)
    wait_all([copies.start(high_ref, high_hbm), copies.start(low_ref, low_hbm)])


def route_kernel(devices, capacity, block_count, list_ref, direction_ref, gate_ref, table_ref, forward_ref, *refs):
    half = devices // 2
    outgoing_refs, (first_ref, last_ref) = refs[:half - 1], refs[half - 1:]
    positions = list_ref.shape[0] + 1
    tile = direction_ref.shape[0] // block_count
    me = lax.axis_index("samples")
    partner = me ^ half
    spare = me ^ 1
    top = block_count * block_count

    def collect(device):
        for j in range(devices):
            first_ref[j] = jnp.int32(top)
            last_ref[j] = jnp.int32(-1)
        found = []
        for row in range(block_count):
            for position in range(positions - 1):
                listed = list_ref[position, device * block_count + row]
                live = listed >= 0
                safe = jnp.maximum(listed, 0)
                other = quotient(safe, block_count)
                far_block = safe - other * block_count
                key = jnp.where(device < other, row * block_count + far_block, far_block * block_count + row)
                first_ref[other] = jnp.minimum(first_ref[other], jnp.where(live, key, top))
                last_ref[other] = jnp.maximum(last_ref[other], jnp.where(live, key, -1))
                found.append((live, other, far_block, key))
        return found

    def blocks_for(device, other):
        blocks = []
        for key in (first_ref[other], last_ref[other]):
            safe = jnp.clip(key, 0, top - 1)
            lower = quotient(safe, block_count)
            higher = safe - lower * block_count
            blocks.append(jnp.where(key == safe, jnp.where(device < other, lower, higher), 0))
        return blocks

    collect(partner)
    for k in range(1, half):
        blocks = blocks_for(partner, me ^ k)
        for slot in range(capacity):
            forward_ref[slot, k] = blocks[slot]
    for entry, (live, other, far_block, key) in enumerate(collect(me)):
        first, last = first_ref[other], last_ref[other]
        handled = jnp.where(me < other, first, last)
        weight = jnp.where(first == last, 1, 2)
        slot = jnp.where(key == first, 0, capacity - 1)
        place = jnp.where(other == partner, devices * capacity + far_block, other * capacity + slot)
        table_ref[0, entry] = jnp.where(live, place, spare * capacity)
        table_ref[1, entry] = jnp.where(live, other, spare)
        table_ref[2, entry] = jnp.where(live & (key == handled), weight, 0)
    for other in range(devices):
        blocks = blocks_for(me, other)
        table_ref[3, other] = jnp.where(me < other, blocks[1], blocks[0])
    near = [blocks_for(me, me ^ k) for k in range(1, half)]
    for k in range(1, half):
        for slot in range(capacity):
            start = pl.multiple_of(near[k - 1][slot] * tile, tile)
            outgoing_refs[k - 1][slot] = direction_ref[pl.ds(start, tile), :]


def forward_kernel(forward_ref, partner_ref, *refs):
    capacity, half = forward_ref.shape
    outgoing_refs = refs[1 - half:]
    tile = outgoing_refs[0].shape[1]
    for k in range(1, half):
        for slot in range(capacity):
            start = pl.multiple_of(forward_ref[slot, k] * tile, tile)
            outgoing_refs[k - 1][slot] = partner_ref[pl.ds(start, tile), :]


def gather_received(devices, capacity, received_refs, gathered_ref):
    half = devices // 2
    me = lax.axis_index("samples")
    near_refs, far_refs, partner_ref = received_refs[:half - 1], received_refs[half - 1:-1], received_refs[-1]
    gathered_ref[pl.ds(devices * capacity, partner_ref.shape[0])] = partner_ref[...]
    for i in range(half - 1):
        mate = me ^ (half - 1 - i)
        gathered_ref[pl.ds(mate * capacity, capacity)] = near_refs[i][...]
        gathered_ref[pl.ds((mate ^ half) * capacity, capacity)] = far_refs[i][...]


def score_products(high_ref, low_ref, values, even_ref, odd_ref):
    count, rows = even_ref.shape[:2]
    for odd, out_ref in enumerate((even_ref, odd_ref)):
        for i in range(0, count, 4):
            here = pl.ds(i * rows, 4 * rows)
            total = product(high_ref[odd, here, :], low_ref[odd, here, :], [values])
            out_ref[pl.ds(i, 4)] = total.reshape(4, rows, -1)


def score_kernel(high_ref, low_ref, values_ref, even_ref, odd_ref):
    score_products(high_ref, low_ref, values_ref[...], even_ref, odd_ref)


def apply_kernel(devices, capacity, table_ref, high_hbm, low_hbm, diagonal_hbm, direction_ref, norm_ref, dosage_high_ref,
                 dosage_low_ref, *refs):
    received_refs = refs[:devices - 1]
    (scaled_hbm, handled_hbm, outgoing_hbm, even_hbm, odd_hbm, gathered_ref, high_ref, low_ref, diagonal_ref, scaled_ref,
     handled_ref, sums_ref, even_ref, odd_ref, semaphores) = refs[-15:]
    copies = Copies(semaphores)
    loads = [
        copies.start(high_hbm, high_ref), copies.start(low_hbm, low_ref), copies.start(diagonal_hbm, diagonal_ref)
    ]
    gather_received(devices, capacity, received_refs, gathered_ref)
    wait_all(loads)
    block_count, tile, depth = high_ref.shape
    others = depth // tile - 1
    cross = jnp.zeros(norm_ref.shape, jnp.float32)
    for row in range(block_count):
        block = pl.ds(row * tile, tile)
        here = direction_ref[block, :]
        blocks = [here] + [gathered_ref[table_ref[0, row * others + i]] for i in range(others)]
        mapped = product(high_ref[row], low_ref[row], blocks)
        scaled_ref[block, :] = mapped * (1.0 / diagonal_ref[block, :])
        cross = cross + column_sums(here * mapped)
    row_ids = lax.broadcasted_iota(jnp.int32, cross.shape, 0)
    sums_ref[...] = jnp.where(row_ids == 1, jnp.sum(cross, axis=0, keepdims=True), norm_ref[...])
    stores = [copies.start(scaled_ref, scaled_hbm)]
    for other in range(devices):
        start = pl.multiple_of(table_ref[3, other] * tile, tile)
        stores.append(copies.start(scaled_ref.at[pl.ds(start, tile)], outgoing_hbm.at[other, pl.ds(0, tile)]))
        stores.append(copies.start(sums_ref, outgoing_hbm.at[other, pl.ds(tile, SUBLANES)]))
    score_products(dosage_high_ref, dosage_low_ref, scaled_ref[...], even_ref, odd_ref)
    stores += [copies.start(odd_ref, odd_hbm), copies.start(even_ref, even_hbm)]
    far = pl.ds(tile, depth - tile)
    for row in range(block_count):
        blocks = []
        for i in range(others):
            weight = table_ref[2, row * others + i].astype(jnp.float32)
            blocks.append(weight * gathered_ref[table_ref[0, row * others + i]])
        handled_ref[pl.ds(row * tile, tile), :] = product(high_ref[row, :, far], low_ref[row, :, far], blocks)
    stores.append(copies.start(handled_ref, handled_hbm))
    wait_all(stores)


def curvature_kernel(devices, table_ref, high_hbm, low_hbm, direction_hbm, diagonal_hbm, scaled_hbm, handled_hbm,
                     later_hbm, *refs):
    (sums_hbm, sums_ref, high_ref, low_ref, direction_ref, diagonal_ref, scaled_ref, handled_ref, later_ref,
     semaphores) = refs[-10:]
    block_count, tile, depth = high_ref.shape
    copies = Copies(semaphores)
    wait_all([copies.start(source, target) for source, target in (
        (later_hbm, later_ref), (scaled_hbm, scaled_ref), (direction_hbm, direction_ref), (high_hbm, high_ref),
        (low_hbm, low_ref), (handled_hbm, handled_ref), (diagonal_hbm, diagonal_ref),
    )])
    others = depth // tile - 1
    first_sums = later_ref[0, pl.ds(tile, SUBLANES), :]
    for other in range(1, devices):
        first_sums = first_sums + later_ref[other, pl.ds(tile, SUBLANES), :]
    rho = first_sums[1:2, :] / first_sums[0:1, :]
    norm = jnp.zeros(first_sums.shape, jnp.float32)
    bend = jnp.zeros(first_sums.shape, jnp.float32)
    for row in range(block_count):
        block = pl.ds(row * tile, tile)
        here = scaled_ref[block, :] - rho * direction_ref[block, :]
        blocks = [here]
        for i in range(others):
            entry = row * others + i
            weight = table_ref[2, entry].astype(jnp.float32)
            blocks.append(weight * later_ref[table_ref[1, entry], pl.ds(0, tile), :])
        mapped = product(high_ref[row], low_ref[row], blocks) - rho * handled_ref[block, :]
        norm = norm + column_sums(here * here * diagonal_ref[block, :])
        bend = bend + column_sums(here * mapped)
    row_ids = lax.broadcasted_iota(jnp.int32, first_sums.shape, 0)
    sums = jnp.where(row_ids == 2, jnp.sum(norm, axis=0, keepdims=True), first_sums)
    sums = jnp.where(row_ids == 3, jnp.sum(bend, axis=0, keepdims=True), sums)
    for i in range(2 * devices):
        sums_ref[i] = sums
    copies.start(sums_ref, sums_hbm).wait()


def add_kernel(kept_ref, taken_ref, *refs):
    near_ref, far_ref = refs[-2:]
    count = near_ref.shape[0]
    near_ref[...] = kept_ref[pl.ds(0, count)] + taken_ref[pl.ds(0, count)]
    far_ref[...] = kept_ref[pl.ds(count, count)] + taken_ref[pl.ds(count, count)]


def odd_kernel(kept_ref, taken_ref, near_ref, far_ref):
    for i in range(near_ref.shape[0]):
        near_ref[i] = kept_ref[2 * i] + taken_ref[2 * i]
        far_ref[i] = kept_ref[2 * i + 1] + taken_ref[2 * i + 1]


def last_add_kernel(first_kept_ref, first_taken_ref, second_kept_ref, second_taken_ref, own_ref, other_ref):
    rows = own_ref.shape[1]
    for i, (kept_ref, taken_ref) in enumerate(
        ((first_kept_ref, first_taken_ref), (second_kept_ref, second_taken_ref))
    ):
        own_ref[i] = kept_ref[0, pl.ds(0, rows), :] + taken_ref[0, pl.ds(0, rows), :]
        other_ref[i] = kept_ref[0, pl.ds(rows, rows), :] + taken_ref[0, pl.ds(rows, rows), :]


def group_kernel(order, own_ref, other_ref, high_ref, low_ref):
    rows = own_ref.shape[0] // (2 * len(order))
    me = lax.axis_index("samples")
    for odd in range(2):
        for i, distance in enumerate(order):
            start = pl.multiple_of((me ^ distance ^ odd) * rows, rows)
            for j, dosage_ref in enumerate((own_ref, other_ref)):
                high, low = split(dosage_ref[pl.ds(start, rows), :])
                here = pl.ds((2 * i + j) * rows, rows)
                high_ref[odd, here, :] = high
                low_ref[odd, here, :] = low


def coefficients(sums, shared):
    norm, cross = sums[0:1, :], sums[1:2, :]
    later_norm, bend = shared[2:3, :], shared[3:4, :]
    curve = norm + cross
    ratio = later_norm / curve
    step = jnp.where(later_norm > 0, later_norm / (later_norm + bend - later_norm * ratio), 0.0)
    start = norm / curve
    return start * (1.0 + step * (ratio + cross / norm)), -start * step


def solved_kernel(devices, direction_hbm, scaled_hbm, sums_ref, solved_hbm, factors_ref, direction_ref, scaled_ref,
                  semaphores):
    people, columns = direction_ref.shape
    column = lax.axis_index("cols")
    copies = Copies(semaphores)
    loads = [copies.start(direction_hbm, direction_ref), copies.start(scaled_hbm, scaled_ref)]

    def total(which):
        sums = sums_ref[which]
        shared = sums
        for i in range(1, devices):
            shared = shared + sums_ref[2 * i + which]
        return sums, shared

    along, across = coefficients(*total(column))
    factors = jnp.concatenate([along, across, *coefficients(*total(1 - column))], axis=0)
    factors_ref[...] = jnp.concatenate([factors, factors], axis=0)
    wait_all(loads)
    stores = []
    part_rows = people // 4
    for part in range(4):
        block = pl.ds(part * part_rows, part_rows)
        direction_ref[block, :] = along * direction_ref[block, :] + across * scaled_ref[block, :]
        stores.append(copies.start(direction_ref.at[block], solved_hbm.at[block]))
    wait_all(stores)


def scores_kernel(norm_scale, factors_ref, own_ref, other_ref, scores_ref):
    columns = own_ref.shape[2]
    column = lax.axis_index("cols")
    for which, rows_ref, place in ((0, own_ref, column), (2, other_ref, 1 - column)):
        along, across = factors_ref[which:which + 1, :], factors_ref[which + 1:which + 2, :]
        here = pl.ds(pl.multiple_of(place * columns, columns), columns)
        scores_ref[:, here] = norm_scale * (along * rows_ref[0] + across * rows_ref[1])


def call(kernel, out_shape, in_specs, out_specs, scratch_shapes=(), limit=VMEM_LIMIT):
    return pl.pallas_call(
        kernel,
        out_shape=out_shape,
        in_specs=in_specs,
        out_specs=out_specs,
        scratch_shapes=list(scratch_shapes),
        compiler_params=pltpu.CompilerParams(vmem_limit_bytes=limit),
    )


def swap(values, axis, devices, step):
    return lax.ppermute(values, axis, [(i, i ^ step) for i in range(devices)])


def after(value, *others):
    return lax.optimization_barrier((value, *others))[0]


def per_device(kinship, relatives, variance, phenotypes, dosage):
    devices = lax.axis_size("samples")
    block_count, positions, tile = kinship.shape[:3]
    people, columns = phenotypes.shape
    variants = dosage.shape[1]
    share_rows = variants // devices
    entries = block_count * (positions - 1)
    capacity = -(-entries // (devices - 1))
    assert capacity <= 2
    hbm = pl.BlockSpec(memory_space=pltpu.HBM)
    anywhere = pl.BlockSpec(memory_space=pl.ANY)
    vmem = pl.BlockSpec(memory_space=pltpu.VMEM)
    smem = pl.BlockSpec(memory_space=pltpu.SMEM)
    float_of = lambda *shape: jax.ShapeDtypeStruct(shape, jnp.float32)
    room = lambda *shape: pltpu.VMEM(shape, jnp.float32)
    full = float_of(people, columns)
    full_room = room(people, columns)
    half = devices // 2
    near_by = list(range(half - 1, 0, -1))
    at_home = lambda *arrays: [pltpu.with_memory_space_constraint(array, pltpu.HBM) for array in arrays]
    kinship, = at_home(kinship)
    tiles_room = pltpu.VMEM((block_count, tile, positions * tile), jnp.bfloat16)
    tiles_out = pltpu.HBM((block_count, tile, positions * tile), jnp.bfloat16)
    full_out = pltpu.HBM((people, columns), jnp.float32)
    direction, direction_kept_hbm, diagonal, norm = call(
        direction_kernel,
        [full, full_out, pltpu.HBM((people, 1), jnp.float32), float_of(SUBLANES, columns)],
        [hbm] * 3,
        [vmem, hbm, hbm, vmem],
        [
            room(*kinship.shape), room(block_count, tile), full_room, room(people, 1),
            pltpu.SemaphoreType.DMA((3 * block_count + 2,)),
        ],
    )(
        kinship, *at_home(variance.reshape(block_count, tile), phenotypes)
    )
    def to_mates(blocks):
        return [swap(blocks[k - 1], "samples", devices, k) for k in near_by]

    bits = half.bit_length() - 1
    even = [sum(((i >> b) & 1) << (bits - b) for b in range(bits)) for i in range(half)]
    steps = [2 << i for i in range(bits)]
    other_dosage = with_layout_constraint(swap(after(dosage, direction), "cols", 2, 1), Layout((0, 1)))
    table, forward, *outgoing = call(
        functools.partial(route_kernel, devices, capacity, block_count),
        [
            jax.ShapeDtypeStruct((4, max(entries, devices)), jnp.int32),
            jax.ShapeDtypeStruct((capacity, half), jnp.int32),
        ] + [float_of(capacity, tile, columns)] * (half - 1),
        [smem, vmem, anywhere],
        [smem, smem] + [vmem] * (half - 1),
        [pltpu.SMEM((devices,), jnp.int32), pltpu.SMEM((devices,), jnp.int32)],
    )(relatives.T, direction, other_dosage)
    high, low = call(
        tiles_kernel, [tiles_out] * 2, [hbm], [hbm] * 2,
        [room(*kinship.shape), tiles_room, tiles_room, pltpu.SemaphoreType.DMA((3,))],
    )(kinship)

    parts = jax.ShapeDtypeStruct((2, variants, people), jnp.bfloat16)
    large = VMEM_LIMIT if variants <= people else LARGE_VMEM
    grouped = call(
        functools.partial(group_kernel, even), [parts] * 2, [vmem] * 2, [vmem] * 2, limit=large
    )(after(dosage, table).T, other_dosage.T)

    products = float_of(half, 2 * share_rows, columns)

    def add_step(kernel, kept, taken, *gates):
        rows = float_of(kept.shape[0] // 2, 2 * share_rows, columns)
        return call(kernel, [rows] * 2, [vmem] * 2 + [hbm] * len(gates), [vmem] * 2)(kept, taken, *gates)

    partner = swap(direction, "samples", devices, half)
    near = to_mates(outgoing)
    direction_even, direction_odd = call(
        score_kernel, [products] * 2, [vmem] * 3, [vmem] * 2, limit=large
    )(*grouped, direction)
    direction_share = swap(direction_odd, "samples", devices, 1)
    far = to_mates(call(
        forward_kernel,
        [float_of(capacity, tile, columns)] * (half - 1),
        [smem, vmem] + [anywhere] * (half + 1) + [hbm] * 2,
        [vmem] * (half - 1),
    )(forward, partner, *near, direction_even, direction_odd, *at_home(high, low)))
    direction_kept, direction_given = add_step(odd_kernel, direction_even, direction_share)
    direction_given, *far = lax.optimization_barrier((direction_given, *far))
    direction_taken = swap(direction_given, "samples", devices, half)
    received = near + far + [partner.reshape(block_count, tile, columns)]
    products_out = pltpu.HBM(products.shape, jnp.float32)
    scaled, handled, outgoing, scaled_even, scaled_odd = call(
        functools.partial(apply_kernel, devices, capacity),
        [
            full_out, full_out, pltpu.HBM((devices, tile + SUBLANES, columns), jnp.float32), products_out, products_out,
        ],
        [smem, hbm, hbm, hbm] + [vmem] * (devices + 3) + [anywhere],
        [hbm] * 5,
        [
            room(devices * capacity + block_count, tile, columns), tiles_room, tiles_room, room(people, 1), full_room,
            full_room, room(SUBLANES, columns), room(*products.shape), room(*products.shape),
            pltpu.SemaphoreType.DMA((2 * devices + 7,)),
        ],
        limit=large,
    )(table, high, low, diagonal, direction, norm, *grouped, *received, direction_share)
    later = lax.all_to_all(outgoing, "samples", split_axis=0, concat_axis=0, tiled=True)
    scaled_odd, direction_taken = lax.optimization_barrier((scaled_odd, direction_taken))
    scaled_share = swap(scaled_odd, "samples", devices, 1)
    for step in steps[:-1]:
        direction_kept, direction_given = add_step(add_kernel, direction_kept, direction_taken)
        direction_taken = swap(direction_given, "samples", devices, step)
    scaled_kept, scaled_given = add_step(add_kernel, scaled_even, scaled_share, direction_taken)
    scaled_taken = swap(scaled_given, "samples", devices, steps[0])
    sums = call(
        functools.partial(curvature_kernel, devices),
        pltpu.HBM((2 * devices, SUBLANES, columns), jnp.float32),
        [smem] + [hbm] * 6 + [anywhere] * 2,
        hbm,
        [
            room(2 * devices, SUBLANES, columns), tiles_room, tiles_room, full_room, room(people, 1), full_room,
            full_room, room(devices, tile + SUBLANES, columns), pltpu.SemaphoreType.DMA((8,)),
        ],
    )(table, *at_home(high, low, direction_kept_hbm, diagonal, scaled, handled), later, scaled_given)
    all_sums = lax.all_to_all(sums, ("samples", "cols"), split_axis=0, concat_axis=0, tiled=True)
    for step in steps[1:]:
        scaled_kept, scaled_given = add_step(add_kernel, scaled_kept, scaled_taken, *at_home(sums))
        scaled_taken = swap(scaled_given, "samples", devices, step)
    rows = float_of(2, share_rows, columns)
    own_scores, other_scores = call(
        last_add_kernel, [rows] * 2, [vmem] * 4, [vmem] * 2
    )(direction_kept, direction_taken, scaled_kept, scaled_taken)
    solved, factors = call(
        functools.partial(solved_kernel, devices),
        [full, float_of(SUBLANES, columns)],
        [hbm, hbm, vmem],
        [hbm, vmem],
        [full_room, full_room, pltpu.SemaphoreType.DMA((6,))],
    )(*at_home(direction_kept_hbm, scaled), all_sums)
    scores = call(
        functools.partial(scores_kernel, 1.0 / math.sqrt(people * devices)),
        float_of(share_rows, 2 * columns), [vmem] * 3, vmem,
    )(factors, own_scores, swap(other_scores, "cols", 2, 1))
    return (solved, scores)


def solution(mesh):
    return jax.shard_map(
        per_device,
        mesh=mesh,
        in_specs=(
            P(("groups", "samples"), None, None, None),
            P("groups", None),
            P(("groups", "samples")),
            P(("groups", "samples"), "cols"),
            P(("groups", "samples"), "cols"),
        ),
        out_specs=(P(("groups", "samples"), "cols"), P(("groups", "cols", "samples"), None)),
        check_vma=False,
    )
```

```python
import functools
import math

import jax
import jax.numpy as jnp
from jax import lax
from jax.experimental import pallas as pl
from jax.experimental.layout import Layout, with_layout_constraint
from jax.experimental.pallas import tpu as pltpu
from jax.sharding import PartitionSpec as P

VMEM_LIMIT = 24 * 1024 * 1024
LARGE_VMEM = 56 * 1024 * 1024
SUBLANES = 8


def split(values):
    high = values.astype(jnp.bfloat16)
    low = (values - high.astype(jnp.float32)).astype(jnp.bfloat16)
    return high, low


def dot(left, right):
    return jnp.dot(left, right, preferred_element_type=jnp.float32)


def on_diagonal(size):
    rows = lax.broadcasted_iota(jnp.int32, (size, size), 0)
    return rows == lax.broadcasted_iota(jnp.int32, (size, size), 1)


def split_tiles(kinship_ref, high_ref, low_ref):
    block_count, positions, tile = kinship_ref.shape[:3]
    diagonal_mask = on_diagonal(tile)
    for row in range(block_count):
        for position in range(positions):
            values = kinship_ref[row, position]
            if position == 0:
                values = jnp.where(diagonal_mask, 0.0, values)
            high, low = split(values)
            high_ref[row, :, pl.ds(position * tile, tile)] = high
            low_ref[row, :, pl.ds(position * tile, tile)] = low


def product(high, low, blocks):
    parts = [split(block) for block in blocks]
    blocks_high = jnp.concatenate([part[0] for part in parts], axis=0)
    blocks_low = jnp.concatenate([part[1] for part in parts], axis=0)
    return dot(high, blocks_high) + (dot(low, blocks_high) + dot(high, blocks_low))


def column_sums(values):
    rows, columns = values.shape
    return jnp.sum(values.reshape(rows // SUBLANES, SUBLANES, columns), axis=0)


class Copies:
    def __init__(self, semaphores):
        self.semaphores = semaphores
        self.count = 0

    def start(self, source, target):
        copy = pltpu.make_async_copy(source, target, self.semaphores.at[self.count])
        self.count += 1
        copy.start()
        return copy


def wait_all(copies):
    for copy in copies:
        copy.wait()


def quotient(value, divisor):
    if divisor & (divisor - 1) == 0:
        return lax.shift_right_logical(value, jnp.int32(divisor.bit_length() - 1))
    return lax.div(value, jnp.int32(divisor))


def direction_kernel(kinship_hbm, variance_hbm, phenotypes_hbm, direction_ref, direction_hbm, diagonal_hbm, sums_ref,
                     kinship_ref, variance_ref, phenotypes_ref, diagonal_ref, semaphores):
    block_count, positions, tile = kinship_ref.shape[:3]
    copies = Copies(semaphores)
    loads = [copies.start(variance_hbm, variance_ref)]
    for row in range(block_count):
        block = pl.ds(row * tile, tile)
        loads.append(copies.start(kinship_hbm.at[row], kinship_ref.at[row]))
        loads.append(copies.start(phenotypes_hbm.at[block], phenotypes_ref.at[block]))
    stores = []
    norm = jnp.zeros((SUBLANES, direction_ref.shape[1]), jnp.float32)
    diagonal_mask = on_diagonal(tile)
    loads[0].wait()
    for row in range(block_count):
        wait_all(loads[1 + 2 * row:3 + 2 * row])
        block = pl.ds(row * tile, tile)
        total = jnp.where(diagonal_mask, variance_ref[row:row + 1, :], kinship_ref[row, 0])
        for position in range(1, positions):
            total = total + kinship_ref[row, position]
        diagonal = jnp.sum(total, axis=1, keepdims=True)
        diagonal_ref[block, :] = diagonal
        here = phenotypes_ref[block, :] * (1.0 / diagonal)
        direction_ref[block, :] = here
        norm = norm + column_sums(here * phenotypes_ref[block, :])
        stores.append(copies.start(direction_ref.at[block], direction_hbm.at[block]))
    stores.append(copies.start(diagonal_ref, diagonal_hbm))
    row_ids = lax.broadcasted_iota(jnp.int32, norm.shape, 0)
    sums_ref[...] = jnp.where(row_ids == 0, jnp.sum(norm, axis=0, keepdims=True), 0.0)
    wait_all(stores)


def tiles_kernel(kinship_hbm, high_hbm, low_hbm, kinship_ref, high_ref, low_ref, semaphores):
    copies = Copies(semaphores)
    copies.start(kinship_hbm, kinship_ref).wait()
    split_tiles(kinship_ref, high_ref, low_ref)
    wait_all([copies.start(high_ref, high_hbm), copies.start(low_ref, low_hbm)])


def route_kernel(devices, capacity, block_count, list_ref, direction_ref, gate_ref, table_ref, forward_ref, *refs):
    half = devices // 2
    outgoing_refs, (first_ref, last_ref) = refs[:half - 1], refs[half - 1:]
    positions = list_ref.shape[0] + 1
    tile = direction_ref.shape[0] // block_count
    me = lax.axis_index("samples")
    partner = me ^ half
    spare = me ^ 1
    top = block_count * block_count

    def collect(device):
        for j in range(devices):
            first_ref[j] = jnp.int32(top)
            last_ref[j] = jnp.int32(-1)
        found = []
        for row in range(block_count):
            for position in range(positions - 1):
                listed = list_ref[position, device * block_count + row]
                live = listed >= 0
                safe = jnp.maximum(listed, 0)
                other = quotient(safe, block_count)
                far_block = safe - other * block_count
                key = jnp.where(device < other, row * block_count + far_block, far_block * block_count + row)
                first_ref[other] = jnp.minimum(first_ref[other], jnp.where(live, key, top))
                last_ref[other] = jnp.maximum(last_ref[other], jnp.where(live, key, -1))
                found.append((live, other, far_block, key))
        return found

    def blocks_for(device, other):
        blocks = []
        for key in (first_ref[other], last_ref[other]):
            safe = jnp.clip(key, 0, top - 1)
            lower = quotient(safe, block_count)
            higher = safe - lower * block_count
            blocks.append(jnp.where(key == safe, jnp.where(device < other, lower, higher), 0))
        return blocks

    collect(partner)
    for k in range(1, half):
        blocks = blocks_for(partner, me ^ k)
        for slot in range(capacity):
            forward_ref[slot, k] = blocks[slot]
    for entry, (live, other, far_block, key) in enumerate(collect(me)):
        first, last = first_ref[other], last_ref[other]
        handled = jnp.where(me < other, first, last)
        weight = jnp.where(first == last, 1, 2)
        slot = jnp.where(key == first, 0, capacity - 1)
        place = jnp.where(other == partner, devices * capacity + far_block, other * capacity + slot)
        table_ref[0, entry] = jnp.where(live, place, spare * capacity)
        table_ref[1, entry] = jnp.where(live, other, spare)
        table_ref[2, entry] = jnp.where(live & (key == handled), weight, 0)
    for other in range(devices):
        blocks = blocks_for(me, other)
        table_ref[3, other] = jnp.where(me < other, blocks[1], blocks[0])
    near = [blocks_for(me, me ^ k) for k in range(1, half)]
    for k in range(1, half):
        for slot in range(capacity):
            start = pl.multiple_of(near[k - 1][slot] * tile, tile)
            outgoing_refs[k - 1][slot] = direction_ref[pl.ds(start, tile), :]


def forward_kernel(forward_ref, partner_ref, *refs):
    capacity, half = forward_ref.shape
    outgoing_refs = refs[1 - half:]
    tile = outgoing_refs[0].shape[1]
    for k in range(1, half):
        for slot in range(capacity):
            start = pl.multiple_of(forward_ref[slot, k] * tile, tile)
            outgoing_refs[k - 1][slot] = partner_ref[pl.ds(start, tile), :]


def gather_received(devices, capacity, received_refs, gathered_ref):
    half = devices // 2
    me = lax.axis_index("samples")
    near_refs, far_refs, partner_ref = received_refs[:half - 1], received_refs[half - 1:-1], received_refs[-1]
    gathered_ref[pl.ds(devices * capacity, partner_ref.shape[0])] = partner_ref[...]
    for i in range(half - 1):
        mate = me ^ (half - 1 - i)
        gathered_ref[pl.ds(mate * capacity, capacity)] = near_refs[i][...]
        gathered_ref[pl.ds((mate ^ half) * capacity, capacity)] = far_refs[i][...]


def score_products(high_ref, low_ref, values, even_ref, odd_ref):
    count, rows = even_ref.shape[:2]
    for odd, out_ref in enumerate((even_ref, odd_ref)):
        for i in range(0, count, 4):
            here = pl.ds(i * rows, 4 * rows)
            total = product(high_ref[odd, here, :], low_ref[odd, here, :], [values])
            out_ref[pl.ds(i, 4)] = total.reshape(4, rows, -1)


def score_kernel(high_ref, low_ref, values_ref, even_ref, odd_ref):
    score_products(high_ref, low_ref, values_ref[...], even_ref, odd_ref)


def apply_kernel(devices, capacity, table_ref, high_hbm, low_hbm, diagonal_hbm, direction_ref, norm_ref, dosage_high_ref,
                 dosage_low_ref, *refs):
    received_refs = refs[:devices - 1]
    (scaled_hbm, handled_hbm, outgoing_hbm, even_hbm, odd_hbm, gathered_ref, high_ref, low_ref, diagonal_ref, scaled_ref,
     handled_ref, sums_ref, even_ref, odd_ref, semaphores) = refs[-15:]
    copies = Copies(semaphores)
    loads = [
        copies.start(high_hbm, high_ref), copies.start(low_hbm, low_ref), copies.start(diagonal_hbm, diagonal_ref)
    ]
    gather_received(devices, capacity, received_refs, gathered_ref)
    wait_all(loads)
    block_count, tile, depth = high_ref.shape
    others = depth // tile - 1
    cross = jnp.zeros(norm_ref.shape, jnp.float32)
    for row in range(block_count):
        block = pl.ds(row * tile, tile)
        here = direction_ref[block, :]
        blocks = [here] + [gathered_ref[table_ref[0, row * others + i]] for i in range(others)]
        mapped = product(high_ref[row], low_ref[row], blocks)
        scaled_ref[block, :] = mapped * (1.0 / diagonal_ref[block, :])
        cross = cross + column_sums(here * mapped)
    row_ids = lax.broadcasted_iota(jnp.int32, cross.shape, 0)
    sums_ref[...] = jnp.where(row_ids == 1, jnp.sum(cross, axis=0, keepdims=True), norm_ref[...])
    stores = [copies.start(scaled_ref, scaled_hbm)]
    for other in range(devices):
        start = pl.multiple_of(table_ref[3, other] * tile, tile)
        stores.append(copies.start(scaled_ref.at[pl.ds(start, tile)], outgoing_hbm.at[other, pl.ds(0, tile)]))
        stores.append(copies.start(sums_ref, outgoing_hbm.at[other, pl.ds(tile, SUBLANES)]))
    score_products(dosage_high_ref, dosage_low_ref, scaled_ref[...], even_ref, odd_ref)
    stores += [copies.start(odd_ref, odd_hbm), copies.start(even_ref, even_hbm)]
    far = pl.ds(tile, depth - tile)
    for row in range(block_count):
        blocks = []
        for i in range(others):
            weight = table_ref[2, row * others + i].astype(jnp.float32)
            blocks.append(weight * gathered_ref[table_ref[0, row * others + i]])
        handled_ref[pl.ds(row * tile, tile), :] = product(high_ref[row, :, far], low_ref[row, :, far], blocks)
    stores.append(copies.start(handled_ref, handled_hbm))
    wait_all(stores)


def curvature_kernel(devices, table_ref, high_hbm, low_hbm, direction_hbm, diagonal_hbm, scaled_hbm, handled_hbm,
                     later_hbm, *refs):
    (sums_hbm, sums_ref, high_ref, low_ref, direction_ref, diagonal_ref, scaled_ref, handled_ref, later_ref,
     semaphores) = refs[-10:]
    block_count, tile, depth = high_ref.shape
    copies = Copies(semaphores)
    wait_all([copies.start(source, target) for source, target in (
        (later_hbm, later_ref), (scaled_hbm, scaled_ref), (direction_hbm, direction_ref), (high_hbm, high_ref),
        (low_hbm, low_ref), (handled_hbm, handled_ref), (diagonal_hbm, diagonal_ref),
    )])
    others = depth // tile - 1
    first_sums = later_ref[0, pl.ds(tile, SUBLANES), :]
    for other in range(1, devices):
        first_sums = first_sums + later_ref[other, pl.ds(tile, SUBLANES), :]
    rho = first_sums[1:2, :] / first_sums[0:1, :]
    norm = jnp.zeros(first_sums.shape, jnp.float32)
    bend = jnp.zeros(first_sums.shape, jnp.float32)
    for row in range(block_count):
        block = pl.ds(row * tile, tile)
        here = scaled_ref[block, :] - rho * direction_ref[block, :]
        blocks = [here]
        for i in range(others):
            entry = row * others + i
            weight = table_ref[2, entry].astype(jnp.float32)
            blocks.append(weight * later_ref[table_ref[1, entry], pl.ds(0, tile), :])
        mapped = product(high_ref[row], low_ref[row], blocks) - rho * handled_ref[block, :]
        norm = norm + column_sums(here * here * diagonal_ref[block, :])
        bend = bend + column_sums(here * mapped)
    row_ids = lax.broadcasted_iota(jnp.int32, first_sums.shape, 0)
    sums = jnp.where(row_ids == 2, jnp.sum(norm, axis=0, keepdims=True), first_sums)
    sums = jnp.where(row_ids == 3, jnp.sum(bend, axis=0, keepdims=True), sums)
    for i in range(2 * devices):
        sums_ref[i] = sums
    copies.start(sums_ref, sums_hbm).wait()


def add_kernel(kept_ref, taken_ref, *refs):
    near_ref, far_ref = refs[-2:]
    count = near_ref.shape[0]
    near_ref[...] = kept_ref[pl.ds(0, count)] + taken_ref[pl.ds(0, count)]
    far_ref[...] = kept_ref[pl.ds(count, count)] + taken_ref[pl.ds(count, count)]


def last_add_kernel(first_kept_ref, first_taken_ref, second_kept_ref, second_taken_ref, own_ref, other_ref):
    rows = own_ref.shape[1]
    for i, (kept_ref, taken_ref) in enumerate(
        ((first_kept_ref, first_taken_ref), (second_kept_ref, second_taken_ref))
    ):
        own_ref[i] = kept_ref[0, pl.ds(0, rows), :] + taken_ref[0, pl.ds(0, rows), :]
        other_ref[i] = kept_ref[0, pl.ds(rows, rows), :] + taken_ref[0, pl.ds(rows, rows), :]


def group_kernel(order, own_ref, other_ref, high_ref, low_ref):
    rows = own_ref.shape[0] // (2 * len(order))
    me = lax.axis_index("samples")
    for odd in range(2):
        for i, distance in enumerate(order):
            start = pl.multiple_of((me ^ distance ^ odd) * rows, rows)
            for j, dosage_ref in enumerate((own_ref, other_ref)):
                high, low = split(dosage_ref[pl.ds(start, rows), :])
                here = pl.ds((2 * i + j) * rows, rows)
                high_ref[odd, here, :] = high
                low_ref[odd, here, :] = low


def coefficients(sums, shared):
    norm, cross = sums[0:1, :], sums[1:2, :]
    later_norm, bend = shared[2:3, :], shared[3:4, :]
    curve = norm + cross
    ratio = later_norm / curve
    step = jnp.where(later_norm > 0, later_norm / (later_norm + bend - later_norm * ratio), 0.0)
    start = norm / curve
    return start * (1.0 + step * (ratio + cross / norm)), -start * step


def solved_kernel(devices, direction_ref, scaled_ref, sums_ref, solved_hbm, factors_ref, solved_ref, semaphores):
    people, columns = direction_ref.shape
    column = lax.axis_index("cols")
    copies = Copies(semaphores)

    def total(which):
        sums = sums_ref[which]
        shared = sums
        for i in range(1, devices):
            shared = shared + sums_ref[2 * i + which]
        return sums, shared

    along, across = coefficients(*total(column))
    factors = jnp.concatenate([along, across, *coefficients(*total(1 - column))], axis=0)
    factors_ref[...] = jnp.concatenate([factors, factors], axis=0)
    stores = []
    part_rows = people // 4
    for part in range(4):
        block = pl.ds(part * part_rows, part_rows)
        solved_ref[block, :] = along * direction_ref[block, :] + across * scaled_ref[block, :]
        stores.append(copies.start(solved_ref.at[block], solved_hbm.at[block]))
    wait_all(stores)


def scores_kernel(norm_scale, factors_ref, own_ref, other_ref, scores_ref):
    columns = own_ref.shape[2]
    column = lax.axis_index("cols")
    for which, rows_ref, place in ((0, own_ref, column), (2, other_ref, 1 - column)):
        along, across = factors_ref[which:which + 1, :], factors_ref[which + 1:which + 2, :]
        here = pl.ds(pl.multiple_of(place * columns, columns), columns)
        scores_ref[:, here] = norm_scale * (along * rows_ref[0] + across * rows_ref[1])


def call(kernel, out_shape, in_specs, out_specs, scratch_shapes=(), limit=VMEM_LIMIT):
    return pl.pallas_call(
        kernel,
        out_shape=out_shape,
        in_specs=in_specs,
        out_specs=out_specs,
        scratch_shapes=list(scratch_shapes),
        compiler_params=pltpu.CompilerParams(vmem_limit_bytes=limit),
    )


def swap(values, axis, devices, step):
    return lax.ppermute(values, axis, [(i, i ^ step) for i in range(devices)])


def after(value, *others):
    return lax.optimization_barrier((value, *others))[0]


def per_device(kinship, relatives, variance, phenotypes, dosage):
    devices = lax.axis_size("samples")
    block_count, positions, tile = kinship.shape[:3]
    people, columns = phenotypes.shape
    variants = dosage.shape[1]
    share_rows = variants // devices
    entries = block_count * (positions - 1)
    capacity = -(-entries // (devices - 1))
    assert capacity <= 2
    hbm = pl.BlockSpec(memory_space=pltpu.HBM)
    anywhere = pl.BlockSpec(memory_space=pl.ANY)
    vmem = pl.BlockSpec(memory_space=pltpu.VMEM)
    smem = pl.BlockSpec(memory_space=pltpu.SMEM)
    float_of = lambda *shape: jax.ShapeDtypeStruct(shape, jnp.float32)
    room = lambda *shape: pltpu.VMEM(shape, jnp.float32)
    full = float_of(people, columns)
    full_room = room(people, columns)
    half = devices // 2
    near_by = list(range(half - 1, 0, -1))
    at_home = lambda *arrays: [pltpu.with_memory_space_constraint(array, pltpu.HBM) for array in arrays]
    kinship, = at_home(kinship)
    tiles_room = pltpu.VMEM((block_count, tile, positions * tile), jnp.bfloat16)
    tiles_out = pltpu.HBM((block_count, tile, positions * tile), jnp.bfloat16)
    full_out = pltpu.HBM((people, columns), jnp.float32)
    direction, direction_kept_hbm, diagonal, norm = call(
        direction_kernel,
        [full, full_out, pltpu.HBM((people, 1), jnp.float32), float_of(SUBLANES, columns)],
        [hbm] * 3,
        [vmem, hbm, hbm, vmem],
        [
            room(*kinship.shape), room(block_count, tile), full_room, room(people, 1),
            pltpu.SemaphoreType.DMA((3 * block_count + 2,)),
        ],
    )(
        kinship, *at_home(variance.reshape(block_count, tile), phenotypes)
    )
    def to_mates(blocks):
        return [swap(blocks[k - 1], "samples", devices, k) for k in near_by]

    bits = half.bit_length() - 1
    even = [sum(((i >> b) & 1) << (bits - b) for b in range(bits)) for i in range(half)]
    steps = [2 << i for i in range(bits)]
    other_dosage = with_layout_constraint(swap(after(dosage, direction), "cols", 2, 1), Layout((0, 1)))
    table, forward, *outgoing = call(
        functools.partial(route_kernel, devices, capacity, block_count),
        [
            jax.ShapeDtypeStruct((4, max(entries, devices)), jnp.int32),
            jax.ShapeDtypeStruct((capacity, half), jnp.int32),
        ] + [float_of(capacity, tile, columns)] * (half - 1),
        [smem, vmem, anywhere],
        [smem, smem] + [vmem] * (half - 1),
        [pltpu.SMEM((devices,), jnp.int32), pltpu.SMEM((devices,), jnp.int32)],
    )(relatives.T, direction, other_dosage)
    high, low = call(
        tiles_kernel, [tiles_out] * 2, [hbm], [hbm] * 2,
        [room(*kinship.shape), tiles_room, tiles_room, pltpu.SemaphoreType.DMA((3,))],
    )(kinship)

    parts = jax.ShapeDtypeStruct((2, variants, people), jnp.bfloat16)
    large = VMEM_LIMIT if variants <= people else LARGE_VMEM
    grouped = call(
        functools.partial(group_kernel, even), [parts] * 2, [vmem] * 2, [vmem] * 2, limit=large
    )(after(dosage, table).T, other_dosage.T)

    products = float_of(half, 2 * share_rows, columns)

    def add_step(kept, taken, *gates):
        rows = float_of(kept.shape[0] // 2, 2 * share_rows, columns)
        return call(
            add_kernel, [rows] * 2, [vmem] * 2 + [hbm] * len(gates), [vmem] * 2
        )(kept, taken, *at_home(*gates))

    partner = swap(direction, "samples", devices, half)
    near = to_mates(outgoing)
    direction_even, direction_odd = call(
        score_kernel, [products] * 2, [vmem] * 3, [vmem] * 2, limit=large
    )(*grouped, direction)
    direction_share = swap(direction_odd, "samples", devices, 1)
    far = to_mates(call(
        forward_kernel,
        [float_of(capacity, tile, columns)] * (half - 1),
        [smem, vmem] + [anywhere] * (half + 1) + [hbm] * 2,
        [vmem] * (half - 1),
    )(forward, partner, *near, direction_even, direction_odd, *at_home(high, low)))
    received = near + far + [partner.reshape(block_count, tile, columns)]
    products_out = pltpu.HBM(products.shape, jnp.float32)
    scaled, handled, outgoing, scaled_even, scaled_odd = call(
        functools.partial(apply_kernel, devices, capacity),
        [
            full_out, full_out, pltpu.HBM((devices, tile + SUBLANES, columns), jnp.float32), products_out, products_out,
        ],
        [smem, hbm, hbm, hbm] + [vmem] * (devices + 3) + [anywhere],
        [hbm] * 5,
        [
            room(devices * capacity + block_count, tile, columns), tiles_room, tiles_room, room(people, 1), full_room,
            full_room, room(SUBLANES, columns), room(*products.shape), room(*products.shape),
            pltpu.SemaphoreType.DMA((2 * devices + 7,)),
        ],
        limit=large,
    )(table, high, low, diagonal, direction, norm, *grouped, *received, direction_share)
    later = lax.all_to_all(outgoing, "samples", split_axis=0, concat_axis=0, tiled=True)
    scaled_share = swap(scaled_odd, "samples", devices, 1)
    direction_kept, direction_given = add_step(direction_even, direction_share)
    direction_taken = swap(after(direction_given, scaled), "samples", devices, steps[0])
    sums = call(
        functools.partial(curvature_kernel, devices),
        pltpu.HBM((2 * devices, SUBLANES, columns), jnp.float32),
        [smem] + [hbm] * 6 + [anywhere],
        hbm,
        [
            room(2 * devices, SUBLANES, columns), tiles_room, tiles_room, full_room, room(people, 1), full_room,
            full_room, room(devices, tile + SUBLANES, columns), pltpu.SemaphoreType.DMA((8,)),
        ],
    )(table, *at_home(high, low, direction_kept_hbm, diagonal, scaled, handled), later)
    all_sums = lax.all_to_all(sums, ("samples", "cols"), split_axis=0, concat_axis=0, tiled=True)
    scaled_kept, scaled_taken = scaled_even, scaled_share
    for step in steps:
        scaled_kept, scaled_given = add_step(scaled_kept, scaled_taken, sums)
        scaled_taken = swap(scaled_given, "samples", devices, step)
    for step in steps[1:]:
        direction_kept, direction_given = add_step(direction_kept, direction_taken, sums)
        direction_taken = swap(direction_given, "samples", devices, step)
    rows = float_of(2, share_rows, columns)
    own_scores, other_scores = call(
        last_add_kernel, [rows] * 2, [vmem] * 4, [vmem] * 2
    )(direction_kept, direction_taken, scaled_kept, scaled_taken)
    solved, factors = call(
        functools.partial(solved_kernel, devices),
        [full, float_of(SUBLANES, columns)],
        [vmem] * 3,
        [hbm, vmem],
        [full_room, pltpu.SemaphoreType.DMA((4,))],
    )(direction_kept_hbm, scaled, all_sums)
    scores = call(
        functools.partial(scores_kernel, 1.0 / math.sqrt(people * devices)),
        float_of(share_rows, 2 * columns), [vmem] * 3, vmem,
    )(factors, own_scores, swap(other_scores, "cols", 2, 1))
    return (solved, scores)


def solution(mesh):
    return jax.shard_map(
        per_device,
        mesh=mesh,
        in_specs=(
            P(("groups", "samples"), None, None, None),
            P("groups", None),
            P(("groups", "samples")),
            P(("groups", "samples"), "cols"),
            P(("groups", "samples"), "cols"),
        ),
        out_specs=(P(("groups", "samples"), "cols"), P(("groups", "cols", "samples"), None)),
        check_vma=False,
    )
```

```python
import functools
import math

import jax
import jax.numpy as jnp
from jax import lax
from jax.experimental import pallas as pl
from jax.experimental.layout import Layout, with_layout_constraint
from jax.experimental.pallas import tpu as pltpu
from jax.sharding import PartitionSpec as P

VMEM_LIMIT = 24 * 1024 * 1024
LARGE_VMEM = 56 * 1024 * 1024
SUBLANES = 8


def split(values):
    high = values.astype(jnp.bfloat16)
    low = (values - high.astype(jnp.float32)).astype(jnp.bfloat16)
    return high, low


def dot(left, right):
    return jnp.dot(left, right, preferred_element_type=jnp.float32)


def on_diagonal(size):
    rows = lax.broadcasted_iota(jnp.int32, (size, size), 0)
    return rows == lax.broadcasted_iota(jnp.int32, (size, size), 1)


def split_tiles(kinship_ref, high_ref, low_ref):
    block_count, positions, tile = kinship_ref.shape[:3]
    diagonal_mask = on_diagonal(tile)
    for row in range(block_count):
        for position in range(positions):
            values = kinship_ref[row, position]
            if position == 0:
                values = jnp.where(diagonal_mask, 0.0, values)
            high, low = split(values)
            high_ref[row, :, pl.ds(position * tile, tile)] = high
            low_ref[row, :, pl.ds(position * tile, tile)] = low


def product(high, low, blocks):
    parts = [split(block) for block in blocks]
    blocks_high = jnp.concatenate([part[0] for part in parts], axis=0)
    blocks_low = jnp.concatenate([part[1] for part in parts], axis=0)
    return dot(high, blocks_high) + (dot(low, blocks_high) + dot(high, blocks_low))


def column_sums(values):
    rows, columns = values.shape
    return jnp.sum(values.reshape(rows // SUBLANES, SUBLANES, columns), axis=0)


class Copies:
    def __init__(self, semaphores):
        self.semaphores = semaphores
        self.count = 0

    def start(self, source, target):
        copy = pltpu.make_async_copy(source, target, self.semaphores.at[self.count])
        self.count += 1
        copy.start()
        return copy


def wait_all(copies):
    for copy in copies:
        copy.wait()


def quotient(value, divisor):
    if divisor & (divisor - 1) == 0:
        return lax.shift_right_logical(value, jnp.int32(divisor.bit_length() - 1))
    return lax.div(value, jnp.int32(divisor))


def direction_kernel(kinship_hbm, variance_hbm, phenotypes_hbm, direction_ref, direction_hbm, diagonal_hbm, sums_ref,
                     kinship_ref, variance_ref, phenotypes_ref, diagonal_ref, semaphores):
    block_count, positions, tile = kinship_ref.shape[:3]
    copies = Copies(semaphores)
    loads = [copies.start(variance_hbm, variance_ref)]
    for row in range(block_count):
        block = pl.ds(row * tile, tile)
        loads.append(copies.start(kinship_hbm.at[row], kinship_ref.at[row]))
        loads.append(copies.start(phenotypes_hbm.at[block], phenotypes_ref.at[block]))
    stores = []
    norm = jnp.zeros((SUBLANES, direction_ref.shape[1]), jnp.float32)
    diagonal_mask = on_diagonal(tile)
    loads[0].wait()
    for row in range(block_count):
        wait_all(loads[1 + 2 * row:3 + 2 * row])
        block = pl.ds(row * tile, tile)
        total = jnp.where(diagonal_mask, variance_ref[row:row + 1, :], kinship_ref[row, 0])
        for position in range(1, positions):
            total = total + kinship_ref[row, position]
        diagonal = jnp.sum(total, axis=1, keepdims=True)
        diagonal_ref[block, :] = diagonal
        here = phenotypes_ref[block, :] * (1.0 / diagonal)
        direction_ref[block, :] = here
        norm = norm + column_sums(here * phenotypes_ref[block, :])
        stores.append(copies.start(direction_ref.at[block], direction_hbm.at[block]))
    stores.append(copies.start(diagonal_ref, diagonal_hbm))
    row_ids = lax.broadcasted_iota(jnp.int32, norm.shape, 0)
    sums_ref[...] = jnp.where(row_ids == 0, jnp.sum(norm, axis=0, keepdims=True), 0.0)
    wait_all(stores)


def tiles_kernel(kinship_hbm, high_hbm, low_hbm, kinship_ref, high_ref, low_ref, semaphores):
    copies = Copies(semaphores)
    copies.start(kinship_hbm, kinship_ref).wait()
    split_tiles(kinship_ref, high_ref, low_ref)
    wait_all([copies.start(high_ref, high_hbm), copies.start(low_ref, low_hbm)])


def route_kernel(devices, capacity, block_count, list_ref, direction_ref, gate_ref, table_ref, forward_ref, *refs):
    half = devices // 2
    outgoing_refs, (first_ref, last_ref) = refs[:half - 1], refs[half - 1:]
    positions = list_ref.shape[0] + 1
    tile = direction_ref.shape[0] // block_count
    me = lax.axis_index("samples")
    partner = me ^ half
    spare = me ^ 1
    top = block_count * block_count

    def collect(device):
        for j in range(devices):
            first_ref[j] = jnp.int32(top)
            last_ref[j] = jnp.int32(-1)
        found = []
        for row in range(block_count):
            for position in range(positions - 1):
                listed = list_ref[position, device * block_count + row]
                live = listed >= 0
                safe = jnp.maximum(listed, 0)
                other = quotient(safe, block_count)
                far_block = safe - other * block_count
                key = jnp.where(device < other, row * block_count + far_block, far_block * block_count + row)
                first_ref[other] = jnp.minimum(first_ref[other], jnp.where(live, key, top))
                last_ref[other] = jnp.maximum(last_ref[other], jnp.where(live, key, -1))
                found.append((live, other, far_block, key))
        return found

    def blocks_for(device, other):
        blocks = []
        for key in (first_ref[other], last_ref[other]):
            safe = jnp.clip(key, 0, top - 1)
            lower = quotient(safe, block_count)
            higher = safe - lower * block_count
            blocks.append(jnp.where(key == safe, jnp.where(device < other, lower, higher), 0))
        return blocks

    collect(partner)
    for k in range(1, half):
        blocks = blocks_for(partner, me ^ k)
        for slot in range(capacity):
            forward_ref[slot, k] = blocks[slot]
    for entry, (live, other, far_block, key) in enumerate(collect(me)):
        first, last = first_ref[other], last_ref[other]
        handled = jnp.where(me < other, first, last)
        weight = jnp.where(first == last, 1, 2)
        slot = jnp.where(key == first, 0, capacity - 1)
        place = jnp.where(other == partner, devices * capacity + far_block, other * capacity + slot)
        table_ref[0, entry] = jnp.where(live, place, spare * capacity)
        table_ref[1, entry] = jnp.where(live, other, spare)
        table_ref[2, entry] = jnp.where(live & (key == handled), weight, 0)
    for other in range(devices):
        blocks = blocks_for(me, other)
        table_ref[3, other] = jnp.where(me < other, blocks[1], blocks[0])
    near = [blocks_for(me, me ^ k) for k in range(1, half)]
    for k in range(1, half):
        for slot in range(capacity):
            start = pl.multiple_of(near[k - 1][slot] * tile, tile)
            outgoing_refs[k - 1][slot] = direction_ref[pl.ds(start, tile), :]


def forward_kernel(forward_ref, partner_ref, *refs):
    capacity, half = forward_ref.shape
    outgoing_refs = refs[1 - half:]
    tile = outgoing_refs[0].shape[1]
    for k in range(1, half):
        for slot in range(capacity):
            start = pl.multiple_of(forward_ref[slot, k] * tile, tile)
            outgoing_refs[k - 1][slot] = partner_ref[pl.ds(start, tile), :]


def gather_received(devices, capacity, received_refs, gathered_ref):
    half = devices // 2
    me = lax.axis_index("samples")
    near_refs, far_refs, partner_ref = received_refs[:half - 1], received_refs[half - 1:-1], received_refs[-1]
    gathered_ref[pl.ds(devices * capacity, partner_ref.shape[0])] = partner_ref[...]
    for i in range(half - 1):
        mate = me ^ (half - 1 - i)
        gathered_ref[pl.ds(mate * capacity, capacity)] = near_refs[i][...]
        gathered_ref[pl.ds((mate ^ half) * capacity, capacity)] = far_refs[i][...]


def score_products(high_ref, low_ref, values, even_ref, odd_ref):
    count, rows = even_ref.shape[:2]
    for odd, out_ref in enumerate((even_ref, odd_ref)):
        for i in range(0, count, 4):
            here = pl.ds(i * rows, 4 * rows)
            total = product(high_ref[odd, here, :], low_ref[odd, here, :], [values])
            out_ref[pl.ds(i, 4)] = total.reshape(4, rows, -1)


def score_kernel(high_ref, low_ref, values_ref, even_ref, odd_ref):
    score_products(high_ref, low_ref, values_ref[...], even_ref, odd_ref)


def apply_kernel(devices, capacity, table_ref, high_hbm, low_hbm, diagonal_hbm, direction_ref, norm_ref, dosage_high_ref,
                 dosage_low_ref, *refs):
    received_refs = refs[:devices - 1]
    (scaled_hbm, handled_hbm, outgoing_hbm, even_hbm, odd_hbm, gathered_ref, high_ref, low_ref, diagonal_ref, scaled_ref,
     handled_ref, sums_ref, even_ref, odd_ref, semaphores) = refs[-15:]
    copies = Copies(semaphores)
    loads = [
        copies.start(high_hbm, high_ref), copies.start(low_hbm, low_ref), copies.start(diagonal_hbm, diagonal_ref)
    ]
    gather_received(devices, capacity, received_refs, gathered_ref)
    wait_all(loads)
    block_count, tile, depth = high_ref.shape
    others = depth // tile - 1
    cross = jnp.zeros(norm_ref.shape, jnp.float32)
    for row in range(block_count):
        block = pl.ds(row * tile, tile)
        here = direction_ref[block, :]
        blocks = [here] + [gathered_ref[table_ref[0, row * others + i]] for i in range(others)]
        mapped = product(high_ref[row], low_ref[row], blocks)
        scaled_ref[block, :] = mapped * (1.0 / diagonal_ref[block, :])
        cross = cross + column_sums(here * mapped)
    row_ids = lax.broadcasted_iota(jnp.int32, cross.shape, 0)
    sums_ref[...] = jnp.where(row_ids == 1, jnp.sum(cross, axis=0, keepdims=True), norm_ref[...])
    stores = [copies.start(scaled_ref, scaled_hbm)]
    for other in range(devices):
        start = pl.multiple_of(table_ref[3, other] * tile, tile)
        stores.append(copies.start(scaled_ref.at[pl.ds(start, tile)], outgoing_hbm.at[other, pl.ds(0, tile)]))
        stores.append(copies.start(sums_ref, outgoing_hbm.at[other, pl.ds(tile, SUBLANES)]))
    score_products(dosage_high_ref, dosage_low_ref, scaled_ref[...], even_ref, odd_ref)
    stores += [copies.start(odd_ref, odd_hbm), copies.start(even_ref, even_hbm)]
    far = pl.ds(tile, depth - tile)
    for row in range(block_count):
        blocks = []
        for i in range(others):
            weight = table_ref[2, row * others + i].astype(jnp.float32)
            blocks.append(weight * gathered_ref[table_ref[0, row * others + i]])
        handled_ref[pl.ds(row * tile, tile), :] = product(high_ref[row, :, far], low_ref[row, :, far], blocks)
    stores.append(copies.start(handled_ref, handled_hbm))
    wait_all(stores)


def curvature_kernel(devices, table_ref, high_hbm, low_hbm, direction_hbm, diagonal_hbm, scaled_hbm, handled_hbm,
                     later_hbm, *refs):
    (sums_hbm, sums_ref, high_ref, low_ref, direction_ref, diagonal_ref, scaled_ref, handled_ref, later_ref,
     semaphores) = refs[-10:]
    block_count, tile, depth = high_ref.shape
    copies = Copies(semaphores)
    wait_all([copies.start(source, target) for source, target in (
        (later_hbm, later_ref), (scaled_hbm, scaled_ref), (direction_hbm, direction_ref), (high_hbm, high_ref),
        (low_hbm, low_ref), (handled_hbm, handled_ref), (diagonal_hbm, diagonal_ref),
    )])
    others = depth // tile - 1
    first_sums = later_ref[0, pl.ds(tile, SUBLANES), :]
    for other in range(1, devices):
        first_sums = first_sums + later_ref[other, pl.ds(tile, SUBLANES), :]
    rho = first_sums[1:2, :] / first_sums[0:1, :]
    norm = jnp.zeros(first_sums.shape, jnp.float32)
    bend = jnp.zeros(first_sums.shape, jnp.float32)
    for row in range(block_count):
        block = pl.ds(row * tile, tile)
        here = scaled_ref[block, :] - rho * direction_ref[block, :]
        blocks = [here]
        for i in range(others):
            entry = row * others + i
            weight = table_ref[2, entry].astype(jnp.float32)
            blocks.append(weight * later_ref[table_ref[1, entry], pl.ds(0, tile), :])
        mapped = product(high_ref[row], low_ref[row], blocks) - rho * handled_ref[block, :]
        norm = norm + column_sums(here * here * diagonal_ref[block, :])
        bend = bend + column_sums(here * mapped)
    row_ids = lax.broadcasted_iota(jnp.int32, first_sums.shape, 0)
    sums = jnp.where(row_ids == 2, jnp.sum(norm, axis=0, keepdims=True), first_sums)
    sums = jnp.where(row_ids == 3, jnp.sum(bend, axis=0, keepdims=True), sums)
    for i in range(2 * devices):
        sums_ref[i] = sums
    copies.start(sums_ref, sums_hbm).wait()


def add_kernel(kept_ref, taken_ref, *refs):
    near_ref, far_ref = refs[-2:]
    count = near_ref.shape[0]
    near_ref[...] = kept_ref[pl.ds(0, count)] + taken_ref[pl.ds(0, count)]
    far_ref[...] = kept_ref[pl.ds(count, count)] + taken_ref[pl.ds(count, count)]


def last_add_kernel(first_kept_ref, first_taken_ref, second_kept_ref, second_taken_ref, own_ref, other_ref):
    rows = own_ref.shape[1]
    for i, (kept_ref, taken_ref) in enumerate(
        ((first_kept_ref, first_taken_ref), (second_kept_ref, second_taken_ref))
    ):
        own_ref[i] = kept_ref[0, pl.ds(0, rows), :] + taken_ref[0, pl.ds(0, rows), :]
        other_ref[i] = kept_ref[0, pl.ds(rows, rows), :] + taken_ref[0, pl.ds(rows, rows), :]


def group_kernel(order, own_ref, other_ref, high_ref, low_ref):
    rows = own_ref.shape[0] // (2 * len(order))
    me = lax.axis_index("samples")
    for odd in range(2):
        for i, distance in enumerate(order):
            start = pl.multiple_of((me ^ distance ^ odd) * rows, rows)
            for j, dosage_ref in enumerate((own_ref, other_ref)):
                high, low = split(dosage_ref[pl.ds(start, rows), :])
                here = pl.ds((2 * i + j) * rows, rows)
                high_ref[odd, here, :] = high
                low_ref[odd, here, :] = low


def coefficients(sums, shared):
    norm, cross = sums[0:1, :], sums[1:2, :]
    later_norm, bend = shared[2:3, :], shared[3:4, :]
    curve = norm + cross
    ratio = later_norm / curve
    step = jnp.where(later_norm > 0, later_norm / (later_norm + bend - later_norm * ratio), 0.0)
    start = norm / curve
    return start * (1.0 + step * (ratio + cross / norm)), -start * step


def solved_kernel(devices, direction_ref, scaled_ref, sums_ref, solved_hbm, factors_ref, solved_ref, semaphores):
    people, columns = direction_ref.shape
    column = lax.axis_index("cols")
    copies = Copies(semaphores)

    def total(which):
        sums = sums_ref[which]
        shared = sums
        for i in range(1, devices):
            shared = shared + sums_ref[2 * i + which]
        return sums, shared

    along, across = coefficients(*total(column))
    factors = jnp.concatenate([along, across, *coefficients(*total(1 - column))], axis=0)
    factors_ref[...] = jnp.concatenate([factors, factors], axis=0)
    stores = []
    part_rows = people // 4
    for part in range(4):
        block = pl.ds(part * part_rows, part_rows)
        solved_ref[block, :] = along * direction_ref[block, :] + across * scaled_ref[block, :]
        stores.append(copies.start(solved_ref.at[block], solved_hbm.at[block]))
    wait_all(stores)


def scores_kernel(norm_scale, factors_ref, own_ref, other_ref, scores_ref):
    columns = own_ref.shape[2]
    column = lax.axis_index("cols")
    for which, rows_ref, place in ((0, own_ref, column), (2, other_ref, 1 - column)):
        along, across = factors_ref[which:which + 1, :], factors_ref[which + 1:which + 2, :]
        here = pl.ds(pl.multiple_of(place * columns, columns), columns)
        scores_ref[:, here] = norm_scale * (along * rows_ref[0] + across * rows_ref[1])


def call(kernel, out_shape, in_specs, out_specs, scratch_shapes=(), limit=VMEM_LIMIT):
    return pl.pallas_call(
        kernel,
        out_shape=out_shape,
        in_specs=in_specs,
        out_specs=out_specs,
        scratch_shapes=list(scratch_shapes),
        compiler_params=pltpu.CompilerParams(vmem_limit_bytes=limit),
    )


def swap(values, axis, devices, step):
    return lax.ppermute(values, axis, [(i, i ^ step) for i in range(devices)])


def after(value, *others):
    return lax.optimization_barrier((value, *others))[0]


def per_device(kinship, relatives, variance, phenotypes, dosage):
    devices = lax.axis_size("samples")
    block_count, positions, tile = kinship.shape[:3]
    people, columns = phenotypes.shape
    variants = dosage.shape[1]
    share_rows = variants // devices
    entries = block_count * (positions - 1)
    capacity = -(-entries // (devices - 1))
    assert capacity <= 2
    hbm = pl.BlockSpec(memory_space=pltpu.HBM)
    anywhere = pl.BlockSpec(memory_space=pl.ANY)
    vmem = pl.BlockSpec(memory_space=pltpu.VMEM)
    smem = pl.BlockSpec(memory_space=pltpu.SMEM)
    float_of = lambda *shape: jax.ShapeDtypeStruct(shape, jnp.float32)
    room = lambda *shape: pltpu.VMEM(shape, jnp.float32)
    full = float_of(people, columns)
    full_room = room(people, columns)
    half = devices // 2
    near_by = list(range(half - 1, 0, -1))
    at_home = lambda *arrays: [pltpu.with_memory_space_constraint(array, pltpu.HBM) for array in arrays]
    kinship, = at_home(kinship)
    tiles_room = pltpu.VMEM((block_count, tile, positions * tile), jnp.bfloat16)
    tiles_out = pltpu.HBM((block_count, tile, positions * tile), jnp.bfloat16)
    full_out = pltpu.HBM((people, columns), jnp.float32)
    direction, direction_kept_hbm, diagonal, norm = call(
        direction_kernel,
        [full, full_out, pltpu.HBM((people, 1), jnp.float32), float_of(SUBLANES, columns)],
        [hbm] * 3,
        [vmem, hbm, hbm, vmem],
        [
            room(*kinship.shape), room(block_count, tile), full_room, room(people, 1),
            pltpu.SemaphoreType.DMA((3 * block_count + 2,)),
        ],
    )(
        kinship, *at_home(variance.reshape(block_count, tile), phenotypes)
    )
    def to_mates(blocks):
        return [swap(blocks[k - 1], "samples", devices, k) for k in near_by]

    bits = half.bit_length() - 1
    even = [sum(((i >> b) & 1) << (bits - b) for b in range(bits)) for i in range(half)]
    steps = [2 << i for i in range(bits)]
    other_dosage = with_layout_constraint(swap(after(dosage, direction), "cols", 2, 1), Layout((0, 1)))
    table, forward, *outgoing = call(
        functools.partial(route_kernel, devices, capacity, block_count),
        [
            jax.ShapeDtypeStruct((4, max(entries, devices)), jnp.int32),
            jax.ShapeDtypeStruct((capacity, half), jnp.int32),
        ] + [float_of(capacity, tile, columns)] * (half - 1),
        [smem, vmem, anywhere],
        [smem, smem] + [vmem] * (half - 1),
        [pltpu.SMEM((devices,), jnp.int32), pltpu.SMEM((devices,), jnp.int32)],
    )(relatives.T, direction, other_dosage)
    high, low = call(
        tiles_kernel, [tiles_out] * 2, [hbm], [hbm] * 2,
        [room(*kinship.shape), tiles_room, tiles_room, pltpu.SemaphoreType.DMA((3,))],
    )(kinship)

    parts = jax.ShapeDtypeStruct((2, variants, people), jnp.bfloat16)
    large = VMEM_LIMIT if variants <= people else LARGE_VMEM
    grouped = call(
        functools.partial(group_kernel, even), [parts] * 2, [vmem] * 2, [vmem] * 2, limit=large
    )(after(dosage, table).T, other_dosage.T)

    products = float_of(half, 2 * share_rows, columns)

    def add_step(kept, taken, *gates):
        rows = float_of(kept.shape[0] // 2, 2 * share_rows, columns)
        return call(
            add_kernel, [rows] * 2, [vmem] * 2 + [hbm] * len(gates), [vmem] * 2
        )(kept, taken, *at_home(*gates))

    partner = swap(direction, "samples", devices, half)
    near = to_mates(outgoing)
    direction_even, direction_odd = call(
        score_kernel, [products] * 2, [vmem] * 3, [vmem] * 2, limit=large
    )(*grouped, direction)
    direction_share = swap(direction_odd, "samples", devices, 1)
    far = to_mates(call(
        forward_kernel,
        [float_of(capacity, tile, columns)] * (half - 1),
        [smem, vmem] + [anywhere] * (half + 1) + [hbm] * 2,
        [vmem] * (half - 1),
    )(forward, partner, *near, direction_even, direction_odd, *at_home(high, low)))
    received = near + far + [partner.reshape(block_count, tile, columns)]
    products_out = pltpu.HBM(products.shape, jnp.float32)
    scaled, handled, outgoing, scaled_even, scaled_odd = call(
        functools.partial(apply_kernel, devices, capacity),
        [
            full_out, full_out, pltpu.HBM((devices, tile + SUBLANES, columns), jnp.float32), products_out, products_out,
        ],
        [smem, hbm, hbm, hbm] + [vmem] * (devices + 3) + [anywhere],
        [hbm] * 5,
        [
            room(devices * capacity + block_count, tile, columns), tiles_room, tiles_room, room(people, 1), full_room,
            full_room, room(SUBLANES, columns), room(*products.shape), room(*products.shape),
            pltpu.SemaphoreType.DMA((2 * devices + 7,)),
        ],
        limit=large,
    )(table, high, low, diagonal, direction, norm, *grouped, *received, direction_share)
    later = lax.all_to_all(outgoing, "samples", split_axis=0, concat_axis=0, tiled=True)
    scaled_share = swap(scaled_odd, "samples", devices, 1)
    direction_kept, direction_given = add_step(direction_even, direction_share)
    direction_taken = swap(after(direction_given, scaled), "samples", devices, steps[0])
    scaled_kept, scaled_given = add_step(scaled_even, scaled_share)
    scaled_taken = swap(scaled_given, "samples", devices, steps[0])
    sums = call(
        functools.partial(curvature_kernel, devices),
        pltpu.HBM((2 * devices, SUBLANES, columns), jnp.float32),
        [smem] + [hbm] * 6 + [anywhere] * 2,
        hbm,
        [
            room(2 * devices, SUBLANES, columns), tiles_room, tiles_room, full_room, room(people, 1), full_room,
            full_room, room(devices, tile + SUBLANES, columns), pltpu.SemaphoreType.DMA((8,)),
        ],
    )(table, *at_home(high, low, direction_kept_hbm, diagonal, scaled, handled), later, scaled_given)
    all_sums = lax.all_to_all(sums, ("samples", "cols"), split_axis=0, concat_axis=0, tiled=True)
    for step in steps[1:]:
        scaled_kept, scaled_given = add_step(scaled_kept, scaled_taken, sums)
        scaled_taken = swap(scaled_given, "samples", devices, step)
    for step in steps[1:]:
        direction_kept, direction_given = add_step(direction_kept, direction_taken, sums)
        direction_taken = swap(direction_given, "samples", devices, step)
    rows = float_of(2, share_rows, columns)
    own_scores, other_scores = call(
        last_add_kernel, [rows] * 2, [vmem] * 4, [vmem] * 2
    )(direction_kept, direction_taken, scaled_kept, scaled_taken)
    solved, factors = call(
        functools.partial(solved_kernel, devices),
        [full, float_of(SUBLANES, columns)],
        [vmem] * 3,
        [hbm, vmem],
        [full_room, pltpu.SemaphoreType.DMA((4,))],
    )(direction_kept_hbm, scaled, all_sums)
    scores = call(
        functools.partial(scores_kernel, 1.0 / math.sqrt(people * devices)),
        float_of(share_rows, 2 * columns), [vmem] * 3, vmem,
    )(factors, own_scores, swap(other_scores, "cols", 2, 1))
    return (solved, scores)


def solution(mesh):
    return jax.shard_map(
        per_device,
        mesh=mesh,
        in_specs=(
            P(("groups", "samples"), None, None, None),
            P("groups", None),
            P(("groups", "samples")),
            P(("groups", "samples"), "cols"),
            P(("groups", "samples"), "cols"),
        ),
        out_specs=(P(("groups", "samples"), "cols"), P(("groups", "cols", "samples"), None)),
        check_vma=False,
    )
```

```python
import functools
import math

import jax
import jax.numpy as jnp
from jax import lax
from jax.experimental import pallas as pl
from jax.experimental.layout import Layout, with_layout_constraint
from jax.experimental.pallas import tpu as pltpu
from jax.sharding import PartitionSpec as P

VMEM_LIMIT = 24 * 1024 * 1024
LARGE_VMEM = 56 * 1024 * 1024
SUBLANES = 8


def split(values):
    high = values.astype(jnp.bfloat16)
    low = (values - high.astype(jnp.float32)).astype(jnp.bfloat16)
    return high, low


def dot(left, right):
    return jnp.dot(left, right, preferred_element_type=jnp.float32)


def on_diagonal(size):
    rows = lax.broadcasted_iota(jnp.int32, (size, size), 0)
    return rows == lax.broadcasted_iota(jnp.int32, (size, size), 1)


def split_tiles(kinship_ref, high_ref, low_ref):
    block_count, positions, tile = kinship_ref.shape[:3]
    diagonal_mask = on_diagonal(tile)
    for row in range(block_count):
        for position in range(positions):
            values = kinship_ref[row, position]
            if position == 0:
                values = jnp.where(diagonal_mask, 0.0, values)
            high, low = split(values)
            high_ref[row, :, pl.ds(position * tile, tile)] = high
            low_ref[row, :, pl.ds(position * tile, tile)] = low


def product(high, low, blocks):
    parts = [split(block) for block in blocks]
    blocks_high = jnp.concatenate([part[0] for part in parts], axis=0)
    blocks_low = jnp.concatenate([part[1] for part in parts], axis=0)
    return dot(high, blocks_high) + (dot(low, blocks_high) + dot(high, blocks_low))


def column_sums(values):
    rows, columns = values.shape
    return jnp.sum(values.reshape(rows // SUBLANES, SUBLANES, columns), axis=0)


class Copies:
    def __init__(self, semaphores):
        self.semaphores = semaphores
        self.count = 0

    def start(self, source, target):
        copy = pltpu.make_async_copy(source, target, self.semaphores.at[self.count])
        self.count += 1
        copy.start()
        return copy


def wait_all(copies):
    for copy in copies:
        copy.wait()


def quotient(value, divisor):
    if divisor & (divisor - 1) == 0:
        return lax.shift_right_logical(value, jnp.int32(divisor.bit_length() - 1))
    return lax.div(value, jnp.int32(divisor))


def direction_kernel(kinship_hbm, variance_hbm, phenotypes_hbm, direction_ref, direction_hbm, diagonal_hbm, sums_ref,
                     kinship_ref, variance_ref, phenotypes_ref, diagonal_ref, semaphores):
    block_count, positions, tile = kinship_ref.shape[:3]
    copies = Copies(semaphores)
    loads = [copies.start(variance_hbm, variance_ref)]
    for row in range(block_count):
        block = pl.ds(row * tile, tile)
        loads.append(copies.start(kinship_hbm.at[row], kinship_ref.at[row]))
        loads.append(copies.start(phenotypes_hbm.at[block], phenotypes_ref.at[block]))
    stores = []
    norm = jnp.zeros((SUBLANES, direction_ref.shape[1]), jnp.float32)
    diagonal_mask = on_diagonal(tile)
    loads[0].wait()
    for row in range(block_count):
        wait_all(loads[1 + 2 * row:3 + 2 * row])
        block = pl.ds(row * tile, tile)
        total = jnp.where(diagonal_mask, variance_ref[row:row + 1, :], kinship_ref[row, 0])
        for position in range(1, positions):
            total = total + kinship_ref[row, position]
        diagonal = jnp.sum(total, axis=1, keepdims=True)
        diagonal_ref[block, :] = diagonal
        here = phenotypes_ref[block, :] * (1.0 / diagonal)
        direction_ref[block, :] = here
        norm = norm + column_sums(here * phenotypes_ref[block, :])
        stores.append(copies.start(direction_ref.at[block], direction_hbm.at[block]))
    stores.append(copies.start(diagonal_ref, diagonal_hbm))
    row_ids = lax.broadcasted_iota(jnp.int32, norm.shape, 0)
    sums_ref[...] = jnp.where(row_ids == 0, jnp.sum(norm, axis=0, keepdims=True), 0.0)
    wait_all(stores)


def tiles_kernel(kinship_hbm, high_hbm, low_hbm, kinship_ref, high_ref, low_ref, semaphores):
    copies = Copies(semaphores)
    copies.start(kinship_hbm, kinship_ref).wait()
    split_tiles(kinship_ref, high_ref, low_ref)
    wait_all([copies.start(high_ref, high_hbm), copies.start(low_ref, low_hbm)])


def route_kernel(devices, capacity, block_count, list_ref, direction_ref, gate_ref, table_ref, forward_ref, *refs):
    half = devices // 2
    outgoing_refs, (first_ref, last_ref) = refs[:half - 1], refs[half - 1:]
    positions = list_ref.shape[0] + 1
    tile = direction_ref.shape[0] // block_count
    me = lax.axis_index("samples")
    partner = me ^ half
    spare = me ^ 1
    top = block_count * block_count

    def collect(device):
        for j in range(devices):
            first_ref[j] = jnp.int32(top)
            last_ref[j] = jnp.int32(-1)
        found = []
        for row in range(block_count):
            for position in range(positions - 1):
                listed = list_ref[position, device * block_count + row]
                live = listed >= 0
                safe = jnp.maximum(listed, 0)
                other = quotient(safe, block_count)
                far_block = safe - other * block_count
                key = jnp.where(device < other, row * block_count + far_block, far_block * block_count + row)
                first_ref[other] = jnp.minimum(first_ref[other], jnp.where(live, key, top))
                last_ref[other] = jnp.maximum(last_ref[other], jnp.where(live, key, -1))
                found.append((live, other, far_block, key))
        return found

    def blocks_for(device, other):
        blocks = []
        for key in (first_ref[other], last_ref[other]):
            safe = jnp.clip(key, 0, top - 1)
            lower = quotient(safe, block_count)
            higher = safe - lower * block_count
            blocks.append(jnp.where(key == safe, jnp.where(device < other, lower, higher), 0))
        return blocks

    collect(partner)
    for k in range(1, half):
        blocks = blocks_for(partner, me ^ k)
        for slot in range(capacity):
            forward_ref[slot, k] = blocks[slot]
    for entry, (live, other, far_block, key) in enumerate(collect(me)):
        first, last = first_ref[other], last_ref[other]
        handled = jnp.where(me < other, first, last)
        weight = jnp.where(first == last, 1, 2)
        slot = jnp.where(key == first, 0, capacity - 1)
        place = jnp.where(other == partner, devices * capacity + far_block, other * capacity + slot)
        table_ref[0, entry] = jnp.where(live, place, spare * capacity)
        table_ref[1, entry] = jnp.where(live, other, spare)
        table_ref[2, entry] = jnp.where(live & (key == handled), weight, 0)
    for other in range(devices):
        blocks = blocks_for(me, other)
        table_ref[3, other] = jnp.where(me < other, blocks[1], blocks[0])
    near = [blocks_for(me, me ^ k) for k in range(1, half)]
    for k in range(1, half):
        for slot in range(capacity):
            start = pl.multiple_of(near[k - 1][slot] * tile, tile)
            outgoing_refs[k - 1][slot] = direction_ref[pl.ds(start, tile), :]


def forward_kernel(forward_ref, partner_ref, *refs):
    capacity, half = forward_ref.shape
    outgoing_refs = refs[1 - half:]
    tile = outgoing_refs[0].shape[1]
    for k in range(1, half):
        for slot in range(capacity):
            start = pl.multiple_of(forward_ref[slot, k] * tile, tile)
            outgoing_refs[k - 1][slot] = partner_ref[pl.ds(start, tile), :]


def gather_received(devices, capacity, received_refs, gathered_ref):
    half = devices // 2
    me = lax.axis_index("samples")
    near_refs, far_refs, partner_ref = received_refs[:half - 1], received_refs[half - 1:-1], received_refs[-1]
    gathered_ref[pl.ds(devices * capacity, partner_ref.shape[0])] = partner_ref[...]
    for i in range(half - 1):
        mate = me ^ (half - 1 - i)
        gathered_ref[pl.ds(mate * capacity, capacity)] = near_refs[i][...]
        gathered_ref[pl.ds((mate ^ half) * capacity, capacity)] = far_refs[i][...]


def score_products(high_ref, low_ref, values, even_ref, odd_ref):
    count, rows = even_ref.shape[:2]
    for odd, out_ref in enumerate((even_ref, odd_ref)):
        for i in range(0, count, 4):
            here = pl.ds(i * rows, 4 * rows)
            total = product(high_ref[odd, here, :], low_ref[odd, here, :], [values])
            out_ref[pl.ds(i, 4)] = total.reshape(4, rows, -1)


def score_kernel(high_ref, low_ref, values_ref, even_ref, odd_ref):
    score_products(high_ref, low_ref, values_ref[...], even_ref, odd_ref)


def apply_kernel(devices, capacity, table_ref, high_ref, low_ref, diagonal_ref, direction_ref, norm_ref, dosage_high_ref,
                 dosage_low_ref, *refs):
    received_refs = refs[:devices - 1]
    (scaled_hbm, handled_hbm, outgoing_hbm, even_hbm, odd_hbm, gathered_ref, scaled_ref, handled_ref, sums_ref, even_ref,
     odd_ref, semaphores) = refs[-12:]
    copies = Copies(semaphores)
    gather_received(devices, capacity, received_refs, gathered_ref)
    block_count, tile, depth = high_ref.shape
    others = depth // tile - 1
    cross = jnp.zeros(norm_ref.shape, jnp.float32)
    for row in range(block_count):
        block = pl.ds(row * tile, tile)
        here = direction_ref[block, :]
        blocks = [here] + [gathered_ref[table_ref[0, row * others + i]] for i in range(others)]
        mapped = product(high_ref[row], low_ref[row], blocks)
        scaled_ref[block, :] = mapped * (1.0 / diagonal_ref[block, :])
        cross = cross + column_sums(here * mapped)
    row_ids = lax.broadcasted_iota(jnp.int32, cross.shape, 0)
    sums_ref[...] = jnp.where(row_ids == 1, jnp.sum(cross, axis=0, keepdims=True), norm_ref[...])
    stores = [copies.start(scaled_ref, scaled_hbm)]
    for other in range(devices):
        start = pl.multiple_of(table_ref[3, other] * tile, tile)
        stores.append(copies.start(scaled_ref.at[pl.ds(start, tile)], outgoing_hbm.at[other, pl.ds(0, tile)]))
        stores.append(copies.start(sums_ref, outgoing_hbm.at[other, pl.ds(tile, SUBLANES)]))
    score_products(dosage_high_ref, dosage_low_ref, scaled_ref[...], even_ref, odd_ref)
    stores += [copies.start(odd_ref, odd_hbm), copies.start(even_ref, even_hbm)]
    far = pl.ds(tile, depth - tile)
    for row in range(block_count):
        blocks = []
        for i in range(others):
            weight = table_ref[2, row * others + i].astype(jnp.float32)
            blocks.append(weight * gathered_ref[table_ref[0, row * others + i]])
        handled_ref[pl.ds(row * tile, tile), :] = product(high_ref[row, :, far], low_ref[row, :, far], blocks)
    stores.append(copies.start(handled_ref, handled_hbm))
    wait_all(stores)


def curvature_kernel(devices, table_ref, high_ref, low_ref, direction_ref, diagonal_ref, scaled_ref, handled_hbm,
                     later_ref, *refs):
    sums_hbm, sums_ref, handled_ref, semaphores = refs[-4:]
    block_count, tile, depth = high_ref.shape
    copies = Copies(semaphores)
    load = copies.start(handled_hbm, handled_ref)
    others = depth // tile - 1
    first_sums = later_ref[0, pl.ds(tile, SUBLANES), :]
    for other in range(1, devices):
        first_sums = first_sums + later_ref[other, pl.ds(tile, SUBLANES), :]
    rho = first_sums[1:2, :] / first_sums[0:1, :]
    norm = jnp.zeros(first_sums.shape, jnp.float32)
    bend = jnp.zeros(first_sums.shape, jnp.float32)
    for row in range(block_count):
        block = pl.ds(row * tile, tile)
        here = scaled_ref[block, :] - rho * direction_ref[block, :]
        blocks = [here]
        for i in range(others):
            entry = row * others + i
            weight = table_ref[2, entry].astype(jnp.float32)
            blocks.append(weight * later_ref[table_ref[1, entry], pl.ds(0, tile), :])
        mapped = product(high_ref[row], low_ref[row], blocks)
        if row == 0:
            load.wait()
        mapped = mapped - rho * handled_ref[block, :]
        norm = norm + column_sums(here * here * diagonal_ref[block, :])
        bend = bend + column_sums(here * mapped)
    row_ids = lax.broadcasted_iota(jnp.int32, first_sums.shape, 0)
    sums = jnp.where(row_ids == 2, jnp.sum(norm, axis=0, keepdims=True), first_sums)
    sums = jnp.where(row_ids == 3, jnp.sum(bend, axis=0, keepdims=True), sums)
    for i in range(2 * devices):
        sums_ref[i] = sums
    copies.start(sums_ref, sums_hbm).wait()


def add_kernel(kept_ref, taken_ref, *refs):
    near_ref, far_ref = refs[-2:]
    count = near_ref.shape[0]
    near_ref[...] = kept_ref[pl.ds(0, count)] + taken_ref[pl.ds(0, count)]
    far_ref[...] = kept_ref[pl.ds(count, count)] + taken_ref[pl.ds(count, count)]


def last_add_kernel(first_kept_ref, first_taken_ref, second_kept_ref, second_taken_ref, own_ref, other_ref):
    rows = own_ref.shape[1]
    for i, (kept_ref, taken_ref) in enumerate(
        ((first_kept_ref, first_taken_ref), (second_kept_ref, second_taken_ref))
    ):
        own_ref[i] = kept_ref[0, pl.ds(0, rows), :] + taken_ref[0, pl.ds(0, rows), :]
        other_ref[i] = kept_ref[0, pl.ds(rows, rows), :] + taken_ref[0, pl.ds(rows, rows), :]


def group_kernel(order, own_ref, other_ref, high_ref, low_ref):
    rows = own_ref.shape[0] // (2 * len(order))
    me = lax.axis_index("samples")
    for odd in range(2):
        for i, distance in enumerate(order):
            start = pl.multiple_of((me ^ distance ^ odd) * rows, rows)
            for j, dosage_ref in enumerate((own_ref, other_ref)):
                high, low = split(dosage_ref[pl.ds(start, rows), :])
                here = pl.ds((2 * i + j) * rows, rows)
                high_ref[odd, here, :] = high
                low_ref[odd, here, :] = low


def coefficients(sums, shared):
    norm, cross = sums[0:1, :], sums[1:2, :]
    later_norm, bend = shared[2:3, :], shared[3:4, :]
    curve = norm + cross
    ratio = later_norm / curve
    step = jnp.where(later_norm > 0, later_norm / (later_norm + bend - later_norm * ratio), 0.0)
    start = norm / curve
    return start * (1.0 + step * (ratio + cross / norm)), -start * step


def solved_kernel(devices, direction_ref, scaled_ref, sums_ref, solved_hbm, factors_ref, solved_ref, semaphores):
    people, columns = direction_ref.shape
    column = lax.axis_index("cols")
    copies = Copies(semaphores)

    def total(which):
        sums = sums_ref[which]
        shared = sums
        for i in range(1, devices):
            shared = shared + sums_ref[2 * i + which]
        return sums, shared

    along, across = coefficients(*total(column))
    factors = jnp.concatenate([along, across, *coefficients(*total(1 - column))], axis=0)
    factors_ref[...] = jnp.concatenate([factors, factors], axis=0)
    stores = []
    part_rows = people // 4
    for part in range(4):
        block = pl.ds(part * part_rows, part_rows)
        solved_ref[block, :] = along * direction_ref[block, :] + across * scaled_ref[block, :]
        stores.append(copies.start(solved_ref.at[block], solved_hbm.at[block]))
    wait_all(stores)


def scores_kernel(norm_scale, factors_ref, own_ref, other_ref, scores_ref):
    columns = own_ref.shape[2]
    column = lax.axis_index("cols")
    for which, rows_ref, place in ((0, own_ref, column), (2, other_ref, 1 - column)):
        along, across = factors_ref[which:which + 1, :], factors_ref[which + 1:which + 2, :]
        here = pl.ds(pl.multiple_of(place * columns, columns), columns)
        scores_ref[:, here] = norm_scale * (along * rows_ref[0] + across * rows_ref[1])


def call(kernel, out_shape, in_specs, out_specs, scratch_shapes=(), limit=VMEM_LIMIT):
    return pl.pallas_call(
        kernel,
        out_shape=out_shape,
        in_specs=in_specs,
        out_specs=out_specs,
        scratch_shapes=list(scratch_shapes),
        compiler_params=pltpu.CompilerParams(vmem_limit_bytes=limit),
    )


def swap(values, axis, devices, step):
    return lax.ppermute(values, axis, [(i, i ^ step) for i in range(devices)])


def after(value, *others):
    return lax.optimization_barrier((value, *others))[0]


def per_device(kinship, relatives, variance, phenotypes, dosage):
    devices = lax.axis_size("samples")
    block_count, positions, tile = kinship.shape[:3]
    people, columns = phenotypes.shape
    variants = dosage.shape[1]
    share_rows = variants // devices
    entries = block_count * (positions - 1)
    capacity = -(-entries // (devices - 1))
    assert capacity <= 2
    hbm = pl.BlockSpec(memory_space=pltpu.HBM)
    anywhere = pl.BlockSpec(memory_space=pl.ANY)
    vmem = pl.BlockSpec(memory_space=pltpu.VMEM)
    smem = pl.BlockSpec(memory_space=pltpu.SMEM)
    float_of = lambda *shape: jax.ShapeDtypeStruct(shape, jnp.float32)
    room = lambda *shape: pltpu.VMEM(shape, jnp.float32)
    full = float_of(people, columns)
    full_room = room(people, columns)
    half = devices // 2
    near_by = list(range(half - 1, 0, -1))
    at_home = lambda *arrays: [pltpu.with_memory_space_constraint(array, pltpu.HBM) for array in arrays]
    kinship, = at_home(kinship)
    tiles_room = pltpu.VMEM((block_count, tile, positions * tile), jnp.bfloat16)
    tiles_out = pltpu.HBM((block_count, tile, positions * tile), jnp.bfloat16)
    full_out = pltpu.HBM((people, columns), jnp.float32)
    direction, direction_kept_hbm, diagonal, norm = call(
        direction_kernel,
        [full, full_out, pltpu.HBM((people, 1), jnp.float32), float_of(SUBLANES, columns)],
        [hbm] * 3,
        [vmem, hbm, hbm, vmem],
        [
            room(*kinship.shape), room(block_count, tile), full_room, room(people, 1),
            pltpu.SemaphoreType.DMA((3 * block_count + 2,)),
        ],
    )(
        kinship, *at_home(variance.reshape(block_count, tile), phenotypes)
    )
    def to_mates(blocks):
        return [swap(blocks[k - 1], "samples", devices, k) for k in near_by]

    bits = half.bit_length() - 1
    even = [sum(((i >> b) & 1) << (bits - b) for b in range(bits)) for i in range(half)]
    steps = [2 << i for i in range(bits)]
    other_dosage = with_layout_constraint(swap(after(dosage, direction), "cols", 2, 1), Layout((0, 1)))
    table, forward, *outgoing = call(
        functools.partial(route_kernel, devices, capacity, block_count),
        [
            jax.ShapeDtypeStruct((4, max(entries, devices)), jnp.int32),
            jax.ShapeDtypeStruct((capacity, half), jnp.int32),
        ] + [float_of(capacity, tile, columns)] * (half - 1),
        [smem, vmem, anywhere],
        [smem, smem] + [vmem] * (half - 1),
        [pltpu.SMEM((devices,), jnp.int32), pltpu.SMEM((devices,), jnp.int32)],
    )(relatives.T, direction, other_dosage)
    high, low = call(
        tiles_kernel, [tiles_out] * 2, [hbm], [hbm] * 2,
        [room(*kinship.shape), tiles_room, tiles_room, pltpu.SemaphoreType.DMA((3,))],
    )(kinship)

    parts = jax.ShapeDtypeStruct((2, variants, people), jnp.bfloat16)
    large = VMEM_LIMIT if variants <= people else LARGE_VMEM
    grouped = call(
        functools.partial(group_kernel, even), [parts] * 2, [vmem] * 2, [vmem] * 2, limit=large
    )(after(dosage, table).T, other_dosage.T)

    products = float_of(half, 2 * share_rows, columns)

    def add_step(kept, taken, *gates):
        rows = float_of(kept.shape[0] // 2, 2 * share_rows, columns)
        return call(
            add_kernel, [rows] * 2, [vmem] * 2 + [hbm] * len(gates), [vmem] * 2
        )(kept, taken, *at_home(*gates))

    partner = swap(direction, "samples", devices, half)
    near = to_mates(outgoing)
    direction_even, direction_odd = call(
        score_kernel, [products] * 2, [vmem] * 3, [vmem] * 2, limit=large
    )(*grouped, direction)
    direction_share = swap(direction_odd, "samples", devices, 1)
    far = to_mates(call(
        forward_kernel,
        [float_of(capacity, tile, columns)] * (half - 1),
        [smem, vmem] + [anywhere] * (half + 1) + [hbm] * 2,
        [vmem] * (half - 1),
    )(forward, partner, *near, direction_even, direction_odd, *at_home(high, low)))
    received = near + far + [partner.reshape(block_count, tile, columns)]
    products_out = pltpu.HBM(products.shape, jnp.float32)
    scaled, handled, outgoing, scaled_even, scaled_odd = call(
        functools.partial(apply_kernel, devices, capacity),
        [
            full_out, full_out, pltpu.HBM((devices, tile + SUBLANES, columns), jnp.float32), products_out, products_out,
        ],
        [smem] + [vmem] * (devices + 6) + [anywhere],
        [hbm] * 5,
        [
            room(devices * capacity + block_count, tile, columns), full_room, full_room, room(SUBLANES, columns), room(*products.shape), room(*products.shape),
            pltpu.SemaphoreType.DMA((2 * devices + 4,)),
        ],
        limit=large,
    )(table, high, low, diagonal, direction, norm, *grouped, *received, direction_share)
    later = lax.all_to_all(outgoing, "samples", split_axis=0, concat_axis=0, tiled=True)
    scaled_share = swap(scaled_odd, "samples", devices, 1)
    direction_kept, direction_given = add_step(direction_even, direction_share)
    direction_taken = swap(after(direction_given, scaled), "samples", devices, steps[0])
    scaled_kept, scaled_given = add_step(scaled_even, scaled_share)
    scaled_taken = swap(scaled_given, "samples", devices, steps[0])
    sums = call(
        functools.partial(curvature_kernel, devices),
        pltpu.HBM((2 * devices, SUBLANES, columns), jnp.float32),
        [smem] + [vmem] * 5 + [hbm, vmem, anywhere],
        hbm,
        [room(2 * devices, SUBLANES, columns), full_room, pltpu.SemaphoreType.DMA((2,))],
    )(table, high, low, direction_kept_hbm, diagonal, scaled, *at_home(handled), later, scaled_given)
    all_sums = lax.all_to_all(sums, ("samples", "cols"), split_axis=0, concat_axis=0, tiled=True)
    for step in steps[1:]:
        scaled_kept, scaled_given = add_step(scaled_kept, scaled_taken, sums)
        scaled_taken = swap(scaled_given, "samples", devices, step)
    for step in steps[1:]:
        direction_kept, direction_given = add_step(direction_kept, direction_taken, sums)
        direction_taken = swap(direction_given, "samples", devices, step)
    rows = float_of(2, share_rows, columns)
    own_scores, other_scores = call(
        last_add_kernel, [rows] * 2, [vmem] * 4, [vmem] * 2
    )(direction_kept, direction_taken, scaled_kept, scaled_taken)
    solved, factors = call(
        functools.partial(solved_kernel, devices),
        [full, float_of(SUBLANES, columns)],
        [vmem] * 3,
        [hbm, vmem],
        [full_room, pltpu.SemaphoreType.DMA((4,))],
    )(direction_kept_hbm, scaled, all_sums)
    scores = call(
        functools.partial(scores_kernel, 1.0 / math.sqrt(people * devices)),
        float_of(share_rows, 2 * columns), [vmem] * 3, vmem,
    )(factors, own_scores, swap(other_scores, "cols", 2, 1))
    return (solved, scores)


def solution(mesh):
    return jax.shard_map(
        per_device,
        mesh=mesh,
        in_specs=(
            P(("groups", "samples"), None, None, None),
            P("groups", None),
            P(("groups", "samples")),
            P(("groups", "samples"), "cols"),
            P(("groups", "samples"), "cols"),
        ),
        out_specs=(P(("groups", "samples"), "cols"), P(("groups", "cols", "samples"), None)),
        check_vma=False,
    )
```

```python
import functools
import math

import jax
import jax.numpy as jnp
from jax import lax
from jax.experimental import pallas as pl
from jax.experimental.layout import Layout, with_layout_constraint
from jax.experimental.pallas import tpu as pltpu
from jax.sharding import PartitionSpec as P

VMEM_LIMIT = 24 * 1024 * 1024
LARGE_VMEM = 56 * 1024 * 1024
SUBLANES = 8


def split(values):
    high = values.astype(jnp.bfloat16)
    low = (values - high.astype(jnp.float32)).astype(jnp.bfloat16)
    return high, low


def dot(left, right):
    return jnp.dot(left, right, preferred_element_type=jnp.float32)


def on_diagonal(size):
    rows = lax.broadcasted_iota(jnp.int32, (size, size), 0)
    return rows == lax.broadcasted_iota(jnp.int32, (size, size), 1)


def split_tiles(kinship_ref, high_ref, low_ref):
    block_count, positions, tile = kinship_ref.shape[:3]
    diagonal_mask = on_diagonal(tile)
    for row in range(block_count):
        for position in range(positions):
            values = kinship_ref[row, position]
            if position == 0:
                values = jnp.where(diagonal_mask, 0.0, values)
            high, low = split(values)
            high_ref[row, :, pl.ds(position * tile, tile)] = high
            low_ref[row, :, pl.ds(position * tile, tile)] = low


def product(high, low, blocks):
    parts = [split(block) for block in blocks]
    blocks_high = jnp.concatenate([part[0] for part in parts], axis=0)
    blocks_low = jnp.concatenate([part[1] for part in parts], axis=0)
    return dot(high, blocks_high) + (dot(low, blocks_high) + dot(high, blocks_low))


def column_sums(values):
    rows, columns = values.shape
    return jnp.sum(values.reshape(rows // SUBLANES, SUBLANES, columns), axis=0)


class Copies:
    def __init__(self, semaphores):
        self.semaphores = semaphores
        self.count = 0

    def start(self, source, target):
        copy = pltpu.make_async_copy(source, target, self.semaphores.at[self.count])
        self.count += 1
        copy.start()
        return copy


def wait_all(copies):
    for copy in copies:
        copy.wait()


def quotient(value, divisor):
    if divisor & (divisor - 1) == 0:
        return lax.shift_right_logical(value, jnp.int32(divisor.bit_length() - 1))
    return lax.div(value, jnp.int32(divisor))


def direction_kernel(kinship_hbm, variance_hbm, phenotypes_hbm, direction_ref, direction_hbm, diagonal_hbm, sums_ref,
                     kinship_ref, variance_ref, phenotypes_ref, diagonal_ref, semaphores):
    block_count, positions, tile = kinship_ref.shape[:3]
    copies = Copies(semaphores)
    loads = [copies.start(variance_hbm, variance_ref)]
    for row in range(block_count):
        block = pl.ds(row * tile, tile)
        loads.append(copies.start(kinship_hbm.at[row], kinship_ref.at[row]))
        loads.append(copies.start(phenotypes_hbm.at[block], phenotypes_ref.at[block]))
    stores = []
    norm = jnp.zeros((SUBLANES, direction_ref.shape[1]), jnp.float32)
    diagonal_mask = on_diagonal(tile)
    loads[0].wait()
    for row in range(block_count):
        wait_all(loads[1 + 2 * row:3 + 2 * row])
        block = pl.ds(row * tile, tile)
        total = jnp.where(diagonal_mask, variance_ref[row:row + 1, :], kinship_ref[row, 0])
        for position in range(1, positions):
            total = total + kinship_ref[row, position]
        diagonal = jnp.sum(total, axis=1, keepdims=True)
        diagonal_ref[block, :] = diagonal
        here = phenotypes_ref[block, :] * (1.0 / diagonal)
        direction_ref[block, :] = here
        norm = norm + column_sums(here * phenotypes_ref[block, :])
        stores.append(copies.start(direction_ref.at[block], direction_hbm.at[block]))
    stores.append(copies.start(diagonal_ref, diagonal_hbm))
    row_ids = lax.broadcasted_iota(jnp.int32, norm.shape, 0)
    sums_ref[...] = jnp.where(row_ids == 0, jnp.sum(norm, axis=0, keepdims=True), 0.0)
    wait_all(stores)


def tiles_kernel(kinship_hbm, high_hbm, low_hbm, kinship_ref, high_ref, low_ref, semaphores):
    copies = Copies(semaphores)
    copies.start(kinship_hbm, kinship_ref).wait()
    split_tiles(kinship_ref, high_ref, low_ref)
    wait_all([copies.start(high_ref, high_hbm), copies.start(low_ref, low_hbm)])


def route_kernel(devices, capacity, block_count, list_ref, direction_ref, gate_ref, table_ref, forward_ref, *refs):
    half = devices // 2
    outgoing_refs, (first_ref, last_ref) = refs[:half - 1], refs[half - 1:]
    positions = list_ref.shape[0] + 1
    tile = direction_ref.shape[0] // block_count
    me = lax.axis_index("samples")
    partner = me ^ half
    spare = me ^ 1
    top = block_count * block_count

    def collect(device):
        for j in range(devices):
            first_ref[j] = jnp.int32(top)
            last_ref[j] = jnp.int32(-1)
        found = []
        for row in range(block_count):
            for position in range(positions - 1):
                listed = list_ref[position, device * block_count + row]
                live = listed >= 0
                safe = jnp.maximum(listed, 0)
                other = quotient(safe, block_count)
                far_block = safe - other * block_count
                key = jnp.where(device < other, row * block_count + far_block, far_block * block_count + row)
                first_ref[other] = jnp.minimum(first_ref[other], jnp.where(live, key, top))
                last_ref[other] = jnp.maximum(last_ref[other], jnp.where(live, key, -1))
                found.append((live, other, far_block, key))
        return found

    def blocks_for(device, other):
        blocks = []
        for key in (first_ref[other], last_ref[other]):
            safe = jnp.clip(key, 0, top - 1)
            lower = quotient(safe, block_count)
            higher = safe - lower * block_count
            blocks.append(jnp.where(key == safe, jnp.where(device < other, lower, higher), 0))
        return blocks

    collect(partner)
    for k in range(1, half):
        blocks = blocks_for(partner, me ^ k)
        for slot in range(capacity):
            forward_ref[slot, k] = blocks[slot]
    for entry, (live, other, far_block, key) in enumerate(collect(me)):
        first, last = first_ref[other], last_ref[other]
        handled = jnp.where(me < other, first, last)
        weight = jnp.where(first == last, 1, 2)
        slot = jnp.where(key == first, 0, capacity - 1)
        place = jnp.where(other == partner, devices * capacity + far_block, other * capacity + slot)
        table_ref[0, entry] = jnp.where(live, place, spare * capacity)
        table_ref[1, entry] = jnp.where(live, other, spare)
        table_ref[2, entry] = jnp.where(live & (key == handled), weight, 0)
    for other in range(devices):
        blocks = blocks_for(me, other)
        table_ref[3, other] = jnp.where(me < other, blocks[1], blocks[0])
    near = [blocks_for(me, me ^ k) for k in range(1, half)]
    for k in range(1, half):
        for slot in range(capacity):
            start = pl.multiple_of(near[k - 1][slot] * tile, tile)
            outgoing_refs[k - 1][slot] = direction_ref[pl.ds(start, tile), :]


def forward_kernel(forward_ref, partner_ref, *refs):
    capacity, half = forward_ref.shape
    outgoing_refs = refs[1 - half:]
    tile = outgoing_refs[0].shape[1]
    for k in range(1, half):
        for slot in range(capacity):
            start = pl.multiple_of(forward_ref[slot, k] * tile, tile)
            outgoing_refs[k - 1][slot] = partner_ref[pl.ds(start, tile), :]


def gather_received(devices, capacity, received_refs, gathered_ref):
    half = devices // 2
    me = lax.axis_index("samples")
    near_refs, far_refs, partner_ref = received_refs[:half - 1], received_refs[half - 1:-1], received_refs[-1]
    gathered_ref[pl.ds(devices * capacity, partner_ref.shape[0])] = partner_ref[...]
    for i in range(half - 1):
        mate = me ^ (half - 1 - i)
        gathered_ref[pl.ds(mate * capacity, capacity)] = near_refs[i][...]
        gathered_ref[pl.ds((mate ^ half) * capacity, capacity)] = far_refs[i][...]


def score_products(high_ref, low_ref, values, even_ref, odd_ref):
    count, rows = even_ref.shape[:2]
    for odd, out_ref in enumerate((even_ref, odd_ref)):
        for i in range(0, count, 4):
            here = pl.ds(i * rows, 4 * rows)
            total = product(high_ref[odd, here, :], low_ref[odd, here, :], [values])
            out_ref[pl.ds(i, 4)] = total.reshape(4, rows, -1)


def score_kernel(high_ref, low_ref, values_ref, even_ref, odd_ref):
    score_products(high_ref, low_ref, values_ref[...], even_ref, odd_ref)


def apply_kernel(devices, capacity, table_ref, high_hbm, low_hbm, diagonal_hbm, direction_ref, norm_ref, dosage_high_ref,
                 dosage_low_ref, *refs):
    received_refs = refs[:devices - 1]
    (scaled_hbm, handled_hbm, outgoing_hbm, even_hbm, odd_hbm, gathered_ref, high_ref, low_ref, diagonal_ref, scaled_ref,
     handled_ref, sums_ref, even_ref, odd_ref, semaphores) = refs[-15:]
    copies = Copies(semaphores)
    loads = [
        copies.start(high_hbm, high_ref), copies.start(low_hbm, low_ref), copies.start(diagonal_hbm, diagonal_ref)
    ]
    gather_received(devices, capacity, received_refs, gathered_ref)
    wait_all(loads)
    block_count, tile, depth = high_ref.shape
    others = depth // tile - 1
    cross = jnp.zeros(norm_ref.shape, jnp.float32)
    for row in range(block_count):
        block = pl.ds(row * tile, tile)
        here = direction_ref[block, :]
        blocks = [here] + [gathered_ref[table_ref[0, row * others + i]] for i in range(others)]
        mapped = product(high_ref[row], low_ref[row], blocks)
        scaled_ref[block, :] = mapped * (1.0 / diagonal_ref[block, :])
        cross = cross + column_sums(here * mapped)
    row_ids = lax.broadcasted_iota(jnp.int32, cross.shape, 0)
    sums_ref[...] = jnp.where(row_ids == 1, jnp.sum(cross, axis=0, keepdims=True), norm_ref[...])
    stores = [copies.start(scaled_ref, scaled_hbm)]
    for other in range(devices):
        start = pl.multiple_of(table_ref[3, other] * tile, tile)
        stores.append(copies.start(scaled_ref.at[pl.ds(start, tile)], outgoing_hbm.at[other, pl.ds(0, tile)]))
        stores.append(copies.start(sums_ref, outgoing_hbm.at[other, pl.ds(tile, SUBLANES)]))
    score_products(dosage_high_ref, dosage_low_ref, scaled_ref[...], even_ref, odd_ref)
    stores += [copies.start(odd_ref, odd_hbm), copies.start(even_ref, even_hbm)]
    far = pl.ds(tile, depth - tile)
    for row in range(block_count):
        blocks = []
        for i in range(others):
            weight = table_ref[2, row * others + i].astype(jnp.float32)
            blocks.append(weight * gathered_ref[table_ref[0, row * others + i]])
        handled_ref[pl.ds(row * tile, tile), :] = product(high_ref[row, :, far], low_ref[row, :, far], blocks)
    stores.append(copies.start(handled_ref, handled_hbm))
    wait_all(stores)


def curvature_kernel(devices, table_ref, high_hbm, low_hbm, direction_hbm, diagonal_hbm, scaled_hbm, handled_hbm,
                     later_ref, *refs):
    sums_ref, high_ref, low_ref, direction_ref, diagonal_ref, scaled_ref, handled_ref, semaphores = refs[-8:]
    block_count, tile, depth = high_ref.shape
    copies = Copies(semaphores)
    wait_all([copies.start(source, target) for source, target in (
        (scaled_hbm, scaled_ref), (direction_hbm, direction_ref), (high_hbm, high_ref), (low_hbm, low_ref),
        (handled_hbm, handled_ref), (diagonal_hbm, diagonal_ref),
    )])
    others = depth // tile - 1
    first_sums = later_ref[0, pl.ds(tile, SUBLANES), :]
    for other in range(1, devices):
        first_sums = first_sums + later_ref[other, pl.ds(tile, SUBLANES), :]
    rho = first_sums[1:2, :] / first_sums[0:1, :]
    norm = jnp.zeros(first_sums.shape, jnp.float32)
    bend = jnp.zeros(first_sums.shape, jnp.float32)
    for row in range(block_count):
        block = pl.ds(row * tile, tile)
        here = scaled_ref[block, :] - rho * direction_ref[block, :]
        blocks = [here]
        for i in range(others):
            entry = row * others + i
            weight = table_ref[2, entry].astype(jnp.float32)
            blocks.append(weight * later_ref[table_ref[1, entry], pl.ds(0, tile), :])
        mapped = product(high_ref[row], low_ref[row], blocks) - rho * handled_ref[block, :]
        norm = norm + column_sums(here * here * diagonal_ref[block, :])
        bend = bend + column_sums(here * mapped)
    row_ids = lax.broadcasted_iota(jnp.int32, first_sums.shape, 0)
    sums = jnp.where(row_ids == 2, jnp.sum(norm, axis=0, keepdims=True), first_sums)
    sums = jnp.where(row_ids == 3, jnp.sum(bend, axis=0, keepdims=True), sums)
    for i in range(2 * devices):
        sums_ref[i] = sums


def add_kernel(kept_ref, taken_ref, *refs):
    near_ref, far_ref = refs[-2:]
    count = near_ref.shape[0]
    near_ref[...] = kept_ref[pl.ds(0, count)] + taken_ref[pl.ds(0, count)]
    far_ref[...] = kept_ref[pl.ds(count, count)] + taken_ref[pl.ds(count, count)]


def last_add_kernel(first_kept_ref, first_taken_ref, second_kept_ref, second_taken_ref, own_ref, other_ref):
    rows = own_ref.shape[1]
    for i, (kept_ref, taken_ref) in enumerate(
        ((first_kept_ref, first_taken_ref), (second_kept_ref, second_taken_ref))
    ):
        own_ref[i] = kept_ref[0, pl.ds(0, rows), :] + taken_ref[0, pl.ds(0, rows), :]
        other_ref[i] = kept_ref[0, pl.ds(rows, rows), :] + taken_ref[0, pl.ds(rows, rows), :]


def group_kernel(order, own_ref, other_ref, high_ref, low_ref):
    rows = own_ref.shape[0] // (2 * len(order))
    me = lax.axis_index("samples")
    for odd in range(2):
        for i, distance in enumerate(order):
            start = pl.multiple_of((me ^ distance ^ odd) * rows, rows)
            for j, dosage_ref in enumerate((own_ref, other_ref)):
                high, low = split(dosage_ref[pl.ds(start, rows), :])
                here = pl.ds((2 * i + j) * rows, rows)
                high_ref[odd, here, :] = high
                low_ref[odd, here, :] = low


def coefficients(sums, shared):
    norm, cross = sums[0:1, :], sums[1:2, :]
    later_norm, bend = shared[2:3, :], shared[3:4, :]
    curve = norm + cross
    ratio = later_norm / curve
    step = jnp.where(later_norm > 0, later_norm / (later_norm + bend - later_norm * ratio), 0.0)
    start = norm / curve
    return start * (1.0 + step * (ratio + cross / norm)), -start * step


def solved_kernel(devices, direction_ref, scaled_ref, sums_ref, solved_hbm, factors_ref, solved_ref, semaphores):
    people, columns = direction_ref.shape
    column = lax.axis_index("cols")
    copies = Copies(semaphores)

    def total(which):
        sums = sums_ref[which]
        shared = sums
        for i in range(1, devices):
            shared = shared + sums_ref[2 * i + which]
        return sums, shared

    along, across = coefficients(*total(column))
    factors = jnp.concatenate([along, across, *coefficients(*total(1 - column))], axis=0)
    factors_ref[...] = jnp.concatenate([factors, factors], axis=0)
    stores = []
    part_rows = people // 4
    for part in range(4):
        block = pl.ds(part * part_rows, part_rows)
        solved_ref[block, :] = along * direction_ref[block, :] + across * scaled_ref[block, :]
        stores.append(copies.start(solved_ref.at[block], solved_hbm.at[block]))
    wait_all(stores)


def scores_kernel(norm_scale, factors_ref, own_ref, other_ref, scores_ref):
    columns = own_ref.shape[2]
    column = lax.axis_index("cols")
    for which, rows_ref, place in ((0, own_ref, column), (2, other_ref, 1 - column)):
        along, across = factors_ref[which:which + 1, :], factors_ref[which + 1:which + 2, :]
        here = pl.ds(pl.multiple_of(place * columns, columns), columns)
        scores_ref[:, here] = norm_scale * (along * rows_ref[0] + across * rows_ref[1])


def call(kernel, out_shape, in_specs, out_specs, scratch_shapes=(), limit=VMEM_LIMIT):
    return pl.pallas_call(
        kernel,
        out_shape=out_shape,
        in_specs=in_specs,
        out_specs=out_specs,
        scratch_shapes=list(scratch_shapes),
        compiler_params=pltpu.CompilerParams(vmem_limit_bytes=limit),
    )


def swap(values, axis, devices, step):
    return lax.ppermute(values, axis, [(i, i ^ step) for i in range(devices)])


def after(value, *others):
    return lax.optimization_barrier((value, *others))[0]


def per_device(kinship, relatives, variance, phenotypes, dosage):
    devices = lax.axis_size("samples")
    block_count, positions, tile = kinship.shape[:3]
    people, columns = phenotypes.shape
    variants = dosage.shape[1]
    share_rows = variants // devices
    entries = block_count * (positions - 1)
    capacity = -(-entries // (devices - 1))
    assert capacity <= 2
    hbm = pl.BlockSpec(memory_space=pltpu.HBM)
    anywhere = pl.BlockSpec(memory_space=pl.ANY)
    vmem = pl.BlockSpec(memory_space=pltpu.VMEM)
    smem = pl.BlockSpec(memory_space=pltpu.SMEM)
    float_of = lambda *shape: jax.ShapeDtypeStruct(shape, jnp.float32)
    room = lambda *shape: pltpu.VMEM(shape, jnp.float32)
    full = float_of(people, columns)
    full_room = room(people, columns)
    half = devices // 2
    near_by = list(range(half - 1, 0, -1))
    at_home = lambda *arrays: [pltpu.with_memory_space_constraint(array, pltpu.HBM) for array in arrays]
    kinship, = at_home(kinship)
    tiles_room = pltpu.VMEM((block_count, tile, positions * tile), jnp.bfloat16)
    tiles_out = pltpu.HBM((block_count, tile, positions * tile), jnp.bfloat16)
    full_out = pltpu.HBM((people, columns), jnp.float32)
    direction, direction_kept_hbm, diagonal, norm = call(
        direction_kernel,
        [full, full_out, pltpu.HBM((people, 1), jnp.float32), float_of(SUBLANES, columns)],
        [hbm] * 3,
        [vmem, hbm, hbm, vmem],
        [
            room(*kinship.shape), room(block_count, tile), full_room, room(people, 1),
            pltpu.SemaphoreType.DMA((3 * block_count + 2,)),
        ],
    )(
        kinship, *at_home(variance.reshape(block_count, tile), phenotypes)
    )
    def to_mates(blocks):
        return [swap(blocks[k - 1], "samples", devices, k) for k in near_by]

    bits = half.bit_length() - 1
    even = [sum(((i >> b) & 1) << (bits - b) for b in range(bits)) for i in range(half)]
    steps = [2 << i for i in range(bits)]
    other_dosage = with_layout_constraint(swap(after(dosage, direction), "cols", 2, 1), Layout((0, 1)))
    table, forward, *outgoing = call(
        functools.partial(route_kernel, devices, capacity, block_count),
        [
            jax.ShapeDtypeStruct((4, max(entries, devices)), jnp.int32),
            jax.ShapeDtypeStruct((capacity, half), jnp.int32),
        ] + [float_of(capacity, tile, columns)] * (half - 1),
        [smem, vmem, anywhere],
        [smem, smem] + [vmem] * (half - 1),
        [pltpu.SMEM((devices,), jnp.int32), pltpu.SMEM((devices,), jnp.int32)],
    )(relatives.T, direction, other_dosage)
    high, low = call(
        tiles_kernel, [tiles_out] * 2, [hbm], [hbm] * 2,
        [room(*kinship.shape), tiles_room, tiles_room, pltpu.SemaphoreType.DMA((3,))],
    )(kinship)

    parts = jax.ShapeDtypeStruct((2, variants, people), jnp.bfloat16)
    large = VMEM_LIMIT if variants <= people else LARGE_VMEM
    grouped = call(
        functools.partial(group_kernel, even), [parts] * 2, [vmem] * 2, [vmem] * 2, limit=large
    )(after(dosage, table).T, other_dosage.T)

    products = float_of(half, 2 * share_rows, columns)

    def add_step(kept, taken, *gates):
        rows = float_of(kept.shape[0] // 2, 2 * share_rows, columns)
        return call(
            add_kernel, [rows] * 2, [vmem] * (2 + len(gates)), [vmem] * 2
        )(kept, taken, *gates)

    partner = swap(direction, "samples", devices, half)
    near = to_mates(outgoing)
    direction_even, direction_odd = call(
        score_kernel, [products] * 2, [vmem] * 3, [vmem] * 2, limit=large
    )(*grouped, direction)
    direction_share = swap(direction_odd, "samples", devices, 1)
    far = to_mates(call(
        forward_kernel,
        [float_of(capacity, tile, columns)] * (half - 1),
        [smem, vmem] + [anywhere] * (half + 1) + [hbm] * 2,
        [vmem] * (half - 1),
    )(forward, partner, *near, direction_even, direction_odd, *at_home(high, low)))
    received = near + far + [partner.reshape(block_count, tile, columns)]
    products_out = pltpu.HBM(products.shape, jnp.float32)
    scaled, handled, outgoing, scaled_even, scaled_odd = call(
        functools.partial(apply_kernel, devices, capacity),
        [
            full_out, full_out, pltpu.HBM((devices, tile + SUBLANES, columns), jnp.float32), products_out, products_out,
        ],
        [smem, hbm, hbm, hbm] + [vmem] * (devices + 3) + [anywhere],
        [hbm] * 5,
        [
            room(devices * capacity + block_count, tile, columns), tiles_room, tiles_room, room(people, 1), full_room,
            full_room, room(SUBLANES, columns), room(*products.shape), room(*products.shape),
            pltpu.SemaphoreType.DMA((2 * devices + 7,)),
        ],
        limit=large,
    )(table, high, low, diagonal, direction, norm, *grouped, *received, direction_share)
    later = lax.all_to_all(outgoing, "samples", split_axis=0, concat_axis=0, tiled=True)
    scaled_share = swap(scaled_odd, "samples", devices, 1)
    direction_kept, direction_given = add_step(direction_even, direction_share)
    direction_taken = swap(after(direction_given, scaled), "samples", devices, steps[0])
    scaled_kept, scaled_given = add_step(scaled_even, scaled_share)
    scaled_taken = swap(scaled_given, "samples", devices, steps[0])
    sums = call(
        functools.partial(curvature_kernel, devices),
        float_of(2 * devices, SUBLANES, columns),
        [smem] + [hbm] * 6 + [vmem, anywhere],
        vmem,
        [tiles_room, tiles_room, full_room, room(people, 1), full_room, full_room, pltpu.SemaphoreType.DMA((6,))],
    )(table, *at_home(high, low, direction_kept_hbm, diagonal, scaled, handled), later, scaled_given)
    all_sums = lax.all_to_all(sums, ("samples", "cols"), split_axis=0, concat_axis=0, tiled=True)
    for step in steps[1:]:
        scaled_kept, scaled_given = add_step(scaled_kept, scaled_taken, sums)
        scaled_taken = swap(scaled_given, "samples", devices, step)
    for step in steps[1:]:
        direction_kept, direction_given = add_step(direction_kept, direction_taken, sums)
        direction_taken = swap(direction_given, "samples", devices, step)
    rows = float_of(2, share_rows, columns)
    own_scores, other_scores = call(
        last_add_kernel, [rows] * 2, [vmem] * 4, [vmem] * 2
    )(direction_kept, direction_taken, scaled_kept, scaled_taken)
    solved, factors = call(
        functools.partial(solved_kernel, devices),
        [full, float_of(SUBLANES, columns)],
        [vmem] * 3,
        [hbm, vmem],
        [full_room, pltpu.SemaphoreType.DMA((4,))],
    )(direction_kept_hbm, scaled, all_sums)
    scores = call(
        functools.partial(scores_kernel, 1.0 / math.sqrt(people * devices)),
        float_of(share_rows, 2 * columns), [vmem] * 3, vmem,
    )(factors, own_scores, swap(other_scores, "cols", 2, 1))
    return (solved, scores)


def solution(mesh):
    return jax.shard_map(
        per_device,
        mesh=mesh,
        in_specs=(
            P(("groups", "samples"), None, None, None),
            P("groups", None),
            P(("groups", "samples")),
            P(("groups", "samples"), "cols"),
            P(("groups", "samples"), "cols"),
        ),
        out_specs=(P(("groups", "samples"), "cols"), P(("groups", "cols", "samples"), None)),
        check_vma=False,
    )
```

```python
import functools
import math

import jax
import jax.numpy as jnp
from jax import lax
from jax.experimental import pallas as pl
from jax.experimental.layout import Layout, with_layout_constraint
from jax.experimental.pallas import tpu as pltpu
from jax.sharding import PartitionSpec as P

VMEM_LIMIT = 24 * 1024 * 1024
LARGE_VMEM = 56 * 1024 * 1024
SUBLANES = 8
LANES = 128


def split(values):
    high = values.astype(jnp.bfloat16)
    low = (values - high.astype(jnp.float32)).astype(jnp.bfloat16)
    return high, low


def dot(left, right):
    return jnp.dot(left, right, preferred_element_type=jnp.float32)


def on_diagonal(size):
    rows = lax.broadcasted_iota(jnp.int32, (size, size), 0)
    return rows == lax.broadcasted_iota(jnp.int32, (size, size), 1)


def wide(values, columns):
    return jnp.concatenate([values] * (columns // LANES), axis=1)


def split_tiles(kinship_ref, high_ref, low_ref):
    block_count, positions, tile = kinship_ref.shape[:3]
    diagonal_mask = on_diagonal(tile)
    for row in range(block_count):
        for position in range(positions):
            values = kinship_ref[row, position]
            if position == 0:
                values = jnp.where(diagonal_mask, 0.0, values)
            high, low = split(values)
            high_ref[row, :, pl.ds(position * tile, tile)] = high
            low_ref[row, :, pl.ds(position * tile, tile)] = low


def product(high, low, blocks):
    parts = [split(block) for block in blocks]
    blocks_high = jnp.concatenate([part[0] for part in parts], axis=0)
    blocks_low = jnp.concatenate([part[1] for part in parts], axis=0)
    return dot(high, blocks_high) + (dot(low, blocks_high) + dot(high, blocks_low))


def column_sums(values):
    rows, columns = values.shape
    return jnp.sum(values.reshape(rows // SUBLANES, SUBLANES, columns), axis=0)


class Copies:
    def __init__(self, semaphores):
        self.semaphores = semaphores
        self.count = 0

    def start(self, source, target):
        copy = pltpu.make_async_copy(source, target, self.semaphores.at[self.count])
        self.count += 1
        copy.start()
        return copy


def wait_all(copies):
    for copy in copies:
        copy.wait()


def quotient(value, divisor):
    if divisor & (divisor - 1) == 0:
        return lax.shift_right_logical(value, jnp.int32(divisor.bit_length() - 1))
    return lax.div(value, jnp.int32(divisor))


def direction_kernel(kinship_hbm, variance_hbm, phenotypes_hbm, direction_ref, direction_hbm, diagonal_hbm, sums_ref,
                     kinship_ref, variance_ref, phenotypes_ref, diagonal_ref, semaphores):
    block_count, positions, tile = kinship_ref.shape[:3]
    copies = Copies(semaphores)
    loads = [copies.start(variance_hbm, variance_ref)]
    for row in range(block_count):
        block = pl.ds(row * tile, tile)
        loads.append(copies.start(kinship_hbm.at[row], kinship_ref.at[row]))
        loads.append(copies.start(phenotypes_hbm.at[block], phenotypes_ref.at[block]))
    stores = []
    norm = jnp.zeros((SUBLANES, direction_ref.shape[1]), jnp.float32)
    diagonal_mask = on_diagonal(tile)
    loads[0].wait()
    for row in range(block_count):
        wait_all(loads[1 + 2 * row:3 + 2 * row])
        block = pl.ds(row * tile, tile)
        total = jnp.where(diagonal_mask, variance_ref[row:row + 1, :], kinship_ref[row, 0])
        for position in range(1, positions):
            total = total + kinship_ref[row, position]
        diagonal = jnp.sum(total, axis=1, keepdims=True)
        diagonal_ref[block, :] = jnp.broadcast_to(diagonal, (tile, LANES))
        here = phenotypes_ref[block, :] * (1.0 / diagonal)
        direction_ref[block, :] = here
        norm = norm + column_sums(here * phenotypes_ref[block, :])
        stores.append(copies.start(direction_ref.at[block], direction_hbm.at[block]))
    stores.append(copies.start(diagonal_ref, diagonal_hbm))
    row_ids = lax.broadcasted_iota(jnp.int32, norm.shape, 0)
    sums_ref[...] = jnp.where(row_ids == 0, jnp.sum(norm, axis=0, keepdims=True), 0.0)
    wait_all(stores)


def tiles_kernel(kinship_hbm, high_hbm, low_hbm, kinship_ref, high_ref, low_ref, semaphores):
    copies = Copies(semaphores)
    copies.start(kinship_hbm, kinship_ref).wait()
    split_tiles(kinship_ref, high_ref, low_ref)
    wait_all([copies.start(high_ref, high_hbm), copies.start(low_ref, low_hbm)])


def route_kernel(devices, capacity, block_count, list_ref, direction_ref, gate_ref, table_ref, forward_ref, *refs):
    half = devices // 2
    outgoing_refs, (first_ref, last_ref) = refs[:half - 1], refs[half - 1:]
    positions = list_ref.shape[0] + 1
    tile = direction_ref.shape[0] // block_count
    me = lax.axis_index("samples")
    partner = me ^ half
    spare = me ^ 1
    top = block_count * block_count

    def collect(device):
        for j in range(devices):
            first_ref[j] = jnp.int32(top)
            last_ref[j] = jnp.int32(-1)
        found = []
        for row in range(block_count):
            for position in range(positions - 1):
                listed = list_ref[position, device * block_count + row]
                live = listed >= 0
                safe = jnp.maximum(listed, 0)
                other = quotient(safe, block_count)
                far_block = safe - other * block_count
                key = jnp.where(device < other, row * block_count + far_block, far_block * block_count + row)
                first_ref[other] = jnp.minimum(first_ref[other], jnp.where(live, key, top))
                last_ref[other] = jnp.maximum(last_ref[other], jnp.where(live, key, -1))
                found.append((live, other, far_block, key))
        return found

    def blocks_for(device, other):
        blocks = []
        for key in (first_ref[other], last_ref[other]):
            safe = jnp.clip(key, 0, top - 1)
            lower = quotient(safe, block_count)
            higher = safe - lower * block_count
            blocks.append(jnp.where(key == safe, jnp.where(device < other, lower, higher), 0))
        return blocks

    collect(partner)
    for k in range(1, half):
        blocks = blocks_for(partner, me ^ k)
        for slot in range(capacity):
            forward_ref[slot, k] = blocks[slot]
    for entry, (live, other, far_block, key) in enumerate(collect(me)):
        first, last = first_ref[other], last_ref[other]
        handled = jnp.where(me < other, first, last)
        weight = jnp.where(first == last, 1, 2)
        slot = jnp.where(key == first, 0, capacity - 1)
        place = jnp.where(other == partner, devices * capacity + far_block, other * capacity + slot)
        table_ref[0, entry] = jnp.where(live, place, spare * capacity)
        table_ref[1, entry] = jnp.where(live, other, spare)
        table_ref[2, entry] = jnp.where(live & (key == handled), weight, 0)
    for other in range(devices):
        blocks = blocks_for(me, other)
        table_ref[3, other] = jnp.where(me < other, blocks[1], blocks[0])
    near = [blocks_for(me, me ^ k) for k in range(1, half)]
    for k in range(1, half):
        for slot in range(capacity):
            start = pl.multiple_of(near[k - 1][slot] * tile, tile)
            outgoing_refs[k - 1][slot] = direction_ref[pl.ds(start, tile), :]


def forward_kernel(forward_ref, partner_ref, *refs):
    capacity, half = forward_ref.shape
    outgoing_refs = refs[1 - half:]
    tile = outgoing_refs[0].shape[1]
    for k in range(1, half):
        for slot in range(capacity):
            start = pl.multiple_of(forward_ref[slot, k] * tile, tile)
            outgoing_refs[k - 1][slot] = partner_ref[pl.ds(start, tile), :]


def gather_received(devices, capacity, received_refs, gathered_ref):
    half = devices // 2
    me = lax.axis_index("samples")
    near_refs, far_refs, partner_ref = received_refs[:half - 1], received_refs[half - 1:-1], received_refs[-1]
    gathered_ref[pl.ds(devices * capacity, partner_ref.shape[0])] = partner_ref[...]
    for i in range(half - 1):
        mate = me ^ (half - 1 - i)
        gathered_ref[pl.ds(mate * capacity, capacity)] = near_refs[i][...]
        gathered_ref[pl.ds((mate ^ half) * capacity, capacity)] = far_refs[i][...]


def score_products(high_ref, low_ref, values, even_ref, odd_ref):
    count, rows = even_ref.shape[:2]
    for odd, out_ref in enumerate((even_ref, odd_ref)):
        for i in range(0, count, 4):
            here = pl.ds(i * rows, 4 * rows)
            total = product(high_ref[odd, here, :], low_ref[odd, here, :], [values])
            out_ref[pl.ds(i, 4)] = total.reshape(4, rows, -1)


def score_kernel(high_ref, low_ref, values_ref, even_ref, odd_ref):
    score_products(high_ref, low_ref, values_ref[...], even_ref, odd_ref)


def apply_kernel(devices, capacity, table_ref, high_hbm, low_hbm, diagonal_hbm, direction_ref, norm_ref, dosage_high_ref,
                 dosage_low_ref, *refs):
    received_refs = refs[:devices - 1]
    (scaled_hbm, handled_hbm, outgoing_hbm, even_hbm, odd_hbm, gathered_ref, high_ref, low_ref, diagonal_ref, scaled_ref,
     handled_ref, sums_ref, even_ref, odd_ref, semaphores) = refs[-15:]
    copies = Copies(semaphores)
    loads = [
        copies.start(high_hbm, high_ref), copies.start(low_hbm, low_ref), copies.start(diagonal_hbm, diagonal_ref)
    ]
    gather_received(devices, capacity, received_refs, gathered_ref)
    wait_all(loads)
    block_count, tile, depth = high_ref.shape
    others = depth // tile - 1
    cross = jnp.zeros(norm_ref.shape, jnp.float32)
    for row in range(block_count):
        block = pl.ds(row * tile, tile)
        here = direction_ref[block, :]
        blocks = [here] + [gathered_ref[table_ref[0, row * others + i]] for i in range(others)]
        mapped = product(high_ref[row], low_ref[row], blocks)
        scaled_ref[block, :] = mapped * wide(1.0 / diagonal_ref[block, :], mapped.shape[1])
        cross = cross + column_sums(here * mapped)
    row_ids = lax.broadcasted_iota(jnp.int32, cross.shape, 0)
    sums_ref[...] = jnp.where(row_ids == 1, jnp.sum(cross, axis=0, keepdims=True), norm_ref[...])
    stores = [copies.start(scaled_ref, scaled_hbm)]
    for other in range(devices):
        start = pl.multiple_of(table_ref[3, other] * tile, tile)
        stores.append(copies.start(scaled_ref.at[pl.ds(start, tile)], outgoing_hbm.at[other, pl.ds(0, tile)]))
        stores.append(copies.start(sums_ref, outgoing_hbm.at[other, pl.ds(tile, SUBLANES)]))
    score_products(dosage_high_ref, dosage_low_ref, scaled_ref[...], even_ref, odd_ref)
    stores += [copies.start(odd_ref, odd_hbm), copies.start(even_ref, even_hbm)]
    far = pl.ds(tile, depth - tile)
    for row in range(block_count):
        blocks = []
        for i in range(others):
            weight = table_ref[2, row * others + i].astype(jnp.float32)
            blocks.append(weight * gathered_ref[table_ref[0, row * others + i]])
        handled_ref[pl.ds(row * tile, tile), :] = product(high_ref[row, :, far], low_ref[row, :, far], blocks)
    stores.append(copies.start(handled_ref, handled_hbm))
    wait_all(stores)


def curvature_kernel(devices, table_ref, high_hbm, low_hbm, direction_hbm, diagonal_hbm, scaled_hbm, handled_hbm,
                     later_ref, *refs):
    sums_ref, high_ref, low_ref, direction_ref, diagonal_ref, scaled_ref, handled_ref, semaphores = refs[-8:]
    block_count, tile, depth = high_ref.shape
    copies = Copies(semaphores)
    wait_all([copies.start(source, target) for source, target in (
        (scaled_hbm, scaled_ref), (direction_hbm, direction_ref), (high_hbm, high_ref), (low_hbm, low_ref),
        (handled_hbm, handled_ref), (diagonal_hbm, diagonal_ref),
    )])
    others = depth // tile - 1
    first_sums = later_ref[0, pl.ds(tile, SUBLANES), :]
    for other in range(1, devices):
        first_sums = first_sums + later_ref[other, pl.ds(tile, SUBLANES), :]
    rho = first_sums[1:2, :] / first_sums[0:1, :]
    norm = jnp.zeros(first_sums.shape, jnp.float32)
    bend = jnp.zeros(first_sums.shape, jnp.float32)
    for row in range(block_count):
        block = pl.ds(row * tile, tile)
        here = scaled_ref[block, :] - rho * direction_ref[block, :]
        blocks = [here]
        for i in range(others):
            entry = row * others + i
            weight = table_ref[2, entry].astype(jnp.float32)
            blocks.append(weight * later_ref[table_ref[1, entry], pl.ds(0, tile), :])
        mapped = product(high_ref[row], low_ref[row], blocks) - rho * handled_ref[block, :]
        norm = norm + column_sums(here * here * wide(diagonal_ref[block, :], here.shape[1]))
        bend = bend + column_sums(here * mapped)
    row_ids = lax.broadcasted_iota(jnp.int32, first_sums.shape, 0)
    sums = jnp.where(row_ids == 2, jnp.sum(norm, axis=0, keepdims=True), first_sums)
    sums = jnp.where(row_ids == 3, jnp.sum(bend, axis=0, keepdims=True), sums)
    for i in range(2 * devices):
        sums_ref[i] = sums


def add_kernel(kept_ref, taken_ref, *refs):
    near_ref, far_ref = refs[-2:]
    count = near_ref.shape[0]
    near_ref[...] = kept_ref[pl.ds(0, count)] + taken_ref[pl.ds(0, count)]
    far_ref[...] = kept_ref[pl.ds(count, count)] + taken_ref[pl.ds(count, count)]


def last_add_kernel(first_kept_ref, first_taken_ref, second_kept_ref, second_taken_ref, own_ref, other_ref):
    rows = own_ref.shape[1]
    for i, (kept_ref, taken_ref) in enumerate(
        ((first_kept_ref, first_taken_ref), (second_kept_ref, second_taken_ref))
    ):
        own_ref[i] = kept_ref[0, pl.ds(0, rows), :] + taken_ref[0, pl.ds(0, rows), :]
        other_ref[i] = kept_ref[0, pl.ds(rows, rows), :] + taken_ref[0, pl.ds(rows, rows), :]


def group_kernel(order, own_ref, other_ref, high_ref, low_ref):
    rows = own_ref.shape[0] // (2 * len(order))
    me = lax.axis_index("samples")
    for odd in range(2):
        for i, distance in enumerate(order):
            start = pl.multiple_of((me ^ distance ^ odd) * rows, rows)
            for j, dosage_ref in enumerate((own_ref, other_ref)):
                high, low = split(dosage_ref[pl.ds(start, rows), :])
                here = pl.ds((2 * i + j) * rows, rows)
                high_ref[odd, here, :] = high
                low_ref[odd, here, :] = low


def coefficients(sums, shared):
    norm, cross = sums[0:1, :], sums[1:2, :]
    later_norm, bend = shared[2:3, :], shared[3:4, :]
    curve = norm + cross
    ratio = later_norm / curve
    step = jnp.where(later_norm > 0, later_norm / (later_norm + bend - later_norm * ratio), 0.0)
    start = norm / curve
    return start * (1.0 + step * (ratio + cross / norm)), -start * step


def solved_kernel(devices, direction_ref, scaled_ref, sums_ref, solved_hbm, factors_ref, solved_ref, semaphores):
    people, columns = direction_ref.shape
    column = lax.axis_index("cols")
    copies = Copies(semaphores)

    def total(which):
        sums = sums_ref[which]
        shared = sums
        for i in range(1, devices):
            shared = shared + sums_ref[2 * i + which]
        return sums, shared

    along, across = coefficients(*total(column))
    factors = jnp.concatenate([along, across, *coefficients(*total(1 - column))], axis=0)
    factors_ref[...] = jnp.concatenate([factors, factors], axis=0)
    stores = []
    part_rows = people // 4
    for part in range(4):
        block = pl.ds(part * part_rows, part_rows)
        solved_ref[block, :] = along * direction_ref[block, :] + across * scaled_ref[block, :]
        stores.append(copies.start(solved_ref.at[block], solved_hbm.at[block]))
    wait_all(stores)


def scores_kernel(norm_scale, factors_ref, own_ref, other_ref, scores_ref):
    columns = own_ref.shape[2]
    column = lax.axis_index("cols")
    for which, rows_ref, place in ((0, own_ref, column), (2, other_ref, 1 - column)):
        along, across = factors_ref[which:which + 1, :], factors_ref[which + 1:which + 2, :]
        here = pl.ds(pl.multiple_of(place * columns, columns), columns)
        scores_ref[:, here] = norm_scale * (along * rows_ref[0] + across * rows_ref[1])


def call(kernel, out_shape, in_specs, out_specs, scratch_shapes=(), limit=VMEM_LIMIT):
    return pl.pallas_call(
        kernel,
        out_shape=out_shape,
        in_specs=in_specs,
        out_specs=out_specs,
        scratch_shapes=list(scratch_shapes),
        compiler_params=pltpu.CompilerParams(vmem_limit_bytes=limit),
    )


def swap(values, axis, devices, step):
    return lax.ppermute(values, axis, [(i, i ^ step) for i in range(devices)])


def after(value, *others):
    return lax.optimization_barrier((value, *others))[0]


def per_device(kinship, relatives, variance, phenotypes, dosage):
    devices = lax.axis_size("samples")
    block_count, positions, tile = kinship.shape[:3]
    people, columns = phenotypes.shape
    variants = dosage.shape[1]
    share_rows = variants // devices
    entries = block_count * (positions - 1)
    capacity = -(-entries // (devices - 1))
    assert capacity <= 2
    hbm = pl.BlockSpec(memory_space=pltpu.HBM)
    anywhere = pl.BlockSpec(memory_space=pl.ANY)
    vmem = pl.BlockSpec(memory_space=pltpu.VMEM)
    smem = pl.BlockSpec(memory_space=pltpu.SMEM)
    float_of = lambda *shape: jax.ShapeDtypeStruct(shape, jnp.float32)
    room = lambda *shape: pltpu.VMEM(shape, jnp.float32)
    full = float_of(people, columns)
    full_room = room(people, columns)
    half = devices // 2
    near_by = list(range(half - 1, 0, -1))
    at_home = lambda *arrays: [pltpu.with_memory_space_constraint(array, pltpu.HBM) for array in arrays]
    kinship, = at_home(kinship)
    tiles_room = pltpu.VMEM((block_count, tile, positions * tile), jnp.bfloat16)
    tiles_out = pltpu.HBM((block_count, tile, positions * tile), jnp.bfloat16)
    full_out = pltpu.HBM((people, columns), jnp.float32)
    direction, direction_kept_hbm, diagonal, norm = call(
        direction_kernel,
        [full, full_out, pltpu.HBM((people, LANES), jnp.float32), float_of(SUBLANES, columns)],
        [hbm] * 3,
        [vmem, hbm, hbm, vmem],
        [
            room(*kinship.shape), room(block_count, tile), full_room, room(people, LANES),
            pltpu.SemaphoreType.DMA((3 * block_count + 2,)),
        ],
    )(
        kinship, *at_home(variance.reshape(block_count, tile), phenotypes)
    )
    def to_mates(blocks):
        return [swap(blocks[k - 1], "samples", devices, k) for k in near_by]

    bits = half.bit_length() - 1
    even = [sum(((i >> b) & 1) << (bits - b) for b in range(bits)) for i in range(half)]
    steps = [2 << i for i in range(bits)]
    other_dosage = with_layout_constraint(swap(after(dosage, direction), "cols", 2, 1), Layout((0, 1)))
    table, forward, *outgoing = call(
        functools.partial(route_kernel, devices, capacity, block_count),
        [
            jax.ShapeDtypeStruct((4, max(entries, devices)), jnp.int32),
            jax.ShapeDtypeStruct((capacity, half), jnp.int32),
        ] + [float_of(capacity, tile, columns)] * (half - 1),
        [smem, vmem, anywhere],
        [smem, smem] + [vmem] * (half - 1),
        [pltpu.SMEM((devices,), jnp.int32), pltpu.SMEM((devices,), jnp.int32)],
    )(relatives.T, direction, other_dosage)
    high, low = call(
        tiles_kernel, [tiles_out] * 2, [hbm], [hbm] * 2,
        [room(*kinship.shape), tiles_room, tiles_room, pltpu.SemaphoreType.DMA((3,))],
    )(kinship)

    parts = jax.ShapeDtypeStruct((2, variants, people), jnp.bfloat16)
    large = VMEM_LIMIT if variants <= people else LARGE_VMEM
    grouped = call(
        functools.partial(group_kernel, even), [parts] * 2, [vmem] * 2, [vmem] * 2, limit=large
    )(after(dosage, table).T, other_dosage.T)

    products = float_of(half, 2 * share_rows, columns)

    def add_step(kept, taken, *gates):
        rows = float_of(kept.shape[0] // 2, 2 * share_rows, columns)
        return call(
            add_kernel, [rows] * 2, [vmem] * (2 + len(gates)), [vmem] * 2
        )(kept, taken, *gates)

    partner = swap(direction, "samples", devices, half)
    near = to_mates(outgoing)
    direction_even, direction_odd = call(
        score_kernel, [products] * 2, [vmem] * 3, [vmem] * 2, limit=large
    )(*grouped, direction)
    direction_share = swap(direction_odd, "samples", devices, 1)
    far = to_mates(call(
        forward_kernel,
        [float_of(capacity, tile, columns)] * (half - 1),
        [smem, vmem] + [anywhere] * (half + 1) + [hbm] * 2,
        [vmem] * (half - 1),
    )(forward, partner, *near, direction_even, direction_odd, *at_home(high, low)))
    received = near + far + [partner.reshape(block_count, tile, columns)]
    products_out = pltpu.HBM(products.shape, jnp.float32)
    scaled, handled, outgoing, scaled_even, scaled_odd = call(
        functools.partial(apply_kernel, devices, capacity),
        [
            full_out, full_out, pltpu.HBM((devices, tile + SUBLANES, columns), jnp.float32), products_out, products_out,
        ],
        [smem, hbm, hbm, hbm] + [vmem] * (devices + 3) + [anywhere],
        [hbm] * 5,
        [
            room(devices * capacity + block_count, tile, columns), tiles_room, tiles_room, room(people, LANES), full_room,
            full_room, room(SUBLANES, columns), room(*products.shape), room(*products.shape),
            pltpu.SemaphoreType.DMA((2 * devices + 7,)),
        ],
        limit=large,
    )(table, high, low, diagonal, direction, norm, *grouped, *received, direction_share)
    later = lax.all_to_all(outgoing, "samples", split_axis=0, concat_axis=0, tiled=True)
    scaled_share = swap(scaled_odd, "samples", devices, 1)
    direction_kept, direction_given = add_step(direction_even, direction_share)
    direction_taken = swap(after(direction_given, scaled), "samples", devices, steps[0])
    scaled_kept, scaled_given = add_step(scaled_even, scaled_share)
    scaled_taken = swap(scaled_given, "samples", devices, steps[0])
    sums = call(
        functools.partial(curvature_kernel, devices),
        float_of(2 * devices, SUBLANES, columns),
        [smem] + [hbm] * 6 + [vmem, anywhere],
        vmem,
        [tiles_room, tiles_room, full_room, room(people, LANES), full_room, full_room, pltpu.SemaphoreType.DMA((6,))],
    )(table, *at_home(high, low, direction_kept_hbm, diagonal, scaled, handled), later, scaled_given)
    all_sums = lax.all_to_all(sums, ("samples", "cols"), split_axis=0, concat_axis=0, tiled=True)
    for step in steps[1:]:
        scaled_kept, scaled_given = add_step(scaled_kept, scaled_taken, sums)
        scaled_taken = swap(scaled_given, "samples", devices, step)
    for step in steps[1:]:
        direction_kept, direction_given = add_step(direction_kept, direction_taken, sums)
        direction_taken = swap(direction_given, "samples", devices, step)
    rows = float_of(2, share_rows, columns)
    own_scores, other_scores = call(
        last_add_kernel, [rows] * 2, [vmem] * 4, [vmem] * 2
    )(direction_kept, direction_taken, scaled_kept, scaled_taken)
    solved, factors = call(
        functools.partial(solved_kernel, devices),
        [full, float_of(SUBLANES, columns)],
        [vmem] * 3,
        [hbm, vmem],
        [full_room, pltpu.SemaphoreType.DMA((4,))],
    )(direction_kept_hbm, scaled, all_sums)
    scores = call(
        functools.partial(scores_kernel, 1.0 / math.sqrt(people * devices)),
        float_of(share_rows, 2 * columns), [vmem] * 3, vmem,
    )(factors, own_scores, swap(other_scores, "cols", 2, 1))
    return (solved, scores)


def solution(mesh):
    return jax.shard_map(
        per_device,
        mesh=mesh,
        in_specs=(
            P(("groups", "samples"), None, None, None),
            P("groups", None),
            P(("groups", "samples")),
            P(("groups", "samples"), "cols"),
            P(("groups", "samples"), "cols"),
        ),
        out_specs=(P(("groups", "samples"), "cols"), P(("groups", "cols", "samples"), None)),
        check_vma=False,
    )
```

```python
import functools
import math

import jax
import jax.numpy as jnp
from jax import lax
from jax.experimental import pallas as pl
from jax.experimental.layout import Layout, with_layout_constraint
from jax.experimental.pallas import tpu as pltpu
from jax.sharding import PartitionSpec as P

VMEM_LIMIT = 24 * 1024 * 1024
LARGE_VMEM = 56 * 1024 * 1024
SUBLANES = 8
LANES = 128


def split(values):
    high = values.astype(jnp.bfloat16)
    low = (values - high.astype(jnp.float32)).astype(jnp.bfloat16)
    return high, low


def dot(left, right):
    return jnp.dot(left, right, preferred_element_type=jnp.float32)


def on_diagonal(size):
    rows = lax.broadcasted_iota(jnp.int32, (size, size), 0)
    return rows == lax.broadcasted_iota(jnp.int32, (size, size), 1)


def wide(values, columns):
    return jnp.concatenate([values] * (columns // LANES), axis=1)


def split_tiles(kinship_ref, high_ref, low_ref):
    block_count, positions, tile = kinship_ref.shape[:3]
    diagonal_mask = on_diagonal(tile)
    for row in range(block_count):
        for position in range(positions):
            values = kinship_ref[row, position]
            if position == 0:
                values = jnp.where(diagonal_mask, 0.0, values)
            high, low = split(values)
            high_ref[row, :, pl.ds(position * tile, tile)] = high
            low_ref[row, :, pl.ds(position * tile, tile)] = low


def product(high, low, blocks):
    parts = [split(block) for block in blocks]
    blocks_high = jnp.concatenate([part[0] for part in parts], axis=0)
    blocks_low = jnp.concatenate([part[1] for part in parts], axis=0)
    return dot(high, blocks_high) + (dot(low, blocks_high) + dot(high, blocks_low))


def column_sums(values):
    rows, columns = values.shape
    return jnp.sum(values.reshape(rows // SUBLANES, SUBLANES, columns), axis=0)


class Copies:
    def __init__(self, semaphores):
        self.semaphores = semaphores
        self.count = 0

    def start(self, source, target):
        copy = pltpu.make_async_copy(source, target, self.semaphores.at[self.count])
        self.count += 1
        copy.start()
        return copy


def wait_all(copies):
    for copy in copies:
        copy.wait()


def quotient(value, divisor):
    if divisor & (divisor - 1) == 0:
        return lax.shift_right_logical(value, jnp.int32(divisor.bit_length() - 1))
    return lax.div(value, jnp.int32(divisor))


def direction_kernel(kinship_hbm, variance_hbm, phenotypes_hbm, direction_ref, direction_hbm, diagonal_hbm, sums_ref,
                     kinship_ref, variance_ref, phenotypes_ref, diagonal_ref, semaphores):
    block_count, positions, tile = kinship_ref.shape[:3]
    copies = Copies(semaphores)
    loads = [copies.start(variance_hbm, variance_ref)]
    for row in range(block_count):
        block = pl.ds(row * tile, tile)
        loads.append(copies.start(kinship_hbm.at[row], kinship_ref.at[row]))
        loads.append(copies.start(phenotypes_hbm.at[block], phenotypes_ref.at[block]))
    stores = []
    norm = jnp.zeros((SUBLANES, direction_ref.shape[1]), jnp.float32)
    diagonal_mask = on_diagonal(tile)
    loads[0].wait()
    for row in range(block_count):
        wait_all(loads[1 + 2 * row:3 + 2 * row])
        block = pl.ds(row * tile, tile)
        total = jnp.where(diagonal_mask, variance_ref[row:row + 1, :], kinship_ref[row, 0])
        for position in range(1, positions):
            total = total + kinship_ref[row, position]
        diagonal = jnp.sum(total, axis=1, keepdims=True)
        diagonal_ref[block, :] = jnp.broadcast_to(diagonal, (tile, LANES))
        here = phenotypes_ref[block, :] * (1.0 / diagonal)
        direction_ref[block, :] = here
        norm = norm + column_sums(here * phenotypes_ref[block, :])
        stores.append(copies.start(direction_ref.at[block], direction_hbm.at[block]))
    stores.append(copies.start(diagonal_ref, diagonal_hbm))
    row_ids = lax.broadcasted_iota(jnp.int32, norm.shape, 0)
    sums_ref[...] = jnp.where(row_ids == 0, jnp.sum(norm, axis=0, keepdims=True), 0.0)
    wait_all(stores)


def tiles_kernel(kinship_hbm, high_hbm, low_hbm, kinship_ref, high_ref, low_ref, semaphores):
    copies = Copies(semaphores)
    copies.start(kinship_hbm, kinship_ref).wait()
    split_tiles(kinship_ref, high_ref, low_ref)
    wait_all([copies.start(high_ref, high_hbm), copies.start(low_ref, low_hbm)])


def route_kernel(devices, capacity, block_count, list_ref, direction_ref, gate_ref, table_ref, forward_ref, *refs):
    half = devices // 2
    outgoing_refs, (first_ref, last_ref) = refs[:half - 1], refs[half - 1:]
    positions = list_ref.shape[0] + 1
    tile = direction_ref.shape[0] // block_count
    me = lax.axis_index("samples")
    partner = me ^ half
    spare = me ^ 1
    top = block_count * block_count

    def collect(device):
        for j in range(devices):
            first_ref[j] = jnp.int32(top)
            last_ref[j] = jnp.int32(-1)
        found = []
        for row in range(block_count):
            for position in range(positions - 1):
                listed = list_ref[position, device * block_count + row]
                live = listed >= 0
                safe = jnp.maximum(listed, 0)
                other = quotient(safe, block_count)
                far_block = safe - other * block_count
                key = jnp.where(device < other, row * block_count + far_block, far_block * block_count + row)
                first_ref[other] = jnp.minimum(first_ref[other], jnp.where(live, key, top))
                last_ref[other] = jnp.maximum(last_ref[other], jnp.where(live, key, -1))
                found.append((live, other, far_block, key))
        return found

    def blocks_for(device, other):
        blocks = []
        for key in (first_ref[other], last_ref[other]):
            safe = jnp.clip(key, 0, top - 1)
            lower = quotient(safe, block_count)
            higher = safe - lower * block_count
            blocks.append(jnp.where(key == safe, jnp.where(device < other, lower, higher), 0))
        return blocks

    collect(partner)
    for k in range(1, half):
        blocks = blocks_for(partner, me ^ k)
        for slot in range(capacity):
            forward_ref[slot, k] = blocks[slot]
    for entry, (live, other, far_block, key) in enumerate(collect(me)):
        first, last = first_ref[other], last_ref[other]
        handled = jnp.where(me < other, first, last)
        weight = jnp.where(first == last, 1, 2)
        slot = jnp.where(key == first, 0, capacity - 1)
        place = jnp.where(other == partner, devices * capacity + far_block, other * capacity + slot)
        table_ref[0, entry] = jnp.where(live, place, spare * capacity)
        table_ref[1, entry] = jnp.where(live, other, spare)
        table_ref[2, entry] = jnp.where(live & (key == handled), weight, 0)
    for other in range(devices):
        blocks = blocks_for(me, other)
        table_ref[3, other] = jnp.where(me < other, blocks[1], blocks[0])
    near = [blocks_for(me, me ^ k) for k in range(1, half)]
    for k in range(1, half):
        for slot in range(capacity):
            start = pl.multiple_of(near[k - 1][slot] * tile, tile)
            outgoing_refs[k - 1][slot] = direction_ref[pl.ds(start, tile), :]


def forward_kernel(forward_ref, partner_ref, *refs):
    capacity, half = forward_ref.shape
    outgoing_refs = refs[1 - half:]
    tile = outgoing_refs[0].shape[1]
    for k in range(1, half):
        for slot in range(capacity):
            start = pl.multiple_of(forward_ref[slot, k] * tile, tile)
            outgoing_refs[k - 1][slot] = partner_ref[pl.ds(start, tile), :]


def gather_received(devices, capacity, received_refs, gathered_ref):
    half = devices // 2
    me = lax.axis_index("samples")
    near_refs, far_refs, partner_ref = received_refs[:half - 1], received_refs[half - 1:-1], received_refs[-1]
    gathered_ref[pl.ds(devices * capacity, partner_ref.shape[0])] = partner_ref[...]
    for i in range(half - 1):
        mate = me ^ (half - 1 - i)
        gathered_ref[pl.ds(mate * capacity, capacity)] = near_refs[i][...]
        gathered_ref[pl.ds((mate ^ half) * capacity, capacity)] = far_refs[i][...]


def score_products(high_ref, low_ref, values, even_ref, odd_ref):
    count, rows = even_ref.shape[:2]
    for odd, out_ref in enumerate((even_ref, odd_ref)):
        for i in range(0, count, 4):
            here = pl.ds(i * rows, 4 * rows)
            total = product(high_ref[odd, here, :], low_ref[odd, here, :], [values])
            out_ref[pl.ds(i, 4)] = total.reshape(4, rows, -1)


def score_kernel(high_ref, low_ref, values_ref, even_ref, odd_ref):
    score_products(high_ref, low_ref, values_ref[...], even_ref, odd_ref)


def apply_kernel(devices, capacity, table_ref, high_hbm, low_hbm, diagonal_hbm, direction_ref, norm_ref, dosage_high_ref,
                 dosage_low_ref, *refs):
    received_refs = refs[:devices - 1]
    (scaled_hbm, handled_hbm, outgoing_hbm, even_hbm, odd_hbm, gathered_ref, high_ref, low_ref, diagonal_ref, scaled_ref,
     handled_ref, sums_ref, even_ref, odd_ref, semaphores) = refs[-15:]
    copies = Copies(semaphores)
    loads = [
        copies.start(high_hbm, high_ref), copies.start(low_hbm, low_ref), copies.start(diagonal_hbm, diagonal_ref)
    ]
    gather_received(devices, capacity, received_refs, gathered_ref)
    wait_all(loads)
    block_count, tile, depth = high_ref.shape
    others = depth // tile - 1
    cross = jnp.zeros(norm_ref.shape, jnp.float32)
    for row in range(block_count):
        block = pl.ds(row * tile, tile)
        here = direction_ref[block, :]
        blocks = [here] + [gathered_ref[table_ref[0, row * others + i]] for i in range(others)]
        mapped = product(high_ref[row], low_ref[row], blocks)
        scaled_ref[block, :] = mapped * wide(1.0 / diagonal_ref[block, :], mapped.shape[1])
        cross = cross + column_sums(here * mapped)
    row_ids = lax.broadcasted_iota(jnp.int32, cross.shape, 0)
    sums_ref[...] = jnp.where(row_ids == 1, jnp.sum(cross, axis=0, keepdims=True), norm_ref[...])
    stores = [copies.start(scaled_ref, scaled_hbm)]
    for other in range(devices):
        start = pl.multiple_of(table_ref[3, other] * tile, tile)
        stores.append(copies.start(scaled_ref.at[pl.ds(start, tile)], outgoing_hbm.at[other, pl.ds(0, tile)]))
        stores.append(copies.start(sums_ref, outgoing_hbm.at[other, pl.ds(tile, SUBLANES)]))
    score_products(dosage_high_ref, dosage_low_ref, scaled_ref[...], even_ref, odd_ref)
    stores += [copies.start(odd_ref, odd_hbm), copies.start(even_ref, even_hbm)]
    far = pl.ds(tile, depth - tile)
    for row in range(block_count):
        blocks = []
        for i in range(others):
            weight = table_ref[2, row * others + i].astype(jnp.float32)
            blocks.append(weight * gathered_ref[table_ref[0, row * others + i]])
        handled_ref[pl.ds(row * tile, tile), :] = product(high_ref[row, :, far], low_ref[row, :, far], blocks)
    stores.append(copies.start(handled_ref, handled_hbm))
    wait_all(stores)


def curvature_kernel(devices, table_ref, high_hbm, low_hbm, direction_hbm, diagonal_hbm, scaled_hbm, handled_hbm,
                     later_ref, *refs):
    sums_ref, high_ref, low_ref, direction_ref, diagonal_ref, scaled_ref, handled_ref, semaphores = refs[-8:]
    block_count, tile, depth = high_ref.shape
    copies = Copies(semaphores)
    wait_all([copies.start(source, target) for source, target in (
        (scaled_hbm, scaled_ref), (direction_hbm, direction_ref), (high_hbm, high_ref), (low_hbm, low_ref),
        (handled_hbm, handled_ref), (diagonal_hbm, diagonal_ref),
    )])
    others = depth // tile - 1
    first_sums = later_ref[0, pl.ds(tile, SUBLANES), :]
    for other in range(1, devices):
        first_sums = first_sums + later_ref[other, pl.ds(tile, SUBLANES), :]
    rho = first_sums[1:2, :] / first_sums[0:1, :]
    norm = jnp.zeros(first_sums.shape, jnp.float32)
    bend = jnp.zeros(first_sums.shape, jnp.float32)
    for row in range(block_count):
        block = pl.ds(row * tile, tile)
        here = scaled_ref[block, :] - rho * direction_ref[block, :]
        blocks = [here]
        for i in range(others):
            entry = row * others + i
            weight = table_ref[2, entry].astype(jnp.float32)
            blocks.append(weight * later_ref[table_ref[1, entry], pl.ds(0, tile), :])
        mapped = product(high_ref[row], low_ref[row], blocks) - rho * handled_ref[block, :]
        norm = norm + column_sums(here * here * wide(diagonal_ref[block, :], here.shape[1]))
        bend = bend + column_sums(here * mapped)
    row_ids = lax.broadcasted_iota(jnp.int32, first_sums.shape, 0)
    sums = jnp.where(row_ids == 2, jnp.sum(norm, axis=0, keepdims=True), first_sums)
    sums = jnp.where(row_ids == 3, jnp.sum(bend, axis=0, keepdims=True), sums)
    for i in range(2 * devices):
        sums_ref[i] = sums


def add_kernel(kept_ref, taken_ref, *refs):
    near_ref, far_ref = refs[-2:]
    count = near_ref.shape[0]
    near_ref[...] = kept_ref[pl.ds(0, count)] + taken_ref[pl.ds(0, count)]
    far_ref[...] = kept_ref[pl.ds(count, count)] + taken_ref[pl.ds(count, count)]


def last_add_kernel(first_kept_ref, first_taken_ref, second_kept_ref, second_taken_ref, own_ref, other_ref):
    rows = own_ref.shape[1]
    for i, (kept_ref, taken_ref) in enumerate(
        ((first_kept_ref, first_taken_ref), (second_kept_ref, second_taken_ref))
    ):
        own_ref[i] = kept_ref[0, pl.ds(0, rows), :] + taken_ref[0, pl.ds(0, rows), :]
        other_ref[i] = kept_ref[0, pl.ds(rows, rows), :] + taken_ref[0, pl.ds(rows, rows), :]


def group_kernel(order, own_ref, other_ref, high_ref, low_ref):
    rows = own_ref.shape[0] // (2 * len(order))
    me = lax.axis_index("samples")
    for odd in range(2):
        for i, distance in enumerate(order):
            start = pl.multiple_of((me ^ distance ^ odd) * rows, rows)
            for j, dosage_ref in enumerate((own_ref, other_ref)):
                high, low = split(dosage_ref[pl.ds(start, rows), :])
                here = pl.ds((2 * i + j) * rows, rows)
                high_ref[odd, here, :] = high
                low_ref[odd, here, :] = low


def coefficients(sums, shared):
    norm, cross = sums[0:1, :], sums[1:2, :]
    later_norm, bend = shared[2:3, :], shared[3:4, :]
    curve = norm + cross
    ratio = later_norm / curve
    step = jnp.where(later_norm > 0, later_norm / (later_norm + bend - later_norm * ratio), 0.0)
    start = norm / curve
    return start * (1.0 + step * (ratio + cross / norm)), -start * step


def solved_kernel(devices, direction_ref, scaled_ref, sums_ref, solved_hbm, factors_ref, solved_ref, semaphores):
    people, columns = direction_ref.shape
    column = lax.axis_index("cols")
    copies = Copies(semaphores)

    def total(which):
        sums = sums_ref[which]
        shared = sums
        for i in range(1, devices):
            shared = shared + sums_ref[2 * i + which]
        return sums, shared

    along, across = coefficients(*total(column))
    factors = jnp.concatenate([along, across, *coefficients(*total(1 - column))], axis=0)
    factors_ref[...] = jnp.concatenate([factors, factors], axis=0)
    stores = []
    part_rows = people // 4
    for part in range(4):
        block = pl.ds(part * part_rows, part_rows)
        solved_ref[block, :] = along * direction_ref[block, :] + across * scaled_ref[block, :]
        stores.append(copies.start(solved_ref.at[block], solved_hbm.at[block]))
    wait_all(stores)


def scores_kernel(norm_scale, factors_ref, own_ref, other_ref, scores_ref):
    columns = own_ref.shape[2]
    column = lax.axis_index("cols")
    for which, rows_ref, place in ((0, own_ref, column), (2, other_ref, 1 - column)):
        along, across = factors_ref[which:which + 1, :], factors_ref[which + 1:which + 2, :]
        here = pl.ds(pl.multiple_of(place * columns, columns), columns)
        scores_ref[:, here] = norm_scale * (along * rows_ref[0] + across * rows_ref[1])


def call(kernel, out_shape, in_specs, out_specs, scratch_shapes=(), limit=VMEM_LIMIT):
    return pl.pallas_call(
        kernel,
        out_shape=out_shape,
        in_specs=in_specs,
        out_specs=out_specs,
        scratch_shapes=list(scratch_shapes),
        compiler_params=pltpu.CompilerParams(vmem_limit_bytes=limit),
    )


def swap(values, axis, devices, step):
    return lax.ppermute(values, axis, [(i, i ^ step) for i in range(devices)])


def after(value, *others):
    return lax.optimization_barrier((value, *others))[0]


def per_device(kinship, relatives, variance, phenotypes, dosage):
    devices = lax.axis_size("samples")
    block_count, positions, tile = kinship.shape[:3]
    people, columns = phenotypes.shape
    variants = dosage.shape[1]
    share_rows = variants // devices
    entries = block_count * (positions - 1)
    capacity = -(-entries // (devices - 1))
    assert capacity <= 2
    hbm = pl.BlockSpec(memory_space=pltpu.HBM)
    anywhere = pl.BlockSpec(memory_space=pl.ANY)
    vmem = pl.BlockSpec(memory_space=pltpu.VMEM)
    smem = pl.BlockSpec(memory_space=pltpu.SMEM)
    float_of = lambda *shape: jax.ShapeDtypeStruct(shape, jnp.float32)
    room = lambda *shape: pltpu.VMEM(shape, jnp.float32)
    full = float_of(people, columns)
    full_room = room(people, columns)
    half = devices // 2
    near_by = list(range(half - 1, 0, -1))
    at_home = lambda *arrays: [pltpu.with_memory_space_constraint(array, pltpu.HBM) for array in arrays]
    kinship, = at_home(kinship)
    tiles_room = pltpu.VMEM((block_count, tile, positions * tile), jnp.bfloat16)
    tiles_out = pltpu.HBM((block_count, tile, positions * tile), jnp.bfloat16)
    full_out = pltpu.HBM((people, columns), jnp.float32)
    direction, direction_kept_hbm, diagonal, norm = call(
        direction_kernel,
        [full, full_out, pltpu.HBM((people, LANES), jnp.float32), float_of(SUBLANES, columns)],
        [hbm] * 3,
        [vmem, hbm, hbm, vmem],
        [
            room(*kinship.shape), room(block_count, tile), full_room, room(people, LANES),
            pltpu.SemaphoreType.DMA((3 * block_count + 2,)),
        ],
    )(
        kinship, *at_home(variance.reshape(block_count, tile), phenotypes)
    )
    def to_mates(blocks):
        return [swap(blocks[k - 1], "samples", devices, k) for k in near_by]

    bits = half.bit_length() - 1
    even = [sum(((i >> b) & 1) << (bits - b) for b in range(bits)) for i in range(half)]
    steps = [2 << i for i in range(bits)]
    other_dosage = with_layout_constraint(swap(after(dosage, direction), "cols", 2, 1), Layout((0, 1)))
    table, forward, *outgoing = call(
        functools.partial(route_kernel, devices, capacity, block_count),
        [
            jax.ShapeDtypeStruct((4, max(entries, devices)), jnp.int32),
            jax.ShapeDtypeStruct((capacity, half), jnp.int32),
        ] + [float_of(capacity, tile, columns)] * (half - 1),
        [smem, vmem, anywhere],
        [smem, smem] + [vmem] * (half - 1),
        [pltpu.SMEM((devices,), jnp.int32), pltpu.SMEM((devices,), jnp.int32)],
    )(relatives.T, direction, other_dosage)
    high, low = call(
        tiles_kernel, [tiles_out] * 2, [hbm], [hbm] * 2,
        [room(*kinship.shape), tiles_room, tiles_room, pltpu.SemaphoreType.DMA((3,))],
    )(kinship)

    parts = jax.ShapeDtypeStruct((2, variants, people), jnp.bfloat16)
    large = VMEM_LIMIT if variants <= people else LARGE_VMEM
    grouped = call(
        functools.partial(group_kernel, even), [parts] * 2, [vmem] * 2, [vmem] * 2, limit=large
    )(after(dosage, table).T, other_dosage.T)

    products = float_of(half, 2 * share_rows, columns)

    def add_step(kept, taken, *gates):
        rows = float_of(kept.shape[0] // 2, 2 * share_rows, columns)
        return call(
            add_kernel, [rows] * 2, [vmem] * (2 + len(gates)), [vmem] * 2
        )(kept, taken, *gates)

    partner = swap(direction, "samples", devices, half)
    near = to_mates(outgoing)
    direction_even, direction_odd = call(
        score_kernel, [products] * 2, [vmem] * 3, [vmem] * 2, limit=large
    )(*grouped, direction)
    direction_share = swap(direction_odd, "samples", devices, 1)
    far = to_mates(call(
        forward_kernel,
        [float_of(capacity, tile, columns)] * (half - 1),
        [smem, vmem] + [anywhere] * 3 + [hbm] * 2,
        [vmem] * (half - 1),
    )(forward, partner, near[0], direction_even, direction_odd, *at_home(high, low)))
    received = near + far + [partner.reshape(block_count, tile, columns)]
    products_out = pltpu.HBM(products.shape, jnp.float32)
    scaled, handled, outgoing, scaled_even, scaled_odd = call(
        functools.partial(apply_kernel, devices, capacity),
        [
            full_out, full_out, pltpu.HBM((devices, tile + SUBLANES, columns), jnp.float32), products_out, products_out,
        ],
        [smem, hbm, hbm, hbm] + [vmem] * (devices + 3) + [anywhere],
        [hbm] * 5,
        [
            room(devices * capacity + block_count, tile, columns), tiles_room, tiles_room, room(people, LANES), full_room,
            full_room, room(SUBLANES, columns), room(*products.shape), room(*products.shape),
            pltpu.SemaphoreType.DMA((2 * devices + 7,)),
        ],
        limit=large,
    )(table, high, low, diagonal, direction, norm, *grouped, *received, direction_share)
    later = lax.all_to_all(outgoing, "samples", split_axis=0, concat_axis=0, tiled=True)
    scaled_share = swap(scaled_odd, "samples", devices, 1)
    direction_kept, direction_given = add_step(direction_even, direction_share)
    direction_taken = swap(after(direction_given, scaled), "samples", devices, steps[0])
    scaled_kept, scaled_given = add_step(scaled_even, scaled_share)
    scaled_taken = swap(scaled_given, "samples", devices, steps[0])
    sums = call(
        functools.partial(curvature_kernel, devices),
        float_of(2 * devices, SUBLANES, columns),
        [smem] + [hbm] * 6 + [vmem, anywhere],
        vmem,
        [tiles_room, tiles_room, full_room, room(people, LANES), full_room, full_room, pltpu.SemaphoreType.DMA((6,))],
    )(table, *at_home(high, low, direction_kept_hbm, diagonal, scaled, handled), later, scaled_given)
    all_sums = lax.all_to_all(sums, ("samples", "cols"), split_axis=0, concat_axis=0, tiled=True)
    for step in steps[1:]:
        scaled_kept, scaled_given = add_step(scaled_kept, scaled_taken, sums)
        scaled_taken = swap(scaled_given, "samples", devices, step)
    for step in steps[1:]:
        direction_kept, direction_given = add_step(direction_kept, direction_taken, sums)
        direction_taken = swap(direction_given, "samples", devices, step)
    rows = float_of(2, share_rows, columns)
    own_scores, other_scores = call(
        last_add_kernel, [rows] * 2, [vmem] * 4, [vmem] * 2
    )(direction_kept, direction_taken, scaled_kept, scaled_taken)
    solved, factors = call(
        functools.partial(solved_kernel, devices),
        [full, float_of(SUBLANES, columns)],
        [vmem] * 3,
        [hbm, vmem],
        [full_room, pltpu.SemaphoreType.DMA((4,))],
    )(direction_kept_hbm, scaled, all_sums)
    scores = call(
        functools.partial(scores_kernel, 1.0 / math.sqrt(people * devices)),
        float_of(share_rows, 2 * columns), [vmem] * 3, vmem,
    )(factors, own_scores, swap(other_scores, "cols", 2, 1))
    return (solved, scores)


def solution(mesh):
    return jax.shard_map(
        per_device,
        mesh=mesh,
        in_specs=(
            P(("groups", "samples"), None, None, None),
            P("groups", None),
            P(("groups", "samples")),
            P(("groups", "samples"), "cols"),
            P(("groups", "samples"), "cols"),
        ),
        out_specs=(P(("groups", "samples"), "cols"), P(("groups", "cols", "samples"), None)),
        check_vma=False,
    )
```

```python
import functools
import math

import jax
import jax.numpy as jnp
from jax import lax
from jax.experimental import pallas as pl
from jax.experimental.layout import Layout, with_layout_constraint
from jax.experimental.pallas import tpu as pltpu
from jax.sharding import PartitionSpec as P

VMEM_LIMIT = 24 * 1024 * 1024
LARGE_VMEM = 56 * 1024 * 1024
SUBLANES = 8
LANES = 128


def split(values):
    high = values.astype(jnp.bfloat16)
    low = (values - high.astype(jnp.float32)).astype(jnp.bfloat16)
    return high, low


def dot(left, right):
    return jnp.dot(left, right, preferred_element_type=jnp.float32)


def on_diagonal(size):
    rows = lax.broadcasted_iota(jnp.int32, (size, size), 0)
    return rows == lax.broadcasted_iota(jnp.int32, (size, size), 1)


def wide(values, columns):
    return jnp.concatenate([values] * (columns // LANES), axis=1)


def split_tiles(kinship_ref, high_ref, low_ref):
    block_count, positions, tile = kinship_ref.shape[:3]
    diagonal_mask = on_diagonal(tile)
    for row in range(block_count):
        for position in range(positions):
            values = kinship_ref[row, position]
            if position == 0:
                values = jnp.where(diagonal_mask, 0.0, values)
            high, low = split(values)
            high_ref[row, :, pl.ds(position * tile, tile)] = high
            low_ref[row, :, pl.ds(position * tile, tile)] = low


def product(high, low, blocks):
    parts = [split(block) for block in blocks]
    blocks_high = jnp.concatenate([part[0] for part in parts], axis=0)
    blocks_low = jnp.concatenate([part[1] for part in parts], axis=0)
    return dot(high, blocks_high) + (dot(low, blocks_high) + dot(high, blocks_low))


def column_sums(values):
    rows, columns = values.shape
    return jnp.sum(values.reshape(rows // SUBLANES, SUBLANES, columns), axis=0)


class Copies:
    def __init__(self, semaphores):
        self.semaphores = semaphores
        self.count = 0

    def start(self, source, target):
        copy = pltpu.make_async_copy(source, target, self.semaphores.at[self.count])
        self.count += 1
        copy.start()
        return copy


def wait_all(copies):
    for copy in copies:
        copy.wait()


def quotient(value, divisor):
    if divisor & (divisor - 1) == 0:
        return lax.shift_right_logical(value, jnp.int32(divisor.bit_length() - 1))
    return lax.div(value, jnp.int32(divisor))


def direction_kernel(kinship_hbm, variance_hbm, phenotypes_hbm, direction_ref, direction_hbm, diagonal_hbm, sums_ref,
                     kinship_ref, variance_ref, phenotypes_ref, diagonal_ref, semaphores):
    block_count, positions, tile = kinship_ref.shape[:3]
    copies = Copies(semaphores)
    loads = [copies.start(variance_hbm, variance_ref)]
    for row in range(block_count):
        block = pl.ds(row * tile, tile)
        loads.append(copies.start(kinship_hbm.at[row], kinship_ref.at[row]))
        loads.append(copies.start(phenotypes_hbm.at[block], phenotypes_ref.at[block]))
    stores = []
    norm = jnp.zeros((SUBLANES, direction_ref.shape[1]), jnp.float32)
    diagonal_mask = on_diagonal(tile)
    loads[0].wait()
    for row in range(block_count):
        wait_all(loads[1 + 2 * row:3 + 2 * row])
        block = pl.ds(row * tile, tile)
        total = jnp.where(diagonal_mask, variance_ref[row:row + 1, :], kinship_ref[row, 0])
        for position in range(1, positions):
            total = total + kinship_ref[row, position]
        diagonal = jnp.sum(total, axis=1, keepdims=True)
        diagonal_ref[block, :] = jnp.broadcast_to(diagonal, (tile, LANES))
        here = phenotypes_ref[block, :] * (1.0 / diagonal)
        direction_ref[block, :] = here
        norm = norm + column_sums(here * phenotypes_ref[block, :])
        stores.append(copies.start(direction_ref.at[block], direction_hbm.at[block]))
    stores.append(copies.start(diagonal_ref, diagonal_hbm))
    row_ids = lax.broadcasted_iota(jnp.int32, norm.shape, 0)
    sums_ref[...] = jnp.where(row_ids == 0, jnp.sum(norm, axis=0, keepdims=True), 0.0)
    wait_all(stores)


def tiles_kernel(kinship_hbm, high_hbm, low_hbm, kinship_ref, high_ref, low_ref, semaphores):
    copies = Copies(semaphores)
    copies.start(kinship_hbm, kinship_ref).wait()
    split_tiles(kinship_ref, high_ref, low_ref)
    wait_all([copies.start(high_ref, high_hbm), copies.start(low_ref, low_hbm)])


def route_kernel(devices, capacity, block_count, list_ref, direction_ref, gate_ref, table_ref, forward_ref, *refs):
    half = devices // 2
    outgoing_refs, (first_ref, last_ref) = refs[:half - 1], refs[half - 1:]
    positions = list_ref.shape[0] + 1
    tile = direction_ref.shape[0] // block_count
    me = lax.axis_index("samples")
    partner = me ^ half
    spare = me ^ 1
    top = block_count * block_count

    def collect(device):
        for j in range(devices):
            first_ref[j] = jnp.int32(top)
            last_ref[j] = jnp.int32(-1)
        found = []
        for row in range(block_count):
            for position in range(positions - 1):
                listed = list_ref[position, device * block_count + row]
                live = listed >= 0
                safe = jnp.maximum(listed, 0)
                other = quotient(safe, block_count)
                far_block = safe - other * block_count
                key = jnp.where(device < other, row * block_count + far_block, far_block * block_count + row)
                first_ref[other] = jnp.minimum(first_ref[other], jnp.where(live, key, top))
                last_ref[other] = jnp.maximum(last_ref[other], jnp.where(live, key, -1))
                found.append((live, other, far_block, key))
        return found

    def blocks_for(device, other):
        blocks = []
        for key in (first_ref[other], last_ref[other]):
            safe = jnp.clip(key, 0, top - 1)
            lower = quotient(safe, block_count)
            higher = safe - lower * block_count
            blocks.append(jnp.where(key == safe, jnp.where(device < other, lower, higher), 0))
        return blocks

    collect(partner)
    for k in range(1, half):
        blocks = blocks_for(partner, me ^ k)
        for slot in range(capacity):
            forward_ref[slot, k] = blocks[slot]
    for entry, (live, other, far_block, key) in enumerate(collect(me)):
        first, last = first_ref[other], last_ref[other]
        handled = jnp.where(me < other, first, last)
        weight = jnp.where(first == last, 1, 2)
        slot = jnp.where(key == first, 0, capacity - 1)
        place = jnp.where(other == partner, devices * capacity + far_block, other * capacity + slot)
        table_ref[0, entry] = jnp.where(live, place, spare * capacity)
        table_ref[1, entry] = jnp.where(live, other, spare)
        table_ref[2, entry] = jnp.where(live & (key == handled), weight, 0)
    for other in range(devices):
        blocks = blocks_for(me, other)
        table_ref[3, other] = jnp.where(me < other, blocks[1], blocks[0])
    near = [blocks_for(me, me ^ k) for k in range(1, half)]
    for k in range(1, half):
        for slot in range(capacity):
            start = pl.multiple_of(near[k - 1][slot] * tile, tile)
            outgoing_refs[k - 1][slot] = direction_ref[pl.ds(start, tile), :]


def forward_kernel(forward_ref, partner_ref, *refs):
    capacity, half = forward_ref.shape
    outgoing_refs = refs[1 - half:]
    tile = outgoing_refs[0].shape[1]
    for k in range(1, half):
        for slot in range(capacity):
            start = pl.multiple_of(forward_ref[slot, k] * tile, tile)
            outgoing_refs[k - 1][slot] = partner_ref[pl.ds(start, tile), :]


def gather_received(devices, capacity, received_refs, gathered_ref):
    half = devices // 2
    me = lax.axis_index("samples")
    near_refs, far_refs, partner_ref = received_refs[:half - 1], received_refs[half - 1:-1], received_refs[-1]
    gathered_ref[pl.ds(devices * capacity, partner_ref.shape[0])] = partner_ref[...]
    for i in range(half - 1):
        mate = me ^ (half - 1 - i)
        gathered_ref[pl.ds(mate * capacity, capacity)] = near_refs[i][...]
        gathered_ref[pl.ds((mate ^ half) * capacity, capacity)] = far_refs[i][...]


def score_products(high_ref, low_ref, values, even_ref, odd_ref):
    count, rows = even_ref.shape[:2]
    for odd, out_ref in enumerate((even_ref, odd_ref)):
        for i in range(0, count, 4):
            here = pl.ds(i * rows, 4 * rows)
            total = product(high_ref[odd, here, :], low_ref[odd, here, :], [values])
            out_ref[pl.ds(i, 4)] = total.reshape(4, rows, -1)


def score_kernel(high_ref, low_ref, values_ref, even_ref, odd_ref):
    score_products(high_ref, low_ref, values_ref[...], even_ref, odd_ref)


def apply_kernel(devices, capacity, table_ref, high_hbm, low_hbm, diagonal_hbm, direction_ref, norm_ref, dosage_high_ref,
                 dosage_low_ref, *refs):
    received_refs = refs[:devices - 1]
    (scaled_hbm, handled_hbm, outgoing_hbm, even_hbm, odd_hbm, gathered_ref, high_ref, low_ref, diagonal_ref, scaled_ref,
     handled_ref, sums_ref, even_ref, odd_ref, semaphores) = refs[-15:]
    copies = Copies(semaphores)
    loads = [
        copies.start(high_hbm, high_ref), copies.start(low_hbm, low_ref), copies.start(diagonal_hbm, diagonal_ref)
    ]
    gather_received(devices, capacity, received_refs, gathered_ref)
    wait_all(loads)
    block_count, tile, depth = high_ref.shape
    others = depth // tile - 1
    cross = jnp.zeros(norm_ref.shape, jnp.float32)
    for row in range(block_count):
        block = pl.ds(row * tile, tile)
        here = direction_ref[block, :]
        blocks = [here] + [gathered_ref[table_ref[0, row * others + i]] for i in range(others)]
        mapped = product(high_ref[row], low_ref[row], blocks)
        scaled_ref[block, :] = mapped * wide(1.0 / diagonal_ref[block, :], mapped.shape[1])
        cross = cross + column_sums(here * mapped)
    row_ids = lax.broadcasted_iota(jnp.int32, cross.shape, 0)
    sums_ref[...] = jnp.where(row_ids == 1, jnp.sum(cross, axis=0, keepdims=True), norm_ref[...])
    stores = [copies.start(scaled_ref, scaled_hbm)]
    for other in range(devices):
        start = pl.multiple_of(table_ref[3, other] * tile, tile)
        stores.append(copies.start(scaled_ref.at[pl.ds(start, tile)], outgoing_hbm.at[other, pl.ds(0, tile)]))
        stores.append(copies.start(sums_ref, outgoing_hbm.at[other, pl.ds(tile, SUBLANES)]))
    score_products(dosage_high_ref, dosage_low_ref, scaled_ref[...], even_ref, odd_ref)
    stores += [copies.start(odd_ref, odd_hbm), copies.start(even_ref, even_hbm)]
    far = pl.ds(tile, depth - tile)
    for row in range(block_count):
        blocks = []
        for i in range(others):
            weight = table_ref[2, row * others + i].astype(jnp.float32)
            blocks.append(weight * gathered_ref[table_ref[0, row * others + i]])
        handled_ref[pl.ds(row * tile, tile), :] = product(high_ref[row, :, far], low_ref[row, :, far], blocks)
    stores.append(copies.start(handled_ref, handled_hbm))
    wait_all(stores)


def curvature_kernel(devices, table_ref, high_ref, low_ref, direction_hbm, diagonal_hbm, scaled_hbm, handled_hbm,
                     later_ref, *refs):
    sums_ref, direction_ref, diagonal_ref, scaled_ref, handled_ref, semaphores = refs[-6:]
    block_count, tile, depth = high_ref.shape
    copies = Copies(semaphores)
    wait_all([copies.start(source, target) for source, target in (
        (scaled_hbm, scaled_ref), (direction_hbm, direction_ref),
        (handled_hbm, handled_ref), (diagonal_hbm, diagonal_ref),
    )])
    others = depth // tile - 1
    first_sums = later_ref[0, pl.ds(tile, SUBLANES), :]
    for other in range(1, devices):
        first_sums = first_sums + later_ref[other, pl.ds(tile, SUBLANES), :]
    rho = first_sums[1:2, :] / first_sums[0:1, :]
    norm = jnp.zeros(first_sums.shape, jnp.float32)
    bend = jnp.zeros(first_sums.shape, jnp.float32)
    for row in range(block_count):
        block = pl.ds(row * tile, tile)
        here = scaled_ref[block, :] - rho * direction_ref[block, :]
        blocks = [here]
        for i in range(others):
            entry = row * others + i
            weight = table_ref[2, entry].astype(jnp.float32)
            blocks.append(weight * later_ref[table_ref[1, entry], pl.ds(0, tile), :])
        mapped = product(high_ref[row], low_ref[row], blocks) - rho * handled_ref[block, :]
        norm = norm + column_sums(here * here * wide(diagonal_ref[block, :], here.shape[1]))
        bend = bend + column_sums(here * mapped)
    row_ids = lax.broadcasted_iota(jnp.int32, first_sums.shape, 0)
    sums = jnp.where(row_ids == 2, jnp.sum(norm, axis=0, keepdims=True), first_sums)
    sums = jnp.where(row_ids == 3, jnp.sum(bend, axis=0, keepdims=True), sums)
    for i in range(2 * devices):
        sums_ref[i] = sums


def add_kernel(kept_ref, taken_ref, *refs):
    near_ref, far_ref = refs[-2:]
    count = near_ref.shape[0]
    near_ref[...] = kept_ref[pl.ds(0, count)] + taken_ref[pl.ds(0, count)]
    far_ref[...] = kept_ref[pl.ds(count, count)] + taken_ref[pl.ds(count, count)]


def last_add_kernel(first_kept_ref, first_taken_ref, second_kept_ref, second_taken_ref, own_ref, other_ref):
    rows = own_ref.shape[1]
    for i, (kept_ref, taken_ref) in enumerate(
        ((first_kept_ref, first_taken_ref), (second_kept_ref, second_taken_ref))
    ):
        own_ref[i] = kept_ref[0, pl.ds(0, rows), :] + taken_ref[0, pl.ds(0, rows), :]
        other_ref[i] = kept_ref[0, pl.ds(rows, rows), :] + taken_ref[0, pl.ds(rows, rows), :]


def group_kernel(order, own_ref, other_ref, high_ref, low_ref):
    rows = own_ref.shape[0] // (2 * len(order))
    me = lax.axis_index("samples")
    for odd in range(2):
        for i, distance in enumerate(order):
            start = pl.multiple_of((me ^ distance ^ odd) * rows, rows)
            for j, dosage_ref in enumerate((own_ref, other_ref)):
                high, low = split(dosage_ref[pl.ds(start, rows), :])
                here = pl.ds((2 * i + j) * rows, rows)
                high_ref[odd, here, :] = high
                low_ref[odd, here, :] = low


def coefficients(sums, shared):
    norm, cross = sums[0:1, :], sums[1:2, :]
    later_norm, bend = shared[2:3, :], shared[3:4, :]
    curve = norm + cross
    ratio = later_norm / curve
    step = jnp.where(later_norm > 0, later_norm / (later_norm + bend - later_norm * ratio), 0.0)
    start = norm / curve
    return start * (1.0 + step * (ratio + cross / norm)), -start * step


def solved_kernel(devices, direction_ref, scaled_ref, sums_ref, solved_hbm, factors_ref, solved_ref, semaphores):
    people, columns = direction_ref.shape
    column = lax.axis_index("cols")
    copies = Copies(semaphores)

    def total(which):
        sums = sums_ref[which]
        shared = sums
        for i in range(1, devices):
            shared = shared + sums_ref[2 * i + which]
        return sums, shared

    along, across = coefficients(*total(column))
    factors = jnp.concatenate([along, across, *coefficients(*total(1 - column))], axis=0)
    factors_ref[...] = jnp.concatenate([factors, factors], axis=0)
    stores = []
    part_rows = people // 4
    for part in range(4):
        block = pl.ds(part * part_rows, part_rows)
        solved_ref[block, :] = along * direction_ref[block, :] + across * scaled_ref[block, :]
        stores.append(copies.start(solved_ref.at[block], solved_hbm.at[block]))
    wait_all(stores)


def scores_kernel(norm_scale, factors_ref, own_ref, other_ref, scores_ref):
    columns = own_ref.shape[2]
    column = lax.axis_index("cols")
    for which, rows_ref, place in ((0, own_ref, column), (2, other_ref, 1 - column)):
        along, across = factors_ref[which:which + 1, :], factors_ref[which + 1:which + 2, :]
        here = pl.ds(pl.multiple_of(place * columns, columns), columns)
        scores_ref[:, here] = norm_scale * (along * rows_ref[0] + across * rows_ref[1])


def call(kernel, out_shape, in_specs, out_specs, scratch_shapes=(), limit=VMEM_LIMIT):
    return pl.pallas_call(
        kernel,
        out_shape=out_shape,
        in_specs=in_specs,
        out_specs=out_specs,
        scratch_shapes=list(scratch_shapes),
        compiler_params=pltpu.CompilerParams(vmem_limit_bytes=limit),
    )


def swap(values, axis, devices, step):
    return lax.ppermute(values, axis, [(i, i ^ step) for i in range(devices)])


def after(value, *others):
    return lax.optimization_barrier((value, *others))[0]


def per_device(kinship, relatives, variance, phenotypes, dosage):
    devices = lax.axis_size("samples")
    block_count, positions, tile = kinship.shape[:3]
    people, columns = phenotypes.shape
    variants = dosage.shape[1]
    share_rows = variants // devices
    entries = block_count * (positions - 1)
    capacity = -(-entries // (devices - 1))
    assert capacity <= 2
    hbm = pl.BlockSpec(memory_space=pltpu.HBM)
    anywhere = pl.BlockSpec(memory_space=pl.ANY)
    vmem = pl.BlockSpec(memory_space=pltpu.VMEM)
    smem = pl.BlockSpec(memory_space=pltpu.SMEM)
    float_of = lambda *shape: jax.ShapeDtypeStruct(shape, jnp.float32)
    room = lambda *shape: pltpu.VMEM(shape, jnp.float32)
    full = float_of(people, columns)
    full_room = room(people, columns)
    half = devices // 2
    near_by = list(range(half - 1, 0, -1))
    at_home = lambda *arrays: [pltpu.with_memory_space_constraint(array, pltpu.HBM) for array in arrays]
    kinship, = at_home(kinship)
    tiles_room = pltpu.VMEM((block_count, tile, positions * tile), jnp.bfloat16)
    tiles_out = pltpu.HBM((block_count, tile, positions * tile), jnp.bfloat16)
    full_out = pltpu.HBM((people, columns), jnp.float32)
    direction, direction_kept_hbm, diagonal, norm = call(
        direction_kernel,
        [full, full_out, pltpu.HBM((people, LANES), jnp.float32), float_of(SUBLANES, columns)],
        [hbm] * 3,
        [vmem, hbm, hbm, vmem],
        [
            room(*kinship.shape), room(block_count, tile), full_room, room(people, LANES),
            pltpu.SemaphoreType.DMA((3 * block_count + 2,)),
        ],
    )(
        kinship, *at_home(variance.reshape(block_count, tile), phenotypes)
    )
    def to_mates(blocks):
        return [swap(blocks[k - 1], "samples", devices, k) for k in near_by]

    bits = half.bit_length() - 1
    even = [sum(((i >> b) & 1) << (bits - b) for b in range(bits)) for i in range(half)]
    steps = [2 << i for i in range(bits)]
    other_dosage = with_layout_constraint(swap(after(dosage, direction), "cols", 2, 1), Layout((0, 1)))
    table, forward, *outgoing = call(
        functools.partial(route_kernel, devices, capacity, block_count),
        [
            jax.ShapeDtypeStruct((4, max(entries, devices)), jnp.int32),
            jax.ShapeDtypeStruct((capacity, half), jnp.int32),
        ] + [float_of(capacity, tile, columns)] * (half - 1),
        [smem, vmem, anywhere],
        [smem, smem] + [vmem] * (half - 1),
        [pltpu.SMEM((devices,), jnp.int32), pltpu.SMEM((devices,), jnp.int32)],
    )(relatives.T, direction, other_dosage)
    high, low = call(
        tiles_kernel, [tiles_out] * 2, [hbm], [hbm] * 2,
        [room(*kinship.shape), tiles_room, tiles_room, pltpu.SemaphoreType.DMA((3,))],
    )(kinship)

    parts = jax.ShapeDtypeStruct((2, variants, people), jnp.bfloat16)
    large = VMEM_LIMIT if variants <= people else LARGE_VMEM
    grouped = call(
        functools.partial(group_kernel, even), [parts] * 2, [vmem] * 2, [vmem] * 2, limit=large
    )(after(dosage, table).T, other_dosage.T)

    products = float_of(half, 2 * share_rows, columns)

    def add_step(kept, taken, *gates):
        rows = float_of(kept.shape[0] // 2, 2 * share_rows, columns)
        return call(
            add_kernel, [rows] * 2, [vmem] * (2 + len(gates)), [vmem] * 2
        )(kept, taken, *gates)

    partner = swap(direction, "samples", devices, half)
    near = to_mates(outgoing)
    direction_even, direction_odd = call(
        score_kernel, [products] * 2, [vmem] * 3, [vmem] * 2, limit=large
    )(*grouped, direction)
    direction_share = swap(direction_odd, "samples", devices, 1)
    far = to_mates(call(
        forward_kernel,
        [float_of(capacity, tile, columns)] * (half - 1),
        [smem, vmem] + [anywhere] * (half + 1) + [hbm] * 2,
        [vmem] * (half - 1),
    )(forward, partner, *near, direction_even, direction_odd, *at_home(high, low)))
    received = near + far + [partner.reshape(block_count, tile, columns)]
    products_out = pltpu.HBM(products.shape, jnp.float32)
    scaled, handled, outgoing, scaled_even, scaled_odd = call(
        functools.partial(apply_kernel, devices, capacity),
        [
            full_out, full_out, pltpu.HBM((devices, tile + SUBLANES, columns), jnp.float32), products_out, products_out,
        ],
        [smem, hbm, hbm, hbm] + [vmem] * (devices + 3) + [anywhere],
        [hbm] * 5,
        [
            room(devices * capacity + block_count, tile, columns), tiles_room, tiles_room, room(people, LANES), full_room,
            full_room, room(SUBLANES, columns), room(*products.shape), room(*products.shape),
            pltpu.SemaphoreType.DMA((2 * devices + 7,)),
        ],
        limit=large,
    )(table, high, low, diagonal, direction, norm, *grouped, *received, direction_share)
    later = lax.all_to_all(outgoing, "samples", split_axis=0, concat_axis=0, tiled=True)
    scaled_share = swap(scaled_odd, "samples", devices, 1)
    direction_kept, direction_given = add_step(direction_even, direction_share)
    direction_taken = swap(after(direction_given, scaled), "samples", devices, steps[0])
    scaled_kept, scaled_given = add_step(scaled_even, scaled_share)
    scaled_taken = swap(scaled_given, "samples", devices, steps[0])
    sums = call(
        functools.partial(curvature_kernel, devices),
        float_of(2 * devices, SUBLANES, columns),
        [smem, vmem, vmem] + [hbm] * 4 + [vmem, anywhere],
        vmem,
        [full_room, room(people, LANES), full_room, full_room, pltpu.SemaphoreType.DMA((4,))],
    )(table, high, low, *at_home(direction_kept_hbm, diagonal, scaled, handled), later, scaled_given)
    all_sums = lax.all_to_all(sums, ("samples", "cols"), split_axis=0, concat_axis=0, tiled=True)
    for step in steps[1:]:
        scaled_kept, scaled_given = add_step(scaled_kept, scaled_taken, sums)
        scaled_taken = swap(scaled_given, "samples", devices, step)
    for step in steps[1:]:
        direction_kept, direction_given = add_step(direction_kept, direction_taken, sums)
        direction_taken = swap(direction_given, "samples", devices, step)
    rows = float_of(2, share_rows, columns)
    own_scores, other_scores = call(
        last_add_kernel, [rows] * 2, [vmem] * 4, [vmem] * 2
    )(direction_kept, direction_taken, scaled_kept, scaled_taken)
    solved, factors = call(
        functools.partial(solved_kernel, devices),
        [full, float_of(SUBLANES, columns)],
        [vmem] * 3,
        [hbm, vmem],
        [full_room, pltpu.SemaphoreType.DMA((4,))],
    )(direction_kept_hbm, scaled, all_sums)
    scores = call(
        functools.partial(scores_kernel, 1.0 / math.sqrt(people * devices)),
        float_of(share_rows, 2 * columns), [vmem] * 3, vmem,
    )(factors, own_scores, swap(other_scores, "cols", 2, 1))
    return (solved, scores)


def solution(mesh):
    return jax.shard_map(
        per_device,
        mesh=mesh,
        in_specs=(
            P(("groups", "samples"), None, None, None),
            P("groups", None),
            P(("groups", "samples")),
            P(("groups", "samples"), "cols"),
            P(("groups", "samples"), "cols"),
        ),
        out_specs=(P(("groups", "samples"), "cols"), P(("groups", "cols", "samples"), None)),
        check_vma=False,
    )
```

```python
import functools
import math

import jax
import jax.numpy as jnp
from jax import lax
from jax.experimental import pallas as pl
from jax.experimental.layout import Layout, with_layout_constraint
from jax.experimental.pallas import tpu as pltpu
from jax.sharding import PartitionSpec as P

VMEM_LIMIT = 24 * 1024 * 1024
LARGE_VMEM = 56 * 1024 * 1024
SUBLANES = 8
LANES = 128


def split(values):
    high = values.astype(jnp.bfloat16)
    low = (values - high.astype(jnp.float32)).astype(jnp.bfloat16)
    return high, low


def dot(left, right):
    return jnp.dot(left, right, preferred_element_type=jnp.float32)


def on_diagonal(size):
    rows = lax.broadcasted_iota(jnp.int32, (size, size), 0)
    return rows == lax.broadcasted_iota(jnp.int32, (size, size), 1)


def wide(values, columns):
    return jnp.concatenate([values] * (columns // LANES), axis=1)


def split_tiles(kinship_ref, high_ref, low_ref):
    block_count, positions, tile = kinship_ref.shape[:3]
    diagonal_mask = on_diagonal(tile)
    for row in range(block_count):
        for position in range(positions):
            values = kinship_ref[row, position]
            if position == 0:
                values = jnp.where(diagonal_mask, 0.0, values)
            high, low = split(values)
            high_ref[row, :, pl.ds(position * tile, tile)] = high
            low_ref[row, :, pl.ds(position * tile, tile)] = low


def product(high, low, blocks):
    parts = [split(block) for block in blocks]
    blocks_high = jnp.concatenate([part[0] for part in parts], axis=0)
    blocks_low = jnp.concatenate([part[1] for part in parts], axis=0)
    return dot(high, blocks_high) + (dot(low, blocks_high) + dot(high, blocks_low))


def column_sums(values):
    rows, columns = values.shape
    return jnp.sum(values.reshape(rows // SUBLANES, SUBLANES, columns), axis=0)


class Copies:
    def __init__(self, semaphores):
        self.semaphores = semaphores
        self.count = 0

    def start(self, source, target):
        copy = pltpu.make_async_copy(source, target, self.semaphores.at[self.count])
        self.count += 1
        copy.start()
        return copy


def wait_all(copies):
    for copy in copies:
        copy.wait()


def quotient(value, divisor):
    if divisor & (divisor - 1) == 0:
        return lax.shift_right_logical(value, jnp.int32(divisor.bit_length() - 1))
    return lax.div(value, jnp.int32(divisor))


def direction_kernel(kinship_hbm, variance_hbm, phenotypes_hbm, direction_ref, direction_hbm, diagonal_hbm, sums_ref,
                     kinship_ref, variance_ref, phenotypes_ref, diagonal_ref, semaphores):
    block_count, positions, tile = kinship_ref.shape[:3]
    copies = Copies(semaphores)
    loads = [copies.start(variance_hbm, variance_ref)]
    for row in range(block_count):
        block = pl.ds(row * tile, tile)
        loads.append(copies.start(kinship_hbm.at[row], kinship_ref.at[row]))
        loads.append(copies.start(phenotypes_hbm.at[block], phenotypes_ref.at[block]))
    stores = []
    norm = jnp.zeros((SUBLANES, direction_ref.shape[1]), jnp.float32)
    diagonal_mask = on_diagonal(tile)
    loads[0].wait()
    for row in range(block_count):
        wait_all(loads[1 + 2 * row:3 + 2 * row])
        block = pl.ds(row * tile, tile)
        total = jnp.where(diagonal_mask, variance_ref[row:row + 1, :], kinship_ref[row, 0])
        for position in range(1, positions):
            total = total + kinship_ref[row, position]
        diagonal = jnp.sum(total, axis=1, keepdims=True)
        diagonal_ref[block, :] = jnp.broadcast_to(diagonal, (tile, LANES))
        here = phenotypes_ref[block, :] * (1.0 / diagonal)
        direction_ref[block, :] = here
        norm = norm + column_sums(here * phenotypes_ref[block, :])
        stores.append(copies.start(direction_ref.at[block], direction_hbm.at[block]))
    stores.append(copies.start(diagonal_ref, diagonal_hbm))
    row_ids = lax.broadcasted_iota(jnp.int32, norm.shape, 0)
    sums_ref[...] = jnp.where(row_ids == 0, jnp.sum(norm, axis=0, keepdims=True), 0.0)
    wait_all(stores)


def tiles_kernel(kinship_hbm, high_hbm, low_hbm, kinship_ref, high_ref, low_ref, semaphores):
    copies = Copies(semaphores)
    copies.start(kinship_hbm, kinship_ref).wait()
    split_tiles(kinship_ref, high_ref, low_ref)
    wait_all([copies.start(high_ref, high_hbm), copies.start(low_ref, low_hbm)])


def route_kernel(devices, capacity, block_count, list_ref, direction_ref, gate_ref, table_ref, forward_ref, *refs):
    half = devices // 2
    outgoing_refs, (first_ref, last_ref) = refs[:half - 1], refs[half - 1:]
    positions = list_ref.shape[0] + 1
    tile = direction_ref.shape[0] // block_count
    me = lax.axis_index("samples")
    partner = me ^ half
    spare = me ^ 1
    top = block_count * block_count

    def collect(device):
        for j in range(devices):
            first_ref[j] = jnp.int32(top)
            last_ref[j] = jnp.int32(-1)
        found = []
        for row in range(block_count):
            for position in range(positions - 1):
                listed = list_ref[position, device * block_count + row]
                live = listed >= 0
                safe = jnp.maximum(listed, 0)
                other = quotient(safe, block_count)
                far_block = safe - other * block_count
                key = jnp.where(device < other, row * block_count + far_block, far_block * block_count + row)
                first_ref[other] = jnp.minimum(first_ref[other], jnp.where(live, key, top))
                last_ref[other] = jnp.maximum(last_ref[other], jnp.where(live, key, -1))
                found.append((live, other, far_block, key))
        return found

    def blocks_for(device, other):
        blocks = []
        for key in (first_ref[other], last_ref[other]):
            safe = jnp.clip(key, 0, top - 1)
            lower = quotient(safe, block_count)
            higher = safe - lower * block_count
            blocks.append(jnp.where(key == safe, jnp.where(device < other, lower, higher), 0))
        return blocks

    collect(partner)
    for k in range(1, half):
        blocks = blocks_for(partner, me ^ k)
        for slot in range(capacity):
            forward_ref[slot, k] = blocks[slot]
    for entry, (live, other, far_block, key) in enumerate(collect(me)):
        first, last = first_ref[other], last_ref[other]
        handled = jnp.where(me < other, first, last)
        weight = jnp.where(first == last, 1, 2)
        slot = jnp.where(key == first, 0, capacity - 1)
        place = jnp.where(other == partner, devices * capacity + far_block, other * capacity + slot)
        table_ref[0, entry] = jnp.where(live, place, spare * capacity)
        table_ref[1, entry] = jnp.where(live, other, spare)
        table_ref[2, entry] = jnp.where(live & (key == handled), weight, 0)
    for other in range(devices):
        blocks = blocks_for(me, other)
        table_ref[3, other] = jnp.where(me < other, blocks[1], blocks[0])
    near = [blocks_for(me, me ^ k) for k in range(1, half)]
    for k in range(1, half):
        for slot in range(capacity):
            start = pl.multiple_of(near[k - 1][slot] * tile, tile)
            outgoing_refs[k - 1][slot] = direction_ref[pl.ds(start, tile), :]


def forward_kernel(forward_ref, partner_ref, *refs):
    capacity, half = forward_ref.shape
    outgoing_refs = refs[1 - half:]
    tile = outgoing_refs[0].shape[1]
    for k in range(1, half):
        for slot in range(capacity):
            start = pl.multiple_of(forward_ref[slot, k] * tile, tile)
            outgoing_refs[k - 1][slot] = partner_ref[pl.ds(start, tile), :]


def gather_received(devices, capacity, received_refs, gathered_ref):
    half = devices // 2
    me = lax.axis_index("samples")
    near_refs, far_refs, partner_ref = received_refs[:half - 1], received_refs[half - 1:-1], received_refs[-1]
    gathered_ref[pl.ds(devices * capacity, partner_ref.shape[0])] = partner_ref[...]
    for i in range(half - 1):
        mate = me ^ (half - 1 - i)
        gathered_ref[pl.ds(mate * capacity, capacity)] = near_refs[i][...]
        gathered_ref[pl.ds((mate ^ half) * capacity, capacity)] = far_refs[i][...]


def score_products(high_ref, low_ref, values, even_ref, odd_ref):
    count, rows = even_ref.shape[:2]
    for odd, out_ref in enumerate((even_ref, odd_ref)):
        for i in range(0, count, 4):
            here = pl.ds(i * rows, 4 * rows)
            total = product(high_ref[odd, here, :], low_ref[odd, here, :], [values])
            out_ref[pl.ds(i, 4)] = total.reshape(4, rows, -1)


def score_kernel(high_ref, low_ref, values_ref, even_ref, odd_ref):
    score_products(high_ref, low_ref, values_ref[...], even_ref, odd_ref)


def apply_kernel(devices, capacity, table_ref, high_hbm, low_hbm, diagonal_hbm, direction_ref, norm_ref, dosage_high_ref,
                 dosage_low_ref, *refs):
    received_refs = refs[:devices - 1]
    (scaled_hbm, handled_hbm, outgoing_hbm, even_hbm, odd_hbm, gathered_ref, high_ref, low_ref, diagonal_ref, scaled_ref,
     handled_ref, sums_ref, even_ref, odd_ref, semaphores) = refs[-15:]
    copies = Copies(semaphores)
    loads = [
        copies.start(high_hbm, high_ref), copies.start(low_hbm, low_ref), copies.start(diagonal_hbm, diagonal_ref)
    ]
    gather_received(devices, capacity, received_refs, gathered_ref)
    wait_all(loads)
    block_count, tile, depth = high_ref.shape
    others = depth // tile - 1
    cross = jnp.zeros(norm_ref.shape, jnp.float32)
    for row in range(block_count):
        block = pl.ds(row * tile, tile)
        here = direction_ref[block, :]
        blocks = [here] + [gathered_ref[table_ref[0, row * others + i]] for i in range(others)]
        mapped = product(high_ref[row], low_ref[row], blocks)
        scaled_ref[block, :] = mapped * wide(1.0 / diagonal_ref[block, :], mapped.shape[1])
        cross = cross + column_sums(here * mapped)
    row_ids = lax.broadcasted_iota(jnp.int32, cross.shape, 0)
    sums_ref[...] = jnp.where(row_ids == 1, jnp.sum(cross, axis=0, keepdims=True), norm_ref[...])
    stores = [copies.start(scaled_ref, scaled_hbm)]
    for other in range(devices):
        start = pl.multiple_of(table_ref[3, other] * tile, tile)
        stores.append(copies.start(scaled_ref.at[pl.ds(start, tile)], outgoing_hbm.at[other, pl.ds(0, tile)]))
        stores.append(copies.start(sums_ref, outgoing_hbm.at[other, pl.ds(tile, SUBLANES)]))
    score_products(dosage_high_ref, dosage_low_ref, scaled_ref[...], even_ref, odd_ref)
    stores += [copies.start(odd_ref, odd_hbm), copies.start(even_ref, even_hbm)]
    far = pl.ds(tile, depth - tile)
    for row in range(block_count):
        blocks = []
        for i in range(others):
            weight = table_ref[2, row * others + i].astype(jnp.float32)
            blocks.append(weight * gathered_ref[table_ref[0, row * others + i]])
        handled_ref[pl.ds(row * tile, tile), :] = product(high_ref[row, :, far], low_ref[row, :, far], blocks)
    stores.append(copies.start(handled_ref, handled_hbm))
    wait_all(stores)


def curvature_kernel(devices, table_ref, high_hbm, low_hbm, direction_hbm, diagonal_hbm, scaled_hbm, handled_hbm,
                     later_ref, *refs):
    sums_ref, high_ref, low_ref, direction_ref, diagonal_ref, scaled_ref, handled_ref, semaphores = refs[-8:]
    block_count, tile, depth = high_ref.shape
    copies = Copies(semaphores)
    wait_all([copies.start(source, target) for source, target in (
        (scaled_hbm, scaled_ref), (direction_hbm, direction_ref), (high_hbm, high_ref), (low_hbm, low_ref),
        (handled_hbm, handled_ref), (diagonal_hbm, diagonal_ref),
    )])
    others = depth // tile - 1
    first_sums = later_ref[0, pl.ds(tile, SUBLANES), :]
    for other in range(1, devices):
        first_sums = first_sums + later_ref[other, pl.ds(tile, SUBLANES), :]
    rho = first_sums[1:2, :] / first_sums[0:1, :]
    norm = jnp.zeros(first_sums.shape, jnp.float32)
    bend = jnp.zeros(first_sums.shape, jnp.float32)
    for row in range(block_count):
        block = pl.ds(row * tile, tile)
        here = scaled_ref[block, :] - rho * direction_ref[block, :]
        blocks = [here]
        for i in range(others):
            entry = row * others + i
            weight = table_ref[2, entry].astype(jnp.float32)
            blocks.append(weight * later_ref[table_ref[1, entry], pl.ds(0, tile), :])
        mapped = product(high_ref[row], low_ref[row], blocks) - rho * handled_ref[block, :]
        norm = norm + column_sums(here * here * wide(diagonal_ref[block, :], here.shape[1]))
        bend = bend + column_sums(here * mapped)
    row_ids = lax.broadcasted_iota(jnp.int32, first_sums.shape, 0)
    sums = jnp.where(row_ids == 2, jnp.sum(norm, axis=0, keepdims=True), first_sums)
    sums = jnp.where(row_ids == 3, jnp.sum(bend, axis=0, keepdims=True), sums)
    for i in range(2 * devices):
        sums_ref[i] = sums


def add_kernel(kept_ref, taken_ref, *refs):
    near_ref, far_ref = refs[-2:]
    count = near_ref.shape[0]
    near_ref[...] = kept_ref[pl.ds(0, count)] + taken_ref[pl.ds(0, count)]
    far_ref[...] = kept_ref[pl.ds(count, count)] + taken_ref[pl.ds(count, count)]


def last_add_kernel(first_kept_ref, first_taken_ref, second_kept_ref, second_taken_ref, own_ref, other_ref):
    rows = own_ref.shape[1]
    for i, (kept_ref, taken_ref) in enumerate(
        ((first_kept_ref, first_taken_ref), (second_kept_ref, second_taken_ref))
    ):
        own_ref[i] = kept_ref[0, pl.ds(0, rows), :] + taken_ref[0, pl.ds(0, rows), :]
        other_ref[i] = kept_ref[0, pl.ds(rows, rows), :] + taken_ref[0, pl.ds(rows, rows), :]


def group_kernel(order, own_ref, other_ref, high_ref, low_ref):
    rows = own_ref.shape[0] // (2 * len(order))
    me = lax.axis_index("samples")
    for odd in range(2):
        for i, distance in enumerate(order):
            start = pl.multiple_of((me ^ distance ^ odd) * rows, rows)
            for j, dosage_ref in enumerate((own_ref, other_ref)):
                high, low = split(dosage_ref[pl.ds(start, rows), :])
                here = pl.ds((2 * i + j) * rows, rows)
                high_ref[odd, here, :] = high
                low_ref[odd, here, :] = low


def coefficients(sums, shared):
    norm, cross = sums[0:1, :], sums[1:2, :]
    later_norm, bend = shared[2:3, :], shared[3:4, :]
    curve = norm + cross
    ratio = later_norm / curve
    step = jnp.where(later_norm > 0, later_norm / (later_norm + bend - later_norm * ratio), 0.0)
    start = norm / curve
    return start * (1.0 + step * (ratio + cross / norm)), -start * step


def solved_kernel(devices, direction_ref, scaled_ref, sums_ref, solved_hbm, factors_ref, solved_ref, semaphores):
    people, columns = direction_ref.shape
    column = lax.axis_index("cols")
    copies = Copies(semaphores)

    def total(which):
        sums = sums_ref[which]
        shared = sums
        for i in range(1, devices):
            shared = shared + sums_ref[2 * i + which]
        return sums, shared

    along, across = coefficients(*total(column))
    factors = jnp.concatenate([along, across, *coefficients(*total(1 - column))], axis=0)
    factors_ref[...] = jnp.concatenate([factors, factors], axis=0)
    stores = []
    part_rows = people // 4
    for part in range(4):
        block = pl.ds(part * part_rows, part_rows)
        solved_ref[block, :] = along * direction_ref[block, :] + across * scaled_ref[block, :]
        stores.append(copies.start(solved_ref.at[block], solved_hbm.at[block]))
    wait_all(stores)


def scores_kernel(norm_scale, factors_ref, own_ref, other_ref, scores_ref):
    columns = own_ref.shape[2]
    column = lax.axis_index("cols")
    for which, rows_ref, place in ((0, own_ref, column), (2, other_ref, 1 - column)):
        along, across = factors_ref[which:which + 1, :], factors_ref[which + 1:which + 2, :]
        here = pl.ds(pl.multiple_of(place * columns, columns), columns)
        scores_ref[:, here] = norm_scale * (along * rows_ref[0] + across * rows_ref[1])


def call(kernel, out_shape, in_specs, out_specs, scratch_shapes=(), limit=VMEM_LIMIT):
    return pl.pallas_call(
        kernel,
        out_shape=out_shape,
        in_specs=in_specs,
        out_specs=out_specs,
        scratch_shapes=list(scratch_shapes),
        compiler_params=pltpu.CompilerParams(vmem_limit_bytes=limit),
    )


def swap(values, axis, devices, step):
    return lax.ppermute(values, axis, [(i, i ^ step) for i in range(devices)])


def after(value, *others):
    return lax.optimization_barrier((value, *others))[0]


def per_device(kinship, relatives, variance, phenotypes, dosage):
    devices = lax.axis_size("samples")
    block_count, positions, tile = kinship.shape[:3]
    people, columns = phenotypes.shape
    variants = dosage.shape[1]
    share_rows = variants // devices
    entries = block_count * (positions - 1)
    capacity = -(-entries // (devices - 1))
    assert capacity <= 2
    hbm = pl.BlockSpec(memory_space=pltpu.HBM)
    anywhere = pl.BlockSpec(memory_space=pl.ANY)
    vmem = pl.BlockSpec(memory_space=pltpu.VMEM)
    smem = pl.BlockSpec(memory_space=pltpu.SMEM)
    float_of = lambda *shape: jax.ShapeDtypeStruct(shape, jnp.float32)
    room = lambda *shape: pltpu.VMEM(shape, jnp.float32)
    full = float_of(people, columns)
    full_room = room(people, columns)
    half = devices // 2
    near_by = list(range(half - 1, 0, -1))
    at_home = lambda *arrays: [pltpu.with_memory_space_constraint(array, pltpu.HBM) for array in arrays]
    kinship, = at_home(kinship)
    tiles_room = pltpu.VMEM((block_count, tile, positions * tile), jnp.bfloat16)
    tiles_out = pltpu.HBM((block_count, tile, positions * tile), jnp.bfloat16)
    full_out = pltpu.HBM((people, columns), jnp.float32)
    direction, direction_kept_hbm, diagonal, norm = call(
        direction_kernel,
        [full, full_out, pltpu.HBM((people, LANES), jnp.float32), float_of(SUBLANES, columns)],
        [hbm] * 3,
        [vmem, hbm, hbm, vmem],
        [
            room(*kinship.shape), room(block_count, tile), full_room, room(people, LANES),
            pltpu.SemaphoreType.DMA((3 * block_count + 2,)),
        ],
    )(
        kinship, *at_home(variance.reshape(block_count, tile), phenotypes)
    )
    def to_mates(blocks):
        return [swap(blocks[k - 1], "samples", devices, k) for k in near_by]

    bits = half.bit_length() - 1
    even = [sum(((i >> b) & 1) << (bits - b) for b in range(bits)) for i in range(half)]
    steps = [2 << i for i in range(bits)]
    other_dosage = with_layout_constraint(swap(after(dosage, direction), "cols", 2, 1), Layout((0, 1)))
    table, forward, *outgoing = call(
        functools.partial(route_kernel, devices, capacity, block_count),
        [
            jax.ShapeDtypeStruct((4, max(entries, devices)), jnp.int32),
            jax.ShapeDtypeStruct((capacity, half), jnp.int32),
        ] + [float_of(capacity, tile, columns)] * (half - 1),
        [smem, vmem, anywhere],
        [smem, smem] + [vmem] * (half - 1),
        [pltpu.SMEM((devices,), jnp.int32), pltpu.SMEM((devices,), jnp.int32)],
    )(relatives.T, direction, other_dosage)
    high, low = call(
        tiles_kernel, [tiles_out] * 2, [hbm], [hbm] * 2,
        [room(*kinship.shape), tiles_room, tiles_room, pltpu.SemaphoreType.DMA((3,))],
    )(kinship)

    parts = jax.ShapeDtypeStruct((2, variants, people), jnp.bfloat16)
    large = VMEM_LIMIT if variants <= people else LARGE_VMEM
    grouped = call(
        functools.partial(group_kernel, even), [parts] * 2, [vmem] * 2, [vmem] * 2, limit=large
    )(after(dosage, table).T, other_dosage.T)

    products = float_of(half, 2 * share_rows, columns)

    def add_step(kept, taken, *gates):
        rows = float_of(kept.shape[0] // 2, 2 * share_rows, columns)
        return call(
            add_kernel, [rows] * 2, [vmem] * (2 + len(gates)), [vmem] * 2
        )(kept, taken, *gates)

    partner = swap(direction, "samples", devices, half)
    near = to_mates(outgoing)
    direction_even, direction_odd = call(
        score_kernel, [products] * 2, [vmem] * 3, [vmem] * 2, limit=large
    )(*grouped, direction)
    direction_share = swap(direction_odd, "samples", devices, 1)
    far = to_mates(call(
        forward_kernel,
        [float_of(capacity, tile, columns)] * (half - 1),
        [smem, vmem] + [anywhere] * (half + 1) + [hbm] * 2,
        [vmem] * (half - 1),
    )(forward, partner, *near, direction_even, direction_odd, *at_home(high, low)))
    received = near + far + [partner.reshape(block_count, tile, columns)]
    products_out = pltpu.HBM(products.shape, jnp.float32)
    scaled, handled, outgoing, scaled_even, scaled_odd = call(
        functools.partial(apply_kernel, devices, capacity),
        [
            full_out, full_out, pltpu.HBM((devices, tile + SUBLANES, columns), jnp.float32), products_out, products_out,
        ],
        [smem, hbm, hbm, hbm] + [vmem] * (devices + 3) + [anywhere],
        [hbm] * 5,
        [
            room(devices * capacity + block_count, tile, columns), tiles_room, tiles_room, room(people, LANES), full_room,
            full_room, room(SUBLANES, columns), room(*products.shape), room(*products.shape),
            pltpu.SemaphoreType.DMA((2 * devices + 7,)),
        ],
        limit=large,
    )(table, high, low, diagonal, direction, norm, *grouped, *received, direction_share)
    later = lax.all_to_all(outgoing, "samples", split_axis=0, concat_axis=0, tiled=True)
    scaled_share = swap(scaled_odd, "samples", devices, 1)
    direction_kept, direction_given = add_step(direction_even, direction_share)
    direction_taken = swap(after(direction_given, scaled), "samples", devices, steps[0])
    scaled_kept, scaled_given = add_step(scaled_even, scaled_share)
    scaled_taken = swap(scaled_given, "samples", devices, steps[0])
    sums = call(
        functools.partial(curvature_kernel, devices),
        float_of(2 * devices, SUBLANES, columns),
        [smem] + [hbm] * 6 + [vmem, anywhere],
        vmem,
        [tiles_room, tiles_room, full_room, room(people, LANES), full_room, full_room, pltpu.SemaphoreType.DMA((6,))],
    )(table, *at_home(high, low, direction_kept_hbm, diagonal, scaled, handled), later, scaled_given)
    all_sums = lax.all_to_all(sums, ("samples", "cols"), split_axis=0, concat_axis=0, tiled=True)
    for step in steps[1:]:
        scaled_kept, scaled_given = add_step(scaled_kept, scaled_taken, sums)
        scaled_taken = swap(scaled_given, "samples", devices, step)
    for step in steps[1:]:
        direction_kept, direction_given = add_step(direction_kept, direction_taken)
        direction_taken = swap(direction_given, "samples", devices, step)
    rows = float_of(2, share_rows, columns)
    own_scores, other_scores = call(
        last_add_kernel, [rows] * 2, [vmem] * 4, [vmem] * 2
    )(direction_kept, direction_taken, scaled_kept, scaled_taken)
    solved, factors = call(
        functools.partial(solved_kernel, devices),
        [full, float_of(SUBLANES, columns)],
        [vmem] * 3,
        [hbm, vmem],
        [full_room, pltpu.SemaphoreType.DMA((4,))],
    )(direction_kept_hbm, scaled, all_sums)
    scores = call(
        functools.partial(scores_kernel, 1.0 / math.sqrt(people * devices)),
        float_of(share_rows, 2 * columns), [vmem] * 3, vmem,
    )(factors, own_scores, swap(other_scores, "cols", 2, 1))
    return (solved, scores)


def solution(mesh):
    return jax.shard_map(
        per_device,
        mesh=mesh,
        in_specs=(
            P(("groups", "samples"), None, None, None),
            P("groups", None),
            P(("groups", "samples")),
            P(("groups", "samples"), "cols"),
            P(("groups", "samples"), "cols"),
        ),
        out_specs=(P(("groups", "samples"), "cols"), P(("groups", "cols", "samples"), None)),
        check_vma=False,
    )
```
